32 devices in a mesh: group: 2 (over y), freq: 4 (over z), rblk: 2 (over x), sblk: 2 (over core).
Axes of the slice: x: 2, y: 2, z: 4, core: 2. Of those that a mesh axis runs over, the one named last changes fastest.
Arguments:
- initial: bfloat16 [256, 512, 512], P(('group', 'sblk'), 'freq', 'rblk'), parts along dimension 0, may hold values from -6 to 6
- response: bfloat16 [16, 2, 2048, 512], P(('group', 'freq'), None, 'sblk', 'rblk'), parts along dimension 0, may hold values from -0.5 to 0.5
- aperture: int32 [16, 16, 4], P(('group', 'freq'), 'sblk', 'rblk'), parts along dimension 0, may hold values from 0 to 1, as said below
- onset_rcv: int32 [256, 512], P('group', 'rblk'), parts along dimension 0, may hold values from 128 to 512
- onset_src: int32 [256, 2048], P('group', 'sblk'), parts along dimension 0, may hold values from 128 to 512
Outputs:
- focusing: bfloat16 [256, 512, 512], P(('group', 'sblk'), 'freq', 'rblk'), parts along dimension 0
The draws below stay inside these ranges and needn't reach their ends.
There are 2 independent parts, one for each index of `group`. The reference program is written for one: setup_inputs(seed, part) draws one part's arguments, and reference() takes and returns one part's arrays. A program takes and returns all parts, laid end to end along the dimension named above; each array names one. Nothing has to cross between parts.
Inputs may be any that keep to these rules, and one draw needn't show every extreme that they name: `aperture`: 1 marks an active source-receiver block pair of that frequency, 0 an inactive one.
All inputs are finite; a program needn't handle non-finite values.
Results may differ from the reference program's by a relative error of at most 0.0085.
Values may be sent and summed in bfloat16 or wider, within the bound.
No kernel may reach another device: no remote copies, remote signals or barrier semaphores. Data moves between devices by JAX's collectives and lax.ppermute only.
A program may use at most 64 MiB of HBM per device.

```python
import math
import jax
import jax.numpy as jnp
from jax import lax

BLOCK = 128
NT = 512
P_SIZE = 128
ITERS = 2
NF = 8
RECV = 512
SRC = 2048
N_RBLK = 2
N_SBLK = 2


def draw_aperture(key, part):
    key = jax.random.fold_in(key, 11)
    depth_levels = jax.random.randint(key, (NF, SRC // BLOCK, RECV // BLOCK), 0, 4)
    order = lax.iota(jnp.int32, NF)
    limit = 1 + 3 * (NF - 1 - order) // NF
    return (depth_levels < limit[:, None, None]).astype(jnp.int32)


def place_ends(drawn, own_key, least, largest):
    longest = drawn.shape.index(max(drawn.shape))
    spots = []
    for shift in (0, 1):
        where = [jax.random.randint(jax.random.fold_in(own_key, axis), (), 0, length) for axis, length in enumerate(drawn.shape)]
        where[longest] = (where[longest] + shift) % drawn.shape[longest]
        spots.append(tuple(where))
    return drawn.at[spots[0]].set(least).at[spots[1]].set(largest)


def block_levels(own_key, shape, cuts, least, largest):
    factor_of = 1.0
    for dim, shards_of in cuts:
        steps = jax.random.uniform(jax.random.fold_in(jax.random.fold_in(own_key, 6), dim), (shards_of,), jnp.float32, least / len(cuts), largest / len(cuts))
        factor_of = factor_of * jnp.repeat(jnp.exp(steps), shape[dim] // shards_of).reshape((-1,) + (1,) * (len(shape) - 1 - dim))
    return factor_of


def noise(key, extent, scale, bound, split=(), kind=jnp.bfloat16):
    gain = block_levels(key, extent, split, -0.22, 0.18) if split else 1.0
    array = jax.random.normal(key, extent, jnp.float32) * scale * gain
    return jnp.minimum(jnp.maximum(array, -bound), bound).astype(kind)


def setup_inputs(seed: int = 0, part: int = 0) -> dict:
    streams_of = jax.random.split(jax.random.key(seed), 6)
    part_keys = jax.random.split(jax.random.fold_in(streams_of[5], part), 6)
    return {
        "initial": noise(part_keys[0], (P_SIZE, NT, RECV), 1.0, 6.0, ((0, 2), (1, 4), (2, 2))),
        "response": noise(part_keys[1], (NF, 2, SRC, RECV), (RECV // 4) ** -0.5, 0.5, ((0, 4), (2, 2), (3, 2))),
        "aperture": draw_aperture(jax.random.fold_in(jax.random.fold_in(streams_of[5], part), 71), part),
        "onset_rcv": place_ends(jax.random.randint(part_keys[3], (P_SIZE, RECV), NT // 4, NT + 1), jax.random.fold_in(part_keys[3], 1), NT // 4, NT).astype(jnp.int32),
        "onset_src": place_ends(jax.random.randint(part_keys[4], (P_SIZE, SRC), NT // 4, NT + 1), jax.random.fold_in(part_keys[4], 1), NT // 4, NT).astype(jnp.int32),
    }


def transform_tables(length, count):
    steps_axis = lax.iota(jnp.int32, length)
    orders = lax.iota(jnp.int32, count) + 1
    phase = (orders[:, None] * steps_axis[None, :]) % length
    angle = phase.astype(jnp.float32) * (2.0 * math.pi / length)
    stacked_fields = jnp.concatenate([jnp.cos(angle), -jnp.sin(angle)], 0)
    forward_table = stacked_fields.astype(jnp.bfloat16)
    inverse_table = (stacked_fields.T * (2.0 / length)).astype(jnp.bfloat16)
    return forward_table, inverse_table


def settle(values):
    return lax.optimization_barrier(values.astype(jnp.bfloat16)).astype(jnp.float32)


def samples_into_spectra(values, forward_table, freq_total):
    out = jnp.einsum("kt,ptn->pkn", forward_table.astype(jnp.float32), values.astype(jnp.float32),
                     precision=lax.Precision.HIGHEST)
    return out.reshape(values.shape[0], 2, freq_total, values.shape[2]).astype(jnp.bfloat16)


def spectra_into_samples(trace_spectra, inverse_table):
    flat = trace_spectra.reshape(trace_spectra.shape[0], -1, trace_spectra.shape[3]).astype(jnp.float32)
    return jnp.einsum("tk,pkn->ptn", inverse_table.astype(jnp.float32), flat, precision=lax.Precision.HIGHEST)


def downgoing_field(gated_traces, trace_spectra):
    focal_all = trace_spectra.shape[0]
    src_width = gated_traces.shape[2]
    by_freq = jnp.moveaxis(trace_spectra, 2, 0)

    def one_freq(pair):
        resp_f, values = pair
        resp_wide = resp_f.astype(jnp.float32).reshape(2, src_width, N_RBLK, -1)
        vals_wide = values.astype(jnp.float32).reshape(focal_all, 2, N_RBLK, -1)
        real_part = (jnp.einsum("sgr,pgr->gps", resp_wide[0], vals_wide[:, 0], precision=lax.Precision.HIGHEST)
                     - jnp.einsum("sgr,pgr->gps", resp_wide[1], vals_wide[:, 1], precision=lax.Precision.HIGHEST))
        imag_part = (jnp.einsum("sgr,pgr->gps", resp_wide[0], vals_wide[:, 1], precision=lax.Precision.HIGHEST)
                     + jnp.einsum("sgr,pgr->gps", resp_wide[1], vals_wide[:, 0], precision=lax.Precision.HIGHEST))
        return jnp.sum(settle(jnp.stack([real_part, imag_part], 2)), 0)

    out = lax.map(one_freq, (gated_traces, by_freq))
    return jnp.transpose(out, (1, 2, 0, 3)).astype(jnp.bfloat16)


def upward(gated_traces, upgoing_spectrum):
    focal_all = upgoing_spectrum.shape[0]
    rcv_width = gated_traces.shape[3]
    by_freq = jnp.moveaxis(upgoing_spectrum, 2, 0)

    def one_freq(pair):
        resp_f, values = pair
        resp_wide = resp_f.astype(jnp.float32).reshape(2, N_SBLK, -1, rcv_width)
        vals_wide = values.astype(jnp.float32).reshape(focal_all, 2, N_SBLK, -1)
        real_part = (jnp.einsum("gsr,pgs->gpr", resp_wide[0], vals_wide[:, 0], precision=lax.Precision.HIGHEST)
                     + jnp.einsum("gsr,pgs->gpr", resp_wide[1], vals_wide[:, 1], precision=lax.Precision.HIGHEST))
        imag_part = (jnp.einsum("gsr,pgs->gpr", resp_wide[0], vals_wide[:, 1], precision=lax.Precision.HIGHEST)
                     - jnp.einsum("gsr,pgs->gpr", resp_wide[1], vals_wide[:, 0], precision=lax.Precision.HIGHEST))
        return jnp.sum(settle(jnp.stack([real_part, imag_part], 2)), 0)

    out = lax.map(one_freq, (gated_traces, by_freq))
    return jnp.transpose(out, (1, 2, 0, 3)).astype(jnp.bfloat16)


def reference(initial, response, aperture, onset_rcv, onset_src):
    samples = initial.shape[1]
    freq_total = response.shape[0]
    forward_table, inverse_table = transform_tables(samples, freq_total)
    mask_full = jnp.repeat(jnp.repeat(aperture, BLOCK, 1), BLOCK, 2).astype(jnp.bfloat16)
    gated_traces = response * mask_full[:, None]
    steps_axis = lax.iota(jnp.int32, samples)
    rcv_gate = (steps_axis[None, :, None] < onset_rcv[:, None, :]).astype(jnp.float32)
    src_gate = (steps_axis[None, :, None] < onset_src[:, None, :]).astype(jnp.float32)
    current = initial
    for step_index in range(ITERS):
        trace_spectra = samples_into_spectra(current, forward_table, freq_total)
        down = downgoing_field(gated_traces, trace_spectra)
        upgoing = (src_gate * spectra_into_samples(down, inverse_table)).astype(jnp.bfloat16)
        upgoing_spectrum = samples_into_spectra(upgoing, forward_table, freq_total)
        back = upward(gated_traces, upgoing_spectrum)
        current = (initial.astype(jnp.float32) - rcv_gate * spectra_into_samples(back, inverse_table)).astype(jnp.bfloat16)
    return current
```

```python
import functools
import math

import jax
import jax.numpy as jnp
import numpy as np
from jax import lax
from jax.experimental import pallas as pl
from jax.experimental.pallas import tpu as pltpu
from jax.sharding import PartitionSpec as P

BLOCK = 128
ITERS = 2
ROWS = 8
CHUNKS = 1
VMEM_BYTES = 48 * 1024 * 1024

BF16 = jnp.bfloat16
F32 = jnp.float32


def field_rows(place, freq_devs, per_dev):
    rows = []
    for step in range(freq_devs):
        first = (place ^ step) * per_dev
        for part in range(2):
            rows.extend((part, first + local) for local in range(per_dev))
    return rows


def fields(samples, freq_total):
    phase = (np.arange(1, freq_total + 1)[:, None] * np.arange(samples)[None, :]) % samples
    angle = phase * (2.0 * math.pi / samples)
    return np.stack([np.cos(angle), -np.sin(angle)])


def forward_tables(samples, freq_devs, per_dev):
    table = fields(samples, freq_devs * per_dev)
    own = samples // freq_devs
    eye = np.eye(ROWS)
    out = []
    for place in range(freq_devs):
        part = np.stack([table[c, j, place * own : (place + 1) * own] for c, j in field_rows(place, freq_devs, per_dev)])
        out.append(np.einsum("kt,pq->kpqt", part, eye).reshape(part.shape[0] * ROWS, ROWS * own))
    return np.stack(out).astype(np.float32).astype(BF16)


def inverse_tables(samples, freq_devs, per_dev):
    table = fields(samples, freq_devs * per_dev) * (2.0 / samples)
    own = samples // freq_devs
    eye = np.eye(ROWS)
    out = []
    for place in range(freq_devs):
        part = np.stack([table[c, j, place * own : (place + 1) * own] for c, j in field_rows(place, freq_devs, per_dev)])
        out.append(np.einsum("kt,pq->ptkq", part, eye).reshape(ROWS * own, part.shape[0] * ROWS))
    return np.stack(out).astype(np.float32).astype(BF16)


def window_tables(samples, freq_devs, per_dev):
    freq_total = freq_devs * per_dev
    order = np.arange(1, freq_total + 1)
    unit = 2j * math.pi / samples
    diff = order[None, :] - order[:, None]
    total = order[None, :] + order[:, None]
    same = np.where(diff == 0, 0.0, 1.0 / (samples * (np.exp(unit * np.where(diff == 0, 1, diff)) - 1.0)))
    mixed = 1.0 / (samples * (np.exp(-unit * total) - 1.0))
    full = np.zeros((2, freq_total, 2, freq_total))
    full[0, :, 0, :] = same.real + mixed.real
    full[0, :, 1, :] = mixed.imag - same.imag
    full[1, :, 0, :] = same.imag + mixed.imag
    full[1, :, 1, :] = same.real - mixed.real
    out = []
    for place in range(freq_devs):
        rows = [c * freq_total + j for c, j in field_rows(place, freq_devs, per_dev)]
        flat = full.reshape(2 * freq_total, 2 * freq_total)[np.ix_(rows, rows)]
        out.append(np.kron(flat, np.eye(ROWS)))
    return np.stack(out).astype(np.float32).astype(BF16)


def call(body, scalars, inputs, outputs, grid, scratch=(), aliases=None, flops=0):
    in_arrays = [value for value, _ in inputs]
    bytes_all = sum(v.size * v.dtype.itemsize for v in in_arrays)
    bytes_all += sum(math.prod(s.shape) * s.dtype.itemsize for s, _ in outputs)
    return pl.pallas_call(
        body,
        grid_spec=pltpu.PrefetchScalarGridSpec(
            num_scalar_prefetch=len(scalars),
            grid=grid,
            in_specs=[spec for _, spec in inputs],
            out_specs=[spec for _, spec in outputs],
            scratch_shapes=list(scratch),
        ),
        out_shape=[shape for shape, _ in outputs],
        input_output_aliases=aliases or {},
        compiler_params=pltpu.CompilerParams(vmem_limit_bytes=VMEM_BYTES),
        cost_estimate=pl.CostEstimate(flops=flops, bytes_accessed=bytes_all, transcendentals=0),
    )(*scalars, *in_arrays)


def whole(array):
    zeros = (0,) * array.ndim
    return pl.BlockSpec(array.shape, lambda *_: zeros)


def mask_half(response, aperture, place, flip, half):
    per_dev, _, src, rcv = response.shape
    src_blocks, rcv_blocks = src // BLOCK, rcv // BLOCK
    steps = half // BLOCK

    def body(place_ref, flags, x_ref, o_ref):
        block = (place_ref[0] ^ flip) * steps + pl.program_id(0)
        for j in range(per_dev):
            for r in range(rcv_blocks):
                on = flags[(j * src_blocks + block) * rcv_blocks + r]
                cut = pl.ds(r * BLOCK, BLOCK)
                value = x_ref[j, :, :, cut]
                o_ref[j, :, :, cut] = value * on.astype(F32).astype(BF16)

    shape = jax.ShapeDtypeStruct((per_dev, 2, half, rcv), BF16)
    block = (per_dev, 2, BLOCK, rcv)
    (out,) = call(
        body,
        (place, aperture.reshape(-1)),
        [(response, pl.BlockSpec(block, lambda i, a, _: (0, 0, (a[0] ^ flip) * steps + i, 0)))],
        [(shape, pl.BlockSpec(block, lambda i, *_: (0, 0, i, 0)))],
        (steps,),
    )
    return out


def first_spectra(initial, table, freq_place, freq_devs, per_dev, first, rows):
    own, rcv = initial.shape[1:]
    tile = 2 * ROWS

    def body(place_ref, x_ref, t_ref, *outs):
        parts = []
        for half in range(2):
            flat = x_ref[half * ROWS : (half + 1) * ROWS].reshape(ROWS * own, rcv)
            value = jnp.dot(t_ref[0], flat, preferred_element_type=F32)
            parts.append(value.reshape(freq_devs, 2, per_dev, ROWS, rcv))
        both = jnp.concatenate(parts, 3).astype(BF16)
        for step, out in enumerate(outs):
            out[...] = both[step]

    shape = jax.ShapeDtypeStruct((2, per_dev, rows, rcv), BF16)
    return call(
        body,
        (freq_place,),
        [
            (initial, pl.BlockSpec((tile, own, rcv), lambda i, _: (first // tile + i, 0, 0))),
            (table, pl.BlockSpec((1,) + table.shape[1:], lambda i, z: (z[0], 0, 0))),
        ],
        [(shape, pl.BlockSpec((2, per_dev, tile, rcv), lambda i, _: (0, 0, i, 0)))] * freq_devs,
        (rows // tile,),
        flops=2 * 2 * freq_devs * per_dev * own * rows * rcv,
    )


def down_products(near, far, kept, moved, freq_place, freq_devs):
    _, per_dev, rows, rcv = near[0].shape
    width = kept.shape[2]
    tile = min(width, 256)
    share = 2 * rows // freq_devs

    def body(place_ref, n0, n1, f0, f1, k_ref, m_ref, *rest):
        outs, held = rest[:freq_devs], rest[freq_devs]
        for j in range(per_dev):
            total = None
            for own, other, resp in ((n0, n1, k_ref), (f0, f1, m_ref)):
                real = jnp.concatenate([own[0, j], other[0, j]], 0)
                imag = jnp.concatenate([own[1, j], other[1, j]], 0)
                for part, lhs in ((0, [real, imag]), (1, [-imag, real])):
                    term = lax.dot_general(
                        jnp.concatenate(lhs, 0),
                        resp[j, part],
                        (((1,), (1,)), ((), ())),
                        preferred_element_type=F32,
                    )
                    total = term if total is None else total + term
            held[0, j] = total[: 2 * rows]
            held[1, j] = total[2 * rows :]
        for step, out in enumerate(outs):
            start = pl.multiple_of((place_ref[0] ^ step) * share, share)
            out[...] = held[:, :, pl.ds(start, share), :].astype(BF16)

    shape = jax.ShapeDtypeStruct((2, per_dev, share, width), BF16)
    resp_spec = pl.BlockSpec((per_dev, 2, tile, rcv), lambda i, _: (0, 0, i, 0))
    return call(
        body,
        (freq_place,),
        [(v, whole(v)) for v in (*near, *far)] + [(kept, resp_spec), (moved, resp_spec)],
        [(shape, pl.BlockSpec((2, per_dev, share, tile), lambda i, _: (0, 0, 0, i)))] * freq_devs,
        (width // tile,),
        scratch=[pltpu.VMEM((2, per_dev, 2 * rows, tile), F32)],
        flops=2 * 8 * per_dev * 2 * rows * width * rcv,
    )


def windowed(messages, tables, matrix, freq_place, per_dev, share):
    cosines, sines, fraction = tables
    freq_devs = len(messages)
    width = messages[0].shape[-1]
    tile = BLOCK
    count = freq_devs * 2 * per_dev * ROWS

    def body(place_ref, c_ref, s_ref, f_ref, g_ref, *rest):
        refs, outs = rest[:freq_devs], rest[freq_devs:]
        data = [ref[...].astype(F32).reshape(2, per_dev, share, tile) for ref in refs]
        made = [[] for _ in outs]
        for first in range(0, share, ROWS):
            cut = slice(first, first + ROWS)
            plain = [value[:, :, cut] for value in data]
            cos = [c_ref[step, :, cut] for step in range(freq_devs)]
            sin = [s_ref[step, :, cut] for step in range(freq_devs)]
            turned = [
                jnp.stack([v[0] * c - v[1] * s, v[0] * s + v[1] * c])
                for v, c, s in zip(plain, cos, sin)
            ]
            flat = [jnp.stack(v).reshape(count, tile).astype(BF16) for v in (turned, plain)]
            mixed = jnp.dot(g_ref[0], jnp.concatenate(flat, 1), preferred_element_type=F32)
            upper = mixed[:, :tile].reshape(freq_devs, 2, per_dev, ROWS, tile)
            lower = mixed[:, tile:].reshape(freq_devs, 2, per_dev, ROWS, tile)
            part = f_ref[cut]
            for step in range(freq_devs):
                c, s, v, up, low = cos[step], sin[step], plain[step], upper[step], lower[step]
                real = c * up[0] + s * up[1] - low[0] + part * v[0]
                imag = c * up[1] - s * up[0] - low[1] + part * v[1]
                made[step].append(jnp.stack([real, imag]))
        for out, value in zip(outs, made):
            out[...] = jnp.concatenate(value, 2).reshape(out.shape).astype(BF16)

    lead = messages[0].shape[:-1]
    zeros = (0,) * len(lead)
    message = pl.BlockSpec(lead + (tile,), lambda i, _: zeros + (i,))
    table = pl.BlockSpec(cosines.shape[:-1] + (tile,), lambda i, _: (0, 0, 0, i))
    return call(
        body,
        (freq_place,),
        [
            (cosines, table),
            (sines, table),
            (fraction, pl.BlockSpec((share, tile), lambda i, _: (0, i))),
            (matrix, pl.BlockSpec((1,) + matrix.shape[1:], lambda i, z: (z[0], 0, 0))),
        ]
        + [(v, message) for v in messages],
        [(jax.ShapeDtypeStruct(v.shape, BF16), message) for v in messages],
        (width // tile,),
        flops=2 * count * count * 2 * width * share // ROWS,
    )


def up_products(messages, kept, moved, freq_place, rows):
    freq_devs = len(messages)
    per_dev, _, src, rcv = kept.shape
    share = messages[0].shape[2]

    def body(place_ref, k_ref, m_ref, *rest):
        refs = rest[:freq_devs]
        keep, send, held = rest[freq_devs:]
        for step, ref in enumerate(refs):
            start = pl.multiple_of((place_ref[0] ^ step) * share, share)
            held[:, pl.ds(start, share), :] = ref[:, 0]
        real, imag = held[0], held[1]
        one = jnp.concatenate([real, imag], 0)
        two = jnp.concatenate([imag, -real], 0)
        for side, resp in enumerate((k_ref, m_ref)):
            total = jnp.dot(one, resp[0, 0], preferred_element_type=F32)
            total = total + jnp.dot(two, resp[0, 1], preferred_element_type=F32)
            for part in range(2):
                first = 2 * rows * part
                keep[side, part, 0] = total[first : first + rows]
                send[side, part, 0] = total[first + rows : first + 2 * rows].astype(BF16)

    resp_spec = pl.BlockSpec((1, 2, src, rcv), lambda j, _: (j, 0, 0, 0))
    message = pl.BlockSpec((2, 1, share, src), lambda j, _: (0, j, 0, 0))
    out_spec = pl.BlockSpec((2, 2, 1, rows, rcv), lambda j, _: (0, 0, j, 0, 0))
    shape = (2, 2, per_dev, rows, rcv)
    return call(
        body,
        (freq_place,),
        [(kept, resp_spec), (moved, resp_spec)] + [(v, message) for v in messages],
        [(jax.ShapeDtypeStruct(shape, F32), out_spec), (jax.ShapeDtypeStruct(shape, BF16), out_spec)],
        (per_dev,),
        scratch=[pltpu.VMEM((2, 2 * rows, src), BF16)],
        flops=2 * 8 * per_dev * 2 * rows * src * rcv,
    )


def dealt(keep, from_core, from_far, freq_place, freq_devs):
    _, _, per_dev, rows, rcv = keep.shape
    share = rows // freq_devs

    def body(place_ref, k_ref, c_ref, x_ref, *rest):
        outs, held = rest[:freq_devs], rest[freq_devs]
        held[...] = k_ref[0] + c_ref[0].astype(F32) + x_ref[...].astype(F32)
        for step, out in enumerate(outs):
            start = pl.multiple_of((place_ref[0] ^ step) * share, share)
            out[...] = held[:, :, pl.ds(start, share), :].reshape(out.shape).astype(BF16)

    first = pl.BlockSpec((1,) + keep.shape[1:], lambda i, _: (0, 0, 0, 0, 0))
    shape = jax.ShapeDtypeStruct((2 * per_dev * share, rcv), BF16)
    return call(
        body,
        (freq_place,),
        [(keep, first), (from_core, first), (from_far, whole(from_far))],
        [(shape, whole(shape))] * freq_devs,
        (1,),
        scratch=[pltpu.VMEM(keep.shape[1:], F32)],
    )


def next_spectra(sums, messages, freq_place):
    freq_devs = len(messages)
    _, per_dev, rows, rcv = sums.shape
    share = rows // freq_devs

    def body(place_ref, s_ref, *rest):
        refs, out, held = rest[:freq_devs], rest[freq_devs], rest[freq_devs + 1]
        for step, ref in enumerate(refs):
            start = pl.multiple_of((place_ref[0] ^ step) * share, share)
            held[:, :, pl.ds(start, share), :] = ref[...].astype(F32).reshape(2, per_dev, share, rcv)
        out[...] = (s_ref[...] - held[...]).astype(BF16)

    (out,) = call(
        body,
        (freq_place,),
        [(sums, whole(sums))] + [(v, whole(v)) for v in messages],
        [(jax.ShapeDtypeStruct(sums.shape, BF16), whole(sums))],
        (1,),
        scratch=[pltpu.VMEM(sums.shape, F32)],
    )
    return out


def updated(initial, onset, messages, table, freq_place, focal_first, first, rows, target):
    freq_devs = len(messages)
    own, rcv = initial.shape[1:]
    per_dev = messages[0].shape[1]
    tile = 2 * ROWS
    count = freq_devs * 2 * per_dev * ROWS

    def body(place_ref, _, x_ref, o_ref, t_ref, *rest):
        refs, out = rest[:freq_devs], rest[-1]
        data = [ref[...].astype(F32) for ref in refs]
        time = lax.broadcasted_iota(jnp.int32, (own, rcv), 0) + place_ref[0] * own
        for half in range(2):
            cut = slice(half * ROWS, (half + 1) * ROWS)
            flat = jnp.stack([v[:, :, cut] for v in data]).reshape(count, rcv).astype(BF16)
            change = jnp.dot(t_ref[0], flat, preferred_element_type=F32)
            for row in range(ROWS):
                spot = half * ROWS + row
                on = time < o_ref[spot : spot + 1, :]
                step = jnp.where(on, change[row * own : (row + 1) * own], 0.0)
                out[spot] = (x_ref[spot].astype(F32) - step).astype(BF16)

    block = pl.BlockSpec((tile, own, rcv), lambda i, *_: (first // tile + i, 0, 0))
    inputs = [
        (initial, block),
        (onset, pl.BlockSpec((tile, rcv), lambda i, _, b: (b[0] + first // tile + i, 0))),
        (table, pl.BlockSpec((1,) + table.shape[1:], lambda i, z, _: (z[0], 0, 0))),
    ] + [(v, pl.BlockSpec((2, per_dev, tile, rcv), lambda i, *_: (0, 0, i, 0))) for v in messages]
    aliases = {}
    if target is not None:
        inputs.append((target, pl.BlockSpec(memory_space=pl.ANY)))
        aliases = {2 + len(inputs) - 1: 0}
    (out,) = call(
        body,
        (freq_place, focal_first),
        inputs,
        [(jax.ShapeDtypeStruct(initial.shape, BF16), block)],
        (rows // tile,),
        aliases=aliases,
        flops=2 * 2 * freq_devs * per_dev * own * rows * rcv,
    )
    return out


def exchanged(value, axis, step):
    return lax.ppermute(value, axis, [(i, i ^ step) for i in range(lax.axis_size(axis))])


def dealt_out(parts):
    return [parts[0]] + [exchanged(parts[step], "freq", step) for step in range(1, len(parts))]


def phases(onset, freq_index, freq_devs, per_dev, samples):
    steps = lax.iota(jnp.int32, freq_devs)
    order = (freq_index ^ steps)[:, None] * per_dev + lax.iota(jnp.int32, per_dev)[None, :] + 1
    phase = order[:, :, None, None] * onset[None, None] % samples
    angle = phase.astype(F32) * (2.0 * math.pi / samples)
    return jnp.cos(angle), jnp.sin(angle), onset.astype(F32) * (1.0 / samples)


def on_device(initial, response, aperture, onset_rcv, onset_src):
    freq_devs = lax.axis_size("freq")
    per_dev = response.shape[0]
    samples = initial.shape[1] * freq_devs
    half_rows = initial.shape[0]
    src_width = response.shape[2] // 2
    rows = half_rows // CHUNKS
    freq_index = lax.axis_index("freq")
    rblk_index = lax.axis_index("rblk")
    sblk_index = lax.axis_index("sblk")
    freq_place = freq_index.reshape(1)
    rblk_place = rblk_index.reshape(1)

    moved = exchanged(mask_half(response, aperture, rblk_place, 1, src_width), "rblk", 1)
    forward = jnp.asarray(forward_tables(samples, freq_devs, per_dev))
    inverse = jnp.asarray(inverse_tables(samples, freq_devs, per_dev))
    matrix = jnp.asarray(window_tables(samples, freq_devs, per_dev))
    kept = mask_half(response, aperture, rblk_place, 0, src_width)

    result = None
    for chunk in range(CHUNKS):
        first = chunk * rows
        parts = first_spectra(initial, forward, freq_place, freq_devs, per_dev, first, rows)
        sums = sum(v.astype(F32) for v in dealt_out(parts))
        spectra = sums.astype(BF16)

        share = 2 * rows // freq_devs
        spot = freq_index * share
        other = (spot >= rows).astype(jnp.int32)
        src_first = (sblk_index ^ other) * half_rows + first + spot - other * rows
        onsets = lax.dynamic_slice(onset_src, (src_first, rblk_index * src_width), (share, src_width))
        src_tables = phases(onsets, freq_index, freq_devs, per_dev, samples)
        rcv_share = rows // freq_devs
        rcv_first = sblk_index * half_rows + first + freq_index * rcv_share
        onsets = lax.dynamic_slice_in_dim(onset_rcv, rcv_first, rcv_share, 0)
        rcv_tables = phases(onsets, freq_index, freq_devs, per_dev, samples)

        for step in range(ITERS):
            far_own = exchanged(spectra, "rblk", 1)
            near = (spectra, exchanged(spectra, "sblk", 1))
            far = (far_own, exchanged(far_own, "sblk", 1))
            messages = dealt_out(down_products(near, far, kept, moved, freq_place, freq_devs))
            messages = windowed(messages, src_tables, matrix, freq_place, per_dev, share)
            keep, send = up_products(dealt_out(messages), kept, moved, freq_place, rows)
            from_core = exchanged(send, "sblk", 1)
            from_far = exchanged((keep[1] + from_core[1].astype(F32)).astype(BF16), "rblk", 1)
            if step < ITERS - 1:
                messages = dealt_out(dealt(keep, from_core, from_far, freq_place, freq_devs))
                messages = windowed(messages, rcv_tables, matrix, freq_place, per_dev, rcv_share)
                spectra = next_spectra(sums, dealt_out(messages), freq_place)
            else:
                back = (keep[0] + from_core[0].astype(F32) + from_far.astype(F32)).astype(BF16)
                messages = [back] + [exchanged(back, "freq", m) for m in range(1, freq_devs)]
                tile_first = (sblk_index * (half_rows // (2 * ROWS))).reshape(1)
                result = updated(
                    initial, onset_rcv, messages, inverse, freq_place, tile_first, first, rows, result
                )
    return result


def transform_tables(length, count):
    table = fields(length, count).reshape(2 * count, length)
    forward_table = jnp.asarray(table.astype(np.float32).astype(BF16))
    inverse_table = jnp.asarray((table.T * (2.0 / length)).astype(np.float32).astype(BF16))
    return forward_table, inverse_table


def settle(values):
    return lax.optimization_barrier(values.astype(BF16)).astype(F32)


def samples_into_spectra(values, forward_table, freq_total):
    out = jnp.einsum("kt,ptn->pkn", forward_table, values, preferred_element_type=F32)
    return out.reshape(values.shape[0], 2, freq_total, values.shape[2]).astype(BF16)


def spectra_into_samples(trace_spectra, inverse_table):
    flat = trace_spectra.reshape(trace_spectra.shape[0], -1, trace_spectra.shape[3])
    return jnp.einsum("tk,pkn->ptn", inverse_table, flat, preferred_element_type=F32)


def dense(spec, gated, real, imag, sign):
    dot = functools.partial(jnp.einsum, spec, preferred_element_type=F32)
    return jnp.stack(
        [dot(gated[:, 0], real) - sign * dot(gated[:, 1], imag), dot(gated[:, 0], imag) + sign * dot(gated[:, 1], real)], 1
    )


def general_device(initial, response, aperture, onset_rcv, onset_src):
    freq_devs, rblk_devs, sblk_devs = (lax.axis_size(a) for a in ("freq", "rblk", "sblk"))
    freq_index, rblk_index, sblk_index = (lax.axis_index(a) for a in ("freq", "rblk", "sblk"))
    freq_total = response.shape[0] * freq_devs
    samples = initial.shape[1] * freq_devs
    focal_all = onset_rcv.shape[0]
    forward_table, inverse_table = transform_tables(samples, freq_total)
    steps_axis = lax.iota(jnp.int32, samples)
    own_axis = freq_index * initial.shape[1] + lax.iota(jnp.int32, initial.shape[1])
    half_rows = focal_all // sblk_devs
    own_onsets = lax.dynamic_slice_in_dim(onset_rcv, sblk_index * half_rows, half_rows, 0)
    rcv_gate = (own_axis[None, :, None] < own_onsets[:, None, :]).astype(F32)
    src_rows = focal_all // (rblk_devs * freq_devs)
    src_first = rblk_index * (focal_all // rblk_devs) + freq_index * src_rows
    src_onsets = lax.dynamic_slice_in_dim(onset_src, src_first, src_rows, 0)
    src_gate = (steps_axis[None, :, None] < src_onsets[:, None, :]).astype(F32)
    mask_full = jnp.repeat(jnp.repeat(aperture, BLOCK, 1), BLOCK, 2).astype(BF16)
    gated = response * mask_full[:, None]
    own_forward = lax.dynamic_slice_in_dim(forward_table, freq_index * initial.shape[1], initial.shape[1], 1)
    own_inverse = lax.dynamic_slice_in_dim(inverse_table, freq_index * initial.shape[1], initial.shape[1], 0)
    current = initial
    for _ in range(ITERS):
        partial = samples_into_spectra(current, own_forward, freq_total)
        spec_back = lax.psum_scatter(partial.astype(F32), "freq", scatter_dimension=2, tiled=True).astype(BF16)
        spec_all = lax.all_gather(spec_back, "sblk", axis=0, tiled=True)
        down = lax.psum_scatter(
            settle(dense("euk,bek->beu", gated, spec_all[:, 0], spec_all[:, 1], 1.0)).astype(BF16),
            "rblk",
            scatter_dimension=0,
            tiled=True,
        )
        src_traces = lax.all_to_all(down, "freq", split_axis=0, concat_axis=2, tiled=True)
        upgoing = (src_gate * spectra_into_samples(src_traces, inverse_table)).astype(BF16)
        upspec = samples_into_spectra(upgoing, forward_table, freq_total)
        up_back = lax.all_to_all(upspec, "freq", split_axis=2, concat_axis=0, tiled=True)
        up_all = lax.all_gather(up_back, "rblk", axis=0, tiled=True)
        sums = dense("qao,bqa->bqo", gated, up_all[:, 0], up_all[:, 1], -1.0).astype(BF16)
        back = lax.psum_scatter(sums, "sblk", scatter_dimension=0, tiled=True)
        traces = lax.all_gather(back, "freq", axis=2, tiled=True)
        update = rcv_gate * spectra_into_samples(traces, own_inverse)
        current = (initial.astype(F32) - update).astype(BF16)
    return current


def fits(initial, response, aperture, onset_rcv, onset_src):
    freq_devs = lax.axis_size("freq")
    if lax.axis_size("rblk") != 2 or lax.axis_size("sblk") != 2 or freq_devs & (freq_devs - 1):
        return False
    rows = initial.shape[0] // CHUNKS
    whole_rows = initial.shape[0] % (CHUNKS * 2 * ROWS * max(1, freq_devs // 2)) == 0 and rows % (ROWS * freq_devs) == 0
    whole_width = response.shape[2] % (4 * BLOCK) == 0 and response.shape[3] % BLOCK == 0
    return whole_rows and whole_width and onset_rcv.shape[0] == 2 * initial.shape[0]


def chosen(*arrays):
    return on_device(*arrays) if fits(*arrays) else general_device(*arrays)


def solution(mesh):
    in_specs = (
        P(("group", "sblk"), "freq", "rblk"),
        P(("group", "freq"), None, "sblk", "rblk"),
        P(("group", "freq"), "sblk", "rblk"),
        P("group", "rblk"),
        P("group", "sblk"),
    )
    out_specs = P(("group", "sblk"), "freq", "rblk")
    return jax.shard_map(chosen, mesh=mesh, in_specs=in_specs, out_specs=out_specs, check_vma=False)
```

```python
import functools
import math

import jax
import jax.numpy as jnp
import numpy as np
from jax import lax
from jax.experimental import pallas as pl
from jax.experimental.pallas import tpu as pltpu
from jax.sharding import PartitionSpec as P

BLOCK = 128
ITERS = 2
ROWS = 8
CHUNKS = 1
VMEM_BYTES = 62 * 1024 * 1024

BF16 = jnp.bfloat16
F32 = jnp.float32


def field_rows(place, freq_devs, per_dev):
    rows = []
    for step in range(freq_devs):
        first = (place ^ step) * per_dev
        for part in range(2):
            rows.extend((part, first + local) for local in range(per_dev))
    return rows


def fields(samples, freq_total):
    phase = (np.arange(1, freq_total + 1)[:, None] * np.arange(samples)[None, :]) % samples
    angle = phase * (2.0 * math.pi / samples)
    return np.stack([np.cos(angle), -np.sin(angle)])


def forward_tables(samples, freq_devs, per_dev):
    table = fields(samples, freq_devs * per_dev)
    own = samples // freq_devs
    eye = np.eye(ROWS)
    out = []
    for place in range(freq_devs):
        part = np.stack([table[c, j, place * own : (place + 1) * own] for c, j in field_rows(place, freq_devs, per_dev)])
        out.append(np.einsum("kt,pq->kpqt", part, eye).reshape(part.shape[0] * ROWS, ROWS * own))
    return np.stack(out).astype(np.float32).astype(BF16)


def inverse_tables(samples, freq_devs, per_dev):
    table = fields(samples, freq_devs * per_dev) * (2.0 / samples)
    own = samples // freq_devs
    eye = np.eye(ROWS)
    out = []
    for place in range(freq_devs):
        part = np.stack([table[c, j, place * own : (place + 1) * own] for c, j in field_rows(place, freq_devs, per_dev)])
        out.append(np.einsum("kt,pq->ptkq", part, eye).reshape(ROWS * own, part.shape[0] * ROWS))
    return np.stack(out).astype(np.float32).astype(BF16)


def window_tables(samples, freq_devs, per_dev):
    freq_total = freq_devs * per_dev
    order = np.arange(1, freq_total + 1)
    unit = 2j * math.pi / samples
    diff = order[None, :] - order[:, None]
    total = order[None, :] + order[:, None]
    same = np.where(diff == 0, 0.0, 1.0 / (samples * (np.exp(unit * np.where(diff == 0, 1, diff)) - 1.0)))
    mixed = 1.0 / (samples * (np.exp(-unit * total) - 1.0))
    full = np.zeros((2, freq_total, 2, freq_total))
    full[0, :, 0, :] = same.real + mixed.real
    full[0, :, 1, :] = mixed.imag - same.imag
    full[1, :, 0, :] = same.imag + mixed.imag
    full[1, :, 1, :] = same.real - mixed.real
    out = []
    for place in range(freq_devs):
        rows = [c * freq_total + j for c, j in field_rows(place, freq_devs, per_dev)]
        flat = full.reshape(2 * freq_total, 2 * freq_total)[np.ix_(rows, rows)]
        out.append(np.kron(flat, np.eye(ROWS)))
    return np.stack(out).astype(np.float32).astype(BF16)


def call(body, scalars, inputs, outputs, grid, scratch=(), aliases=None, flops=0):
    in_arrays = [value for value, _ in inputs]
    bytes_all = sum(v.size * v.dtype.itemsize for v in in_arrays)
    bytes_all += sum(math.prod(s.shape) * s.dtype.itemsize for s, _ in outputs)
    return pl.pallas_call(
        body,
        grid_spec=pltpu.PrefetchScalarGridSpec(
            num_scalar_prefetch=len(scalars),
            grid=grid,
            in_specs=[spec for _, spec in inputs],
            out_specs=[spec for _, spec in outputs],
            scratch_shapes=list(scratch),
        ),
        out_shape=[shape for shape, _ in outputs],
        input_output_aliases=aliases or {},
        compiler_params=pltpu.CompilerParams(vmem_limit_bytes=VMEM_BYTES),
        cost_estimate=pl.CostEstimate(flops=flops, bytes_accessed=bytes_all, transcendentals=0),
    )(*scalars, *in_arrays)


def whole(array):
    zeros = (0,) * array.ndim
    return pl.BlockSpec(array.shape, lambda *_: zeros)


def mask_half(response, aperture, place, flip, half):
    per_dev, _, _, rcv = response.shape
    rcv_blocks = rcv // BLOCK
    steps = half // BLOCK

    def body(place_ref, flags, x_ref, o_ref):
        block = (place_ref[0] ^ flip) * steps + pl.program_id(0)
        for j in range(per_dev):
            for r in range(rcv_blocks):
                on = flags[j, block, r]
                cut = pl.ds(r * BLOCK, BLOCK)
                value = x_ref[j, :, :, cut]
                o_ref[j, :, :, cut] = value * on.astype(F32).astype(BF16)

    shape = jax.ShapeDtypeStruct((per_dev, 2, half, rcv), BF16)
    block = (per_dev, 2, BLOCK, rcv)
    (out,) = call(
        body,
        (place, aperture),
        [(response, pl.BlockSpec(block, lambda i, a, _: (0, 0, (a[0] ^ flip) * steps + i, 0)))],
        [(shape, pl.BlockSpec(block, lambda i, *_: (0, 0, i, 0)))],
        (steps,),
    )
    return out


def first_spectra(initial, table, freq_place, freq_devs, per_dev, first, rows):
    own, rcv = initial.shape[1:]
    tile = 2 * ROWS

    def body(place_ref, x_ref, t_ref, *outs):
        parts = []
        for half in range(2):
            flat = x_ref[half * ROWS : (half + 1) * ROWS].reshape(ROWS * own, rcv)
            value = jnp.dot(t_ref[0], flat, preferred_element_type=F32)
            parts.append(value.reshape(freq_devs, 2, per_dev, ROWS, rcv))
        both = jnp.concatenate(parts, 3).astype(BF16)
        for step, out in enumerate(outs):
            out[...] = both[step]

    shape = jax.ShapeDtypeStruct((2, per_dev, rows, rcv), BF16)
    return call(
        body,
        (freq_place,),
        [
            (initial, pl.BlockSpec((tile, own, rcv), lambda i, _: (first // tile + i, 0, 0))),
            (table, pl.BlockSpec((1,) + table.shape[1:], lambda i, z: (z[0], 0, 0))),
        ],
        [(shape, pl.BlockSpec((2, per_dev, tile, rcv), lambda i, _: (0, 0, i, 0)))] * freq_devs,
        (rows // tile,),
        flops=2 * 2 * freq_devs * per_dev * own * rows * rcv,
    )


def down_products(near, far, kept, moved, freq_place, freq_devs):
    _, per_dev, rows, rcv = near[0].shape
    width = kept.shape[2]
    tile = min(width, 256)
    share = 2 * rows // freq_devs

    def body(place_ref, n0, n1, f0, f1, k_ref, m_ref, *rest):
        outs, held = rest[:freq_devs], rest[freq_devs]
        for j in range(per_dev):
            total = None
            for own, other, resp in ((n0, n1, k_ref), (f0, f1, m_ref)):
                real = jnp.concatenate([own[0, j], other[0, j]], 0)
                imag = jnp.concatenate([own[1, j], other[1, j]], 0)
                for part, lhs in ((0, [real, imag]), (1, [-imag, real])):
                    term = lax.dot_general(
                        jnp.concatenate(lhs, 0),
                        resp[j, part],
                        (((1,), (1,)), ((), ())),
                        preferred_element_type=F32,
                    )
                    total = term if total is None else total + term
            held[0, j] = total[: 2 * rows]
            held[1, j] = total[2 * rows :]
        for step, out in enumerate(outs):
            start = pl.multiple_of((place_ref[0] ^ step) * share, share)
            out[...] = held[:, :, pl.ds(start, share), :].astype(BF16)

    shape = jax.ShapeDtypeStruct((2, per_dev, share, width), BF16)
    resp_spec = pl.BlockSpec((per_dev, 2, tile, rcv), lambda i, _: (0, 0, i, 0))
    return call(
        body,
        (freq_place,),
        [(v, whole(v)) for v in (*near, *far)] + [(kept, resp_spec), (moved, resp_spec)],
        [(shape, pl.BlockSpec((2, per_dev, share, tile), lambda i, _: (0, 0, 0, i)))] * freq_devs,
        (width // tile,),
        scratch=[pltpu.VMEM((2, per_dev, 2 * rows, tile), F32)],
        flops=2 * 8 * per_dev * 2 * rows * width * rcv,
    )


def windowed(messages, tables, matrix, freq_place, per_dev, share):
    cosines, sines, fraction = tables
    freq_devs = len(messages)
    width = messages[0].shape[-1]
    tile = BLOCK
    count = freq_devs * 2 * per_dev * ROWS

    def body(place_ref, c_ref, s_ref, f_ref, g_ref, *rest):
        refs, outs = rest[:freq_devs], rest[freq_devs:]
        data = [ref[...].astype(F32).reshape(2, per_dev, share, tile) for ref in refs]
        made = [[] for _ in outs]
        for first in range(0, share, ROWS):
            cut = slice(first, first + ROWS)
            plain = [value[:, :, cut] for value in data]
            cos = [c_ref[step, :, cut] for step in range(freq_devs)]
            sin = [s_ref[step, :, cut] for step in range(freq_devs)]
            turned = [
                jnp.stack([v[0] * c - v[1] * s, v[0] * s + v[1] * c])
                for v, c, s in zip(plain, cos, sin)
            ]
            flat = [jnp.stack(v).reshape(count, tile).astype(BF16) for v in (turned, plain)]
            mixed = jnp.dot(g_ref[0], jnp.concatenate(flat, 1), preferred_element_type=F32)
            upper = mixed[:, :tile].reshape(freq_devs, 2, per_dev, ROWS, tile)
            lower = mixed[:, tile:].reshape(freq_devs, 2, per_dev, ROWS, tile)
            part = f_ref[cut]
            for step in range(freq_devs):
                c, s, v, up, low = cos[step], sin[step], plain[step], upper[step], lower[step]
                real = c * up[0] + s * up[1] - low[0] + part * v[0]
                imag = c * up[1] - s * up[0] - low[1] + part * v[1]
                made[step].append(jnp.stack([real, imag]))
        for out, value in zip(outs, made):
            out[...] = jnp.concatenate(value, 2).reshape(out.shape).astype(BF16)

    lead = messages[0].shape[:-1]
    zeros = (0,) * len(lead)
    message = pl.BlockSpec(lead + (tile,), lambda i, _: zeros + (i,))
    table = pl.BlockSpec(cosines.shape[:-1] + (tile,), lambda i, _: (0, 0, 0, i))
    return call(
        body,
        (freq_place,),
        [
            (cosines, table),
            (sines, table),
            (fraction, pl.BlockSpec((share, tile), lambda i, _: (0, i))),
            (matrix, pl.BlockSpec((1,) + matrix.shape[1:], lambda i, z: (z[0], 0, 0))),
        ]
        + [(v, message) for v in messages],
        [(jax.ShapeDtypeStruct(v.shape, BF16), message) for v in messages],
        (width // tile,),
        flops=2 * count * count * 2 * width * share // ROWS,
    )


def up_products(messages, kept, moved, freq_place, rows):
    freq_devs = len(messages)
    per_dev, _, src, rcv = kept.shape
    share = messages[0].shape[2]

    def body(place_ref, k_ref, m_ref, *rest):
        refs = rest[:freq_devs]
        keep, send, held = rest[freq_devs:]
        for step, ref in enumerate(refs):
            start = pl.multiple_of((place_ref[0] ^ step) * share, share)
            held[:, pl.ds(start, share), :] = ref[:, 0]
        real, imag = held[0], held[1]
        one = jnp.concatenate([real, imag], 0)
        two = jnp.concatenate([imag, -real], 0)
        for side, resp in enumerate((k_ref, m_ref)):
            total = jnp.dot(one, resp[0, 0], preferred_element_type=F32)
            total = total + jnp.dot(two, resp[0, 1], preferred_element_type=F32)
            for part in range(2):
                first = 2 * rows * part
                keep[side, part, 0] = total[first : first + rows]
                send[side, part, 0] = total[first + rows : first + 2 * rows].astype(BF16)

    resp_spec = pl.BlockSpec((1, 2, src, rcv), lambda j, _: (j, 0, 0, 0))
    message = pl.BlockSpec((2, 1, share, src), lambda j, _: (0, j, 0, 0))
    out_spec = pl.BlockSpec((2, 2, 1, rows, rcv), lambda j, _: (0, 0, j, 0, 0))
    shape = (2, 2, per_dev, rows, rcv)
    return call(
        body,
        (freq_place,),
        [(kept, resp_spec), (moved, resp_spec)] + [(v, message) for v in messages],
        [(jax.ShapeDtypeStruct(shape, F32), out_spec), (jax.ShapeDtypeStruct(shape, BF16), out_spec)],
        (per_dev,),
        scratch=[pltpu.VMEM((2, 2 * rows, src), BF16)],
        flops=2 * 8 * per_dev * 2 * rows * src * rcv,
    )


def next_spectra(sums, messages, tables, matrix, freq_place):
    cosines, sines, fraction = tables
    freq_devs = len(messages)
    _, per_dev, rows, rcv = sums.shape
    tile = BLOCK
    count = freq_devs * 2 * per_dev * ROWS
    own = 2 * per_dev * ROWS

    def body(place_ref, u_ref, c_ref, s_ref, f_ref, g_ref, *rest):
        refs, out = rest[:freq_devs], rest[freq_devs]
        data = [ref[...].astype(F32) for ref in refs]
        made = []
        for first in range(0, rows, ROWS):
            cut = slice(first, first + ROWS)
            plain = [value[:, :, cut] for value in data]
            cos = [c_ref[step, :, cut] for step in range(freq_devs)]
            sin = [s_ref[step, :, cut] for step in range(freq_devs)]
            turned = [
                jnp.stack([v[0] * c - v[1] * s, v[0] * s + v[1] * c])
                for v, c, s in zip(plain, cos, sin)
            ]
            flat = [jnp.stack(v).reshape(count, tile).astype(BF16) for v in (turned, plain)]
            mixed = jnp.dot(g_ref[0], jnp.concatenate(flat, 1), preferred_element_type=F32)
            up = mixed[:, :tile].reshape(2, per_dev, ROWS, tile)
            low = mixed[:, tile:].reshape(2, per_dev, ROWS, tile)
            c, s, v, part = cos[0], sin[0], plain[0], f_ref[cut]
            real = c * up[0] + s * up[1] - low[0] + part * v[0]
            imag = c * up[1] - s * up[0] - low[1] + part * v[1]
            made.append(jnp.stack([real, imag]))
        out[...] = (u_ref[...] - jnp.concatenate(made, 2)).astype(BF16)

    block = pl.BlockSpec((2, per_dev, rows, tile), lambda i, _: (0, 0, 0, i))
    table = pl.BlockSpec(cosines.shape[:-1] + (tile,), lambda i, _: (0, 0, 0, i))
    (out,) = call(
        body,
        (freq_place,),
        [
            (sums, block),
            (cosines, table),
            (sines, table),
            (fraction, pl.BlockSpec((rows, tile), lambda i, _: (0, i))),
            (matrix, pl.BlockSpec((1, own, count), lambda i, z: (z[0], 0, 0))),
        ]
        + [(v, block) for v in messages],
        [(jax.ShapeDtypeStruct(sums.shape, BF16), block)],
        (rcv // tile,),
        flops=2 * own * count * 2 * rcv * rows // ROWS,
    )
    return out


def updated(initial, onset, messages, table, freq_place, focal_first, first, rows, target):
    freq_devs = len(messages)
    own, rcv = initial.shape[1:]
    per_dev = messages[0].shape[1]
    tile = 2 * ROWS
    count = freq_devs * 2 * per_dev * ROWS

    def body(place_ref, _, x_ref, o_ref, t_ref, *rest):
        refs, out = rest[:freq_devs], rest[-1]
        data = [ref[...].astype(F32) for ref in refs]
        time = lax.broadcasted_iota(jnp.int32, (own, rcv), 0) + place_ref[0] * own
        for half in range(2):
            cut = slice(half * ROWS, (half + 1) * ROWS)
            flat = jnp.stack([v[:, :, cut] for v in data]).reshape(count, rcv).astype(BF16)
            change = jnp.dot(t_ref[0], flat, preferred_element_type=F32)
            for row in range(ROWS):
                spot = half * ROWS + row
                on = time < o_ref[spot : spot + 1, :]
                step = jnp.where(on, change[row * own : (row + 1) * own], 0.0)
                out[spot] = (x_ref[spot].astype(F32) - step).astype(BF16)

    block = pl.BlockSpec((tile, own, rcv), lambda i, *_: (first // tile + i, 0, 0))
    inputs = [
        (initial, block),
        (onset, pl.BlockSpec((tile, rcv), lambda i, _, b: (b[0] + first // tile + i, 0))),
        (table, pl.BlockSpec((1,) + table.shape[1:], lambda i, z, _: (z[0], 0, 0))),
    ] + [(v, pl.BlockSpec((2, per_dev, tile, rcv), lambda i, *_: (0, 0, i, 0))) for v in messages]
    aliases = {}
    if target is not None:
        inputs.append((target, pl.BlockSpec(memory_space=pl.ANY)))
        aliases = {2 + len(inputs) - 1: 0}
    (out,) = call(
        body,
        (freq_place, focal_first),
        inputs,
        [(jax.ShapeDtypeStruct(initial.shape, BF16), block)],
        (rows // tile,),
        aliases=aliases,
        flops=2 * 2 * freq_devs * per_dev * own * rows * rcv,
    )
    return out


def exchanged(value, axis, step):
    return lax.ppermute(value, axis, [(i, i ^ step) for i in range(lax.axis_size(axis))])


def partners(count):
    return sorted(range(1, count), key=lambda step: (step.bit_length() < count.bit_length() - 1, step))


def dealt_out(parts):
    out = list(parts)
    for step in partners(len(parts)):
        out[step] = exchanged(parts[step], "freq", step)
    return out


def spread(value, count):
    return dealt_out([value] * count)


def phases(onset, freq_index, freq_devs, per_dev, samples):
    steps = lax.iota(jnp.int32, freq_devs)
    order = (freq_index ^ steps)[:, None] * per_dev + lax.iota(jnp.int32, per_dev)[None, :] + 1
    phase = order[:, :, None, None] * onset[None, None] % samples
    angle = phase.astype(F32) * (2.0 * math.pi / samples)
    return jnp.cos(angle), jnp.sin(angle), onset.astype(F32) * (1.0 / samples)


def on_device(initial, response, aperture, onset_rcv, onset_src):
    freq_devs = lax.axis_size("freq")
    per_dev = response.shape[0]
    samples = initial.shape[1] * freq_devs
    half_rows = initial.shape[0]
    src_width = response.shape[2] // 2
    rows = half_rows // CHUNKS
    freq_index = lax.axis_index("freq")
    rblk_index = lax.axis_index("rblk")
    sblk_index = lax.axis_index("sblk")
    freq_place = freq_index.reshape(1)
    rblk_place = rblk_index.reshape(1)

    moved = exchanged(mask_half(response, aperture, rblk_place, 1, src_width), "rblk", 1)
    forward = jnp.asarray(forward_tables(samples, freq_devs, per_dev))
    inverse = jnp.asarray(inverse_tables(samples, freq_devs, per_dev))
    matrix = jnp.asarray(window_tables(samples, freq_devs, per_dev))
    kept = mask_half(response, aperture, rblk_place, 0, src_width)

    result = None
    for chunk in range(CHUNKS):
        first = chunk * rows
        parts = first_spectra(initial, forward, freq_place, freq_devs, per_dev, first, rows)
        sums = sum(v.astype(F32) for v in dealt_out(parts))
        spectra = sums.astype(BF16)

        share = 2 * rows // freq_devs
        spot = freq_index * share
        other = (spot >= rows).astype(jnp.int32)
        src_first = (sblk_index ^ other) * half_rows + first + spot - other * rows
        onsets = lax.dynamic_slice(onset_src, (src_first, rblk_index * src_width), (share, src_width))
        src_tables = phases(onsets, freq_index, freq_devs, per_dev, samples)
        onsets = lax.dynamic_slice_in_dim(onset_rcv, sblk_index * half_rows + first, rows, 0)
        rcv_tables = phases(onsets, freq_index, freq_devs, per_dev, samples)

        for step in range(ITERS):
            far_own = exchanged(spectra, "rblk", 1)
            near = (spectra, exchanged(spectra, "sblk", 1))
            far = (far_own, exchanged(far_own, "sblk", 1))
            messages = dealt_out(down_products(near, far, kept, moved, freq_place, freq_devs))
            messages = windowed(messages, src_tables, matrix, freq_place, per_dev, share)
            keep, send = up_products(dealt_out(messages), kept, moved, freq_place, rows)
            from_core = exchanged(send, "sblk", 1)
            from_far = exchanged((keep[1] + from_core[1].astype(F32)).astype(BF16), "rblk", 1)
            back = (keep[0] + from_core[0].astype(F32) + from_far.astype(F32)).astype(BF16)
            messages = spread(back, freq_devs)
            if step < ITERS - 1:
                spectra = next_spectra(sums, messages, rcv_tables, matrix, freq_place)
            else:
                tile_first = (sblk_index * (half_rows // (2 * ROWS))).reshape(1)
                result = updated(
                    initial, onset_rcv, messages, inverse, freq_place, tile_first, first, rows, result
                )
    return result


def transform_tables(length, count):
    table = fields(length, count).reshape(2 * count, length)
    forward_table = jnp.asarray(table.astype(np.float32).astype(BF16))
    inverse_table = jnp.asarray((table.T * (2.0 / length)).astype(np.float32).astype(BF16))
    return forward_table, inverse_table


def settle(values):
    return lax.optimization_barrier(values.astype(BF16)).astype(F32)


def samples_into_spectra(values, forward_table, freq_total):
    out = jnp.einsum("kt,ptn->pkn", forward_table, values, preferred_element_type=F32)
    return out.reshape(values.shape[0], 2, freq_total, values.shape[2]).astype(BF16)


def spectra_into_samples(trace_spectra, inverse_table):
    flat = trace_spectra.reshape(trace_spectra.shape[0], -1, trace_spectra.shape[3])
    return jnp.einsum("tk,pkn->ptn", inverse_table, flat, preferred_element_type=F32)


def dense(spec, gated, real, imag, sign):
    dot = functools.partial(jnp.einsum, spec, preferred_element_type=F32)
    return jnp.stack(
        [dot(gated[:, 0], real) - sign * dot(gated[:, 1], imag), dot(gated[:, 0], imag) + sign * dot(gated[:, 1], real)], 1
    )


def general_device(initial, response, aperture, onset_rcv, onset_src):
    freq_devs, rblk_devs, sblk_devs = (lax.axis_size(a) for a in ("freq", "rblk", "sblk"))
    freq_index, rblk_index, sblk_index = (lax.axis_index(a) for a in ("freq", "rblk", "sblk"))
    freq_total = response.shape[0] * freq_devs
    samples = initial.shape[1] * freq_devs
    focal_all = onset_rcv.shape[0]
    forward_table, inverse_table = transform_tables(samples, freq_total)
    steps_axis = lax.iota(jnp.int32, samples)
    own_axis = freq_index * initial.shape[1] + lax.iota(jnp.int32, initial.shape[1])
    half_rows = focal_all // sblk_devs
    own_onsets = lax.dynamic_slice_in_dim(onset_rcv, sblk_index * half_rows, half_rows, 0)
    rcv_gate = (own_axis[None, :, None] < own_onsets[:, None, :]).astype(F32)
    src_rows = focal_all // (rblk_devs * freq_devs)
    src_first = rblk_index * (focal_all // rblk_devs) + freq_index * src_rows
    src_onsets = lax.dynamic_slice_in_dim(onset_src, src_first, src_rows, 0)
    src_gate = (steps_axis[None, :, None] < src_onsets[:, None, :]).astype(F32)
    mask_full = jnp.repeat(jnp.repeat(aperture, BLOCK, 1), BLOCK, 2).astype(BF16)
    gated = response * mask_full[:, None]
    own_forward = lax.dynamic_slice_in_dim(forward_table, freq_index * initial.shape[1], initial.shape[1], 1)
    own_inverse = lax.dynamic_slice_in_dim(inverse_table, freq_index * initial.shape[1], initial.shape[1], 0)
    current = initial
    for _ in range(ITERS):
        partial = samples_into_spectra(current, own_forward, freq_total)
        spec_back = lax.psum_scatter(partial.astype(F32), "freq", scatter_dimension=2, tiled=True).astype(BF16)
        spec_all = lax.all_gather(spec_back, "sblk", axis=0, tiled=True)
        down = lax.psum_scatter(
            settle(dense("euk,bek->beu", gated, spec_all[:, 0], spec_all[:, 1], 1.0)).astype(BF16),
            "rblk",
            scatter_dimension=0,
            tiled=True,
        )
        src_traces = lax.all_to_all(down, "freq", split_axis=0, concat_axis=2, tiled=True)
        upgoing = (src_gate * spectra_into_samples(src_traces, inverse_table)).astype(BF16)
        upspec = samples_into_spectra(upgoing, forward_table, freq_total)
        up_back = lax.all_to_all(upspec, "freq", split_axis=2, concat_axis=0, tiled=True)
        up_all = lax.all_gather(up_back, "rblk", axis=0, tiled=True)
        sums = dense("qao,bqa->bqo", gated, up_all[:, 0], up_all[:, 1], -1.0).astype(BF16)
        back = lax.psum_scatter(sums, "sblk", scatter_dimension=0, tiled=True)
        traces = lax.all_gather(back, "freq", axis=2, tiled=True)
        update = rcv_gate * spectra_into_samples(traces, own_inverse)
        current = (initial.astype(F32) - update).astype(BF16)
    return current


def fits(initial, response, aperture, onset_rcv, onset_src):
    freq_devs = lax.axis_size("freq")
    if lax.axis_size("rblk") != 2 or lax.axis_size("sblk") != 2 or freq_devs & (freq_devs - 1):
        return False
    rows = initial.shape[0] // CHUNKS
    whole_rows = initial.shape[0] % (CHUNKS * 2 * ROWS * max(1, freq_devs // 2)) == 0 and rows % (2 * ROWS) == 0
    whole_width = response.shape[2] % (4 * BLOCK) == 0 and response.shape[3] % BLOCK == 0
    return whole_rows and whole_width and onset_rcv.shape[0] == 2 * initial.shape[0]


def chosen(*arrays):
    return on_device(*arrays) if fits(*arrays) else general_device(*arrays)


def solution(mesh):
    in_specs = (
        P(("group", "sblk"), "freq", "rblk"),
        P(("group", "freq"), None, "sblk", "rblk"),
        P(("group", "freq"), "sblk", "rblk"),
        P("group", "rblk"),
        P("group", "sblk"),
    )
    out_specs = P(("group", "sblk"), "freq", "rblk")
    return jax.shard_map(chosen, mesh=mesh, in_specs=in_specs, out_specs=out_specs, check_vma=False)
```

```python
import functools
import math

import jax
import jax.numpy as jnp
import numpy as np
from jax import lax
from jax.experimental import pallas as pl
from jax.experimental.pallas import tpu as pltpu
from jax.sharding import PartitionSpec as P

BLOCK = 128
ITERS = 2
ROWS = 8
CHUNKS = 1
VMEM_BYTES = 16 * 1024 * 1024

BF16 = jnp.bfloat16
F32 = jnp.float32


def field_rows(place, freq_devs, per_dev):
    rows = []
    for step in range(freq_devs):
        first = (place ^ step) * per_dev
        for part in range(2):
            rows.extend((part, first + local) for local in range(per_dev))
    return rows


def fields(samples, freq_total):
    phase = (np.arange(1, freq_total + 1)[:, None] * np.arange(samples)[None, :]) % samples
    angle = phase * (2.0 * math.pi / samples)
    return np.stack([np.cos(angle), -np.sin(angle)])


def forward_tables(samples, freq_devs, per_dev):
    table = fields(samples, freq_devs * per_dev)
    own = samples // freq_devs
    eye = np.eye(ROWS)
    out = []
    for place in range(freq_devs):
        part = np.stack([table[c, j, place * own : (place + 1) * own] for c, j in field_rows(place, freq_devs, per_dev)])
        out.append(np.einsum("kt,pq->kpqt", part, eye).reshape(part.shape[0] * ROWS, ROWS * own))
    return np.stack(out).astype(np.float32).astype(BF16)


def inverse_tables(samples, freq_devs, per_dev):
    table = fields(samples, freq_devs * per_dev) * (2.0 / samples)
    own = samples // freq_devs
    eye = np.eye(ROWS)
    out = []
    for place in range(freq_devs):
        part = np.stack([table[c, j, place * own : (place + 1) * own] for c, j in field_rows(place, freq_devs, per_dev)])
        out.append(np.einsum("kt,pq->ptkq", part, eye).reshape(ROWS * own, part.shape[0] * ROWS))
    return np.stack(out).astype(np.float32).astype(BF16)


def window_tables(samples, freq_devs, per_dev):
    freq_total = freq_devs * per_dev
    order = np.arange(1, freq_total + 1)
    unit = 2j * math.pi / samples
    diff = order[None, :] - order[:, None]
    total = order[None, :] + order[:, None]
    same = np.where(diff == 0, 0.0, 1.0 / (samples * (np.exp(unit * np.where(diff == 0, 1, diff)) - 1.0)))
    mixed = 1.0 / (samples * (np.exp(-unit * total) - 1.0))
    full = np.zeros((2, freq_total, 2, freq_total))
    full[0, :, 0, :] = same.real + mixed.real
    full[0, :, 1, :] = mixed.imag - same.imag
    full[1, :, 0, :] = same.imag + mixed.imag
    full[1, :, 1, :] = same.real - mixed.real
    out = []
    for place in range(freq_devs):
        rows = [c * freq_total + j for c, j in field_rows(place, freq_devs, per_dev)]
        flat = full.reshape(2 * freq_total, 2 * freq_total)[np.ix_(rows, rows)]
        out.append(np.kron(flat, np.eye(ROWS)))
    return np.stack(out).astype(np.float32).astype(BF16)


def call(body, scalars, inputs, outputs, grid, scratch=(), aliases=None, flops=0):
    in_arrays = [value for value, _ in inputs]
    bytes_all = sum(v.size * v.dtype.itemsize for v in in_arrays)
    bytes_all += sum(math.prod(s.shape) * s.dtype.itemsize for s, _ in outputs)
    return pl.pallas_call(
        body,
        grid_spec=pltpu.PrefetchScalarGridSpec(
            num_scalar_prefetch=len(scalars),
            grid=grid,
            in_specs=[spec for _, spec in inputs],
            out_specs=[spec for _, spec in outputs],
            scratch_shapes=list(scratch),
        ),
        out_shape=[shape for shape, _ in outputs],
        input_output_aliases=aliases or {},
        compiler_params=pltpu.CompilerParams(vmem_limit_bytes=VMEM_BYTES),
        cost_estimate=pl.CostEstimate(flops=flops, bytes_accessed=bytes_all, transcendentals=0),
    )(*scalars, *in_arrays)


def whole(array):
    zeros = (0,) * array.ndim
    return pl.BlockSpec(array.shape, lambda *_: zeros)


def mask_half(response, aperture, place, flip, half):
    per_dev, _, _, rcv = response.shape
    rcv_blocks = rcv // BLOCK
    steps = half // BLOCK

    def body(place_ref, flags, x_ref, o_ref):
        block = (place_ref[0] ^ flip) * steps + pl.program_id(0)
        for j in range(per_dev):
            for r in range(rcv_blocks):
                on = flags[j, block, r]
                cut = pl.ds(r * BLOCK, BLOCK)
                value = x_ref[j, :, :, cut]
                o_ref[j, :, :, cut] = value * on.astype(F32).astype(BF16)

    shape = jax.ShapeDtypeStruct((per_dev, 2, half, rcv), BF16)
    block = (per_dev, 2, BLOCK, rcv)
    (out,) = call(
        body,
        (place, aperture),
        [(response, pl.BlockSpec(block, lambda i, a, _: (0, 0, (a[0] ^ flip) * steps + i, 0)))],
        [(shape, pl.BlockSpec(block, lambda i, *_: (0, 0, i, 0)))],
        (steps,),
    )
    return out


def first_spectra(initial, table, freq_place, freq_devs, per_dev, first, rows):
    own, rcv = initial.shape[1:]
    tile = 2 * ROWS

    def body(place_ref, x_ref, t_ref, *outs):
        parts = []
        for half in range(2):
            flat = x_ref[half * ROWS : (half + 1) * ROWS].reshape(ROWS * own, rcv)
            value = jnp.dot(t_ref[0], flat, preferred_element_type=F32)
            parts.append(value.reshape(freq_devs, 2, per_dev, ROWS, rcv))
        both = jnp.concatenate(parts, 3).astype(BF16)
        for step, out in enumerate(outs):
            out[...] = both[step]

    shape = jax.ShapeDtypeStruct((2, per_dev, rows, rcv), BF16)
    return call(
        body,
        (freq_place,),
        [
            (initial, pl.BlockSpec((tile, own, rcv), lambda i, _: (first // tile + i, 0, 0))),
            (table, pl.BlockSpec((1,) + table.shape[1:], lambda i, z: (z[0], 0, 0))),
        ],
        [(shape, pl.BlockSpec((2, per_dev, tile, rcv), lambda i, _: (0, 0, i, 0)))] * freq_devs,
        (rows // tile,),
        flops=2 * 2 * freq_devs * per_dev * own * rows * rcv,
    )


def down_products(near, far, kept, moved, freq_place, freq_devs):
    _, per_dev, rows, rcv = near[0].shape
    width = kept.shape[2]
    tile = min(width, 256)
    share = 2 * rows // freq_devs

    def body(place_ref, n0, n1, f0, f1, k_ref, m_ref, *rest):
        outs, held = rest[:freq_devs], rest[freq_devs]
        for j in range(per_dev):
            total = None
            for own, other, resp in ((n0, n1, k_ref), (f0, f1, m_ref)):
                real = jnp.concatenate([own[0, j], other[0, j]], 0)
                imag = jnp.concatenate([own[1, j], other[1, j]], 0)
                for part, lhs in ((0, [real, imag]), (1, [-imag, real])):
                    term = lax.dot_general(
                        jnp.concatenate(lhs, 0),
                        resp[j, part],
                        (((1,), (1,)), ((), ())),
                        preferred_element_type=F32,
                    )
                    total = term if total is None else total + term
            held[0, j] = total[: 2 * rows]
            held[1, j] = total[2 * rows :]
        for step, out in enumerate(outs):
            start = pl.multiple_of((place_ref[0] ^ step) * share, share)
            out[...] = held[:, :, pl.ds(start, share), :].astype(BF16)

    shape = jax.ShapeDtypeStruct((2, per_dev, share, width), BF16)
    resp_spec = pl.BlockSpec((per_dev, 2, tile, rcv), lambda i, _: (0, 0, i, 0))
    return call(
        body,
        (freq_place,),
        [(v, whole(v)) for v in (*near, *far)] + [(kept, resp_spec), (moved, resp_spec)],
        [(shape, pl.BlockSpec((2, per_dev, share, tile), lambda i, _: (0, 0, 0, i)))] * freq_devs,
        (width // tile,),
        scratch=[pltpu.VMEM((2, per_dev, 2 * rows, tile), F32)],
        flops=2 * 8 * per_dev * 2 * rows * width * rcv,
    )


def windowed(messages, tables, matrix, freq_place, per_dev, share):
    cosines, sines, fraction = tables
    freq_devs = len(messages)
    width = messages[0].shape[-1]
    tile = BLOCK
    count = freq_devs * 2 * per_dev * ROWS

    def body(place_ref, c_ref, s_ref, f_ref, g_ref, *rest):
        refs, outs = rest[:freq_devs], rest[freq_devs:]
        data = [ref[...].astype(F32).reshape(2, per_dev, share, tile) for ref in refs]
        made = [[] for _ in outs]
        for first in range(0, share, ROWS):
            cut = slice(first, first + ROWS)
            plain = [value[:, :, cut] for value in data]
            cos = [c_ref[step, :, cut] for step in range(freq_devs)]
            sin = [s_ref[step, :, cut] for step in range(freq_devs)]
            turned = [
                jnp.stack([v[0] * c - v[1] * s, v[0] * s + v[1] * c])
                for v, c, s in zip(plain, cos, sin)
            ]
            flat = [jnp.stack(v).reshape(count, tile).astype(BF16) for v in (turned, plain)]
            mixed = jnp.dot(g_ref[0], jnp.concatenate(flat, 1), preferred_element_type=F32)
            upper = mixed[:, :tile].reshape(freq_devs, 2, per_dev, ROWS, tile)
            lower = mixed[:, tile:].reshape(freq_devs, 2, per_dev, ROWS, tile)
            part = f_ref[cut]
            for step in range(freq_devs):
                c, s, v, up, low = cos[step], sin[step], plain[step], upper[step], lower[step]
                real = c * up[0] + s * up[1] - low[0] + part * v[0]
                imag = c * up[1] - s * up[0] - low[1] + part * v[1]
                made[step].append(jnp.stack([real, imag]))
        for out, value in zip(outs, made):
            out[...] = jnp.concatenate(value, 2).reshape(out.shape).astype(BF16)

    lead = messages[0].shape[:-1]
    zeros = (0,) * len(lead)
    message = pl.BlockSpec(lead + (tile,), lambda i, _: zeros + (i,))
    table = pl.BlockSpec(cosines.shape[:-1] + (tile,), lambda i, _: (0, 0, 0, i))
    return call(
        body,
        (freq_place,),
        [
            (cosines, table),
            (sines, table),
            (fraction, pl.BlockSpec((share, tile), lambda i, _: (0, i))),
            (matrix, pl.BlockSpec((1,) + matrix.shape[1:], lambda i, z: (z[0], 0, 0))),
        ]
        + [(v, message) for v in messages],
        [(jax.ShapeDtypeStruct(v.shape, BF16), message) for v in messages],
        (width // tile,),
        flops=2 * count * count * 2 * width * share // ROWS,
    )


def up_products(messages, kept, moved, freq_place, rows):
    freq_devs = len(messages)
    per_dev, _, src, rcv = kept.shape
    share = messages[0].shape[2]

    def body(place_ref, k_ref, m_ref, *rest):
        refs = rest[:freq_devs]
        keep, send, held = rest[freq_devs:]
        for step, ref in enumerate(refs):
            start = pl.multiple_of((place_ref[0] ^ step) * share, share)
            held[:, pl.ds(start, share), :] = ref[:, 0]
        real, imag = held[0], held[1]
        one = jnp.concatenate([real, imag], 0)
        two = jnp.concatenate([imag, -real], 0)
        for side, resp in enumerate((k_ref, m_ref)):
            total = jnp.dot(one, resp[0, 0], preferred_element_type=F32)
            total = total + jnp.dot(two, resp[0, 1], preferred_element_type=F32)
            for part in range(2):
                first = 2 * rows * part
                keep[side, part, 0] = total[first : first + rows]
                send[side, part, 0] = total[first + rows : first + 2 * rows].astype(BF16)

    resp_spec = pl.BlockSpec((1, 2, src, rcv), lambda j, _: (j, 0, 0, 0))
    message = pl.BlockSpec((2, 1, share, src), lambda j, _: (0, j, 0, 0))
    out_spec = pl.BlockSpec((2, 2, 1, rows, rcv), lambda j, _: (0, 0, j, 0, 0))
    shape = (2, 2, per_dev, rows, rcv)
    return call(
        body,
        (freq_place,),
        [(kept, resp_spec), (moved, resp_spec)] + [(v, message) for v in messages],
        [(jax.ShapeDtypeStruct(shape, F32), out_spec), (jax.ShapeDtypeStruct(shape, BF16), out_spec)],
        (per_dev,),
        scratch=[pltpu.VMEM((2, 2 * rows, src), BF16)],
        flops=2 * 8 * per_dev * 2 * rows * src * rcv,
    )


def next_spectra(sums, messages, tables, matrix, freq_place):
    cosines, sines, fraction = tables
    freq_devs = len(messages)
    _, per_dev, rows, rcv = sums.shape
    tile = BLOCK
    count = freq_devs * 2 * per_dev * ROWS
    own = 2 * per_dev * ROWS

    def body(place_ref, u_ref, c_ref, s_ref, f_ref, g_ref, *rest):
        refs, out = rest[:freq_devs], rest[freq_devs]
        data = [ref[...].astype(F32) for ref in refs]
        made = []
        for first in range(0, rows, ROWS):
            cut = slice(first, first + ROWS)
            plain = [value[:, :, cut] for value in data]
            cos = [c_ref[step, :, cut] for step in range(freq_devs)]
            sin = [s_ref[step, :, cut] for step in range(freq_devs)]
            turned = [
                jnp.stack([v[0] * c - v[1] * s, v[0] * s + v[1] * c])
                for v, c, s in zip(plain, cos, sin)
            ]
            flat = [jnp.stack(v).reshape(count, tile).astype(BF16) for v in (turned, plain)]
            mixed = jnp.dot(g_ref[0], jnp.concatenate(flat, 1), preferred_element_type=F32)
            up = mixed[:, :tile].reshape(2, per_dev, ROWS, tile)
            low = mixed[:, tile:].reshape(2, per_dev, ROWS, tile)
            c, s, v, part = cos[0], sin[0], plain[0], f_ref[cut]
            real = c * up[0] + s * up[1] - low[0] + part * v[0]
            imag = c * up[1] - s * up[0] - low[1] + part * v[1]
            made.append(jnp.stack([real, imag]))
        out[...] = (u_ref[...] - jnp.concatenate(made, 2)).astype(BF16)

    block = pl.BlockSpec((2, per_dev, rows, tile), lambda i, _: (0, 0, 0, i))
    table = pl.BlockSpec(cosines.shape[:-1] + (tile,), lambda i, _: (0, 0, 0, i))
    (out,) = call(
        body,
        (freq_place,),
        [
            (sums, block),
            (cosines, table),
            (sines, table),
            (fraction, pl.BlockSpec((rows, tile), lambda i, _: (0, i))),
            (matrix, pl.BlockSpec((1, own, count), lambda i, z: (z[0], 0, 0))),
        ]
        + [(v, block) for v in messages],
        [(jax.ShapeDtypeStruct(sums.shape, BF16), block)],
        (rcv // tile,),
        flops=2 * own * count * 2 * rcv * rows // ROWS,
    )
    return out


def updated(initial, onset, messages, table, freq_place, focal_first, first, rows, target):
    freq_devs = len(messages)
    own, rcv = initial.shape[1:]
    per_dev = messages[0].shape[1]
    tile = 2 * ROWS
    count = freq_devs * 2 * per_dev * ROWS

    def body(place_ref, _, x_ref, o_ref, t_ref, *rest):
        refs, out = rest[:freq_devs], rest[-1]
        data = [ref[...].astype(F32) for ref in refs]
        time = lax.broadcasted_iota(jnp.int32, (own, rcv), 0) + place_ref[0] * own
        for half in range(2):
            cut = slice(half * ROWS, (half + 1) * ROWS)
            flat = jnp.stack([v[:, :, cut] for v in data]).reshape(count, rcv).astype(BF16)
            change = jnp.dot(t_ref[0], flat, preferred_element_type=F32)
            for row in range(ROWS):
                spot = half * ROWS + row
                on = time < o_ref[spot : spot + 1, :]
                step = jnp.where(on, change[row * own : (row + 1) * own], 0.0)
                out[spot] = (x_ref[spot].astype(F32) - step).astype(BF16)

    block = pl.BlockSpec((tile, own, rcv), lambda i, *_: (first // tile + i, 0, 0))
    inputs = [
        (initial, block),
        (onset, pl.BlockSpec((tile, rcv), lambda i, _, b: (b[0] + first // tile + i, 0))),
        (table, pl.BlockSpec((1,) + table.shape[1:], lambda i, z, _: (z[0], 0, 0))),
    ] + [(v, pl.BlockSpec((2, per_dev, tile, rcv), lambda i, *_: (0, 0, i, 0))) for v in messages]
    aliases = {}
    if target is not None:
        inputs.append((target, pl.BlockSpec(memory_space=pl.ANY)))
        aliases = {2 + len(inputs) - 1: 0}
    (out,) = call(
        body,
        (freq_place, focal_first),
        inputs,
        [(jax.ShapeDtypeStruct(initial.shape, BF16), block)],
        (rows // tile,),
        aliases=aliases,
        flops=2 * 2 * freq_devs * per_dev * own * rows * rcv,
    )
    return out


def exchanged(value, axis, step):
    return lax.ppermute(value, axis, [(i, i ^ step) for i in range(lax.axis_size(axis))])


def partners(count):
    return sorted(range(1, count), key=lambda step: (step.bit_length() < count.bit_length() - 1, step))


def dealt_out(parts):
    out = list(parts)
    for step in partners(len(parts)):
        out[step] = exchanged(parts[step], "freq", step)
    return out


def spread(value, count):
    return dealt_out([value] * count)


def phases(onset, freq_index, freq_devs, per_dev, samples):
    steps = lax.iota(jnp.int32, freq_devs)
    order = (freq_index ^ steps)[:, None] * per_dev + lax.iota(jnp.int32, per_dev)[None, :] + 1
    phase = order[:, :, None, None] * onset[None, None] % samples
    angle = phase.astype(F32) * (2.0 * math.pi / samples)
    return jnp.cos(angle), jnp.sin(angle), onset.astype(F32) * (1.0 / samples)


def on_device(initial, response, aperture, onset_rcv, onset_src):
    freq_devs = lax.axis_size("freq")
    per_dev = response.shape[0]
    samples = initial.shape[1] * freq_devs
    half_rows = initial.shape[0]
    src_width = response.shape[2] // 2
    rows = half_rows // CHUNKS
    freq_index = lax.axis_index("freq")
    rblk_index = lax.axis_index("rblk")
    sblk_index = lax.axis_index("sblk")
    freq_place = freq_index.reshape(1)
    rblk_place = rblk_index.reshape(1)

    moved = exchanged(mask_half(response, aperture, rblk_place, 1, src_width), "rblk", 1)
    forward = jnp.asarray(forward_tables(samples, freq_devs, per_dev))
    inverse = jnp.asarray(inverse_tables(samples, freq_devs, per_dev))
    matrix = jnp.asarray(window_tables(samples, freq_devs, per_dev))
    kept = mask_half(response, aperture, rblk_place, 0, src_width)

    result = None
    for chunk in range(CHUNKS):
        first = chunk * rows
        parts = first_spectra(initial, forward, freq_place, freq_devs, per_dev, first, rows)
        sums = sum(v.astype(F32) for v in dealt_out(parts))
        spectra = sums.astype(BF16)

        share = 2 * rows // freq_devs
        spot = freq_index * share
        other = (spot >= rows).astype(jnp.int32)
        src_first = (sblk_index ^ other) * half_rows + first + spot - other * rows
        onsets = lax.dynamic_slice(onset_src, (src_first, rblk_index * src_width), (share, src_width))
        src_tables = phases(onsets, freq_index, freq_devs, per_dev, samples)
        onsets = lax.dynamic_slice_in_dim(onset_rcv, sblk_index * half_rows + first, rows, 0)
        rcv_tables = phases(onsets, freq_index, freq_devs, per_dev, samples)

        for step in range(ITERS):
            far_own = exchanged(spectra, "rblk", 1)
            near = (spectra, exchanged(spectra, "sblk", 1))
            far = (far_own, exchanged(far_own, "sblk", 1))
            messages = dealt_out(down_products(near, far, kept, moved, freq_place, freq_devs))
            messages = windowed(messages, src_tables, matrix, freq_place, per_dev, share)
            keep, send = up_products(dealt_out(messages), kept, moved, freq_place, rows)
            from_core = exchanged(send, "sblk", 1)
            from_far = exchanged((keep[1] + from_core[1].astype(F32)).astype(BF16), "rblk", 1)
            back = (keep[0] + from_core[0].astype(F32) + from_far.astype(F32)).astype(BF16)
            messages = spread(back, freq_devs)
            if step < ITERS - 1:
                spectra = next_spectra(sums, messages, rcv_tables, matrix, freq_place)
            else:
                tile_first = (sblk_index * (half_rows // (2 * ROWS))).reshape(1)
                result = updated(
                    initial, onset_rcv, messages, inverse, freq_place, tile_first, first, rows, result
                )
    return result


def transform_tables(length, count):
    table = fields(length, count).reshape(2 * count, length)
    forward_table = jnp.asarray(table.astype(np.float32).astype(BF16))
    inverse_table = jnp.asarray((table.T * (2.0 / length)).astype(np.float32).astype(BF16))
    return forward_table, inverse_table


def settle(values):
    return lax.optimization_barrier(values.astype(BF16)).astype(F32)


def samples_into_spectra(values, forward_table, freq_total):
    out = jnp.einsum("kt,ptn->pkn", forward_table, values, preferred_element_type=F32)
    return out.reshape(values.shape[0], 2, freq_total, values.shape[2]).astype(BF16)


def spectra_into_samples(trace_spectra, inverse_table):
    flat = trace_spectra.reshape(trace_spectra.shape[0], -1, trace_spectra.shape[3])
    return jnp.einsum("tk,pkn->ptn", inverse_table, flat, preferred_element_type=F32)


def dense(spec, gated, real, imag, sign):
    dot = functools.partial(jnp.einsum, spec, preferred_element_type=F32)
    return jnp.stack(
        [dot(gated[:, 0], real) - sign * dot(gated[:, 1], imag), dot(gated[:, 0], imag) + sign * dot(gated[:, 1], real)], 1
    )


def general_device(initial, response, aperture, onset_rcv, onset_src):
    freq_devs, rblk_devs, sblk_devs = (lax.axis_size(a) for a in ("freq", "rblk", "sblk"))
    freq_index, rblk_index, sblk_index = (lax.axis_index(a) for a in ("freq", "rblk", "sblk"))
    freq_total = response.shape[0] * freq_devs
    samples = initial.shape[1] * freq_devs
    focal_all = onset_rcv.shape[0]
    forward_table, inverse_table = transform_tables(samples, freq_total)
    steps_axis = lax.iota(jnp.int32, samples)
    own_axis = freq_index * initial.shape[1] + lax.iota(jnp.int32, initial.shape[1])
    half_rows = focal_all // sblk_devs
    own_onsets = lax.dynamic_slice_in_dim(onset_rcv, sblk_index * half_rows, half_rows, 0)
    rcv_gate = (own_axis[None, :, None] < own_onsets[:, None, :]).astype(F32)
    src_rows = focal_all // (rblk_devs * freq_devs)
    src_first = rblk_index * (focal_all // rblk_devs) + freq_index * src_rows
    src_onsets = lax.dynamic_slice_in_dim(onset_src, src_first, src_rows, 0)
    src_gate = (steps_axis[None, :, None] < src_onsets[:, None, :]).astype(F32)
    mask_full = jnp.repeat(jnp.repeat(aperture, BLOCK, 1), BLOCK, 2).astype(BF16)
    gated = response * mask_full[:, None]
    own_forward = lax.dynamic_slice_in_dim(forward_table, freq_index * initial.shape[1], initial.shape[1], 1)
    own_inverse = lax.dynamic_slice_in_dim(inverse_table, freq_index * initial.shape[1], initial.shape[1], 0)
    current = initial
    for _ in range(ITERS):
        partial = samples_into_spectra(current, own_forward, freq_total)
        spec_back = lax.psum_scatter(partial.astype(F32), "freq", scatter_dimension=2, tiled=True).astype(BF16)
        spec_all = lax.all_gather(spec_back, "sblk", axis=0, tiled=True)
        down = lax.psum_scatter(
            settle(dense("euk,bek->beu", gated, spec_all[:, 0], spec_all[:, 1], 1.0)).astype(BF16),
            "rblk",
            scatter_dimension=0,
            tiled=True,
        )
        src_traces = lax.all_to_all(down, "freq", split_axis=0, concat_axis=2, tiled=True)
        upgoing = (src_gate * spectra_into_samples(src_traces, inverse_table)).astype(BF16)
        upspec = samples_into_spectra(upgoing, forward_table, freq_total)
        up_back = lax.all_to_all(upspec, "freq", split_axis=2, concat_axis=0, tiled=True)
        up_all = lax.all_gather(up_back, "rblk", axis=0, tiled=True)
        sums = dense("qao,bqa->bqo", gated, up_all[:, 0], up_all[:, 1], -1.0).astype(BF16)
        back = lax.psum_scatter(sums, "sblk", scatter_dimension=0, tiled=True)
        traces = lax.all_gather(back, "freq", axis=2, tiled=True)
        update = rcv_gate * spectra_into_samples(traces, own_inverse)
        current = (initial.astype(F32) - update).astype(BF16)
    return current


def fits(initial, response, aperture, onset_rcv, onset_src):
    freq_devs = lax.axis_size("freq")
    if lax.axis_size("rblk") != 2 or lax.axis_size("sblk") != 2 or freq_devs & (freq_devs - 1):
        return False
    rows = initial.shape[0] // CHUNKS
    whole_rows = initial.shape[0] % (CHUNKS * 2 * ROWS * max(1, freq_devs // 2)) == 0 and rows % (2 * ROWS) == 0
    whole_width = response.shape[2] % (4 * BLOCK) == 0 and response.shape[3] % BLOCK == 0
    return whole_rows and whole_width and onset_rcv.shape[0] == 2 * initial.shape[0]


def chosen(*arrays):
    return on_device(*arrays) if fits(*arrays) else general_device(*arrays)


def solution(mesh):
    in_specs = (
        P(("group", "sblk"), "freq", "rblk"),
        P(("group", "freq"), None, "sblk", "rblk"),
        P(("group", "freq"), "sblk", "rblk"),
        P("group", "rblk"),
        P("group", "sblk"),
    )
    out_specs = P(("group", "sblk"), "freq", "rblk")
    return jax.shard_map(chosen, mesh=mesh, in_specs=in_specs, out_specs=out_specs, check_vma=False)
```

```python
import functools
import math

import jax
import jax.numpy as jnp
import numpy as np
from jax import lax
from jax.experimental import pallas as pl
from jax.experimental.pallas import tpu as pltpu
from jax.sharding import PartitionSpec as P

BLOCK = 128
ITERS = 2
ROWS = 8
CHUNKS = 2
VMEM_BYTES = 16 * 1024 * 1024

BF16 = jnp.bfloat16
F32 = jnp.float32


def field_rows(place, freq_devs, per_dev):
    rows = []
    for step in range(freq_devs):
        first = (place ^ step) * per_dev
        for part in range(2):
            rows.extend((part, first + local) for local in range(per_dev))
    return rows


def fields(samples, freq_total):
    phase = (np.arange(1, freq_total + 1)[:, None] * np.arange(samples)[None, :]) % samples
    angle = phase * (2.0 * math.pi / samples)
    return np.stack([np.cos(angle), -np.sin(angle)])


def forward_tables(samples, freq_devs, per_dev):
    table = fields(samples, freq_devs * per_dev)
    own = samples // freq_devs
    eye = np.eye(ROWS)
    out = []
    for place in range(freq_devs):
        part = np.stack([table[c, j, place * own : (place + 1) * own] for c, j in field_rows(place, freq_devs, per_dev)])
        out.append(np.einsum("kt,pq->kpqt", part, eye).reshape(part.shape[0] * ROWS, ROWS * own))
    return np.stack(out).astype(np.float32).astype(BF16)


def inverse_tables(samples, freq_devs, per_dev):
    table = fields(samples, freq_devs * per_dev) * (2.0 / samples)
    own = samples // freq_devs
    eye = np.eye(ROWS)
    out = []
    for place in range(freq_devs):
        part = np.stack([table[c, j, place * own : (place + 1) * own] for c, j in field_rows(place, freq_devs, per_dev)])
        out.append(np.einsum("kt,pq->ptkq", part, eye).reshape(ROWS * own, part.shape[0] * ROWS))
    return np.stack(out).astype(np.float32).astype(BF16)


def window_tables(samples, freq_devs, per_dev):
    freq_total = freq_devs * per_dev
    order = np.arange(1, freq_total + 1)
    unit = 2j * math.pi / samples
    diff = order[None, :] - order[:, None]
    total = order[None, :] + order[:, None]
    same = np.where(diff == 0, 0.0, 1.0 / (samples * (np.exp(unit * np.where(diff == 0, 1, diff)) - 1.0)))
    mixed = 1.0 / (samples * (np.exp(-unit * total) - 1.0))
    full = np.zeros((2, freq_total, 2, freq_total))
    full[0, :, 0, :] = same.real + mixed.real
    full[0, :, 1, :] = mixed.imag - same.imag
    full[1, :, 0, :] = same.imag + mixed.imag
    full[1, :, 1, :] = same.real - mixed.real
    out = []
    for place in range(freq_devs):
        rows = [c * freq_total + j for c, j in field_rows(place, freq_devs, per_dev)]
        flat = full.reshape(2 * freq_total, 2 * freq_total)[np.ix_(rows, rows)]
        out.append(np.kron(flat, np.eye(ROWS)))
    return np.stack(out).astype(np.float32).astype(BF16)


def call(body, scalars, inputs, outputs, grid, scratch=(), aliases=None, flops=0):
    in_arrays = [value for value, _ in inputs]
    bytes_all = sum(v.size * v.dtype.itemsize for v in in_arrays)
    bytes_all += sum(math.prod(s.shape) * s.dtype.itemsize for s, _ in outputs)
    return pl.pallas_call(
        body,
        grid_spec=pltpu.PrefetchScalarGridSpec(
            num_scalar_prefetch=len(scalars),
            grid=grid,
            in_specs=[spec for _, spec in inputs],
            out_specs=[spec for _, spec in outputs],
            scratch_shapes=list(scratch),
        ),
        out_shape=[shape for shape, _ in outputs],
        input_output_aliases=aliases or {},
        compiler_params=pltpu.CompilerParams(vmem_limit_bytes=VMEM_BYTES),
        cost_estimate=pl.CostEstimate(flops=flops, bytes_accessed=bytes_all, transcendentals=0),
    )(*scalars, *in_arrays)


def whole(array):
    zeros = (0,) * array.ndim
    return pl.BlockSpec(array.shape, lambda *_: zeros)


def mask_half(response, aperture, place, flip, half):
    per_dev, _, _, rcv = response.shape
    rcv_blocks = rcv // BLOCK
    steps = half // BLOCK

    def body(place_ref, flags, x_ref, o_ref):
        block = (place_ref[0] ^ flip) * steps + pl.program_id(0)
        for j in range(per_dev):
            for r in range(rcv_blocks):
                on = flags[j, block, r]
                cut = pl.ds(r * BLOCK, BLOCK)
                value = x_ref[j, :, :, cut]
                o_ref[j, :, :, cut] = value * on.astype(F32).astype(BF16)

    shape = jax.ShapeDtypeStruct((per_dev, 2, half, rcv), BF16)
    block = (per_dev, 2, BLOCK, rcv)
    (out,) = call(
        body,
        (place, aperture),
        [(response, pl.BlockSpec(block, lambda i, a, _: (0, 0, (a[0] ^ flip) * steps + i, 0)))],
        [(shape, pl.BlockSpec(block, lambda i, *_: (0, 0, i, 0)))],
        (steps,),
    )
    return out


def first_spectra(initial, table, freq_place, freq_devs, per_dev, first, rows):
    own, rcv = initial.shape[1:]
    tile = 2 * ROWS

    def body(place_ref, x_ref, t_ref, *outs):
        parts = []
        for half in range(2):
            flat = x_ref[half * ROWS : (half + 1) * ROWS].reshape(ROWS * own, rcv)
            value = jnp.dot(t_ref[0], flat, preferred_element_type=F32)
            parts.append(value.reshape(freq_devs, 2, per_dev, ROWS, rcv))
        both = jnp.concatenate(parts, 3).astype(BF16)
        for step, out in enumerate(outs):
            out[...] = both[step]

    shape = jax.ShapeDtypeStruct((2, per_dev, rows, rcv), BF16)
    return call(
        body,
        (freq_place,),
        [
            (initial, pl.BlockSpec((tile, own, rcv), lambda i, _: (first // tile + i, 0, 0))),
            (table, pl.BlockSpec((1,) + table.shape[1:], lambda i, z: (z[0], 0, 0))),
        ],
        [(shape, pl.BlockSpec((2, per_dev, tile, rcv), lambda i, _: (0, 0, i, 0)))] * freq_devs,
        (rows // tile,),
        flops=2 * 2 * freq_devs * per_dev * own * rows * rcv,
    )


def down_products(near, far, kept, moved, freq_place, freq_devs):
    _, per_dev, rows, rcv = near[0].shape
    width = kept.shape[2]
    tile = min(width, 256)
    share = 2 * rows // freq_devs

    def body(place_ref, n0, n1, f0, f1, k_ref, m_ref, *rest):
        outs, held = rest[:freq_devs], rest[freq_devs]
        for j in range(per_dev):
            total = None
            for own, other, resp in ((n0, n1, k_ref), (f0, f1, m_ref)):
                real = jnp.concatenate([own[0, j], other[0, j]], 0)
                imag = jnp.concatenate([own[1, j], other[1, j]], 0)
                for part, lhs in ((0, [real, imag]), (1, [-imag, real])):
                    term = lax.dot_general(
                        jnp.concatenate(lhs, 0),
                        resp[j, part],
                        (((1,), (1,)), ((), ())),
                        preferred_element_type=F32,
                    )
                    total = term if total is None else total + term
            held[0, j] = total[: 2 * rows]
            held[1, j] = total[2 * rows :]
        for step, out in enumerate(outs):
            start = pl.multiple_of((place_ref[0] ^ step) * share, share)
            out[...] = held[:, :, pl.ds(start, share), :].astype(BF16)

    shape = jax.ShapeDtypeStruct((2, per_dev, share, width), BF16)
    resp_spec = pl.BlockSpec((per_dev, 2, tile, rcv), lambda i, _: (0, 0, i, 0))
    return call(
        body,
        (freq_place,),
        [(v, whole(v)) for v in (*near, *far)] + [(kept, resp_spec), (moved, resp_spec)],
        [(shape, pl.BlockSpec((2, per_dev, share, tile), lambda i, _: (0, 0, 0, i)))] * freq_devs,
        (width // tile,),
        scratch=[pltpu.VMEM((2, per_dev, 2 * rows, tile), F32)],
        flops=2 * 8 * per_dev * 2 * rows * width * rcv,
    )


def windowed(messages, tables, matrix, freq_place, per_dev, share):
    cosines, sines, fraction = tables
    freq_devs = len(messages)
    width = messages[0].shape[-1]
    tile = BLOCK
    count = freq_devs * 2 * per_dev * ROWS

    def body(place_ref, c_ref, s_ref, f_ref, g_ref, *rest):
        refs, outs = rest[:freq_devs], rest[freq_devs:]
        data = [ref[...].astype(F32).reshape(2, per_dev, share, tile) for ref in refs]
        made = [[] for _ in outs]
        for first in range(0, share, ROWS):
            cut = slice(first, first + ROWS)
            plain = [value[:, :, cut] for value in data]
            cos = [c_ref[step, :, cut] for step in range(freq_devs)]
            sin = [s_ref[step, :, cut] for step in range(freq_devs)]
            turned = [
                jnp.stack([v[0] * c - v[1] * s, v[0] * s + v[1] * c])
                for v, c, s in zip(plain, cos, sin)
            ]
            flat = [jnp.stack(v).reshape(count, tile).astype(BF16) for v in (turned, plain)]
            mixed = jnp.dot(g_ref[0], jnp.concatenate(flat, 1), preferred_element_type=F32)
            upper = mixed[:, :tile].reshape(freq_devs, 2, per_dev, ROWS, tile)
            lower = mixed[:, tile:].reshape(freq_devs, 2, per_dev, ROWS, tile)
            part = f_ref[cut]
            for step in range(freq_devs):
                c, s, v, up, low = cos[step], sin[step], plain[step], upper[step], lower[step]
                real = c * up[0] + s * up[1] - low[0] + part * v[0]
                imag = c * up[1] - s * up[0] - low[1] + part * v[1]
                made[step].append(jnp.stack([real, imag]))
        for out, value in zip(outs, made):
            out[...] = jnp.concatenate(value, 2).reshape(out.shape).astype(BF16)

    lead = messages[0].shape[:-1]
    zeros = (0,) * len(lead)
    message = pl.BlockSpec(lead + (tile,), lambda i, _: zeros + (i,))
    table = pl.BlockSpec(cosines.shape[:-1] + (tile,), lambda i, _: (0, 0, 0, i))
    return call(
        body,
        (freq_place,),
        [
            (cosines, table),
            (sines, table),
            (fraction, pl.BlockSpec((share, tile), lambda i, _: (0, i))),
            (matrix, pl.BlockSpec((1,) + matrix.shape[1:], lambda i, z: (z[0], 0, 0))),
        ]
        + [(v, message) for v in messages],
        [(jax.ShapeDtypeStruct(v.shape, BF16), message) for v in messages],
        (width // tile,),
        flops=2 * count * count * 2 * width * share // ROWS,
    )


def up_products(messages, kept, moved, freq_place, rows):
    freq_devs = len(messages)
    per_dev, _, src, rcv = kept.shape
    share = messages[0].shape[2]

    def body(place_ref, k_ref, m_ref, *rest):
        refs = rest[:freq_devs]
        keep, send, held = rest[freq_devs:]
        for step, ref in enumerate(refs):
            start = pl.multiple_of((place_ref[0] ^ step) * share, share)
            held[:, pl.ds(start, share), :] = ref[:, 0]
        real, imag = held[0], held[1]
        one = jnp.concatenate([real, imag], 0)
        two = jnp.concatenate([imag, -real], 0)
        for side, resp in enumerate((k_ref, m_ref)):
            total = jnp.dot(one, resp[0, 0], preferred_element_type=F32)
            total = total + jnp.dot(two, resp[0, 1], preferred_element_type=F32)
            for part in range(2):
                first = 2 * rows * part
                keep[side, part, 0] = total[first : first + rows]
                send[side, part, 0] = total[first + rows : first + 2 * rows].astype(BF16)

    resp_spec = pl.BlockSpec((1, 2, src, rcv), lambda j, _: (j, 0, 0, 0))
    message = pl.BlockSpec((2, 1, share, src), lambda j, _: (0, j, 0, 0))
    out_spec = pl.BlockSpec((2, 2, 1, rows, rcv), lambda j, _: (0, 0, j, 0, 0))
    shape = (2, 2, per_dev, rows, rcv)
    return call(
        body,
        (freq_place,),
        [(kept, resp_spec), (moved, resp_spec)] + [(v, message) for v in messages],
        [(jax.ShapeDtypeStruct(shape, F32), out_spec), (jax.ShapeDtypeStruct(shape, BF16), out_spec)],
        (per_dev,),
        scratch=[pltpu.VMEM((2, 2 * rows, src), BF16)],
        flops=2 * 8 * per_dev * 2 * rows * src * rcv,
    )


def next_spectra(sums, messages, tables, matrix, freq_place):
    cosines, sines, fraction = tables
    freq_devs = len(messages)
    _, per_dev, rows, rcv = sums.shape
    tile = BLOCK
    count = freq_devs * 2 * per_dev * ROWS
    own = 2 * per_dev * ROWS

    def body(place_ref, u_ref, c_ref, s_ref, f_ref, g_ref, *rest):
        refs, out = rest[:freq_devs], rest[freq_devs]
        data = [ref[...].astype(F32) for ref in refs]
        made = []
        for first in range(0, rows, ROWS):
            cut = slice(first, first + ROWS)
            plain = [value[:, :, cut] for value in data]
            cos = [c_ref[step, :, cut] for step in range(freq_devs)]
            sin = [s_ref[step, :, cut] for step in range(freq_devs)]
            turned = [
                jnp.stack([v[0] * c - v[1] * s, v[0] * s + v[1] * c])
                for v, c, s in zip(plain, cos, sin)
            ]
            flat = [jnp.stack(v).reshape(count, tile).astype(BF16) for v in (turned, plain)]
            mixed = jnp.dot(g_ref[0], jnp.concatenate(flat, 1), preferred_element_type=F32)
            up = mixed[:, :tile].reshape(2, per_dev, ROWS, tile)
            low = mixed[:, tile:].reshape(2, per_dev, ROWS, tile)
            c, s, v, part = cos[0], sin[0], plain[0], f_ref[cut]
            real = c * up[0] + s * up[1] - low[0] + part * v[0]
            imag = c * up[1] - s * up[0] - low[1] + part * v[1]
            made.append(jnp.stack([real, imag]))
        out[...] = (u_ref[...] - jnp.concatenate(made, 2)).astype(BF16)

    block = pl.BlockSpec((2, per_dev, rows, tile), lambda i, _: (0, 0, 0, i))
    table = pl.BlockSpec(cosines.shape[:-1] + (tile,), lambda i, _: (0, 0, 0, i))
    (out,) = call(
        body,
        (freq_place,),
        [
            (sums, block),
            (cosines, table),
            (sines, table),
            (fraction, pl.BlockSpec((rows, tile), lambda i, _: (0, i))),
            (matrix, pl.BlockSpec((1, own, count), lambda i, z: (z[0], 0, 0))),
        ]
        + [(v, block) for v in messages],
        [(jax.ShapeDtypeStruct(sums.shape, BF16), block)],
        (rcv // tile,),
        flops=2 * own * count * 2 * rcv * rows // ROWS,
    )
    return out


def updated(initial, onset, messages, table, freq_place, focal_first, first, rows, target):
    freq_devs = len(messages)
    own, rcv = initial.shape[1:]
    per_dev = messages[0].shape[1]
    tile = 2 * ROWS
    count = freq_devs * 2 * per_dev * ROWS

    def body(place_ref, _, x_ref, o_ref, t_ref, *rest):
        refs, out = rest[:freq_devs], rest[-1]
        data = [ref[...].astype(F32) for ref in refs]
        time = lax.broadcasted_iota(jnp.int32, (own, rcv), 0) + place_ref[0] * own
        for half in range(2):
            cut = slice(half * ROWS, (half + 1) * ROWS)
            flat = jnp.stack([v[:, :, cut] for v in data]).reshape(count, rcv).astype(BF16)
            change = jnp.dot(t_ref[0], flat, preferred_element_type=F32)
            for row in range(ROWS):
                spot = half * ROWS + row
                on = time < o_ref[spot : spot + 1, :]
                step = jnp.where(on, change[row * own : (row + 1) * own], 0.0)
                out[spot] = (x_ref[spot].astype(F32) - step).astype(BF16)

    block = pl.BlockSpec((tile, own, rcv), lambda i, *_: (first // tile + i, 0, 0))
    inputs = [
        (initial, block),
        (onset, pl.BlockSpec((tile, rcv), lambda i, _, b: (b[0] + first // tile + i, 0))),
        (table, pl.BlockSpec((1,) + table.shape[1:], lambda i, z, _: (z[0], 0, 0))),
    ] + [(v, pl.BlockSpec((2, per_dev, tile, rcv), lambda i, *_: (0, 0, i, 0))) for v in messages]
    aliases = {}
    if target is not None:
        inputs.append((target, pl.BlockSpec(memory_space=pl.ANY)))
        aliases = {2 + len(inputs) - 1: 0}
    (out,) = call(
        body,
        (freq_place, focal_first),
        inputs,
        [(jax.ShapeDtypeStruct(initial.shape, BF16), block)],
        (rows // tile,),
        aliases=aliases,
        flops=2 * 2 * freq_devs * per_dev * own * rows * rcv,
    )
    return out


def exchanged(value, axis, step):
    return lax.ppermute(value, axis, [(i, i ^ step) for i in range(lax.axis_size(axis))])


def partners(count):
    return sorted(range(1, count), key=lambda step: (step.bit_length() < count.bit_length() - 1, step))


def dealt_out(parts):
    out = list(parts)
    for step in partners(len(parts)):
        out[step] = exchanged(parts[step], "freq", step)
    return out


def spread(value, count):
    return dealt_out([value] * count)


def phases(onset, freq_index, freq_devs, per_dev, samples):
    steps = lax.iota(jnp.int32, freq_devs)
    order = (freq_index ^ steps)[:, None] * per_dev + lax.iota(jnp.int32, per_dev)[None, :] + 1
    phase = order[:, :, None, None] * onset[None, None] % samples
    angle = phase.astype(F32) * (2.0 * math.pi / samples)
    return jnp.cos(angle), jnp.sin(angle), onset.astype(F32) * (1.0 / samples)


def on_device(initial, response, aperture, onset_rcv, onset_src):
    freq_devs = lax.axis_size("freq")
    per_dev = response.shape[0]
    samples = initial.shape[1] * freq_devs
    half_rows = initial.shape[0]
    src_width = response.shape[2] // 2
    rows = half_rows // CHUNKS
    freq_index = lax.axis_index("freq")
    rblk_index = lax.axis_index("rblk")
    sblk_index = lax.axis_index("sblk")
    freq_place = freq_index.reshape(1)
    rblk_place = rblk_index.reshape(1)

    moved = exchanged(mask_half(response, aperture, rblk_place, 1, src_width), "rblk", 1)
    forward = jnp.asarray(forward_tables(samples, freq_devs, per_dev))
    inverse = jnp.asarray(inverse_tables(samples, freq_devs, per_dev))
    matrix = jnp.asarray(window_tables(samples, freq_devs, per_dev))
    kept = mask_half(response, aperture, rblk_place, 0, src_width)

    result = None
    for chunk in range(CHUNKS):
        first = chunk * rows
        parts = first_spectra(initial, forward, freq_place, freq_devs, per_dev, first, rows)
        sums = sum(v.astype(F32) for v in dealt_out(parts))
        spectra = sums.astype(BF16)

        share = 2 * rows // freq_devs
        spot = freq_index * share
        other = (spot >= rows).astype(jnp.int32)
        src_first = (sblk_index ^ other) * half_rows + first + spot - other * rows
        onsets = lax.dynamic_slice(onset_src, (src_first, rblk_index * src_width), (share, src_width))
        src_tables = phases(onsets, freq_index, freq_devs, per_dev, samples)
        onsets = lax.dynamic_slice_in_dim(onset_rcv, sblk_index * half_rows + first, rows, 0)
        rcv_tables = phases(onsets, freq_index, freq_devs, per_dev, samples)

        for step in range(ITERS):
            far_own = exchanged(spectra, "rblk", 1)
            near = (spectra, exchanged(spectra, "sblk", 1))
            far = (far_own, exchanged(far_own, "sblk", 1))
            messages = dealt_out(down_products(near, far, kept, moved, freq_place, freq_devs))
            messages = windowed(messages, src_tables, matrix, freq_place, per_dev, share)
            keep, send = up_products(dealt_out(messages), kept, moved, freq_place, rows)
            from_core = exchanged(send, "sblk", 1)
            from_far = exchanged((keep[1] + from_core[1].astype(F32)).astype(BF16), "rblk", 1)
            back = (keep[0] + from_core[0].astype(F32) + from_far.astype(F32)).astype(BF16)
            messages = spread(back, freq_devs)
            if step < ITERS - 1:
                spectra = next_spectra(sums, messages, rcv_tables, matrix, freq_place)
            else:
                tile_first = (sblk_index * (half_rows // (2 * ROWS))).reshape(1)
                result = updated(
                    initial, onset_rcv, messages, inverse, freq_place, tile_first, first, rows, result
                )
    return result


def transform_tables(length, count):
    table = fields(length, count).reshape(2 * count, length)
    forward_table = jnp.asarray(table.astype(np.float32).astype(BF16))
    inverse_table = jnp.asarray((table.T * (2.0 / length)).astype(np.float32).astype(BF16))
    return forward_table, inverse_table


def settle(values):
    return lax.optimization_barrier(values.astype(BF16)).astype(F32)


def samples_into_spectra(values, forward_table, freq_total):
    out = jnp.einsum("kt,ptn->pkn", forward_table, values, preferred_element_type=F32)
    return out.reshape(values.shape[0], 2, freq_total, values.shape[2]).astype(BF16)


def spectra_into_samples(trace_spectra, inverse_table):
    flat = trace_spectra.reshape(trace_spectra.shape[0], -1, trace_spectra.shape[3])
    return jnp.einsum("tk,pkn->ptn", inverse_table, flat, preferred_element_type=F32)


def dense(spec, gated, real, imag, sign):
    dot = functools.partial(jnp.einsum, spec, preferred_element_type=F32)
    return jnp.stack(
        [dot(gated[:, 0], real) - sign * dot(gated[:, 1], imag), dot(gated[:, 0], imag) + sign * dot(gated[:, 1], real)], 1
    )


def general_device(initial, response, aperture, onset_rcv, onset_src):
    freq_devs, rblk_devs, sblk_devs = (lax.axis_size(a) for a in ("freq", "rblk", "sblk"))
    freq_index, rblk_index, sblk_index = (lax.axis_index(a) for a in ("freq", "rblk", "sblk"))
    freq_total = response.shape[0] * freq_devs
    samples = initial.shape[1] * freq_devs
    focal_all = onset_rcv.shape[0]
    forward_table, inverse_table = transform_tables(samples, freq_total)
    steps_axis = lax.iota(jnp.int32, samples)
    own_axis = freq_index * initial.shape[1] + lax.iota(jnp.int32, initial.shape[1])
    half_rows = focal_all // sblk_devs
    own_onsets = lax.dynamic_slice_in_dim(onset_rcv, sblk_index * half_rows, half_rows, 0)
    rcv_gate = (own_axis[None, :, None] < own_onsets[:, None, :]).astype(F32)
    src_rows = focal_all // (rblk_devs * freq_devs)
    src_first = rblk_index * (focal_all // rblk_devs) + freq_index * src_rows
    src_onsets = lax.dynamic_slice_in_dim(onset_src, src_first, src_rows, 0)
    src_gate = (steps_axis[None, :, None] < src_onsets[:, None, :]).astype(F32)
    mask_full = jnp.repeat(jnp.repeat(aperture, BLOCK, 1), BLOCK, 2).astype(BF16)
    gated = response * mask_full[:, None]
    own_forward = lax.dynamic_slice_in_dim(forward_table, freq_index * initial.shape[1], initial.shape[1], 1)
    own_inverse = lax.dynamic_slice_in_dim(inverse_table, freq_index * initial.shape[1], initial.shape[1], 0)
    current = initial
    for _ in range(ITERS):
        partial = samples_into_spectra(current, own_forward, freq_total)
        spec_back = lax.psum_scatter(partial.astype(F32), "freq", scatter_dimension=2, tiled=True).astype(BF16)
        spec_all = lax.all_gather(spec_back, "sblk", axis=0, tiled=True)
        down = lax.psum_scatter(
            settle(dense("euk,bek->beu", gated, spec_all[:, 0], spec_all[:, 1], 1.0)).astype(BF16),
            "rblk",
            scatter_dimension=0,
            tiled=True,
        )
        src_traces = lax.all_to_all(down, "freq", split_axis=0, concat_axis=2, tiled=True)
        upgoing = (src_gate * spectra_into_samples(src_traces, inverse_table)).astype(BF16)
        upspec = samples_into_spectra(upgoing, forward_table, freq_total)
        up_back = lax.all_to_all(upspec, "freq", split_axis=2, concat_axis=0, tiled=True)
        up_all = lax.all_gather(up_back, "rblk", axis=0, tiled=True)
        sums = dense("qao,bqa->bqo", gated, up_all[:, 0], up_all[:, 1], -1.0).astype(BF16)
        back = lax.psum_scatter(sums, "sblk", scatter_dimension=0, tiled=True)
        traces = lax.all_gather(back, "freq", axis=2, tiled=True)
        update = rcv_gate * spectra_into_samples(traces, own_inverse)
        current = (initial.astype(F32) - update).astype(BF16)
    return current


def fits(initial, response, aperture, onset_rcv, onset_src):
    freq_devs = lax.axis_size("freq")
    if lax.axis_size("rblk") != 2 or lax.axis_size("sblk") != 2 or freq_devs & (freq_devs - 1):
        return False
    rows = initial.shape[0] // CHUNKS
    whole_rows = initial.shape[0] % (CHUNKS * 2 * ROWS * max(1, freq_devs // 2)) == 0 and rows % (2 * ROWS) == 0
    whole_width = response.shape[2] % (4 * BLOCK) == 0 and response.shape[3] % BLOCK == 0
    return whole_rows and whole_width and onset_rcv.shape[0] == 2 * initial.shape[0]


def chosen(*arrays):
    return on_device(*arrays) if fits(*arrays) else general_device(*arrays)


def solution(mesh):
    in_specs = (
        P(("group", "sblk"), "freq", "rblk"),
        P(("group", "freq"), None, "sblk", "rblk"),
        P(("group", "freq"), "sblk", "rblk"),
        P("group", "rblk"),
        P("group", "sblk"),
    )
    out_specs = P(("group", "sblk"), "freq", "rblk")
    return jax.shard_map(chosen, mesh=mesh, in_specs=in_specs, out_specs=out_specs, check_vma=False)
```

```python
import functools
import math

import jax
import jax.numpy as jnp
import numpy as np
from jax import lax
from jax.experimental import pallas as pl
from jax.experimental.pallas import tpu as pltpu
from jax.sharding import PartitionSpec as P

BLOCK = 128
ITERS = 2
ROWS = 8
CHUNKS = 1
VMEM_BYTES = 16 * 1024 * 1024
WIDE_VMEM_BYTES = 60 * 1024 * 1024

BF16 = jnp.bfloat16
F32 = jnp.float32


def ways(count):
    far = sorted(range(1, count), key=lambda step: (step.bit_length() < count.bit_length() - 1, step))
    return [0] + far


def field_rows(place, freq_devs, per_dev):
    rows = []
    for step in ways(freq_devs):
        first = (place ^ step) * per_dev
        for part in range(2):
            rows.extend((part, first + local) for local in range(per_dev))
    return rows


def fields(samples, freq_total):
    phase = (np.arange(1, freq_total + 1)[:, None] * np.arange(samples)[None, :]) % samples
    angle = phase * (2.0 * math.pi / samples)
    return np.stack([np.cos(angle), -np.sin(angle)])


def forward_tables(samples, freq_devs, per_dev):
    table = fields(samples, freq_devs * per_dev)
    own = samples // freq_devs
    eye = np.eye(ROWS)
    out = []
    for place in range(freq_devs):
        part = np.stack([table[c, j, place * own : (place + 1) * own] for c, j in field_rows(place, freq_devs, per_dev)])
        out.append(np.einsum("kt,pq->kpqt", part, eye).reshape(part.shape[0] * ROWS, ROWS * own))
    return np.stack(out).astype(np.float32).astype(BF16)


def inverse_tables(samples, freq_devs, per_dev):
    table = fields(samples, freq_devs * per_dev) * (2.0 / samples)
    own = samples // freq_devs
    eye = np.eye(ROWS)
    out = []
    for place in range(freq_devs):
        part = np.stack([table[c, j, place * own : (place + 1) * own] for c, j in field_rows(place, freq_devs, per_dev)])
        out.append(np.einsum("kt,pq->ptkq", part, eye).reshape(ROWS * own, part.shape[0] * ROWS))
    return np.stack(out).astype(np.float32).astype(BF16)


def window_tables(samples, freq_devs, per_dev):
    freq_total = freq_devs * per_dev
    order = np.arange(1, freq_total + 1)
    unit = 2j * math.pi / samples
    diff = order[None, :] - order[:, None]
    total = order[None, :] + order[:, None]
    same = np.where(diff == 0, 0.0, 1.0 / (samples * (np.exp(unit * np.where(diff == 0, 1, diff)) - 1.0)))
    mixed = 1.0 / (samples * (np.exp(-unit * total) - 1.0))
    full = np.zeros((2, freq_total, 2, freq_total))
    full[0, :, 0, :] = same.real + mixed.real
    full[0, :, 1, :] = mixed.imag - same.imag
    full[1, :, 0, :] = same.imag + mixed.imag
    full[1, :, 1, :] = same.real - mixed.real
    out = []
    for place in range(freq_devs):
        rows = [c * freq_total + j for c, j in field_rows(place, freq_devs, per_dev)]
        flat = full.reshape(2 * freq_total, 2 * freq_total)[np.ix_(rows, rows)]
        out.append(np.kron(flat, np.eye(ROWS)))
    return np.stack(out).astype(np.float32).astype(BF16)


def call(body, scalars, inputs, outputs, grid, scratch=(), aliases=None, flops=0, vmem=VMEM_BYTES):
    in_arrays = [value for value, _ in inputs]
    bytes_all = sum(v.size * v.dtype.itemsize for v in in_arrays)
    bytes_all += sum(math.prod(s.shape) * s.dtype.itemsize for s, _ in outputs)
    return pl.pallas_call(
        body,
        grid_spec=pltpu.PrefetchScalarGridSpec(
            num_scalar_prefetch=len(scalars),
            grid=grid,
            in_specs=[spec for _, spec in inputs],
            out_specs=[spec for _, spec in outputs],
            scratch_shapes=list(scratch),
        ),
        out_shape=[shape for shape, _ in outputs],
        input_output_aliases=aliases or {},
        compiler_params=pltpu.CompilerParams(vmem_limit_bytes=vmem),
        cost_estimate=pl.CostEstimate(flops=flops, bytes_accessed=bytes_all, transcendentals=0),
    )(*scalars, *in_arrays)


def whole(array):
    zeros = (0,) * array.ndim
    return pl.BlockSpec(array.shape, lambda *_: zeros)


def streamed(step, steps, copies):
    @pl.when(step == 0)
    def _():
        copies(0).start()

    @pl.when(step + 1 < steps)
    def _():
        copies(step + 1).start()

    copies(step).wait()


def mask_half(response, aperture, place, flip, half, vmem):
    per_dev, _, _, rcv = response.shape
    rcv_blocks = rcv // BLOCK
    steps = half // BLOCK

    def body(place_ref, flags, x_hbm, o_ref, slots, sems):
        step = pl.program_id(0)
        base = (place_ref[0] ^ flip) * steps

        def copies(k):
            rows = pl.ds(pl.multiple_of((base + k) * BLOCK, BLOCK), BLOCK)
            return pltpu.make_async_copy(x_hbm.at[:, :, rows, :], slots.at[k % 2], sems.at[k % 2])

        streamed(step, steps, copies)
        for j in range(per_dev):
            for r in range(rcv_blocks):
                on = flags[j, base + step, r]
                cut = pl.ds(r * BLOCK, BLOCK)
                o_ref[j, :, :, cut] = slots[step % 2, j, :, :, cut] * on.astype(F32).astype(BF16)

    shape = jax.ShapeDtypeStruct((per_dev, 2, half, rcv), BF16)
    block = (per_dev, 2, BLOCK, rcv)
    (out,) = call(
        body,
        (place, aperture),
        [(response, pl.BlockSpec(memory_space=pltpu.HBM))],
        [(shape, pl.BlockSpec(block, lambda i, *_: (0, 0, i, 0)))],
        (steps,),
        scratch=[pltpu.VMEM((2,) + block, BF16), pltpu.SemaphoreType.DMA((2,))],
        vmem=vmem,
    )
    return out


def first_spectra(initial, table, freq_place, freq_devs, per_dev, first, rows):
    own, rcv = initial.shape[1:]
    tile = 2 * ROWS
    steps = rows // tile

    def body(place_ref, x_hbm, t_hbm, *rest):
        outs = rest[:freq_devs]
        slots, sems, t_ref, t_sem = rest[freq_devs:]
        step = pl.program_id(0)
        fetch = pltpu.make_async_copy(t_hbm.at[place_ref[0]], t_ref, t_sem)

        @pl.when(step == 0)
        def _():
            fetch.start()

        def copies(k):
            cut = pl.ds(first + k * tile, tile)
            return pltpu.make_async_copy(x_hbm.at[cut], slots.at[k % 2], sems.at[k % 2])

        streamed(step, steps, copies)

        @pl.when(step == 0)
        def _():
            fetch.wait()

        parts = []
        for half in range(2):
            flat = slots[step % 2, half * ROWS : (half + 1) * ROWS].reshape(ROWS * own, rcv)
            value = jnp.dot(t_ref[...], flat, preferred_element_type=F32)
            parts.append(value.reshape(freq_devs, 2, per_dev, ROWS, rcv))
        both = jnp.concatenate(parts, 3).astype(BF16)
        for at, out in enumerate(outs):
            out[...] = both[at]

    shape = jax.ShapeDtypeStruct((2, per_dev, rows, rcv), BF16)
    hbm = pl.BlockSpec(memory_space=pltpu.HBM)
    return call(
        body,
        (freq_place,),
        [(initial, hbm), (table, hbm)],
        [(shape, pl.BlockSpec((2, per_dev, tile, rcv), lambda i, _: (0, 0, i, 0)))] * freq_devs,
        (steps,),
        scratch=[
            pltpu.VMEM((2, tile, own, rcv), BF16),
            pltpu.SemaphoreType.DMA((2,)),
            pltpu.VMEM(table.shape[1:], BF16),
            pltpu.SemaphoreType.DMA,
        ],
        flops=2 * 2 * freq_devs * per_dev * own * rows * rcv,
    )


def down_products(near, far, responses, freq_place, freq_devs):
    _, per_dev, rows, rcv = near.shape
    width = responses[0][0].shape[2]
    tile = min(width, 256)
    steps = width // tile
    share = rows // freq_devs

    def body(place_ref, n_ref, f_ref, k0, m0, k1, m1, *rest):
        outs, held = rest[:freq_devs], rest[freq_devs]

        def products(pairs):
            for j in range(per_dev):
                total = None
                for lhs_ref, resp in pairs:
                    real, imag = lhs_ref[0, j], lhs_ref[1, j]
                    for part, lhs in ((0, [real, imag]), (1, [-imag, real])):
                        term = lax.dot_general(
                            jnp.concatenate(lhs, 0),
                            resp[j, part],
                            (((1,), (1,)), ((), ())),
                            preferred_element_type=F32,
                        )
                        total = term if total is None else total + term
                held[0, j] = total[:rows]
                held[1, j] = total[rows:]

        step = pl.program_id(0)

        @pl.when(step < steps)
        def _():
            products(((n_ref, k0), (f_ref, m0)))

        @pl.when(step >= steps)
        def _():
            products(((n_ref, k1), (f_ref, m1)))

        for way, out in zip(ways(freq_devs), outs):
            start = pl.multiple_of((place_ref[0] ^ way) * share, share)
            out[...] = held[:, :, pl.ds(start, share), :].astype(BF16)

    shape = jax.ShapeDtypeStruct((2, per_dev, share, 2 * width), BF16)
    block = (per_dev, 2, tile, rcv)
    low = pl.BlockSpec(block, lambda i, _: (0, 0, jnp.minimum(i, steps - 1), 0))
    high = pl.BlockSpec(block, lambda i, _: (0, 0, jnp.maximum(i - steps, 0), 0))
    (k0, m0), (k1, m1) = responses
    return call(
        body,
        (freq_place,),
        [(near, whole(near)), (far, whole(far)), (k0, low), (m0, low), (k1, high), (m1, high)],
        [(shape, pl.BlockSpec((2, per_dev, share, tile), lambda i, _: (0, 0, 0, i)))] * freq_devs,
        (2 * steps,),
        scratch=[pltpu.VMEM((2, per_dev, rows, tile), F32)],
        flops=2 * 8 * per_dev * rows * 2 * width * rcv,
    )


def windowed(messages, tables, matrix, freq_place, per_dev, share):
    cosines, sines, fraction = tables
    freq_devs = len(messages)
    width = messages[0].shape[-1]
    tile = BLOCK
    count = freq_devs * 2 * per_dev * ROWS

    def body(place_ref, c_ref, s_ref, f_ref, g_ref, *rest):
        refs, outs = rest[:freq_devs], rest[freq_devs:]
        data = [ref[...].astype(F32).reshape(2, per_dev, share, tile) for ref in refs]
        made = [[] for _ in outs]
        for first in range(0, share, ROWS):
            cut = slice(first, first + ROWS)
            plain = [value[:, :, cut] for value in data]
            cos = [c_ref[step, :, cut] for step in range(freq_devs)]
            sin = [s_ref[step, :, cut] for step in range(freq_devs)]
            turned = [
                jnp.stack([v[0] * c - v[1] * s, v[0] * s + v[1] * c])
                for v, c, s in zip(plain, cos, sin)
            ]
            flat = [jnp.stack(v).reshape(count, tile).astype(BF16) for v in (turned, plain)]
            mixed = jnp.dot(g_ref[0], jnp.concatenate(flat, 1), preferred_element_type=F32)
            upper = mixed[:, :tile].reshape(freq_devs, 2, per_dev, ROWS, tile)
            lower = mixed[:, tile:].reshape(freq_devs, 2, per_dev, ROWS, tile)
            part = f_ref[cut]
            for step in range(freq_devs):
                c, s, v, up, low = cos[step], sin[step], plain[step], upper[step], lower[step]
                real = c * up[0] + s * up[1] - low[0] + part * v[0]
                imag = c * up[1] - s * up[0] - low[1] + part * v[1]
                made[step].append(jnp.stack([real, imag]))
        for out, value in zip(outs, made):
            out[...] = jnp.concatenate(value, 2).reshape(out.shape).astype(BF16)

    lead = messages[0].shape[:-1]
    zeros = (0,) * len(lead)
    message = pl.BlockSpec(lead + (tile,), lambda i, _: zeros + (i,))
    table = pl.BlockSpec(cosines.shape[:-1] + (tile,), lambda i, _: (0, 0, 0, i))
    return call(
        body,
        (freq_place,),
        [
            (cosines, table),
            (sines, table),
            (fraction, pl.BlockSpec((share, tile), lambda i, _: (0, i))),
            (matrix, pl.BlockSpec((1,) + matrix.shape[1:], lambda i, z: (z[0], 0, 0))),
        ]
        + [(v, message) for v in messages],
        [(jax.ShapeDtypeStruct(v.shape, BF16), message) for v in messages],
        (width // tile,),
        flops=2 * count * count * 2 * width * share // ROWS,
    )


def up_products(messages, responses, freq_place, rows):
    freq_devs = len(messages)
    (k0, m0), (k1, m1) = responses
    per_dev, _, src, rcv = k0.shape
    share = messages[0].shape[2]

    def body(place_ref, k0_ref, m0_ref, k1_ref, m1_ref, *rest):
        refs = rest[:freq_devs]
        keep, send, held = rest[freq_devs:]
        for way, ref in zip(ways(freq_devs), refs):
            start = pl.multiple_of((place_ref[0] ^ way) * share, share)
            held[:, pl.ds(start, share), :] = ref[:, 0]
        for out, pair in ((send, (m0_ref, m1_ref)), (keep, (k0_ref, k1_ref))):
            total = None
            for half, resp in enumerate(pair):
                cut = pl.ds(half * src, src)
                real, imag = held[0, :, cut], held[1, :, cut]
                for part, lhs in ((0, [real, imag]), (1, [imag, -real])):
                    term = jnp.dot(jnp.concatenate(lhs, 0), resp[0, part], preferred_element_type=F32)
                    total = term if total is None else total + term
            for part in range(2):
                out[part, 0] = total[rows * part : rows * (part + 1)].astype(out.dtype)

    resp_spec = pl.BlockSpec((1, 2, src, rcv), lambda j, _: (j, 0, 0, 0))
    message = pl.BlockSpec((2, 1, share, 2 * src), lambda j, _: (0, j, 0, 0))
    out_spec = pl.BlockSpec((2, 1, rows, rcv), lambda j, _: (0, j, 0, 0))
    shape = (2, per_dev, rows, rcv)
    return call(
        body,
        (freq_place,),
        [(v, resp_spec) for v in (k0, m0, k1, m1)] + [(v, message) for v in messages],
        [(jax.ShapeDtypeStruct(shape, F32), out_spec), (jax.ShapeDtypeStruct(shape, BF16), out_spec)],
        (per_dev,),
        scratch=[pltpu.VMEM((2, rows, 2 * src), BF16)],
        flops=2 * 8 * per_dev * rows * 2 * src * rcv,
    )


def next_spectra(sums, messages, tables, matrix, freq_place):
    cosines, sines, fraction = tables
    freq_devs = len(messages)
    _, per_dev, rows, rcv = sums.shape
    tile = BLOCK
    count = freq_devs * 2 * per_dev * ROWS
    own = 2 * per_dev * ROWS

    def body(place_ref, u_ref, c_ref, s_ref, f_ref, g_ref, *rest):
        refs, out = rest[:freq_devs], rest[freq_devs]
        data = [ref[...].astype(F32) for ref in refs]
        made = []
        for first in range(0, rows, ROWS):
            cut = slice(first, first + ROWS)
            plain = [value[:, :, cut] for value in data]
            cos = [c_ref[step, :, cut] for step in range(freq_devs)]
            sin = [s_ref[step, :, cut] for step in range(freq_devs)]
            turned = [
                jnp.stack([v[0] * c - v[1] * s, v[0] * s + v[1] * c])
                for v, c, s in zip(plain, cos, sin)
            ]
            flat = [jnp.stack(v).reshape(count, tile).astype(BF16) for v in (turned, plain)]
            mixed = jnp.dot(g_ref[0], jnp.concatenate(flat, 1), preferred_element_type=F32)
            up = mixed[:, :tile].reshape(2, per_dev, ROWS, tile)
            low = mixed[:, tile:].reshape(2, per_dev, ROWS, tile)
            c, s, v, part = cos[0], sin[0], plain[0], f_ref[cut]
            real = c * up[0] + s * up[1] - low[0] + part * v[0]
            imag = c * up[1] - s * up[0] - low[1] + part * v[1]
            made.append(jnp.stack([real, imag]))
        out[...] = (u_ref[...] - jnp.concatenate(made, 2)).astype(BF16)

    block = pl.BlockSpec((2, per_dev, rows, tile), lambda i, _: (0, 0, 0, i))
    table = pl.BlockSpec(cosines.shape[:-1] + (tile,), lambda i, _: (0, 0, 0, i))
    (out,) = call(
        body,
        (freq_place,),
        [
            (sums, block),
            (cosines, table),
            (sines, table),
            (fraction, pl.BlockSpec((rows, tile), lambda i, _: (0, i))),
            (matrix, pl.BlockSpec((1, own, count), lambda i, z: (z[0], 0, 0))),
        ]
        + [(v, block) for v in messages],
        [(jax.ShapeDtypeStruct(sums.shape, BF16), block)],
        (rcv // tile,),
        flops=2 * own * count * 2 * rcv * rows // ROWS,
    )
    return out


def updated(initial, onset, messages, table, freq_place, focal_first, first, rows, target):
    freq_devs = len(messages)
    own, rcv = initial.shape[1:]
    per_dev = messages[0].shape[1]
    tile = 2 * ROWS
    steps = rows // tile
    count = freq_devs * 2 * per_dev * ROWS

    def body(place_ref, _, x_hbm, t_hbm, o_ref, *rest):
        refs = rest[:freq_devs]
        out, slots, sems, t_ref, t_sem = rest[-5:]
        step = pl.program_id(0)
        fetch = pltpu.make_async_copy(t_hbm.at[place_ref[0]], t_ref, t_sem)

        @pl.when(step == 0)
        def _():
            fetch.start()

        def copies(k):
            cut = pl.ds(first + k * tile, tile)
            return pltpu.make_async_copy(x_hbm.at[cut], slots.at[k % 2], sems.at[k % 2])

        streamed(step, steps, copies)

        @pl.when(step == 0)
        def _():
            fetch.wait()

        data = [ref[...].astype(F32) for ref in refs]
        time = lax.broadcasted_iota(jnp.int32, (own, rcv), 0) + place_ref[0] * own
        for half in range(2):
            cut = slice(half * ROWS, (half + 1) * ROWS)
            flat = jnp.stack([v[:, :, cut] for v in data]).reshape(count, rcv).astype(BF16)
            change = jnp.dot(t_ref[...], flat, preferred_element_type=F32)
            for row in range(ROWS):
                spot = half * ROWS + row
                on = time < o_ref[spot : spot + 1, :]
                moved = jnp.where(on, change[row * own : (row + 1) * own], 0.0)
                out[spot] = (slots[step % 2, spot].astype(F32) - moved).astype(BF16)

    hbm = pl.BlockSpec(memory_space=pltpu.HBM)
    inputs = [
        (initial, hbm),
        (table, hbm),
        (onset, pl.BlockSpec((tile, rcv), lambda i, _, b: (b[0] + first // tile + i, 0))),
    ] + [(v, pl.BlockSpec((2, per_dev, tile, rcv), lambda i, *_: (0, 0, i, 0))) for v in messages]
    aliases = {}
    if target is not None:
        inputs.append((target, hbm))
        aliases = {2 + len(inputs) - 1: 0}
    (out,) = call(
        body,
        (freq_place, focal_first),
        inputs,
        [(jax.ShapeDtypeStruct(initial.shape, BF16), pl.BlockSpec((tile, own, rcv), lambda i, *_: (first // tile + i, 0, 0)))],
        (steps,),
        scratch=[
            pltpu.VMEM((2, tile, own, rcv), BF16),
            pltpu.SemaphoreType.DMA((2,)),
            pltpu.VMEM(table.shape[1:], BF16),
            pltpu.SemaphoreType.DMA,
        ],
        aliases=aliases,
        vmem=WIDE_VMEM_BYTES,
        flops=2 * 2 * freq_devs * per_dev * own * rows * rcv,
    )
    return out


def exchanged(value, axis, step):
    return lax.ppermute(value, axis, [(i, i ^ step) for i in range(lax.axis_size(axis))])


def dealt_out(parts):
    return [exchanged(part, "freq", step) if step else part for part, step in zip(parts, ways(len(parts)))]


def spread(value, count):
    return dealt_out([value] * count)


def phases(onset, freq_index, freq_devs, per_dev, samples):
    steps = jnp.asarray(ways(freq_devs), jnp.int32)
    order = (freq_index ^ steps)[:, None] * per_dev + lax.iota(jnp.int32, per_dev)[None, :] + 1
    phase = order[:, :, None, None] * onset[None, None] % samples
    angle = phase.astype(F32) * (2.0 * math.pi / samples)
    return jnp.cos(angle), jnp.sin(angle), onset.astype(F32) * (1.0 / samples)


def on_device(initial, response, aperture, onset_rcv, onset_src):
    freq_devs = lax.axis_size("freq")
    per_dev = response.shape[0]
    samples = initial.shape[1] * freq_devs
    half_rows = initial.shape[0]
    src_width = response.shape[2] // 2
    rows = half_rows // CHUNKS
    share = rows // freq_devs
    freq_index = lax.axis_index("freq")
    rblk_index = lax.axis_index("rblk")
    sblk_index = lax.axis_index("sblk")
    freq_place = freq_index.reshape(1)
    rblk_place = rblk_index.reshape(1)

    moved = exchanged(mask_half(response, aperture, rblk_place, 1, src_width, WIDE_VMEM_BYTES), "rblk", 1)
    kept = mask_half(response, aperture, rblk_place, 0, src_width, VMEM_BYTES)
    kept_pair = exchanged(kept, "sblk", 1)
    responses = None
    forward = jnp.asarray(forward_tables(samples, freq_devs, per_dev))
    inverse = jnp.asarray(inverse_tables(samples, freq_devs, per_dev))
    matrix = jnp.asarray(window_tables(samples, freq_devs, per_dev))

    result = None
    for chunk in range(CHUNKS):
        first = chunk * rows
        parts = first_spectra(initial, forward, freq_place, freq_devs, per_dev, first, rows)
        sums = sum(v.astype(F32) for v in dealt_out(parts))
        spectra = sums.astype(BF16)
        if responses is None:
            moved, spectra = lax.optimization_barrier((moved, spectra))
            responses = ((kept, moved), (kept_pair, exchanged(moved, "sblk", 1)))

        def src_onsets(core):
            spot = core * half_rows + first + freq_index * share
            return lax.dynamic_slice(onset_src, (spot, rblk_index * src_width), (share, src_width))

        onsets = [src_onsets(sblk_index), exchanged(src_onsets(1 - sblk_index), "sblk", 1)]
        src_tables = phases(jnp.concatenate(onsets, 1), freq_index, freq_devs, per_dev, samples)
        onsets = lax.dynamic_slice_in_dim(onset_rcv, sblk_index * half_rows + first, rows, 0)
        rcv_tables = phases(onsets, freq_index, freq_devs, per_dev, samples)

        for step in range(ITERS):
            far = exchanged(spectra, "rblk", 1)
            messages = dealt_out(down_products(spectra, far, responses, freq_place, freq_devs))
            messages = windowed(messages, src_tables, matrix, freq_place, per_dev, share)
            keep, send = up_products(dealt_out(messages), responses, freq_place, rows)
            back = (keep + exchanged(send, "rblk", 1).astype(F32)).astype(BF16)
            messages = spread(back, freq_devs)
            if step < ITERS - 1:
                spectra = next_spectra(sums, messages, rcv_tables, matrix, freq_place)
            else:
                tile_first = (sblk_index * (half_rows // (2 * ROWS))).reshape(1)
                result = updated(
                    initial, onset_rcv, messages, inverse, freq_place, tile_first, first, rows, result
                )
    return result


def transform_tables(length, count):
    table = fields(length, count).reshape(2 * count, length)
    forward_table = jnp.asarray(table.astype(np.float32).astype(BF16))
    inverse_table = jnp.asarray((table.T * (2.0 / length)).astype(np.float32).astype(BF16))
    return forward_table, inverse_table


def settle(values):
    return lax.optimization_barrier(values.astype(BF16)).astype(F32)


def samples_into_spectra(values, forward_table, freq_total):
    out = jnp.einsum("kt,ptn->pkn", forward_table, values, preferred_element_type=F32)
    return out.reshape(values.shape[0], 2, freq_total, values.shape[2]).astype(BF16)


def spectra_into_samples(trace_spectra, inverse_table):
    flat = trace_spectra.reshape(trace_spectra.shape[0], -1, trace_spectra.shape[3])
    return jnp.einsum("tk,pkn->ptn", inverse_table, flat, preferred_element_type=F32)


def dense(spec, gated, real, imag, sign):
    dot = functools.partial(jnp.einsum, spec, preferred_element_type=F32)
    return jnp.stack(
        [dot(gated[:, 0], real) - sign * dot(gated[:, 1], imag), dot(gated[:, 0], imag) + sign * dot(gated[:, 1], real)], 1
    )


def general_device(initial, response, aperture, onset_rcv, onset_src):
    freq_devs, rblk_devs, sblk_devs = (lax.axis_size(a) for a in ("freq", "rblk", "sblk"))
    freq_index, rblk_index, sblk_index = (lax.axis_index(a) for a in ("freq", "rblk", "sblk"))
    freq_total = response.shape[0] * freq_devs
    samples = initial.shape[1] * freq_devs
    focal_all = onset_rcv.shape[0]
    forward_table, inverse_table = transform_tables(samples, freq_total)
    steps_axis = lax.iota(jnp.int32, samples)
    own_axis = freq_index * initial.shape[1] + lax.iota(jnp.int32, initial.shape[1])
    half_rows = focal_all // sblk_devs
    own_onsets = lax.dynamic_slice_in_dim(onset_rcv, sblk_index * half_rows, half_rows, 0)
    rcv_gate = (own_axis[None, :, None] < own_onsets[:, None, :]).astype(F32)
    src_rows = focal_all // (rblk_devs * freq_devs)
    src_first = rblk_index * (focal_all // rblk_devs) + freq_index * src_rows
    src_onsets = lax.dynamic_slice_in_dim(onset_src, src_first, src_rows, 0)
    src_gate = (steps_axis[None, :, None] < src_onsets[:, None, :]).astype(F32)
    mask_full = jnp.repeat(jnp.repeat(aperture, BLOCK, 1), BLOCK, 2).astype(BF16)
    gated = response * mask_full[:, None]
    own_forward = lax.dynamic_slice_in_dim(forward_table, freq_index * initial.shape[1], initial.shape[1], 1)
    own_inverse = lax.dynamic_slice_in_dim(inverse_table, freq_index * initial.shape[1], initial.shape[1], 0)
    current = initial
    for _ in range(ITERS):
        partial = samples_into_spectra(current, own_forward, freq_total)
        spec_back = lax.psum_scatter(partial.astype(F32), "freq", scatter_dimension=2, tiled=True).astype(BF16)
        spec_all = lax.all_gather(spec_back, "sblk", axis=0, tiled=True)
        down = lax.psum_scatter(
            settle(dense("euk,bek->beu", gated, spec_all[:, 0], spec_all[:, 1], 1.0)).astype(BF16),
            "rblk",
            scatter_dimension=0,
            tiled=True,
        )
        src_traces = lax.all_to_all(down, "freq", split_axis=0, concat_axis=2, tiled=True)
        upgoing = (src_gate * spectra_into_samples(src_traces, inverse_table)).astype(BF16)
        upspec = samples_into_spectra(upgoing, forward_table, freq_total)
        up_back = lax.all_to_all(upspec, "freq", split_axis=2, concat_axis=0, tiled=True)
        up_all = lax.all_gather(up_back, "rblk", axis=0, tiled=True)
        sums = dense("qao,bqa->bqo", gated, up_all[:, 0], up_all[:, 1], -1.0).astype(BF16)
        back = lax.psum_scatter(sums, "sblk", scatter_dimension=0, tiled=True)
        traces = lax.all_gather(back, "freq", axis=2, tiled=True)
        update = rcv_gate * spectra_into_samples(traces, own_inverse)
        current = (initial.astype(F32) - update).astype(BF16)
    return current


def fits(initial, response, aperture, onset_rcv, onset_src):
    freq_devs = lax.axis_size("freq")
    if lax.axis_size("rblk") != 2 or lax.axis_size("sblk") != 2 or freq_devs & (freq_devs - 1):
        return False
    rows = initial.shape[0] // CHUNKS
    whole_rows = initial.shape[0] % CHUNKS == 0 and rows % (2 * ROWS * freq_devs) == 0
    whole_width = response.shape[2] % (4 * BLOCK) == 0 and response.shape[3] % BLOCK == 0
    return whole_rows and whole_width and onset_rcv.shape[0] == 2 * initial.shape[0]


def chosen(*arrays):
    return on_device(*arrays) if fits(*arrays) else general_device(*arrays)


def solution(mesh):
    in_specs = (
        P(("group", "sblk"), "freq", "rblk"),
        P(("group", "freq"), None, "sblk", "rblk"),
        P(("group", "freq"), "sblk", "rblk"),
        P("group", "rblk"),
        P("group", "sblk"),
    )
    out_specs = P(("group", "sblk"), "freq", "rblk")
    return jax.shard_map(chosen, mesh=mesh, in_specs=in_specs, out_specs=out_specs, check_vma=False)
```

```python
import functools
import math

import jax
import jax.numpy as jnp
import numpy as np
from jax import lax
from jax.experimental import pallas as pl
from jax.experimental.pallas import tpu as pltpu
from jax.sharding import PartitionSpec as P

BLOCK = 128
ITERS = 2
ROWS = 8
CHUNKS = 1
VMEM_BYTES = 16 * 1024 * 1024

BF16 = jnp.bfloat16
F32 = jnp.float32


def ways(count):
    far = sorted(range(1, count), key=lambda step: (step.bit_length() < count.bit_length() - 1, step))
    return [0] + far


def field_rows(place, freq_devs, per_dev):
    rows = []
    for step in ways(freq_devs):
        first = (place ^ step) * per_dev
        for part in range(2):
            rows.extend((part, first + local) for local in range(per_dev))
    return rows


def fields(samples, freq_total):
    phase = (np.arange(1, freq_total + 1)[:, None] * np.arange(samples)[None, :]) % samples
    angle = phase * (2.0 * math.pi / samples)
    return np.stack([np.cos(angle), -np.sin(angle)])


def forward_tables(samples, freq_devs, per_dev):
    table = fields(samples, freq_devs * per_dev)
    own = samples // freq_devs
    out = []
    for place in range(freq_devs):
        part = [table[c, j, place * own : (place + 1) * own] for c, j in field_rows(place, freq_devs, per_dev)]
        out.append(np.repeat(np.stack(part), ROWS, 0))
    return np.stack(out).astype(np.float32).astype(BF16)


def inverse_tables(samples, freq_devs, per_dev):
    out = forward_tables(samples, freq_devs, per_dev).astype(np.float32)
    exact = fields(samples, freq_devs * per_dev) * (2.0 / samples)
    own = samples // freq_devs
    for place in range(freq_devs):
        part = [exact[c, j, place * own : (place + 1) * own] for c, j in field_rows(place, freq_devs, per_dev)]
        out[place] = np.repeat(np.stack(part), ROWS, 0)
    return np.swapaxes(out, 1, 2).astype(BF16)


def window_tables(samples, freq_devs, per_dev):
    freq_total = freq_devs * per_dev
    order = np.arange(1, freq_total + 1)
    unit = 2j * math.pi / samples
    diff = order[None, :] - order[:, None]
    total = order[None, :] + order[:, None]
    same = np.where(diff == 0, 0.0, 1.0 / (samples * (np.exp(unit * np.where(diff == 0, 1, diff)) - 1.0)))
    mixed = 1.0 / (samples * (np.exp(-unit * total) - 1.0))
    full = np.zeros((2, freq_total, 2, freq_total))
    full[0, :, 0, :] = same.real + mixed.real
    full[0, :, 1, :] = mixed.imag - same.imag
    full[1, :, 0, :] = same.imag + mixed.imag
    full[1, :, 1, :] = same.real - mixed.real
    out = []
    for place in range(freq_devs):
        rows = [c * freq_total + j for c, j in field_rows(place, freq_devs, per_dev)]
        flat = full.reshape(2 * freq_total, 2 * freq_total)[np.ix_(rows, rows)]
        out.append(np.kron(flat, np.eye(ROWS)))
    return np.stack(out).astype(np.float32).astype(BF16)


def call(body, scalars, inputs, outputs, grid, scratch=(), aliases=None, flops=0):
    in_arrays = [value for value, _ in inputs]
    bytes_all = sum(v.size * v.dtype.itemsize for v in in_arrays)
    bytes_all += sum(math.prod(s.shape) * s.dtype.itemsize for s, _ in outputs)
    return pl.pallas_call(
        body,
        grid_spec=pltpu.PrefetchScalarGridSpec(
            num_scalar_prefetch=len(scalars),
            grid=grid,
            in_specs=[spec for _, spec in inputs],
            out_specs=[spec for _, spec in outputs],
            scratch_shapes=list(scratch),
        ),
        out_shape=[shape for shape, _ in outputs],
        input_output_aliases=aliases or {},
        compiler_params=pltpu.CompilerParams(vmem_limit_bytes=VMEM_BYTES),
        cost_estimate=pl.CostEstimate(flops=flops, bytes_accessed=bytes_all, transcendentals=0),
    )(*scalars, *in_arrays)


def whole(array):
    zeros = (0,) * array.ndim
    return pl.BlockSpec(array.shape, lambda *_: zeros)


def masked_halves(response, aperture, place):
    per_dev, _, src, rcv = response.shape
    half = src // 2
    steps = half // BLOCK

    def body(place_ref, flags, x_ref, keep, send):
        for flip, out in ((1, send), (0, keep)):
            for step in range(steps):
                block = (place_ref[0] ^ flip) * steps + step
                rows = pl.ds(pl.multiple_of(block * BLOCK, BLOCK), BLOCK)
                to = pl.ds(step * BLOCK, BLOCK)
                for j in range(per_dev):
                    for r in range(rcv // BLOCK):
                        on = flags[j, block, r].astype(F32).astype(BF16)
                        at = pl.ds(r * BLOCK, BLOCK)
                        out[j, :, to, at] = x_ref[j, :, rows, at] * on

    shape = jax.ShapeDtypeStruct((per_dev, 2, half, rcv), BF16)
    return call(body, (place, aperture), [(response, whole(response))], [(shape, whole(shape))] * 2, (1,))


def first_spectra(initial, table, freq_place, freq_devs, per_dev, first, rows):
    own, rcv = initial.shape[1:]
    tile = 2 * ROWS
    count = table.shape[1]

    def body(place_ref, x_ref, t_ref, *rest):
        outs, spread_ref = rest[:freq_devs], rest[freq_devs]
        base = t_ref[place_ref[0]].astype(F32)
        lane = lax.broadcasted_iota(jnp.int32, (count, own), 0) % ROWS
        for row in range(ROWS):
            spread_ref[:, row * own : (row + 1) * own] = jnp.where(lane == row, base, 0.0).astype(BF16)
        for at in range(rows // tile):
            parts = []
            for half in range(2):
                start = first + at * tile + half * ROWS
                flat = x_ref[start : start + ROWS].reshape(ROWS * own, rcv)
                value = jnp.dot(spread_ref[...], flat, preferred_element_type=F32)
                parts.append(value.reshape(freq_devs, 2, per_dev, ROWS, rcv))
            both = jnp.concatenate(parts, 3).astype(BF16)
            for step, out in enumerate(outs):
                out[:, :, at * tile : (at + 1) * tile, :] = both[step]

    shape = jax.ShapeDtypeStruct((2, per_dev, rows, rcv), BF16)
    return call(
        body,
        (freq_place,),
        [(initial, whole(initial)), (table, whole(table))],
        [(shape, whole(shape))] * freq_devs,
        (1,),
        scratch=[pltpu.VMEM((count, ROWS * own), BF16)],
        flops=2 * 2 * freq_devs * per_dev * own * rows * rcv,
    )


def down_products(near, far, responses, freq_place, freq_devs):
    _, per_dev, rows, rcv = near.shape
    width = responses[0][0].shape[2]
    tile = min(width, 256)
    share = rows // freq_devs

    def body(place_ref, n_ref, f_ref, k0, m0, k1, m1, *rest):
        outs, held = rest[:freq_devs], rest[freq_devs]
        sides = []
        for ref in (n_ref, f_ref):
            for j in range(per_dev):
                real, imag = ref[0, j], ref[1, j]
                sides.append((jnp.concatenate([real, imag], 0), jnp.concatenate([-imag, real], 0)))
        for half, pair in enumerate(((k0, m0), (k1, m1))):
            for at in range(width // tile):
                cut = slice(at * tile, (at + 1) * tile)
                for j in range(per_dev):
                    total = None
                    for side, resp in enumerate(pair):
                        for part, lhs in enumerate(sides[side * per_dev + j]):
                            term = lax.dot_general(
                                lhs, resp[j, part, cut], (((1,), (1,)), ((), ())), preferred_element_type=F32
                            )
                            total = term if total is None else total + term
                    held[0, j] = total[:rows]
                    held[1, j] = total[rows:]
                to = slice(half * width + at * tile, half * width + (at + 1) * tile)
                for way, out in zip(ways(freq_devs), outs):
                    start = pl.multiple_of((place_ref[0] ^ way) * share, share)
                    out[:, :, :, to] = held[:, :, pl.ds(start, share), :].astype(BF16)

    shape = jax.ShapeDtypeStruct((2, per_dev, share, 2 * width), BF16)
    (k0, m0), (k1, m1) = responses
    return call(
        body,
        (freq_place,),
        [(v, whole(v)) for v in (near, far, k0, m0, k1, m1)],
        [(shape, whole(shape))] * freq_devs,
        (1,),
        scratch=[pltpu.VMEM((2, per_dev, rows, tile), F32)],
        flops=2 * 8 * per_dev * rows * 2 * width * rcv,
    )


def mixed_fields(plain, cos, sin, matrix):
    tile = plain[0].shape[-1]
    turned = [
        jnp.stack([v[0] * c - v[1] * s, v[0] * s + v[1] * c]) for v, c, s in zip(plain, cos, sin)
    ]
    flat = [jnp.stack(v).reshape(matrix.shape[1], tile).astype(BF16) for v in (turned, plain)]
    mixed = jnp.dot(matrix, jnp.concatenate(flat, 1), preferred_element_type=F32)
    shape = (-1, 2) + plain[0].shape[1:]
    return mixed[:, :tile].reshape(shape), mixed[:, tile:].reshape(shape)


def unturned(up, low, value, cos, sin, part):
    real = cos * up[0] + sin * up[1] - low[0] + part * value[0]
    imag = cos * up[1] - sin * up[0] - low[1] + part * value[1]
    return jnp.stack([real, imag])


def tiles(width, body):
    def at(step, carry):
        body(pl.ds(pl.multiple_of(step * BLOCK, BLOCK), BLOCK))
        return carry

    lax.fori_loop(0, width // BLOCK, at, 0)


def windowed(messages, tables, matrix, freq_place, per_dev, share):
    cosines, sines, fraction = tables
    freq_devs = len(messages)
    width = messages[0].shape[-1]
    count = freq_devs * 2 * per_dev * ROWS

    def body(place_ref, c_ref, s_ref, f_ref, g_ref, *rest):
        refs, outs = rest[:freq_devs], rest[freq_devs:]
        matrix_here = g_ref[place_ref[0]]

        def one(at):
            data = [ref[:, :, :, at].astype(F32) for ref in refs]
            made = [[] for _ in outs]
            for first in range(0, share, ROWS):
                cut = slice(first, first + ROWS)
                plain = [value[:, :, cut] for value in data]
                cos = [c_ref[step, :, cut, at] for step in range(freq_devs)]
                sin = [s_ref[step, :, cut, at] for step in range(freq_devs)]
                up, low = mixed_fields(plain, cos, sin, matrix_here)
                part = f_ref[cut, at]
                for step in range(freq_devs):
                    made[step].append(unturned(up[step], low[step], plain[step], cos[step], sin[step], part))
            for out, value in zip(outs, made):
                out[:, :, :, at] = jnp.concatenate(value, 2).astype(BF16)

        tiles(width, one)

    inputs = (cosines, sines, fraction, matrix, *messages)
    return call(
        body,
        (freq_place,),
        [(v, whole(v)) for v in inputs],
        [(jax.ShapeDtypeStruct(v.shape, BF16), whole(v)) for v in messages],
        (1,),
        flops=2 * count * count * 2 * width * share // ROWS,
    )


def up_products(messages, responses, freq_place, rows):
    freq_devs = len(messages)
    (k0, m0), (k1, m1) = responses
    per_dev, _, src, rcv = k0.shape
    share = messages[0].shape[2]

    def body(place_ref, k0_ref, m0_ref, k1_ref, m1_ref, *rest):
        refs = rest[:freq_devs]
        keep, send, held = rest[freq_devs:]
        for way, ref in zip(ways(freq_devs), refs):
            start = pl.multiple_of((place_ref[0] ^ way) * share, share)
            held[:, :, pl.ds(start, share), :] = ref[...]
        for j in range(per_dev):
            for out, pair in ((send, (m0_ref, m1_ref)), (keep, (k0_ref, k1_ref))):
                total = None
                for half, resp in enumerate(pair):
                    cut = slice(half * src, (half + 1) * src)
                    real, imag = held[0, j, :, cut], held[1, j, :, cut]
                    for part, lhs in ((0, [real, imag]), (1, [imag, -real])):
                        term = jnp.dot(jnp.concatenate(lhs, 0), resp[j, part], preferred_element_type=F32)
                        total = term if total is None else total + term
                for part in range(2):
                    out[part, j] = total[rows * part : rows * (part + 1)].astype(out.dtype)

    shapes = [jax.ShapeDtypeStruct((2, per_dev, rows, rcv), kind) for kind in (F32, BF16)]
    return call(
        body,
        (freq_place,),
        [(v, whole(v)) for v in (k0, m0, k1, m1, *messages)],
        [(v, whole(v)) for v in shapes],
        (1,),
        scratch=[pltpu.VMEM((2, per_dev, rows, 2 * src), BF16)],
        flops=2 * 8 * per_dev * rows * 2 * src * rcv,
    )


def next_spectra(sums, messages, tables, matrix, freq_place):
    cosines, sines, fraction = tables
    freq_devs = len(messages)
    _, per_dev, rows, rcv = sums.shape
    count = freq_devs * 2 * per_dev * ROWS
    own = 2 * per_dev * ROWS

    def body(place_ref, u_ref, c_ref, s_ref, f_ref, g_ref, *rest):
        refs, out = rest[:freq_devs], rest[freq_devs]
        matrix_here = g_ref[place_ref[0], :own]

        def one(at):
            for base in range(0, rows, 2 * ROWS):
                pair = slice(base, base + 2 * ROWS)
                data = [ref[:, :, pair, at].astype(F32) for ref in refs]
                made = []
                for half in range(2):
                    plain = [value[:, :, half * ROWS : (half + 1) * ROWS] for value in data]
                    cut = slice(base + half * ROWS, base + (half + 1) * ROWS)
                    cos = [c_ref[step, :, cut, at] for step in range(freq_devs)]
                    sin = [s_ref[step, :, cut, at] for step in range(freq_devs)]
                    up, low = mixed_fields(plain, cos, sin, matrix_here)
                    made.append(unturned(up[0], low[0], plain[0], cos[0], sin[0], f_ref[cut, at]))
                out[:, :, pair, at] = (u_ref[:, :, pair, at] - jnp.concatenate(made, 2)).astype(BF16)

        tiles(rcv, one)

    inputs = (sums, cosines, sines, fraction, matrix, *messages)
    (out,) = call(
        body,
        (freq_place,),
        [(v, whole(v)) for v in inputs],
        [(jax.ShapeDtypeStruct(sums.shape, BF16), whole(sums))],
        (1,),
        flops=2 * own * count * 2 * rcv * rows // ROWS,
    )
    return out


def updated(initial, onset, messages, table, freq_place, focal_first, first, rows, target):
    freq_devs = len(messages)
    own, rcv = initial.shape[1:]
    per_dev = messages[0].shape[1]
    tile = 2 * ROWS
    count = table.shape[2]

    def body(place_ref, focal_ref, x_ref, o_ref, t_ref, *rest):
        refs = rest[:freq_devs]
        out, spread_ref = rest[-2:]
        step = pl.program_id(0)

        @pl.when(step == 0)
        def _():
            base = t_ref[place_ref[0]].astype(F32)
            lane = lax.broadcasted_iota(jnp.int32, (own, count), 1) % ROWS
            for row in range(ROWS):
                spread_ref[row * own : (row + 1) * own] = jnp.where(lane == row, base, 0.0).astype(BF16)

        here = pl.ds(pl.multiple_of(step * tile, tile), tile)
        data = [ref[:, :, here, :].astype(F32) for ref in refs]
        onsets = o_ref[pl.ds(pl.multiple_of(focal_ref[0] + first + step * tile, tile), tile), :]
        time = lax.broadcasted_iota(jnp.int32, (own, rcv), 0) + place_ref[0] * own
        for half in range(2):
            cut = slice(half * ROWS, (half + 1) * ROWS)
            flat = jnp.stack([v[:, :, cut] for v in data]).reshape(count, rcv).astype(BF16)
            change = jnp.dot(spread_ref[...], flat, preferred_element_type=F32)
            for row in range(ROWS):
                spot = half * ROWS + row
                on = time < onsets[spot : spot + 1, :]
                moved = jnp.where(on, change[row * own : (row + 1) * own], 0.0)
                out[spot] = (x_ref[first + step * tile + spot].astype(F32) - moved).astype(BF16)

    inputs = [(v, whole(v)) for v in (initial, onset, table, *messages)]
    aliases = {}
    if target is not None:
        inputs.append((target, pl.BlockSpec(memory_space=pl.ANY)))
        aliases = {2 + len(inputs) - 1: 0}
    (out,) = call(
        body,
        (freq_place, focal_first),
        inputs,
        [(jax.ShapeDtypeStruct(initial.shape, BF16), pl.BlockSpec((tile, own, rcv), lambda i, *_: (first // tile + i, 0, 0)))],
        (rows // tile,),
        scratch=[pltpu.VMEM((ROWS * own, count), BF16)],
        aliases=aliases,
        flops=2 * 2 * freq_devs * per_dev * own * rows * rcv,
    )
    return out


def exchanged(value, axis, step):
    return lax.ppermute(value, axis, [(i, i ^ step) for i in range(lax.axis_size(axis))])


def dealt_out(parts):
    return [exchanged(part, "freq", step) if step else part for part, step in zip(parts, ways(len(parts)))]


def spread(value, count):
    return dealt_out([value] * count)


def phases(onset, freq_index, freq_devs, per_dev, samples):
    steps = jnp.asarray(ways(freq_devs), jnp.int32)
    order = (freq_index ^ steps)[:, None] * per_dev + lax.iota(jnp.int32, per_dev)[None, :] + 1
    phase = order[:, :, None, None] * onset[None, None] % samples
    angle = phase.astype(F32) * (2.0 * math.pi / samples)
    return jnp.cos(angle), jnp.sin(angle), onset.astype(F32) * (1.0 / samples)


def on_device(initial, response, aperture, onset_rcv, onset_src):
    freq_devs = lax.axis_size("freq")
    per_dev = response.shape[0]
    samples = initial.shape[1] * freq_devs
    half_rows = initial.shape[0]
    src_width = response.shape[2] // 2
    rows = half_rows // CHUNKS
    share = rows // freq_devs
    freq_index = lax.axis_index("freq")
    rblk_index = lax.axis_index("rblk")
    sblk_index = lax.axis_index("sblk")
    freq_place = freq_index.reshape(1)
    rblk_place = rblk_index.reshape(1)

    kept, moved = masked_halves(response, aperture, rblk_place)
    moved = exchanged(moved, "rblk", 1)
    kept_pair = exchanged(kept, "sblk", 1)
    responses = None
    forward = jnp.asarray(forward_tables(samples, freq_devs, per_dev))
    inverse = jnp.asarray(inverse_tables(samples, freq_devs, per_dev))
    matrix = jnp.asarray(window_tables(samples, freq_devs, per_dev))

    result = None
    for chunk in range(CHUNKS):
        first = chunk * rows
        parts = first_spectra(initial, forward, freq_place, freq_devs, per_dev, first, rows)
        sums = sum(v.astype(F32) for v in dealt_out(parts))
        spectra = sums.astype(BF16)
        far = exchanged(spectra, "rblk", 1)
        if responses is None:
            moved, far = lax.optimization_barrier((moved, far))
            responses = ((kept, moved), (kept_pair, exchanged(moved, "sblk", 1)))

        def src_onsets(core):
            spot = core * half_rows + first + freq_index * share
            return lax.dynamic_slice(onset_src, (spot, rblk_index * src_width), (share, src_width))

        onsets = [src_onsets(sblk_index), exchanged(src_onsets(1 - sblk_index), "sblk", 1)]
        src_tables = phases(jnp.concatenate(onsets, 1), freq_index, freq_devs, per_dev, samples)
        onsets = lax.dynamic_slice_in_dim(onset_rcv, sblk_index * half_rows + first, rows, 0)
        rcv_tables = phases(onsets, freq_index, freq_devs, per_dev, samples)

        for step in range(ITERS):
            far = far if step == 0 else exchanged(spectra, "rblk", 1)
            messages = dealt_out(down_products(spectra, far, responses, freq_place, freq_devs))
            messages = windowed(messages, src_tables, matrix, freq_place, per_dev, share)
            keep, send = up_products(dealt_out(messages), responses, freq_place, rows)
            back = (keep + exchanged(send, "rblk", 1).astype(F32)).astype(BF16)
            messages = spread(back, freq_devs)
            if step < ITERS - 1:
                spectra = next_spectra(sums, messages, rcv_tables, matrix, freq_place)
            else:
                tile_first = (sblk_index * half_rows).reshape(1)
                result = updated(
                    initial, onset_rcv, messages, inverse, freq_place, tile_first, first, rows, result
                )
    return result


def transform_tables(length, count):
    table = fields(length, count).reshape(2 * count, length)
    forward_table = jnp.asarray(table.astype(np.float32).astype(BF16))
    inverse_table = jnp.asarray((table.T * (2.0 / length)).astype(np.float32).astype(BF16))
    return forward_table, inverse_table


def settle(values):
    return lax.optimization_barrier(values.astype(BF16)).astype(F32)


def samples_into_spectra(values, forward_table, freq_total):
    out = jnp.einsum("kt,ptn->pkn", forward_table, values, preferred_element_type=F32)
    return out.reshape(values.shape[0], 2, freq_total, values.shape[2]).astype(BF16)


def spectra_into_samples(trace_spectra, inverse_table):
    flat = trace_spectra.reshape(trace_spectra.shape[0], -1, trace_spectra.shape[3])
    return jnp.einsum("tk,pkn->ptn", inverse_table, flat, preferred_element_type=F32)


def dense(spec, gated, real, imag, sign):
    dot = functools.partial(jnp.einsum, spec, preferred_element_type=F32)
    return jnp.stack(
        [dot(gated[:, 0], real) - sign * dot(gated[:, 1], imag), dot(gated[:, 0], imag) + sign * dot(gated[:, 1], real)], 1
    )


def general_device(initial, response, aperture, onset_rcv, onset_src):
    freq_devs, rblk_devs, sblk_devs = (lax.axis_size(a) for a in ("freq", "rblk", "sblk"))
    freq_index, rblk_index, sblk_index = (lax.axis_index(a) for a in ("freq", "rblk", "sblk"))
    freq_total = response.shape[0] * freq_devs
    samples = initial.shape[1] * freq_devs
    focal_all = onset_rcv.shape[0]
    forward_table, inverse_table = transform_tables(samples, freq_total)
    steps_axis = lax.iota(jnp.int32, samples)
    own_axis = freq_index * initial.shape[1] + lax.iota(jnp.int32, initial.shape[1])
    half_rows = focal_all // sblk_devs
    own_onsets = lax.dynamic_slice_in_dim(onset_rcv, sblk_index * half_rows, half_rows, 0)
    rcv_gate = (own_axis[None, :, None] < own_onsets[:, None, :]).astype(F32)
    src_rows = focal_all // (rblk_devs * freq_devs)
    src_first = rblk_index * (focal_all // rblk_devs) + freq_index * src_rows
    src_onsets = lax.dynamic_slice_in_dim(onset_src, src_first, src_rows, 0)
    src_gate = (steps_axis[None, :, None] < src_onsets[:, None, :]).astype(F32)
    mask_full = jnp.repeat(jnp.repeat(aperture, BLOCK, 1), BLOCK, 2).astype(BF16)
    gated = response * mask_full[:, None]
    own_forward = lax.dynamic_slice_in_dim(forward_table, freq_index * initial.shape[1], initial.shape[1], 1)
    own_inverse = lax.dynamic_slice_in_dim(inverse_table, freq_index * initial.shape[1], initial.shape[1], 0)
    current = initial
    for _ in range(ITERS):
        partial = samples_into_spectra(current, own_forward, freq_total)
        spec_back = lax.psum_scatter(partial.astype(F32), "freq", scatter_dimension=2, tiled=True).astype(BF16)
        spec_all = lax.all_gather(spec_back, "sblk", axis=0, tiled=True)
        down = lax.psum_scatter(
            settle(dense("euk,bek->beu", gated, spec_all[:, 0], spec_all[:, 1], 1.0)).astype(BF16),
            "rblk",
            scatter_dimension=0,
            tiled=True,
        )
        src_traces = lax.all_to_all(down, "freq", split_axis=0, concat_axis=2, tiled=True)
        upgoing = (src_gate * spectra_into_samples(src_traces, inverse_table)).astype(BF16)
        upspec = samples_into_spectra(upgoing, forward_table, freq_total)
        up_back = lax.all_to_all(upspec, "freq", split_axis=2, concat_axis=0, tiled=True)
        up_all = lax.all_gather(up_back, "rblk", axis=0, tiled=True)
        sums = dense("qao,bqa->bqo", gated, up_all[:, 0], up_all[:, 1], -1.0).astype(BF16)
        back = lax.psum_scatter(sums, "sblk", scatter_dimension=0, tiled=True)
        traces = lax.all_gather(back, "freq", axis=2, tiled=True)
        update = rcv_gate * spectra_into_samples(traces, own_inverse)
        current = (initial.astype(F32) - update).astype(BF16)
    return current


def fits(initial, response, aperture, onset_rcv, onset_src):
    freq_devs = lax.axis_size("freq")
    if lax.axis_size("rblk") != 2 or lax.axis_size("sblk") != 2 or freq_devs & (freq_devs - 1):
        return False
    rows = initial.shape[0] // CHUNKS
    whole_rows = initial.shape[0] % CHUNKS == 0 and rows % (2 * ROWS * freq_devs) == 0
    whole_width = response.shape[2] % (4 * BLOCK) == 0 and response.shape[3] % BLOCK == 0
    return whole_rows and whole_width and onset_rcv.shape[0] == 2 * initial.shape[0]


def chosen(*arrays):
    return on_device(*arrays) if fits(*arrays) else general_device(*arrays)


def solution(mesh):
    in_specs = (
        P(("group", "sblk"), "freq", "rblk"),
        P(("group", "freq"), None, "sblk", "rblk"),
        P(("group", "freq"), "sblk", "rblk"),
        P("group", "rblk"),
        P("group", "sblk"),
    )
    out_specs = P(("group", "sblk"), "freq", "rblk")
    return jax.shard_map(chosen, mesh=mesh, in_specs=in_specs, out_specs=out_specs, check_vma=False)
```

```python
import functools
import math

import jax
import jax.numpy as jnp
import numpy as np
from jax import lax
from jax.experimental import pallas as pl
from jax.experimental.pallas import tpu as pltpu
from jax.sharding import PartitionSpec as P

BLOCK = 128
ITERS = 2
ROWS = 8
CHUNKS = 1
VMEM_BYTES = 6 * 1024 * 1024

BF16 = jnp.bfloat16
F32 = jnp.float32


def ways(count):
    far = sorted(range(1, count), key=lambda step: (step.bit_length() < count.bit_length() - 1, step))
    return [0] + far


def field_rows(place, freq_devs, per_dev):
    rows = []
    for step in ways(freq_devs):
        first = (place ^ step) * per_dev
        for part in range(2):
            rows.extend((part, first + local) for local in range(per_dev))
    return rows


def fields(samples, freq_total):
    phase = (np.arange(1, freq_total + 1)[:, None] * np.arange(samples)[None, :]) % samples
    angle = phase * (2.0 * math.pi / samples)
    return np.stack([np.cos(angle), -np.sin(angle)])


def forward_tables(samples, freq_devs, per_dev):
    table = fields(samples, freq_devs * per_dev)
    own = samples // freq_devs
    out = []
    for place in range(freq_devs):
        part = [table[c, j, place * own : (place + 1) * own] for c, j in field_rows(place, freq_devs, per_dev)]
        out.append(np.repeat(np.stack(part), ROWS, 0))
    return np.stack(out).astype(np.float32).astype(BF16)


def inverse_tables(samples, freq_devs, per_dev):
    out = forward_tables(samples, freq_devs, per_dev).astype(np.float32)
    exact = fields(samples, freq_devs * per_dev) * (2.0 / samples)
    own = samples // freq_devs
    for place in range(freq_devs):
        part = [exact[c, j, place * own : (place + 1) * own] for c, j in field_rows(place, freq_devs, per_dev)]
        out[place] = np.repeat(np.stack(part), ROWS, 0)
    return np.swapaxes(out, 1, 2).astype(BF16)


def window_tables(samples, freq_devs, per_dev):
    freq_total = freq_devs * per_dev
    order = np.arange(1, freq_total + 1)
    unit = 2j * math.pi / samples
    diff = order[None, :] - order[:, None]
    total = order[None, :] + order[:, None]
    same = np.where(diff == 0, 0.0, 1.0 / (samples * (np.exp(unit * np.where(diff == 0, 1, diff)) - 1.0)))
    mixed = 1.0 / (samples * (np.exp(-unit * total) - 1.0))
    full = np.zeros((2, freq_total, 2, freq_total))
    full[0, :, 0, :] = same.real + mixed.real
    full[0, :, 1, :] = mixed.imag - same.imag
    full[1, :, 0, :] = same.imag + mixed.imag
    full[1, :, 1, :] = same.real - mixed.real
    out = []
    for place in range(freq_devs):
        rows = [c * freq_total + j for c, j in field_rows(place, freq_devs, per_dev)]
        flat = full.reshape(2 * freq_total, 2 * freq_total)[np.ix_(rows, rows)]
        out.append(np.kron(flat, np.eye(ROWS)))
    return np.stack(out).astype(np.float32).astype(BF16)


def call(body, scalars, inputs, outputs, grid, scratch=(), aliases=None, flops=0):
    in_arrays = [value for value, _ in inputs]
    bytes_all = sum(v.size * v.dtype.itemsize for v in in_arrays)
    bytes_all += sum(math.prod(s.shape) * s.dtype.itemsize for s, _ in outputs)
    return pl.pallas_call(
        body,
        grid_spec=pltpu.PrefetchScalarGridSpec(
            num_scalar_prefetch=len(scalars),
            grid=grid,
            in_specs=[spec for _, spec in inputs],
            out_specs=[spec for _, spec in outputs],
            scratch_shapes=list(scratch),
        ),
        out_shape=[shape for shape, _ in outputs],
        input_output_aliases=aliases or {},
        compiler_params=pltpu.CompilerParams(vmem_limit_bytes=VMEM_BYTES),
        cost_estimate=pl.CostEstimate(flops=flops, bytes_accessed=bytes_all, transcendentals=0),
    )(*scalars, *in_arrays)


def whole(array):
    zeros = (0,) * array.ndim
    return pl.BlockSpec(array.shape, lambda *_: zeros)


def masked_halves(response, aperture, place):
    per_dev, _, src, rcv = response.shape
    half = src // 2
    steps = half // BLOCK

    def body(place_ref, flags, x_ref, *outs):
        for flip in (1, 0):
            for j in range(per_dev):
                out = outs[flip * per_dev + j]
                for step in range(steps):
                    block = (place_ref[0] ^ flip) * steps + step
                    rows = pl.ds(pl.multiple_of(block * BLOCK, BLOCK), BLOCK)
                    to = slice(step * BLOCK, (step + 1) * BLOCK)
                    for r in range(rcv // BLOCK):
                        on = flags[j, block, r] != 0
                        spots = [(c, slice(r * BLOCK, (r + 1) * BLOCK)) for c in range(2)]

                        @pl.when(on)
                        def _():
                            for c, at in spots:
                                out[to, c * rcv + at.start : c * rcv + at.stop] = x_ref[j, c, rows, at]

                        @pl.when(jnp.logical_not(on))
                        def _():
                            for c, at in spots:
                                out[to, c * rcv + at.start : c * rcv + at.stop] = jnp.zeros((BLOCK, BLOCK), BF16)

    shape = jax.ShapeDtypeStruct((half, 2 * rcv), BF16)
    outs = call(body, (place, aperture), [(response, whole(response))], [(shape, whole(shape))] * (2 * per_dev), (1,))
    return outs[:per_dev], outs[per_dev:]


def first_spectra(initial, table, freq_place, freq_devs, per_dev, first, rows):
    own, rcv = initial.shape[1:]
    tile = 2 * ROWS
    count = table.shape[1]

    def body(place_ref, x_ref, t_ref, *rest):
        outs, spread_ref = rest[:freq_devs], rest[freq_devs]
        base = t_ref[place_ref[0]].astype(F32)
        lane = lax.broadcasted_iota(jnp.int32, (count, own), 0) % ROWS
        for row in range(ROWS):
            spread_ref[:, row * own : (row + 1) * own] = jnp.where(lane == row, base, 0.0).astype(BF16)
        for at in range(rows // tile):
            parts = []
            for half in range(2):
                start = first + at * tile + half * ROWS
                flat = x_ref[start : start + ROWS].reshape(ROWS * own, rcv)
                value = jnp.dot(spread_ref[...], flat, preferred_element_type=F32)
                parts.append(value.reshape(freq_devs, 2, per_dev, ROWS, rcv))
            both = jnp.concatenate(parts, 3).astype(BF16)
            for step, out in enumerate(outs):
                out[:, :, at * tile : (at + 1) * tile, :] = both[step]

    shape = jax.ShapeDtypeStruct((2, per_dev, rows, rcv), BF16)
    return call(
        body,
        (freq_place,),
        [(initial, whole(initial)), (table, whole(table))],
        [(shape, whole(shape))] * freq_devs,
        (1,),
        scratch=[pltpu.VMEM((count, ROWS * own), BF16)],
        flops=2 * 2 * freq_devs * per_dev * own * rows * rcv,
    )


def down_products(near, far, responses, freq_place, freq_devs):
    _, per_dev, rows, rcv = near.shape
    flat = [v for by_half in responses for pair in by_half for v in pair]
    width = flat[0].shape[0]
    tile = min(width, 256)
    share = rows // freq_devs

    def body(place_ref, n_ref, f_ref, *rest):
        resp, outs, held = rest[: len(flat)], rest[len(flat) : -1], rest[-1]
        for j in range(per_dev):
            sides = []
            for ref in (n_ref, f_ref):
                real, imag = ref[0, j], ref[1, j]
                sides.append(jnp.concatenate([jnp.concatenate([real, -imag], 1), jnp.concatenate([imag, real], 1)], 0))
            for half in range(2):
                pair = resp[(j * 2 + half) * 2 : (j * 2 + half) * 2 + 2]
                for at in range(width // tile):
                    cut = slice(at * tile, (at + 1) * tile)
                    total = sum(
                        lax.dot_general(lhs, ref[cut], (((1,), (1,)), ((), ())), preferred_element_type=F32)
                        for lhs, ref in zip(sides, pair)
                    )
                    to = slice(half * width + at * tile, half * width + (at + 1) * tile)
                    held[0, j, :, to] = total[:rows]
                    held[1, j, :, to] = total[rows:]
        for way, out in zip(ways(freq_devs), outs):
            start = pl.multiple_of((place_ref[0] ^ way) * share, share)
            out[...] = held[:, :, pl.ds(start, share), :].astype(BF16)

    shape = jax.ShapeDtypeStruct((2, per_dev, share, 2 * width), BF16)
    return call(
        body,
        (freq_place,),
        [(v, whole(v)) for v in (near, far, *flat)],
        [(shape, whole(shape))] * freq_devs,
        (1,),
        scratch=[pltpu.VMEM((2, per_dev, rows, 2 * width), F32)],
        flops=2 * 8 * per_dev * rows * 2 * width * rcv,
    )


def mixed_fields(plain, cos, sin, matrix):
    tile = plain[0].shape[-1]
    turned = [
        jnp.stack([v[0] * c - v[1] * s, v[0] * s + v[1] * c]) for v, c, s in zip(plain, cos, sin)
    ]
    flat = [jnp.stack(v).reshape(matrix.shape[1], tile).astype(BF16) for v in (turned, plain)]
    mixed = jnp.dot(matrix, jnp.concatenate(flat, 1), preferred_element_type=F32)
    shape = (-1, 2) + plain[0].shape[1:]
    return mixed[:, :tile].reshape(shape), mixed[:, tile:].reshape(shape)


def unturned(up, low, value, cos, sin, part):
    real = cos * up[0] + sin * up[1] - low[0] + part * value[0]
    imag = cos * up[1] - sin * up[0] - low[1] + part * value[1]
    return jnp.stack([real, imag])


def tiles(width, body):
    def at(step, carry):
        body(pl.ds(pl.multiple_of(step * BLOCK, BLOCK), BLOCK))
        return carry

    lax.fori_loop(0, width // BLOCK, at, 0, unroll=2)


def windowed(messages, tables, matrix, freq_place, per_dev, share):
    cosines, sines, fraction = tables
    freq_devs = len(messages)
    width = messages[0].shape[-1]
    count = freq_devs * 2 * per_dev * ROWS

    def body(place_ref, c_ref, s_ref, f_ref, g_ref, *rest):
        refs, outs = rest[:freq_devs], rest[freq_devs:]
        matrix_here = g_ref[place_ref[0]]

        def one(at):
            data = [ref[:, :, :, at].astype(F32) for ref in refs]
            made = [[] for _ in outs]
            for first in range(0, share, ROWS):
                cut = slice(first, first + ROWS)
                plain = [value[:, :, cut] for value in data]
                cos = [c_ref[step, :, cut, at] for step in range(freq_devs)]
                sin = [s_ref[step, :, cut, at] for step in range(freq_devs)]
                up, low = mixed_fields(plain, cos, sin, matrix_here)
                part = f_ref[cut, at]
                for step in range(freq_devs):
                    made[step].append(unturned(up[step], low[step], plain[step], cos[step], sin[step], part))
            for out, value in zip(outs, made):
                out[:, :, :, at] = jnp.concatenate(value, 2).astype(BF16)

        tiles(width, one)

    inputs = (cosines, sines, fraction, matrix, *messages)
    return call(
        body,
        (freq_place,),
        [(v, whole(v)) for v in inputs],
        [(jax.ShapeDtypeStruct(v.shape, BF16), whole(v)) for v in messages],
        (1,),
        flops=2 * count * count * 2 * width * share // ROWS,
    )


def up_products(messages, responses, freq_place, rows):
    freq_devs = len(messages)
    flat = [v for by_half in responses for pair in by_half for v in pair]
    src, rcv = flat[0].shape[0], flat[0].shape[1] // 2
    _, per_dev, share, _ = messages[0].shape

    def body(place_ref, *rest):
        resp, refs = rest[: len(flat)], rest[len(flat) : len(flat) + freq_devs]
        keep, send, held = rest[len(flat) + freq_devs :]
        for way, ref in zip(ways(freq_devs), refs):
            for part in range(2):
                start = pl.multiple_of(part * rows + (place_ref[0] ^ way) * share, share)
                held[:, pl.ds(start, share), :] = ref[part]
        for j in range(per_dev):
            for side, out in ((1, send), (0, keep)):
                total = sum(
                    jnp.dot(
                        held[j, :, half * src : (half + 1) * src],
                        resp[(j * 2 + half) * 2 + side][...],
                        preferred_element_type=F32,
                    )
                    for half in range(2)
                )
                out[0, j] = (total[:rows, :rcv] + total[rows:, rcv:]).astype(out.dtype)
                out[1, j] = (total[rows:, :rcv] - total[:rows, rcv:]).astype(out.dtype)

    shapes = [jax.ShapeDtypeStruct((2, per_dev, rows, rcv), kind) for kind in (F32, BF16)]
    return call(
        body,
        (freq_place,),
        [(v, whole(v)) for v in (*flat, *messages)],
        [(v, whole(v)) for v in shapes],
        (1,),
        scratch=[pltpu.VMEM((per_dev, 2 * rows, 2 * src), BF16)],
        flops=2 * 8 * per_dev * rows * 2 * src * rcv,
    )


def next_spectra(sums, messages, tables, matrix, freq_place):
    cosines, sines, fraction = tables
    freq_devs = len(messages)
    _, per_dev, rows, rcv = sums.shape
    count = freq_devs * 2 * per_dev * ROWS
    own = 2 * per_dev * ROWS

    def body(place_ref, u_ref, c_ref, s_ref, f_ref, g_ref, *rest):
        refs, out = rest[:freq_devs], rest[freq_devs]
        matrix_here = g_ref[place_ref[0], :own]

        def one(at):
            for base in range(0, rows, 2 * ROWS):
                pair = slice(base, base + 2 * ROWS)
                data = [ref[:, :, pair, at].astype(F32) for ref in refs]
                made = []
                for half in range(2):
                    plain = [value[:, :, half * ROWS : (half + 1) * ROWS] for value in data]
                    cut = slice(base + half * ROWS, base + (half + 1) * ROWS)
                    cos = [c_ref[step, :, cut, at] for step in range(freq_devs)]
                    sin = [s_ref[step, :, cut, at] for step in range(freq_devs)]
                    up, low = mixed_fields(plain, cos, sin, matrix_here)
                    made.append(unturned(up[0], low[0], plain[0], cos[0], sin[0], f_ref[cut, at]))
                out[:, :, pair, at] = (u_ref[:, :, pair, at] - jnp.concatenate(made, 2)).astype(BF16)

        tiles(rcv, one)

    inputs = (sums, cosines, sines, fraction, matrix, *messages)
    (out,) = call(
        body,
        (freq_place,),
        [(v, whole(v)) for v in inputs],
        [(jax.ShapeDtypeStruct(sums.shape, BF16), whole(sums))],
        (1,),
        flops=2 * own * count * 2 * rcv * rows // ROWS,
    )
    return out


def updated(initial, onset, messages, table, freq_place, focal_first, first, rows, target):
    freq_devs = len(messages)
    own, rcv = initial.shape[1:]
    per_dev = messages[0].shape[1]
    tile = 2 * ROWS
    count = table.shape[2]

    def body(place_ref, focal_ref, x_ref, o_ref, t_ref, *rest):
        refs = rest[:freq_devs]
        out, spread_ref = rest[-2:]
        step = pl.program_id(0)

        @pl.when(step == 0)
        def _():
            base = t_ref[place_ref[0]].astype(F32)
            lane = lax.broadcasted_iota(jnp.int32, (own, count), 1) % ROWS
            for row in range(ROWS):
                spread_ref[row * own : (row + 1) * own] = jnp.where(lane == row, base, 0.0).astype(BF16)

        here = pl.ds(pl.multiple_of(step * tile, tile), tile)
        data = [ref[:, :, here, :].astype(F32) for ref in refs]
        onsets = o_ref[pl.ds(pl.multiple_of(focal_ref[0] + first + step * tile, tile), tile), :]
        time = lax.broadcasted_iota(jnp.int32, (own, rcv), 0) + place_ref[0] * own
        for half in range(2):
            cut = slice(half * ROWS, (half + 1) * ROWS)
            flat = jnp.stack([v[:, :, cut] for v in data]).reshape(count, rcv).astype(BF16)
            change = jnp.dot(spread_ref[...], flat, preferred_element_type=F32)
            for row in range(ROWS):
                spot = half * ROWS + row
                on = time < onsets[spot : spot + 1, :]
                moved = jnp.where(on, change[row * own : (row + 1) * own], 0.0)
                out[spot] = (x_ref[first + step * tile + spot].astype(F32) - moved).astype(BF16)

    inputs = [(v, whole(v)) for v in (initial, onset, table, *messages)]
    aliases = {}
    if target is not None:
        inputs.append((target, pl.BlockSpec(memory_space=pl.ANY)))
        aliases = {2 + len(inputs) - 1: 0}
    (out,) = call(
        body,
        (freq_place, focal_first),
        inputs,
        [(jax.ShapeDtypeStruct(initial.shape, BF16), pl.BlockSpec((tile, own, rcv), lambda i, *_: (first // tile + i, 0, 0)))],
        (rows // tile,),
        scratch=[pltpu.VMEM((ROWS * own, count), BF16)],
        aliases=aliases,
        flops=2 * 2 * freq_devs * per_dev * own * rows * rcv,
    )
    return out


def exchanged(value, axis, step):
    return lax.ppermute(value, axis, [(i, i ^ step) for i in range(lax.axis_size(axis))])


def dealt_out(parts):
    return [exchanged(part, "freq", step) if step else part for part, step in zip(parts, ways(len(parts)))]


def spread(value, count):
    return dealt_out([value] * count)


def phases(onset, freq_index, freq_devs, per_dev, samples):
    steps = jnp.asarray(ways(freq_devs), jnp.int32)
    order = (freq_index ^ steps)[:, None] * per_dev + lax.iota(jnp.int32, per_dev)[None, :] + 1
    phase = order[:, :, None, None] * onset[None, None] % samples
    angle = phase.astype(F32) * (2.0 * math.pi / samples)
    return jnp.cos(angle), jnp.sin(angle), onset.astype(F32) * (1.0 / samples)


def on_device(initial, response, aperture, onset_rcv, onset_src):
    freq_devs = lax.axis_size("freq")
    per_dev = response.shape[0]
    samples = initial.shape[1] * freq_devs
    half_rows = initial.shape[0]
    src_width = response.shape[2] // 2
    rows = half_rows // CHUNKS
    share = rows // freq_devs
    freq_index = lax.axis_index("freq")
    rblk_index = lax.axis_index("rblk")
    sblk_index = lax.axis_index("sblk")
    freq_place = freq_index.reshape(1)
    rblk_place = rblk_index.reshape(1)

    kept, moved = masked_halves(response, aperture, rblk_place)
    moved = [exchanged(v, "rblk", 1) for v in moved]
    kept_pair = [exchanged(v, "sblk", 1) for v in kept]
    responses = None
    forward = jnp.asarray(forward_tables(samples, freq_devs, per_dev))
    inverse = jnp.asarray(inverse_tables(samples, freq_devs, per_dev))
    matrix = jnp.asarray(window_tables(samples, freq_devs, per_dev))

    result = None
    for chunk in range(CHUNKS):
        first = chunk * rows
        parts = first_spectra(initial, forward, freq_place, freq_devs, per_dev, first, rows)
        sums = sum(v.astype(F32) for v in dealt_out(parts))
        spectra = sums.astype(BF16)
        far = exchanged(spectra, "rblk", 1)
        if responses is None:
            before, moved_pair = spectra, []
            for at in range(per_dev):
                moved[at], before = lax.optimization_barrier((moved[at], before))
                spectra, far = (spectra, before) if at else (before, far)
                moved_pair.append(exchanged(moved[at], "sblk", 1))
                before = far
            responses = [((kept[j], moved[j]), (kept_pair[j], moved_pair[j])) for j in range(per_dev)]

        def src_onsets(core):
            spot = core * half_rows + first + freq_index * share
            return lax.dynamic_slice(onset_src, (spot, rblk_index * src_width), (share, src_width))

        onsets = [src_onsets(sblk_index), exchanged(src_onsets(1 - sblk_index), "sblk", 1)]
        src_tables = phases(jnp.concatenate(onsets, 1), freq_index, freq_devs, per_dev, samples)
        onsets = lax.dynamic_slice_in_dim(onset_rcv, sblk_index * half_rows + first, rows, 0)
        rcv_tables = phases(onsets, freq_index, freq_devs, per_dev, samples)

        for step in range(ITERS):
            far = far if step == 0 else exchanged(spectra, "rblk", 1)
            messages = dealt_out(down_products(spectra, far, responses, freq_place, freq_devs))
            messages = windowed(messages, src_tables, matrix, freq_place, per_dev, share)
            keep, send = up_products(dealt_out(messages), responses, freq_place, rows)
            back = (keep + exchanged(send, "rblk", 1).astype(F32)).astype(BF16)
            messages = spread(back, freq_devs)
            if step < ITERS - 1:
                spectra = next_spectra(sums, messages, rcv_tables, matrix, freq_place)
            else:
                tile_first = (sblk_index * half_rows).reshape(1)
                result = updated(
                    initial, onset_rcv, messages, inverse, freq_place, tile_first, first, rows, result
                )
    return result


def transform_tables(length, count):
    table = fields(length, count).reshape(2 * count, length)
    forward_table = jnp.asarray(table.astype(np.float32).astype(BF16))
    inverse_table = jnp.asarray((table.T * (2.0 / length)).astype(np.float32).astype(BF16))
    return forward_table, inverse_table


def settle(values):
    return lax.optimization_barrier(values.astype(BF16)).astype(F32)


def samples_into_spectra(values, forward_table, freq_total):
    out = jnp.einsum("kt,ptn->pkn", forward_table, values, preferred_element_type=F32)
    return out.reshape(values.shape[0], 2, freq_total, values.shape[2]).astype(BF16)


def spectra_into_samples(trace_spectra, inverse_table):
    flat = trace_spectra.reshape(trace_spectra.shape[0], -1, trace_spectra.shape[3])
    return jnp.einsum("tk,pkn->ptn", inverse_table, flat, preferred_element_type=F32)


def dense(spec, gated, real, imag, sign):
    dot = functools.partial(jnp.einsum, spec, preferred_element_type=F32)
    return jnp.stack(
        [dot(gated[:, 0], real) - sign * dot(gated[:, 1], imag), dot(gated[:, 0], imag) + sign * dot(gated[:, 1], real)], 1
    )


def general_device(initial, response, aperture, onset_rcv, onset_src):
    freq_devs, rblk_devs, sblk_devs = (lax.axis_size(a) for a in ("freq", "rblk", "sblk"))
    freq_index, rblk_index, sblk_index = (lax.axis_index(a) for a in ("freq", "rblk", "sblk"))
    freq_total = response.shape[0] * freq_devs
    samples = initial.shape[1] * freq_devs
    focal_all = onset_rcv.shape[0]
    forward_table, inverse_table = transform_tables(samples, freq_total)
    steps_axis = lax.iota(jnp.int32, samples)
    own_axis = freq_index * initial.shape[1] + lax.iota(jnp.int32, initial.shape[1])
    half_rows = focal_all // sblk_devs
    own_onsets = lax.dynamic_slice_in_dim(onset_rcv, sblk_index * half_rows, half_rows, 0)
    rcv_gate = (own_axis[None, :, None] < own_onsets[:, None, :]).astype(F32)
    src_rows = focal_all // (rblk_devs * freq_devs)
    src_first = rblk_index * (focal_all // rblk_devs) + freq_index * src_rows
    src_onsets = lax.dynamic_slice_in_dim(onset_src, src_first, src_rows, 0)
    src_gate = (steps_axis[None, :, None] < src_onsets[:, None, :]).astype(F32)
    mask_full = jnp.repeat(jnp.repeat(aperture, BLOCK, 1), BLOCK, 2).astype(BF16)
    gated = response * mask_full[:, None]
    own_forward = lax.dynamic_slice_in_dim(forward_table, freq_index * initial.shape[1], initial.shape[1], 1)
    own_inverse = lax.dynamic_slice_in_dim(inverse_table, freq_index * initial.shape[1], initial.shape[1], 0)
    current = initial
    for _ in range(ITERS):
        partial = samples_into_spectra(current, own_forward, freq_total)
        spec_back = lax.psum_scatter(partial.astype(F32), "freq", scatter_dimension=2, tiled=True).astype(BF16)
        spec_all = lax.all_gather(spec_back, "sblk", axis=0, tiled=True)
        down = lax.psum_scatter(
            settle(dense("euk,bek->beu", gated, spec_all[:, 0], spec_all[:, 1], 1.0)).astype(BF16),
            "rblk",
            scatter_dimension=0,
            tiled=True,
        )
        src_traces = lax.all_to_all(down, "freq", split_axis=0, concat_axis=2, tiled=True)
        upgoing = (src_gate * spectra_into_samples(src_traces, inverse_table)).astype(BF16)
        upspec = samples_into_spectra(upgoing, forward_table, freq_total)
        up_back = lax.all_to_all(upspec, "freq", split_axis=2, concat_axis=0, tiled=True)
        up_all = lax.all_gather(up_back, "rblk", axis=0, tiled=True)
        sums = dense("qao,bqa->bqo", gated, up_all[:, 0], up_all[:, 1], -1.0).astype(BF16)
        back = lax.psum_scatter(sums, "sblk", scatter_dimension=0, tiled=True)
        traces = lax.all_gather(back, "freq", axis=2, tiled=True)
        update = rcv_gate * spectra_into_samples(traces, own_inverse)
        current = (initial.astype(F32) - update).astype(BF16)
    return current


def fits(initial, response, aperture, onset_rcv, onset_src):
    freq_devs = lax.axis_size("freq")
    if lax.axis_size("rblk") != 2 or lax.axis_size("sblk") != 2 or freq_devs & (freq_devs - 1):
        return False
    rows = initial.shape[0] // CHUNKS
    whole_rows = initial.shape[0] % CHUNKS == 0 and rows % (2 * ROWS * freq_devs) == 0
    whole_width = response.shape[2] % (4 * BLOCK) == 0 and response.shape[3] % BLOCK == 0
    return whole_rows and whole_width and onset_rcv.shape[0] == 2 * initial.shape[0]


def chosen(*arrays):
    return on_device(*arrays) if fits(*arrays) else general_device(*arrays)


def solution(mesh):
    in_specs = (
        P(("group", "sblk"), "freq", "rblk"),
        P(("group", "freq"), None, "sblk", "rblk"),
        P(("group", "freq"), "sblk", "rblk"),
        P("group", "rblk"),
        P("group", "sblk"),
    )
    out_specs = P(("group", "sblk"), "freq", "rblk")
    return jax.shard_map(chosen, mesh=mesh, in_specs=in_specs, out_specs=out_specs, check_vma=False)
```

```python
import functools
import math

import jax
import jax.numpy as jnp
import numpy as np
from jax import lax
from jax.experimental import pallas as pl
from jax.experimental.pallas import tpu as pltpu
from jax.sharding import PartitionSpec as P

BLOCK = 128
ITERS = 2
ROWS = 8
CHUNKS = 1
VMEM_BYTES = 6 * 1024 * 1024

BF16 = jnp.bfloat16
F32 = jnp.float32


def ways(count):
    far = sorted(range(1, count), key=lambda step: (step.bit_length() < count.bit_length() - 1, step))
    return [0] + far


def field_rows(place, freq_devs, per_dev):
    rows = []
    for step in ways(freq_devs):
        first = (place ^ step) * per_dev
        for part in range(2):
            rows.extend((part, first + local) for local in range(per_dev))
    return rows


def fields(samples, freq_total):
    phase = (np.arange(1, freq_total + 1)[:, None] * np.arange(samples)[None, :]) % samples
    angle = phase * (2.0 * math.pi / samples)
    return np.stack([np.cos(angle), -np.sin(angle)])


def forward_tables(samples, freq_devs, per_dev):
    table = fields(samples, freq_devs * per_dev)
    own = samples // freq_devs
    out = []
    for place in range(freq_devs):
        part = [table[c, j, place * own : (place + 1) * own] for c, j in field_rows(place, freq_devs, per_dev)]
        out.append(np.repeat(np.stack(part), ROWS, 0))
    return np.stack(out).astype(np.float32).astype(BF16)


def inverse_tables(samples, freq_devs, per_dev):
    out = forward_tables(samples, freq_devs, per_dev).astype(np.float32)
    exact = fields(samples, freq_devs * per_dev) * (2.0 / samples)
    own = samples // freq_devs
    for place in range(freq_devs):
        part = [exact[c, j, place * own : (place + 1) * own] for c, j in field_rows(place, freq_devs, per_dev)]
        out[place] = np.repeat(np.stack(part), ROWS, 0)
    return np.swapaxes(out, 1, 2).astype(BF16)


def window_tables(samples, freq_devs, per_dev):
    freq_total = freq_devs * per_dev
    order = np.arange(1, freq_total + 1)
    unit = 2j * math.pi / samples
    diff = order[None, :] - order[:, None]
    total = order[None, :] + order[:, None]
    same = np.where(diff == 0, 0.0, 1.0 / (samples * (np.exp(unit * np.where(diff == 0, 1, diff)) - 1.0)))
    mixed = 1.0 / (samples * (np.exp(-unit * total) - 1.0))
    full = np.zeros((2, freq_total, 2, freq_total))
    full[0, :, 0, :] = same.real + mixed.real
    full[0, :, 1, :] = mixed.imag - same.imag
    full[1, :, 0, :] = same.imag + mixed.imag
    full[1, :, 1, :] = same.real - mixed.real
    out = []
    for place in range(freq_devs):
        rows = [c * freq_total + j for c, j in field_rows(place, freq_devs, per_dev)]
        flat = full.reshape(2 * freq_total, 2 * freq_total)[np.ix_(rows, rows)]
        out.append(np.kron(flat, np.eye(ROWS)))
    return np.stack(out).astype(np.float32).astype(BF16)


def call(body, scalars, inputs, outputs, grid, scratch=(), aliases=None, flops=0):
    in_arrays = [value for value, _ in inputs]
    bytes_all = sum(v.size * v.dtype.itemsize for v in in_arrays)
    bytes_all += sum(math.prod(s.shape) * s.dtype.itemsize for s, _ in outputs)
    return pl.pallas_call(
        body,
        grid_spec=pltpu.PrefetchScalarGridSpec(
            num_scalar_prefetch=len(scalars),
            grid=grid,
            in_specs=[spec for _, spec in inputs],
            out_specs=[spec for _, spec in outputs],
            scratch_shapes=list(scratch),
        ),
        out_shape=[shape for shape, _ in outputs],
        input_output_aliases=aliases or {},
        compiler_params=pltpu.CompilerParams(vmem_limit_bytes=VMEM_BYTES),
        cost_estimate=pl.CostEstimate(flops=flops, bytes_accessed=bytes_all, transcendentals=0),
    )(*scalars, *in_arrays)


def whole(array):
    zeros = (0,) * array.ndim
    return pl.BlockSpec(array.shape, lambda *_: zeros)


def masked_halves(response, aperture, place):
    per_dev, _, src, rcv = response.shape
    half = src // 2
    steps = half // BLOCK

    def body(place_ref, flags, x_ref, *outs):
        lane = lax.broadcasted_iota(jnp.int32, (1, rcv), 1) // BLOCK
        for flip in (1, 0):
            for j in range(per_dev):
                out = outs[flip * per_dev + j]
                for step in range(steps):
                    block = (place_ref[0] ^ flip) * steps + step
                    on = flags[j, pl.ds(block, 1), :].astype(F32)
                    row = sum(jnp.where(lane == r, on[:, r : r + 1], 0.0) for r in range(rcv // BLOCK))
                    gate = jnp.broadcast_to(row, (BLOCK, rcv)).astype(BF16)
                    rows = pl.ds(pl.multiple_of(block * BLOCK, BLOCK), BLOCK)
                    to = slice(step * BLOCK, (step + 1) * BLOCK)
                    for c in range(2):
                        out[to, c * rcv : (c + 1) * rcv] = x_ref[j, c, rows, :] * gate

    shape = jax.ShapeDtypeStruct((half, 2 * rcv), BF16)
    inputs = [(v, whole(v)) for v in (aperture, response)]
    outs = call(body, (place,), inputs, [(shape, whole(shape))] * (2 * per_dev), (1,))
    return outs[:per_dev], outs[per_dev:]


def first_spectra(initial, table, freq_place, freq_devs, per_dev, first, rows):
    own, rcv = initial.shape[1:]
    tile = 2 * ROWS
    count = table.shape[1]

    def body(place_ref, x_ref, t_ref, *rest):
        outs, spread_ref = rest[:freq_devs], rest[freq_devs]
        base = t_ref[place_ref[0]].astype(F32)
        lane = lax.broadcasted_iota(jnp.int32, (count, own), 0) % ROWS
        for row in range(ROWS):
            spread_ref[:, row * own : (row + 1) * own] = jnp.where(lane == row, base, 0.0).astype(BF16)
        for at in range(rows // tile):
            parts = []
            for half in range(2):
                start = first + at * tile + half * ROWS
                flat = x_ref[start : start + ROWS].reshape(ROWS * own, rcv)
                value = jnp.dot(spread_ref[...], flat, preferred_element_type=F32)
                parts.append(value.reshape(freq_devs, 2, per_dev, ROWS, rcv))
            both = jnp.concatenate(parts, 3).astype(BF16)
            for step, out in enumerate(outs):
                out[:, :, at * tile : (at + 1) * tile, :] = both[step]

    shape = jax.ShapeDtypeStruct((2, per_dev, rows, rcv), BF16)
    return call(
        body,
        (freq_place,),
        [(initial, whole(initial)), (table, whole(table))],
        [(shape, whole(shape))] * freq_devs,
        (1,),
        scratch=[pltpu.VMEM((count, ROWS * own), BF16)],
        flops=2 * 2 * freq_devs * per_dev * own * rows * rcv,
    )


def summed(parts):
    def body(*refs):
        total = sum(ref[...].astype(F32) for ref in refs[:-2])
        refs[-2][...] = total
        refs[-1][...] = total.astype(BF16)

    shapes = [jax.ShapeDtypeStruct(parts[0].shape, kind) for kind in (F32, BF16)]
    return call(body, (), [(v, whole(v)) for v in parts], [(v, whole(v)) for v in shapes], (1,))


def added(keep, received):
    def body(k_ref, r_ref, out):
        out[...] = (k_ref[...] + r_ref[...].astype(F32)).astype(BF16)

    shape = jax.ShapeDtypeStruct(keep.shape, BF16)
    (out,) = call(body, (), [(v, whole(v)) for v in (keep, received)], [(shape, whole(shape))], (1,))
    return out


def src_onsets(onset, places, half_rows, first, share, width):
    def body(freq, rblk, sblk, o_ref, own, other):
        lanes = pl.ds(pl.multiple_of(rblk[0] * width, BLOCK), width)
        for core, out in ((sblk[0], own), (1 - sblk[0], other)):
            spot = pl.multiple_of(core * half_rows + first + freq[0] * share, ROWS)
            out[...] = o_ref[pl.ds(spot, share), lanes]

    shape = jax.ShapeDtypeStruct((share, width), onset.dtype)
    return call(body, places, [(onset, whole(onset))], [(shape, whole(shape))] * 2, (1,))


def sine_terms():
    square = (np.cos(np.linspace(0.0, math.pi, 200)) + 1.0) / 32.0
    y = np.sqrt(np.maximum(square, 1e-12))
    return [float(v) for v in np.polynomial.polynomial.polyfit(square, np.sin(2.0 * math.pi * y) / y, 6)]


def phase_tables(onsets, places, freq_devs, per_dev, samples, rows=None, first=0, half_rows=0):
    terms = sine_terms()
    count = rows or onsets[0].shape[0]
    widths = [v.shape[1] for v in onsets]

    def sine(y):
        square = y * y
        total = jnp.full_like(y, terms[-1])
        for term in terms[-2::-1]:
            total = total * square + term
        return total * y

    def body(freq, _, sblk, *refs):
        cosines, sines, fraction = refs[-3:]
        at = 0
        for ref, width in zip(refs, widths):
            if rows:
                value = ref[pl.ds(pl.multiple_of(sblk[0] * half_rows + first, ROWS), rows), :]
            else:
                value = ref[...]
            part = value.astype(F32) * (1.0 / samples)
            to = slice(at, at + width)
            fraction[:, to] = part
            for step, way in enumerate(ways(freq_devs)):
                for j in range(per_dev):
                    order = ((freq[0] ^ way) * per_dev + j + 1).astype(F32)
                    turn = part * order
                    turn = turn - jnp.floor(turn + 0.5)
                    size = jnp.abs(turn)
                    folded = jnp.where(size > 0.25, jnp.where(turn > 0.0, 0.5, -0.5) - turn, turn)
                    cosines[step, j, :, to] = sine(0.25 - size)
                    sines[step, j, :, to] = sine(folded)
            at += width

    table = jax.ShapeDtypeStruct((freq_devs, per_dev, count, sum(widths)), F32)
    shapes = [table, table, jax.ShapeDtypeStruct((count, sum(widths)), F32)]
    return call(body, places, [(v, whole(v)) for v in onsets], [(v, whole(v)) for v in shapes], (1,))


def down_products(near, far, responses, freq_place, freq_devs):
    _, per_dev, rows, rcv = near.shape
    flat = [v for by_half in responses for pair in by_half for v in pair]
    width = flat[0].shape[0]
    tile = min(width, 256)
    share = rows // freq_devs

    def body(place_ref, n_ref, f_ref, *rest):
        resp, outs, held = rest[: len(flat)], rest[len(flat) : -1], rest[-1]
        for j in range(per_dev):
            sides = []
            for ref in (n_ref, f_ref):
                real, imag = ref[0, j], ref[1, j]
                sides.append(jnp.concatenate([jnp.concatenate([real, -imag], 1), jnp.concatenate([imag, real], 1)], 0))
            for half in range(2):
                pair = resp[(j * 2 + half) * 2 : (j * 2 + half) * 2 + 2]
                for at in range(width // tile):
                    cut = slice(at * tile, (at + 1) * tile)
                    total = sum(
                        lax.dot_general(lhs, ref[cut], (((1,), (1,)), ((), ())), preferred_element_type=F32)
                        for lhs, ref in zip(sides, pair)
                    )
                    to = slice(half * width + at * tile, half * width + (at + 1) * tile)
                    held[0, j, :, to] = total[:rows]
                    held[1, j, :, to] = total[rows:]
        for way, out in zip(ways(freq_devs), outs):
            start = pl.multiple_of((place_ref[0] ^ way) * share, share)
            out[...] = held[:, :, pl.ds(start, share), :].astype(BF16)

    shape = jax.ShapeDtypeStruct((2, per_dev, share, 2 * width), BF16)
    return call(
        body,
        (freq_place,),
        [(v, whole(v)) for v in (near, far, *flat)],
        [(shape, whole(shape))] * freq_devs,
        (1,),
        scratch=[pltpu.VMEM((2, per_dev, rows, 2 * width), F32)],
        flops=2 * 8 * per_dev * rows * 2 * width * rcv,
    )


def mixed_fields(plain, cos, sin, matrix):
    tile = plain[0].shape[-1]
    turned = [
        jnp.stack([v[0] * c - v[1] * s, v[0] * s + v[1] * c]) for v, c, s in zip(plain, cos, sin)
    ]
    flat = [jnp.stack(v).reshape(matrix.shape[1], tile).astype(BF16) for v in (turned, plain)]
    mixed = jnp.dot(matrix, jnp.concatenate(flat, 1), preferred_element_type=F32)
    shape = (-1, 2) + plain[0].shape[1:]
    return mixed[:, :tile].reshape(shape), mixed[:, tile:].reshape(shape)


def unturned(up, low, value, cos, sin, part):
    real = cos * up[0] + sin * up[1] - low[0] + part * value[0]
    imag = cos * up[1] - sin * up[0] - low[1] + part * value[1]
    return jnp.stack([real, imag])


def tiles(width, body):
    def at(step, carry):
        body(pl.ds(pl.multiple_of(step * BLOCK, BLOCK), BLOCK))
        return carry

    lax.fori_loop(0, width // BLOCK, at, 0, unroll=2)


def windowed(messages, tables, matrix, freq_place, per_dev, share):
    cosines, sines, fraction = tables
    freq_devs = len(messages)
    width = messages[0].shape[-1]
    count = freq_devs * 2 * per_dev * ROWS

    def body(place_ref, c_ref, s_ref, f_ref, g_ref, *rest):
        refs, outs = rest[:freq_devs], rest[freq_devs:]
        matrix_here = g_ref[place_ref[0]]

        def one(at):
            data = [ref[:, :, :, at].astype(F32) for ref in refs]
            made = [[] for _ in outs]
            for first in range(0, share, ROWS):
                cut = slice(first, first + ROWS)
                plain = [value[:, :, cut] for value in data]
                cos = [c_ref[step, :, cut, at] for step in range(freq_devs)]
                sin = [s_ref[step, :, cut, at] for step in range(freq_devs)]
                up, low = mixed_fields(plain, cos, sin, matrix_here)
                part = f_ref[cut, at]
                for step in range(freq_devs):
                    made[step].append(unturned(up[step], low[step], plain[step], cos[step], sin[step], part))
            for out, value in zip(outs, made):
                out[:, :, :, at] = jnp.concatenate(value, 2).astype(BF16)

        tiles(width, one)

    inputs = (cosines, sines, fraction, matrix, *messages)
    return call(
        body,
        (freq_place,),
        [(v, whole(v)) for v in inputs],
        [(jax.ShapeDtypeStruct(v.shape, BF16), whole(v)) for v in messages],
        (1,),
        flops=2 * count * count * 2 * width * share // ROWS,
    )


def up_products(messages, responses, freq_place, rows):
    freq_devs = len(messages)
    flat = [v for by_half in responses for pair in by_half for v in pair]
    src, rcv = flat[0].shape[0], flat[0].shape[1] // 2
    _, per_dev, share, _ = messages[0].shape

    def body(place_ref, *rest):
        resp, refs = rest[: len(flat)], rest[len(flat) : len(flat) + freq_devs]
        keep, send, held = rest[len(flat) + freq_devs :]
        for way, ref in zip(ways(freq_devs), refs):
            for part in range(2):
                start = pl.multiple_of(part * rows + (place_ref[0] ^ way) * share, share)
                held[:, pl.ds(start, share), :] = ref[part]
        for j in range(per_dev):
            for side, out in ((1, send), (0, keep)):
                total = sum(
                    jnp.dot(
                        held[j, :, half * src : (half + 1) * src],
                        resp[(j * 2 + half) * 2 + side][...],
                        preferred_element_type=F32,
                    )
                    for half in range(2)
                )
                out[0, j] = (total[:rows, :rcv] + total[rows:, rcv:]).astype(out.dtype)
                out[1, j] = (total[rows:, :rcv] - total[:rows, rcv:]).astype(out.dtype)

    shapes = [jax.ShapeDtypeStruct((2, per_dev, rows, rcv), kind) for kind in (F32, BF16)]
    return call(
        body,
        (freq_place,),
        [(v, whole(v)) for v in (*flat, *messages)],
        [(v, whole(v)) for v in shapes],
        (1,),
        scratch=[pltpu.VMEM((per_dev, 2 * rows, 2 * src), BF16)],
        flops=2 * 8 * per_dev * rows * 2 * src * rcv,
    )


def next_spectra(sums, messages, tables, matrix, freq_place):
    cosines, sines, fraction = tables
    freq_devs = len(messages)
    _, per_dev, rows, rcv = sums.shape
    count = freq_devs * 2 * per_dev * ROWS
    own = 2 * per_dev * ROWS

    def body(place_ref, u_ref, c_ref, s_ref, f_ref, g_ref, *rest):
        refs, out = rest[:freq_devs], rest[freq_devs]
        matrix_here = g_ref[place_ref[0], :own]

        def one(at):
            for base in range(0, rows, 2 * ROWS):
                pair = slice(base, base + 2 * ROWS)
                data = [ref[:, :, pair, at].astype(F32) for ref in refs]
                made = []
                for half in range(2):
                    plain = [value[:, :, half * ROWS : (half + 1) * ROWS] for value in data]
                    cut = slice(base + half * ROWS, base + (half + 1) * ROWS)
                    cos = [c_ref[step, :, cut, at] for step in range(freq_devs)]
                    sin = [s_ref[step, :, cut, at] for step in range(freq_devs)]
                    up, low = mixed_fields(plain, cos, sin, matrix_here)
                    made.append(unturned(up[0], low[0], plain[0], cos[0], sin[0], f_ref[cut, at]))
                out[:, :, pair, at] = (u_ref[:, :, pair, at] - jnp.concatenate(made, 2)).astype(BF16)

        tiles(rcv, one)

    inputs = (sums, cosines, sines, fraction, matrix, *messages)
    (out,) = call(
        body,
        (freq_place,),
        [(v, whole(v)) for v in inputs],
        [(jax.ShapeDtypeStruct(sums.shape, BF16), whole(sums))],
        (1,),
        flops=2 * own * count * 2 * rcv * rows // ROWS,
    )
    return out


def updated(initial, onset, messages, table, freq_place, focal_first, first, rows, target):
    freq_devs = len(messages)
    own, rcv = initial.shape[1:]
    per_dev = messages[0].shape[1]
    tile = 2 * ROWS
    count = table.shape[2]

    def body(place_ref, focal_ref, x_ref, o_ref, t_ref, *rest):
        refs = rest[:freq_devs]
        out, spread_ref = rest[-2:]
        step = pl.program_id(0)

        @pl.when(step == 0)
        def _():
            base = t_ref[place_ref[0]].astype(F32)
            lane = lax.broadcasted_iota(jnp.int32, (own, count), 1) % ROWS
            for row in range(ROWS):
                spread_ref[row * own : (row + 1) * own] = jnp.where(lane == row, base, 0.0).astype(BF16)

        here = pl.ds(pl.multiple_of(step * tile, tile), tile)
        data = [ref[:, :, here, :].astype(F32) for ref in refs]
        onsets = o_ref[pl.ds(pl.multiple_of(focal_ref[0] + first + step * tile, tile), tile), :]
        time = lax.broadcasted_iota(jnp.int32, (own, rcv), 0) + place_ref[0] * own
        for half in range(2):
            cut = slice(half * ROWS, (half + 1) * ROWS)
            flat = jnp.stack([v[:, :, cut] for v in data]).reshape(count, rcv).astype(BF16)
            change = jnp.dot(spread_ref[...], flat, preferred_element_type=F32)
            for row in range(ROWS):
                spot = half * ROWS + row
                on = time < onsets[spot : spot + 1, :]
                moved = jnp.where(on, change[row * own : (row + 1) * own], 0.0)
                out[spot] = (x_ref[first + step * tile + spot].astype(F32) - moved).astype(BF16)

    inputs = [(v, whole(v)) for v in (initial, onset, table, *messages)]
    aliases = {}
    if target is not None:
        inputs.append((target, pl.BlockSpec(memory_space=pl.ANY)))
        aliases = {2 + len(inputs) - 1: 0}
    (out,) = call(
        body,
        (freq_place, focal_first),
        inputs,
        [(jax.ShapeDtypeStruct(initial.shape, BF16), pl.BlockSpec((tile, own, rcv), lambda i, *_: (first // tile + i, 0, 0)))],
        (rows // tile,),
        scratch=[pltpu.VMEM((ROWS * own, count), BF16)],
        aliases=aliases,
        flops=2 * 2 * freq_devs * per_dev * own * rows * rcv,
    )
    return out


def exchanged(value, axis, step):
    return lax.ppermute(value, axis, [(i, i ^ step) for i in range(lax.axis_size(axis))])


def dealt_out(parts):
    return [exchanged(part, "freq", step) if step else part for part, step in zip(parts, ways(len(parts)))]


def spread(value, count):
    return dealt_out([value] * count)


def on_device(initial, response, aperture, onset_rcv, onset_src):
    freq_devs = lax.axis_size("freq")
    per_dev = response.shape[0]
    samples = initial.shape[1] * freq_devs
    half_rows = initial.shape[0]
    src_width = response.shape[2] // 2
    rows = half_rows // CHUNKS
    share = rows // freq_devs
    freq_index = lax.axis_index("freq")
    rblk_index = lax.axis_index("rblk")
    sblk_index = lax.axis_index("sblk")
    freq_place = freq_index.reshape(1)
    places = tuple(index.reshape(1) for index in (freq_index, rblk_index, sblk_index))

    kept, moved = masked_halves(response, aperture, places[1])
    moved = [exchanged(v, "rblk", 1) for v in moved]
    kept_pair = [exchanged(v, "sblk", 1) for v in kept]
    responses = None
    forward = jnp.asarray(forward_tables(samples, freq_devs, per_dev))
    inverse = jnp.asarray(inverse_tables(samples, freq_devs, per_dev))
    matrix = jnp.asarray(window_tables(samples, freq_devs, per_dev))

    result = None
    for chunk in range(CHUNKS):
        first = chunk * rows
        parts = first_spectra(initial, forward, freq_place, freq_devs, per_dev, first, rows)
        sums, spectra = summed(dealt_out(parts))
        far = exchanged(spectra, "rblk", 1)
        if responses is None:
            before, moved_pair = spectra, []
            for at in range(per_dev):
                moved[at], before = lax.optimization_barrier((moved[at], before))
                spectra, far = (spectra, before) if at else (before, far)
                moved_pair.append(exchanged(moved[at], "sblk", 1))
                before = far
            responses = [((kept[j], moved[j]), (kept_pair[j], moved_pair[j])) for j in range(per_dev)]

        own, other = src_onsets(onset_src, places, half_rows, first, share, src_width)
        src_tables = phase_tables((own, exchanged(other, "sblk", 1)), places, freq_devs, per_dev, samples)
        rcv_tables = phase_tables((onset_rcv,), places, freq_devs, per_dev, samples, rows, first, half_rows)

        for step in range(ITERS):
            far = far if step == 0 else exchanged(spectra, "rblk", 1)
            messages = dealt_out(down_products(spectra, far, responses, freq_place, freq_devs))
            messages = windowed(messages, src_tables, matrix, freq_place, per_dev, share)
            keep, send = up_products(dealt_out(messages), responses, freq_place, rows)
            back = added(keep, exchanged(send, "rblk", 1))
            messages = spread(back, freq_devs)
            if step < ITERS - 1:
                spectra = next_spectra(sums, messages, rcv_tables, matrix, freq_place)
            else:
                tile_first = (sblk_index * half_rows).reshape(1)
                result = updated(
                    initial, onset_rcv, messages, inverse, freq_place, tile_first, first, rows, result
                )
    return result


def transform_tables(length, count):
    table = fields(length, count).reshape(2 * count, length)
    forward_table = jnp.asarray(table.astype(np.float32).astype(BF16))
    inverse_table = jnp.asarray((table.T * (2.0 / length)).astype(np.float32).astype(BF16))
    return forward_table, inverse_table


def settle(values):
    return lax.optimization_barrier(values.astype(BF16)).astype(F32)


def samples_into_spectra(values, forward_table, freq_total):
    out = jnp.einsum("kt,ptn->pkn", forward_table, values, preferred_element_type=F32)
    return out.reshape(values.shape[0], 2, freq_total, values.shape[2]).astype(BF16)


def spectra_into_samples(trace_spectra, inverse_table):
    flat = trace_spectra.reshape(trace_spectra.shape[0], -1, trace_spectra.shape[3])
    return jnp.einsum("tk,pkn->ptn", inverse_table, flat, preferred_element_type=F32)


def dense(spec, gated, real, imag, sign):
    dot = functools.partial(jnp.einsum, spec, preferred_element_type=F32)
    return jnp.stack(
        [dot(gated[:, 0], real) - sign * dot(gated[:, 1], imag), dot(gated[:, 0], imag) + sign * dot(gated[:, 1], real)], 1
    )


def general_device(initial, response, aperture, onset_rcv, onset_src):
    freq_devs, rblk_devs, sblk_devs = (lax.axis_size(a) for a in ("freq", "rblk", "sblk"))
    freq_index, rblk_index, sblk_index = (lax.axis_index(a) for a in ("freq", "rblk", "sblk"))
    freq_total = response.shape[0] * freq_devs
    samples = initial.shape[1] * freq_devs
    focal_all = onset_rcv.shape[0]
    forward_table, inverse_table = transform_tables(samples, freq_total)
    steps_axis = lax.iota(jnp.int32, samples)
    own_axis = freq_index * initial.shape[1] + lax.iota(jnp.int32, initial.shape[1])
    half_rows = focal_all // sblk_devs
    own_onsets = lax.dynamic_slice_in_dim(onset_rcv, sblk_index * half_rows, half_rows, 0)
    rcv_gate = (own_axis[None, :, None] < own_onsets[:, None, :]).astype(F32)
    src_rows = focal_all // (rblk_devs * freq_devs)
    src_first = rblk_index * (focal_all // rblk_devs) + freq_index * src_rows
    src_onsets = lax.dynamic_slice_in_dim(onset_src, src_first, src_rows, 0)
    src_gate = (steps_axis[None, :, None] < src_onsets[:, None, :]).astype(F32)
    mask_full = jnp.repeat(jnp.repeat(aperture, BLOCK, 1), BLOCK, 2).astype(BF16)
    gated = response * mask_full[:, None]
    own_forward = lax.dynamic_slice_in_dim(forward_table, freq_index * initial.shape[1], initial.shape[1], 1)
    own_inverse = lax.dynamic_slice_in_dim(inverse_table, freq_index * initial.shape[1], initial.shape[1], 0)
    current = initial
    for _ in range(ITERS):
        partial = samples_into_spectra(current, own_forward, freq_total)
        spec_back = lax.psum_scatter(partial.astype(F32), "freq", scatter_dimension=2, tiled=True).astype(BF16)
        spec_all = lax.all_gather(spec_back, "sblk", axis=0, tiled=True)
        down = lax.psum_scatter(
            settle(dense("euk,bek->beu", gated, spec_all[:, 0], spec_all[:, 1], 1.0)).astype(BF16),
            "rblk",
            scatter_dimension=0,
            tiled=True,
        )
        src_traces = lax.all_to_all(down, "freq", split_axis=0, concat_axis=2, tiled=True)
        upgoing = (src_gate * spectra_into_samples(src_traces, inverse_table)).astype(BF16)
        upspec = samples_into_spectra(upgoing, forward_table, freq_total)
        up_back = lax.all_to_all(upspec, "freq", split_axis=2, concat_axis=0, tiled=True)
        up_all = lax.all_gather(up_back, "rblk", axis=0, tiled=True)
        sums = dense("qao,bqa->bqo", gated, up_all[:, 0], up_all[:, 1], -1.0).astype(BF16)
        back = lax.psum_scatter(sums, "sblk", scatter_dimension=0, tiled=True)
        traces = lax.all_gather(back, "freq", axis=2, tiled=True)
        update = rcv_gate * spectra_into_samples(traces, own_inverse)
        current = (initial.astype(F32) - update).astype(BF16)
    return current


def fits(initial, response, aperture, onset_rcv, onset_src):
    freq_devs = lax.axis_size("freq")
    if lax.axis_size("rblk") != 2 or lax.axis_size("sblk") != 2 or freq_devs & (freq_devs - 1):
        return False
    rows = initial.shape[0] // CHUNKS
    whole_rows = initial.shape[0] % CHUNKS == 0 and rows % (2 * ROWS * freq_devs) == 0
    whole_width = response.shape[2] % (4 * BLOCK) == 0 and response.shape[3] % BLOCK == 0
    return whole_rows and whole_width and onset_rcv.shape[0] == 2 * initial.shape[0]


def chosen(*arrays):
    return on_device(*arrays) if fits(*arrays) else general_device(*arrays)


def solution(mesh):
    in_specs = (
        P(("group", "sblk"), "freq", "rblk"),
        P(("group", "freq"), None, "sblk", "rblk"),
        P(("group", "freq"), "sblk", "rblk"),
        P("group", "rblk"),
        P("group", "sblk"),
    )
    out_specs = P(("group", "sblk"), "freq", "rblk")
    return jax.shard_map(chosen, mesh=mesh, in_specs=in_specs, out_specs=out_specs, check_vma=False)
```

```python
import functools
import math

import jax
import jax.numpy as jnp
import numpy as np
from jax import lax
from jax.experimental import pallas as pl
from jax.experimental.pallas import tpu as pltpu
from jax.sharding import PartitionSpec as P

BLOCK = 128
ITERS = 2
ROWS = 8
CHUNKS = 1
VMEM_BYTES = 6 * 1024 * 1024

BF16 = jnp.bfloat16
F32 = jnp.float32


def ways(count):
    far = sorted(range(1, count), key=lambda step: (step.bit_length() < count.bit_length() - 1, step))
    return [0] + far


def field_rows(place, freq_devs, per_dev):
    rows = []
    for step in ways(freq_devs):
        first = (place ^ step) * per_dev
        for part in range(2):
            rows.extend((part, first + local) for local in range(per_dev))
    return rows


def fields(samples, freq_total):
    phase = (np.arange(1, freq_total + 1)[:, None] * np.arange(samples)[None, :]) % samples
    angle = phase * (2.0 * math.pi / samples)
    return np.stack([np.cos(angle), -np.sin(angle)])


def forward_tables(samples, freq_devs, per_dev):
    table = fields(samples, freq_devs * per_dev)
    own = samples // freq_devs
    out = []
    for place in range(freq_devs):
        part = [table[c, j, place * own : (place + 1) * own] for c, j in field_rows(place, freq_devs, per_dev)]
        out.append(np.repeat(np.stack(part), ROWS, 0))
    return np.stack(out).astype(np.float32).astype(BF16)


def inverse_tables(samples, freq_devs, per_dev):
    out = forward_tables(samples, freq_devs, per_dev).astype(np.float32)
    exact = fields(samples, freq_devs * per_dev) * (2.0 / samples)
    own = samples // freq_devs
    for place in range(freq_devs):
        part = [exact[c, j, place * own : (place + 1) * own] for c, j in field_rows(place, freq_devs, per_dev)]
        out[place] = np.repeat(np.stack(part), ROWS, 0)
    return np.swapaxes(out, 1, 2).astype(BF16)


def window_tables(samples, freq_devs, per_dev):
    freq_total = freq_devs * per_dev
    order = np.arange(1, freq_total + 1)
    unit = 2j * math.pi / samples
    diff = order[None, :] - order[:, None]
    total = order[None, :] + order[:, None]
    same = np.where(diff == 0, 0.0, 1.0 / (samples * (np.exp(unit * np.where(diff == 0, 1, diff)) - 1.0)))
    mixed = 1.0 / (samples * (np.exp(-unit * total) - 1.0))
    full = np.zeros((2, freq_total, 2, freq_total))
    full[0, :, 0, :] = same.real + mixed.real
    full[0, :, 1, :] = mixed.imag - same.imag
    full[1, :, 0, :] = same.imag + mixed.imag
    full[1, :, 1, :] = same.real - mixed.real
    out = []
    for place in range(freq_devs):
        rows = [c * freq_total + j for c, j in field_rows(place, freq_devs, per_dev)]
        flat = full.reshape(2 * freq_total, 2 * freq_total)[np.ix_(rows, rows)]
        out.append(np.kron(flat, np.eye(ROWS)))
    return np.stack(out).astype(np.float32).astype(BF16)


def call(body, scalars, inputs, outputs, grid, scratch=(), aliases=None, flops=0):
    in_arrays = [value for value, _ in inputs]
    bytes_all = sum(v.size * v.dtype.itemsize for v in in_arrays)
    bytes_all += sum(math.prod(s.shape) * s.dtype.itemsize for s, _ in outputs)
    return pl.pallas_call(
        body,
        grid_spec=pltpu.PrefetchScalarGridSpec(
            num_scalar_prefetch=len(scalars),
            grid=grid,
            in_specs=[spec for _, spec in inputs],
            out_specs=[spec for _, spec in outputs],
            scratch_shapes=list(scratch),
        ),
        out_shape=[shape for shape, _ in outputs],
        input_output_aliases=aliases or {},
        compiler_params=pltpu.CompilerParams(vmem_limit_bytes=VMEM_BYTES),
        cost_estimate=pl.CostEstimate(flops=flops, bytes_accessed=bytes_all, transcendentals=0),
    )(*scalars, *in_arrays)


def whole(array):
    zeros = (0,) * array.ndim
    return pl.BlockSpec(array.shape, lambda *_: zeros)


def masked_halves(response, aperture, place):
    per_dev, _, src, rcv = response.shape
    half = src // 2
    steps = half // BLOCK

    def body(place_ref, flags, x_ref, *outs):
        lane = lax.broadcasted_iota(jnp.int32, (1, rcv), 1) // BLOCK
        for flip in (1, 0):
            for j in range(per_dev):
                out = outs[flip * per_dev + j]
                for step in range(steps):
                    block = (place_ref[0] ^ flip) * steps + step
                    on = flags[j, pl.ds(block, 1), :].astype(F32)
                    row = sum(jnp.where(lane == r, on[:, r : r + 1], 0.0) for r in range(rcv // BLOCK))
                    gate = jnp.broadcast_to(row, (BLOCK, rcv)).astype(BF16)
                    rows = pl.ds(pl.multiple_of(block * BLOCK, BLOCK), BLOCK)
                    to = slice(step * BLOCK, (step + 1) * BLOCK)
                    for c in range(2):
                        out[to, c * rcv : (c + 1) * rcv] = x_ref[j, c, rows, :] * gate

    shape = jax.ShapeDtypeStruct((half, 2 * rcv), BF16)
    inputs = [(v, whole(v)) for v in (aperture, response)]
    outs = call(body, (place,), inputs, [(shape, whole(shape))] * (2 * per_dev), (1,))
    return outs[:per_dev], outs[per_dev:]


def first_spectra(initial, table, freq_place, freq_devs, per_dev, first, rows):
    own, rcv = initial.shape[1:]
    tile = 2 * ROWS
    count = table.shape[1]

    def body(place_ref, x_ref, t_ref, *rest):
        outs, spread_ref = rest[:freq_devs], rest[freq_devs]
        base = t_ref[place_ref[0]].astype(F32)
        lane = lax.broadcasted_iota(jnp.int32, (count, own), 0) % ROWS
        for row in range(ROWS):
            spread_ref[:, row * own : (row + 1) * own] = jnp.where(lane == row, base, 0.0).astype(BF16)
        for at in range(rows // tile):
            parts = []
            for half in range(2):
                start = first + at * tile + half * ROWS
                flat = x_ref[start : start + ROWS].reshape(ROWS * own, rcv)
                value = jnp.dot(spread_ref[...], flat, preferred_element_type=F32)
                parts.append(value.reshape(freq_devs, 2, per_dev, ROWS, rcv))
            both = jnp.concatenate(parts, 3).astype(BF16)
            for step, out in enumerate(outs):
                out[:, :, at * tile : (at + 1) * tile, :] = both[step]

    shape = jax.ShapeDtypeStruct((2, per_dev, rows, rcv), BF16)
    return call(
        body,
        (freq_place,),
        [(initial, whole(initial)), (table, whole(table))],
        [(shape, whole(shape))] * freq_devs,
        (1,),
        scratch=[pltpu.VMEM((count, ROWS * own), BF16)],
        flops=2 * 2 * freq_devs * per_dev * own * rows * rcv,
    )


def summed(parts):
    def body(*refs):
        total = sum(ref[...].astype(F32) for ref in refs[:-2])
        refs[-2][...] = total
        refs[-1][...] = total.astype(BF16)

    shapes = [jax.ShapeDtypeStruct(parts[0].shape, kind) for kind in (F32, BF16)]
    return call(body, (), [(v, whole(v)) for v in parts], [(v, whole(v)) for v in shapes], (1,))


def added(keep, received):
    def body(k_ref, r_ref, out):
        out[...] = (k_ref[...] + r_ref[...].astype(F32)).astype(BF16)

    shape = jax.ShapeDtypeStruct(keep.shape, BF16)
    (out,) = call(body, (), [(v, whole(v)) for v in (keep, received)], [(shape, whole(shape))], (1,))
    return out


def sine_terms():
    square = (np.cos(np.linspace(0.0, math.pi, 200)) + 1.0) / 32.0
    y = np.sqrt(np.maximum(square, 1e-12))
    return [float(v) for v in np.polynomial.polynomial.polyfit(square, np.sin(2.0 * math.pi * y) / y, 6)]


def phase_tables(groups, samples):
    terms = sine_terms()
    flat = [v for group in groups for v in group]

    def sine(y):
        square = y * y
        total = jnp.full_like(y, terms[-1])
        for term in terms[-2::-1]:
            total = total * square + term
        return total * y

    def body(*refs):
        refs, outs = list(refs[: len(flat)]), list(refs[len(flat) :])
        for group in groups:
            cosine, sines, fraction = outs[:3]
            del outs[:3]
            at = 0
            for _ in group:
                ref = refs.pop(0)
                to = slice(at, at + ref.shape[1])
                at = to.stop
                part = ref[...].astype(F32) * (1.0 / samples)
                turn = part - jnp.floor(part + 0.5)
                size = jnp.abs(turn)
                folded = jnp.where(size > 0.25, jnp.where(turn > 0.0, 0.5, -0.5) - turn, turn)
                cosine[:, to] = sine(0.25 - size)
                sines[:, to] = sine(folded)
                fraction[:, to] = part

    shapes = []
    for group in groups:
        shapes += [jax.ShapeDtypeStruct((group[0].shape[0], sum(v.shape[1] for v in group)), F32)] * 3
    outs = call(body, (), [(v, whole(v)) for v in flat], [(v, whole(v)) for v in shapes], (1,))
    return [tuple(outs[at : at + 3]) for at in range(0, len(outs), 3)]


def down_products(near, far, responses, freq_place, freq_devs):
    _, per_dev, rows, rcv = near.shape
    flat = [v for by_half in responses for pair in by_half for v in pair]
    width = flat[0].shape[0]
    tile = min(width, 256)
    share = rows // freq_devs

    def body(place_ref, n_ref, f_ref, *rest):
        resp, outs, held = rest[: len(flat)], rest[len(flat) : -1], rest[-1]
        for j in range(per_dev):
            sides = []
            for ref in (n_ref, f_ref):
                real, imag = ref[0, j], ref[1, j]
                sides.append(jnp.concatenate([jnp.concatenate([real, -imag], 1), jnp.concatenate([imag, real], 1)], 0))
            for half in range(2):
                pair = resp[(j * 2 + half) * 2 : (j * 2 + half) * 2 + 2]
                for at in range(width // tile):
                    cut = slice(at * tile, (at + 1) * tile)
                    total = sum(
                        lax.dot_general(lhs, ref[cut], (((1,), (1,)), ((), ())), preferred_element_type=F32)
                        for lhs, ref in zip(sides, pair)
                    )
                    to = slice(half * width + at * tile, half * width + (at + 1) * tile)
                    held[0, j, :, to] = total[:rows]
                    held[1, j, :, to] = total[rows:]
        for way, out in zip(ways(freq_devs), outs):
            start = pl.multiple_of((place_ref[0] ^ way) * share, share)
            out[...] = held[:, :, pl.ds(start, share), :].astype(BF16)

    shape = jax.ShapeDtypeStruct((2, per_dev, share, 2 * width), BF16)
    return call(
        body,
        (freq_place,),
        [(v, whole(v)) for v in (near, far, *flat)],
        [(shape, whole(shape))] * freq_devs,
        (1,),
        scratch=[pltpu.VMEM((2, per_dev, rows, 2 * width), F32)],
        flops=2 * 8 * per_dev * rows * 2 * width * rcv,
    )


def turn_powers(cosine, sine, place, freq_devs, per_dev):
    powers = [(cosine, sine)]
    for _ in range(1, freq_devs * per_dev):
        real, imag = powers[-1]
        powers.append((real * cosine - imag * sine, real * sine + imag * cosine))
    stacked = [jnp.stack([v[part] for v in powers]) for part in range(2)]
    out = []
    for value in stacked:
        groups = [value[g * per_dev : (g + 1) * per_dev] for g in range(freq_devs)]
        bit = 1
        while bit < freq_devs:
            on = jnp.broadcast_to(place & bit, groups[0].shape) != 0
            groups = [jnp.where(on, groups[g ^ bit], groups[g]) for g in range(freq_devs)]
            bit *= 2
        out.append([groups[way] for way in ways(freq_devs)])
    return out


def mixed_fields(plain, cos, sin, matrix):
    tile = plain[0].shape[-1]
    turned = [
        jnp.stack([v[0] * c - v[1] * s, v[0] * s + v[1] * c]) for v, c, s in zip(plain, cos, sin)
    ]
    flat = [jnp.stack(v).reshape(matrix.shape[1], tile).astype(BF16) for v in (turned, plain)]
    mixed = jnp.dot(matrix, jnp.concatenate(flat, 1), preferred_element_type=F32)
    shape = (-1, 2) + plain[0].shape[1:]
    return mixed[:, :tile].reshape(shape), mixed[:, tile:].reshape(shape)


def unturned(up, low, value, cos, sin, part):
    real = cos * up[0] + sin * up[1] - low[0] + part * value[0]
    imag = cos * up[1] - sin * up[0] - low[1] + part * value[1]
    return jnp.stack([real, imag])


def tiles(width, body):
    def at(step, carry):
        body(pl.ds(pl.multiple_of(step * BLOCK, BLOCK), BLOCK))
        return carry

    lax.fori_loop(0, width // BLOCK, at, 0, unroll=2)


def windowed(messages, tables, matrix, freq_place, per_dev, share):
    cosines, sines, fraction = tables
    freq_devs = len(messages)
    width = messages[0].shape[-1]
    count = freq_devs * 2 * per_dev * ROWS

    def body(place_ref, c_ref, s_ref, f_ref, g_ref, *rest):
        refs, outs = rest[:freq_devs], rest[freq_devs:]
        matrix_here = g_ref[place_ref[0]]

        def one(at):
            data = [ref[:, :, :, at].astype(F32) for ref in refs]
            made = [[] for _ in outs]
            for first in range(0, share, ROWS):
                cut = slice(first, first + ROWS)
                plain = [value[:, :, cut] for value in data]
                cos, sin = turn_powers(c_ref[cut, at], s_ref[cut, at], place_ref[0], freq_devs, per_dev)
                up, low = mixed_fields(plain, cos, sin, matrix_here)
                part = f_ref[cut, at]
                for step in range(freq_devs):
                    made[step].append(unturned(up[step], low[step], plain[step], cos[step], sin[step], part))
            for out, value in zip(outs, made):
                out[:, :, :, at] = jnp.concatenate(value, 2).astype(BF16)

        tiles(width, one)

    inputs = (cosines, sines, fraction, matrix, *messages)
    return call(
        body,
        (freq_place,),
        [(v, whole(v)) for v in inputs],
        [(jax.ShapeDtypeStruct(v.shape, BF16), whole(v)) for v in messages],
        (1,),
        flops=2 * count * count * 2 * width * share // ROWS,
    )


def up_products(messages, responses, freq_place, rows):
    freq_devs = len(messages)
    flat = [v for by_half in responses for pair in by_half for v in pair]
    src, rcv = flat[0].shape[0], flat[0].shape[1] // 2
    _, per_dev, share, _ = messages[0].shape

    def body(place_ref, *rest):
        resp, refs = rest[: len(flat)], rest[len(flat) : len(flat) + freq_devs]
        keep, send, held = rest[len(flat) + freq_devs :]
        for way, ref in zip(ways(freq_devs), refs):
            for part in range(2):
                start = pl.multiple_of(part * rows + (place_ref[0] ^ way) * share, share)
                held[:, pl.ds(start, share), :] = ref[part]
        for j in range(per_dev):
            for side, out in ((1, send), (0, keep)):
                total = sum(
                    jnp.dot(
                        held[j, :, half * src : (half + 1) * src],
                        resp[(j * 2 + half) * 2 + side][...],
                        preferred_element_type=F32,
                    )
                    for half in range(2)
                )
                out[0, j] = (total[:rows, :rcv] + total[rows:, rcv:]).astype(out.dtype)
                out[1, j] = (total[rows:, :rcv] - total[:rows, rcv:]).astype(out.dtype)

    shapes = [jax.ShapeDtypeStruct((2, per_dev, rows, rcv), kind) for kind in (F32, BF16)]
    return call(
        body,
        (freq_place,),
        [(v, whole(v)) for v in (*flat, *messages)],
        [(v, whole(v)) for v in shapes],
        (1,),
        scratch=[pltpu.VMEM((per_dev, 2 * rows, 2 * src), BF16)],
        flops=2 * 8 * per_dev * rows * 2 * src * rcv,
    )


def next_spectra(sums, messages, tables, matrix, freq_place):
    cosines, sines, fraction = tables
    freq_devs = len(messages)
    _, per_dev, rows, rcv = sums.shape
    count = freq_devs * 2 * per_dev * ROWS
    own = 2 * per_dev * ROWS

    def body(place_ref, u_ref, c_ref, s_ref, f_ref, g_ref, *rest):
        refs, out = rest[:freq_devs], rest[freq_devs]
        matrix_here = g_ref[place_ref[0], :own]

        def one(at):
            for base in range(0, rows, 2 * ROWS):
                pair = slice(base, base + 2 * ROWS)
                data = [ref[:, :, pair, at].astype(F32) for ref in refs]
                made = []
                for half in range(2):
                    plain = [value[:, :, half * ROWS : (half + 1) * ROWS] for value in data]
                    cut = slice(base + half * ROWS, base + (half + 1) * ROWS)
                    cos, sin = turn_powers(c_ref[cut, at], s_ref[cut, at], place_ref[0], freq_devs, per_dev)
                    up, low = mixed_fields(plain, cos, sin, matrix_here)
                    made.append(unturned(up[0], low[0], plain[0], cos[0], sin[0], f_ref[cut, at]))
                out[:, :, pair, at] = (u_ref[:, :, pair, at] - jnp.concatenate(made, 2)).astype(BF16)

        tiles(rcv, one)

    inputs = (sums, cosines, sines, fraction, matrix, *messages)
    (out,) = call(
        body,
        (freq_place,),
        [(v, whole(v)) for v in inputs],
        [(jax.ShapeDtypeStruct(sums.shape, BF16), whole(sums))],
        (1,),
        flops=2 * own * count * 2 * rcv * rows // ROWS,
    )
    return out


def updated(initial, onset, messages, table, freq_place, focal_first, first, rows, target):
    freq_devs = len(messages)
    own, rcv = initial.shape[1:]
    per_dev = messages[0].shape[1]
    tile = 2 * ROWS
    count = table.shape[2]

    def body(place_ref, focal_ref, x_ref, o_ref, t_ref, *rest):
        refs = rest[:freq_devs]
        out, spread_ref = rest[-2:]
        step = pl.program_id(0)

        @pl.when(step == 0)
        def _():
            base = t_ref[place_ref[0]].astype(F32)
            lane = lax.broadcasted_iota(jnp.int32, (own, count), 1) % ROWS
            for row in range(ROWS):
                spread_ref[row * own : (row + 1) * own] = jnp.where(lane == row, base, 0.0).astype(BF16)

        here = pl.ds(pl.multiple_of(step * tile, tile), tile)
        data = [ref[:, :, here, :].astype(F32) for ref in refs]
        onsets = o_ref[pl.ds(pl.multiple_of(focal_ref[0] + first + step * tile, tile), tile), :]
        time = lax.broadcasted_iota(jnp.int32, (own, rcv), 0) + place_ref[0] * own
        for half in range(2):
            cut = slice(half * ROWS, (half + 1) * ROWS)
            flat = jnp.stack([v[:, :, cut] for v in data]).reshape(count, rcv).astype(BF16)
            change = jnp.dot(spread_ref[...], flat, preferred_element_type=F32)
            for row in range(ROWS):
                spot = half * ROWS + row
                on = time < onsets[spot : spot + 1, :]
                moved = jnp.where(on, change[row * own : (row + 1) * own], 0.0)
                out[spot] = (x_ref[first + step * tile + spot].astype(F32) - moved).astype(BF16)

    inputs = [(v, whole(v)) for v in (initial, onset, table, *messages)]
    aliases = {}
    if target is not None:
        inputs.append((target, pl.BlockSpec(memory_space=pl.ANY)))
        aliases = {2 + len(inputs) - 1: 0}
    (out,) = call(
        body,
        (freq_place, focal_first),
        inputs,
        [(jax.ShapeDtypeStruct(initial.shape, BF16), pl.BlockSpec((tile, own, rcv), lambda i, *_: (first // tile + i, 0, 0)))],
        (rows // tile,),
        scratch=[pltpu.VMEM((ROWS * own, count), BF16)],
        aliases=aliases,
        flops=2 * 2 * freq_devs * per_dev * own * rows * rcv,
    )
    return out


def exchanged(value, axis, step):
    return lax.ppermute(value, axis, [(i, i ^ step) for i in range(lax.axis_size(axis))])


def dealt_out(parts):
    return [exchanged(part, "freq", step) if step else part for part, step in zip(parts, ways(len(parts)))]


def spread(value, count):
    return dealt_out([value] * count)


def on_device(initial, response, aperture, onset_rcv, onset_src):
    freq_devs = lax.axis_size("freq")
    per_dev = response.shape[0]
    samples = initial.shape[1] * freq_devs
    half_rows = initial.shape[0]
    src_width = response.shape[2] // 2
    rows = half_rows // CHUNKS
    share = rows // freq_devs
    freq_index = lax.axis_index("freq")
    rblk_index = lax.axis_index("rblk")
    sblk_index = lax.axis_index("sblk")
    freq_place = freq_index.reshape(1)
    places = tuple(index.reshape(1) for index in (freq_index, rblk_index, sblk_index))

    kept, moved = masked_halves(response, aperture, places[1])
    moved = [exchanged(v, "rblk", 1) for v in moved]
    kept_pair = [exchanged(v, "sblk", 1) for v in kept]
    responses = None
    forward = jnp.asarray(forward_tables(samples, freq_devs, per_dev))
    inverse = jnp.asarray(inverse_tables(samples, freq_devs, per_dev))
    matrix = jnp.asarray(window_tables(samples, freq_devs, per_dev))

    result = None
    for chunk in range(CHUNKS):
        first = chunk * rows
        parts = first_spectra(initial, forward, freq_place, freq_devs, per_dev, first, rows)
        sums, spectra = summed(dealt_out(parts))
        far = exchanged(spectra, "rblk", 1)
        if responses is None:
            before, moved_pair = spectra, []
            for at in range(per_dev):
                moved[at], before = lax.optimization_barrier((moved[at], before))
                spectra, far = (spectra, before) if at else (before, far)
                moved_pair.append(exchanged(moved[at], "sblk", 1))
                before = far
            responses = [((kept[j], moved[j]), (kept_pair[j], moved_pair[j])) for j in range(per_dev)]

        def src_onsets(core):
            spot = core * half_rows + first + freq_index * share
            return lax.dynamic_slice(onset_src, (spot, rblk_index * src_width), (share, src_width))

        onsets = (src_onsets(sblk_index), exchanged(src_onsets(1 - sblk_index), "sblk", 1))
        rcv_onsets = lax.dynamic_slice_in_dim(onset_rcv, sblk_index * half_rows + first, rows, 0)
        src_tables, rcv_tables = phase_tables((onsets, (rcv_onsets,)), samples)

        for step in range(ITERS):
            far = far if step == 0 else exchanged(spectra, "rblk", 1)
            messages = dealt_out(down_products(spectra, far, responses, freq_place, freq_devs))
            messages = windowed(messages, src_tables, matrix, freq_place, per_dev, share)
            keep, send = up_products(dealt_out(messages), responses, freq_place, rows)
            back = added(keep, exchanged(send, "rblk", 1))
            messages = spread(back, freq_devs)
            if step < ITERS - 1:
                spectra = next_spectra(sums, messages, rcv_tables, matrix, freq_place)
            else:
                tile_first = (sblk_index * half_rows).reshape(1)
                result = updated(
                    initial, onset_rcv, messages, inverse, freq_place, tile_first, first, rows, result
                )
    return result


def transform_tables(length, count):
    table = fields(length, count).reshape(2 * count, length)
    forward_table = jnp.asarray(table.astype(np.float32).astype(BF16))
    inverse_table = jnp.asarray((table.T * (2.0 / length)).astype(np.float32).astype(BF16))
    return forward_table, inverse_table


def settle(values):
    return lax.optimization_barrier(values.astype(BF16)).astype(F32)


def samples_into_spectra(values, forward_table, freq_total):
    out = jnp.einsum("kt,ptn->pkn", forward_table, values, preferred_element_type=F32)
    return out.reshape(values.shape[0], 2, freq_total, values.shape[2]).astype(BF16)


def spectra_into_samples(trace_spectra, inverse_table):
    flat = trace_spectra.reshape(trace_spectra.shape[0], -1, trace_spectra.shape[3])
    return jnp.einsum("tk,pkn->ptn", inverse_table, flat, preferred_element_type=F32)


def dense(spec, gated, real, imag, sign):
    dot = functools.partial(jnp.einsum, spec, preferred_element_type=F32)
    return jnp.stack(
        [dot(gated[:, 0], real) - sign * dot(gated[:, 1], imag), dot(gated[:, 0], imag) + sign * dot(gated[:, 1], real)], 1
    )


def general_device(initial, response, aperture, onset_rcv, onset_src):
    freq_devs, rblk_devs, sblk_devs = (lax.axis_size(a) for a in ("freq", "rblk", "sblk"))
    freq_index, rblk_index, sblk_index = (lax.axis_index(a) for a in ("freq", "rblk", "sblk"))
    freq_total = response.shape[0] * freq_devs
    samples = initial.shape[1] * freq_devs
    focal_all = onset_rcv.shape[0]
    forward_table, inverse_table = transform_tables(samples, freq_total)
    steps_axis = lax.iota(jnp.int32, samples)
    own_axis = freq_index * initial.shape[1] + lax.iota(jnp.int32, initial.shape[1])
    half_rows = focal_all // sblk_devs
    own_onsets = lax.dynamic_slice_in_dim(onset_rcv, sblk_index * half_rows, half_rows, 0)
    rcv_gate = (own_axis[None, :, None] < own_onsets[:, None, :]).astype(F32)
    src_rows = focal_all // (rblk_devs * freq_devs)
    src_first = rblk_index * (focal_all // rblk_devs) + freq_index * src_rows
    src_onsets = lax.dynamic_slice_in_dim(onset_src, src_first, src_rows, 0)
    src_gate = (steps_axis[None, :, None] < src_onsets[:, None, :]).astype(F32)
    mask_full = jnp.repeat(jnp.repeat(aperture, BLOCK, 1), BLOCK, 2).astype(BF16)
    gated = response * mask_full[:, None]
    own_forward = lax.dynamic_slice_in_dim(forward_table, freq_index * initial.shape[1], initial.shape[1], 1)
    own_inverse = lax.dynamic_slice_in_dim(inverse_table, freq_index * initial.shape[1], initial.shape[1], 0)
    current = initial
    for _ in range(ITERS):
        partial = samples_into_spectra(current, own_forward, freq_total)
        spec_back = lax.psum_scatter(partial.astype(F32), "freq", scatter_dimension=2, tiled=True).astype(BF16)
        spec_all = lax.all_gather(spec_back, "sblk", axis=0, tiled=True)
        down = lax.psum_scatter(
            settle(dense("euk,bek->beu", gated, spec_all[:, 0], spec_all[:, 1], 1.0)).astype(BF16),
            "rblk",
            scatter_dimension=0,
            tiled=True,
        )
        src_traces = lax.all_to_all(down, "freq", split_axis=0, concat_axis=2, tiled=True)
        upgoing = (src_gate * spectra_into_samples(src_traces, inverse_table)).astype(BF16)
        upspec = samples_into_spectra(upgoing, forward_table, freq_total)
        up_back = lax.all_to_all(upspec, "freq", split_axis=2, concat_axis=0, tiled=True)
        up_all = lax.all_gather(up_back, "rblk", axis=0, tiled=True)
        sums = dense("qao,bqa->bqo", gated, up_all[:, 0], up_all[:, 1], -1.0).astype(BF16)
        back = lax.psum_scatter(sums, "sblk", scatter_dimension=0, tiled=True)
        traces = lax.all_gather(back, "freq", axis=2, tiled=True)
        update = rcv_gate * spectra_into_samples(traces, own_inverse)
        current = (initial.astype(F32) - update).astype(BF16)
    return current


def fits(initial, response, aperture, onset_rcv, onset_src):
    freq_devs = lax.axis_size("freq")
    if lax.axis_size("rblk") != 2 or lax.axis_size("sblk") != 2 or freq_devs & (freq_devs - 1):
        return False
    rows = initial.shape[0] // CHUNKS
    whole_rows = initial.shape[0] % CHUNKS == 0 and rows % (2 * ROWS * freq_devs) == 0
    whole_width = response.shape[2] % (4 * BLOCK) == 0 and response.shape[3] % BLOCK == 0
    return whole_rows and whole_width and onset_rcv.shape[0] == 2 * initial.shape[0]


def chosen(*arrays):
    return on_device(*arrays) if fits(*arrays) else general_device(*arrays)


def solution(mesh):
    in_specs = (
        P(("group", "sblk"), "freq", "rblk"),
        P(("group", "freq"), None, "sblk", "rblk"),
        P(("group", "freq"), "sblk", "rblk"),
        P("group", "rblk"),
        P("group", "sblk"),
    )
    out_specs = P(("group", "sblk"), "freq", "rblk")
    return jax.shard_map(chosen, mesh=mesh, in_specs=in_specs, out_specs=out_specs, check_vma=False)
```

```python
import functools
import math

import jax
import jax.numpy as jnp
import numpy as np
from jax import lax
from jax.experimental import pallas as pl
from jax.experimental.pallas import tpu as pltpu
from jax.sharding import PartitionSpec as P

BLOCK = 128
ITERS = 2
ROWS = 8
CHUNKS = 1
VMEM_BYTES = 6 * 1024 * 1024

BF16 = jnp.bfloat16
F32 = jnp.float32


def ways(count):
    far = sorted(range(1, count), key=lambda step: (step.bit_length() < count.bit_length() - 1, step))
    return [0] + far


def field_rows(place, freq_devs, per_dev):
    rows = []
    for step in ways(freq_devs):
        first = (place ^ step) * per_dev
        for part in range(2):
            rows.extend((part, first + local) for local in range(per_dev))
    return rows


def fields(samples, freq_total):
    phase = (np.arange(1, freq_total + 1)[:, None] * np.arange(samples)[None, :]) % samples
    angle = phase * (2.0 * math.pi / samples)
    return np.stack([np.cos(angle), -np.sin(angle)])


def forward_tables(samples, freq_devs, per_dev):
    table = fields(samples, freq_devs * per_dev)
    own = samples // freq_devs
    out = []
    for place in range(freq_devs):
        part = [table[c, j, place * own : (place + 1) * own] for c, j in field_rows(place, freq_devs, per_dev)]
        out.append(np.repeat(np.stack(part), ROWS, 0))
    return np.stack(out).astype(np.float32).astype(BF16)


def inverse_tables(samples, freq_devs, per_dev):
    out = forward_tables(samples, freq_devs, per_dev).astype(np.float32)
    exact = fields(samples, freq_devs * per_dev) * (2.0 / samples)
    own = samples // freq_devs
    for place in range(freq_devs):
        part = [exact[c, j, place * own : (place + 1) * own] for c, j in field_rows(place, freq_devs, per_dev)]
        out[place] = np.repeat(np.stack(part), ROWS, 0)
    return np.swapaxes(out, 1, 2).astype(BF16)


def window_tables(samples, freq_devs, per_dev):
    freq_total = freq_devs * per_dev
    order = np.arange(1, freq_total + 1)
    unit = 2j * math.pi / samples
    diff = order[None, :] - order[:, None]
    total = order[None, :] + order[:, None]
    same = np.where(diff == 0, 0.0, 1.0 / (samples * (np.exp(unit * np.where(diff == 0, 1, diff)) - 1.0)))
    mixed = 1.0 / (samples * (np.exp(-unit * total) - 1.0))
    full = np.zeros((2, freq_total, 2, freq_total))
    full[0, :, 0, :] = same.real + mixed.real
    full[0, :, 1, :] = mixed.imag - same.imag
    full[1, :, 0, :] = same.imag + mixed.imag
    full[1, :, 1, :] = same.real - mixed.real
    out = []
    for place in range(freq_devs):
        rows = [c * freq_total + j for c, j in field_rows(place, freq_devs, per_dev)]
        flat = full.reshape(2 * freq_total, 2 * freq_total)[np.ix_(rows, rows)]
        out.append(np.kron(flat, np.eye(ROWS)))
    return np.stack(out).astype(np.float32).astype(BF16)


def call(body, scalars, inputs, outputs, grid, scratch=(), aliases=None, flops=0):
    in_arrays = [value for value, _ in inputs]
    bytes_all = sum(v.size * v.dtype.itemsize for v in in_arrays)
    bytes_all += sum(math.prod(s.shape) * s.dtype.itemsize for s, _ in outputs)
    return pl.pallas_call(
        body,
        grid_spec=pltpu.PrefetchScalarGridSpec(
            num_scalar_prefetch=len(scalars),
            grid=grid,
            in_specs=[spec for _, spec in inputs],
            out_specs=[spec for _, spec in outputs],
            scratch_shapes=list(scratch),
        ),
        out_shape=[shape for shape, _ in outputs],
        input_output_aliases=aliases or {},
        compiler_params=pltpu.CompilerParams(vmem_limit_bytes=VMEM_BYTES),
        cost_estimate=pl.CostEstimate(flops=flops, bytes_accessed=bytes_all, transcendentals=0),
    )(*scalars, *in_arrays)


def whole(array):
    zeros = (0,) * array.ndim
    return pl.BlockSpec(array.shape, lambda *_: zeros)


def masked_halves(response, aperture, places):
    per_dev, _, src, rcv = response.shape
    half = src // 2
    steps = half // BLOCK

    def body(_, rblk, __, flags, x_ref, *outs):
        lane = lax.broadcasted_iota(jnp.int32, (1, rcv), 1) // BLOCK
        for flip in (1, 0):
            for j in range(per_dev):
                out = outs[flip * per_dev + j]
                for step in range(steps):
                    block = (rblk[0] ^ flip) * steps + step
                    on = flags[j, pl.ds(block, 1), :].astype(F32)
                    row = sum(jnp.where(lane == r, on[:, r : r + 1], 0.0) for r in range(rcv // BLOCK))
                    gate = jnp.broadcast_to(row, (BLOCK, rcv)).astype(BF16)
                    rows = pl.ds(pl.multiple_of(block * BLOCK, BLOCK), BLOCK)
                    to = slice(step * BLOCK, (step + 1) * BLOCK)
                    for c in range(2):
                        out[to, c * rcv : (c + 1) * rcv] = x_ref[j, c, rows, :] * gate

    shape = jax.ShapeDtypeStruct((half, 2 * rcv), BF16)
    inputs = [(v, whole(v)) for v in (aperture, response)]
    outs = call(body, places, inputs, [(shape, whole(shape))] * (2 * per_dev), (1,))
    return outs[:per_dev], outs[per_dev:]


def first_spectra(initial, table, freq_place, freq_devs, per_dev, first, rows):
    own, rcv = initial.shape[1:]
    tile = 2 * ROWS
    count = table.shape[1]

    def body(place_ref, x_ref, t_ref, *rest):
        outs, spread_ref = rest[:freq_devs], rest[freq_devs]
        base = t_ref[place_ref[0]].astype(F32)
        lane = lax.broadcasted_iota(jnp.int32, (count, own), 0) % ROWS
        for row in range(ROWS):
            spread_ref[:, row * own : (row + 1) * own] = jnp.where(lane == row, base, 0.0).astype(BF16)
        for at in range(rows // tile):
            parts = []
            for half in range(2):
                start = first + at * tile + half * ROWS
                flat = x_ref[start : start + ROWS].reshape(ROWS * own, rcv)
                value = jnp.dot(spread_ref[...], flat, preferred_element_type=F32)
                parts.append(value.reshape(freq_devs, 2, per_dev, ROWS, rcv))
            both = jnp.concatenate(parts, 3).astype(BF16)
            for step, out in enumerate(outs):
                out[:, :, at * tile : (at + 1) * tile, :] = both[step]

    shape = jax.ShapeDtypeStruct((2, per_dev, rows, rcv), BF16)
    return call(
        body,
        (freq_place,),
        [(initial, whole(initial)), (table, whole(table))],
        [(shape, whole(shape))] * freq_devs,
        (1,),
        scratch=[pltpu.VMEM((count, ROWS * own), BF16)],
        flops=2 * 2 * freq_devs * per_dev * own * rows * rcv,
    )


def summed(parts):
    def body(*refs):
        total = sum(ref[...].astype(F32) for ref in refs[:-2])
        refs[-2][...] = total
        refs[-1][...] = total.astype(BF16)

    shapes = [jax.ShapeDtypeStruct(parts[0].shape, kind) for kind in (F32, BF16)]
    return call(body, (), [(v, whole(v)) for v in parts], [(v, whole(v)) for v in shapes], (1,))


def added(keep, received):
    def body(k_ref, r_ref, out):
        out[...] = (k_ref[...] + r_ref[...].astype(F32)).astype(BF16)

    shape = jax.ShapeDtypeStruct(keep.shape, BF16)
    (out,) = call(body, (), [(v, whole(v)) for v in (keep, received)], [(shape, whole(shape))], (1,))
    return out


def src_onsets(onset, places, half_rows, first, share, width):
    def body(freq, rblk, sblk, o_ref, own, other):
        lanes = pl.ds(pl.multiple_of(rblk[0] * width, BLOCK), width)
        for core, out in ((sblk[0], own), (1 - sblk[0], other)):
            spot = pl.multiple_of(core * half_rows + first + freq[0] * share, ROWS)
            out[...] = o_ref[pl.ds(spot, share), lanes]

    shape = jax.ShapeDtypeStruct((share, width), onset.dtype)
    return call(body, places, [(onset, whole(onset))], [(shape, whole(shape))] * 2, (1,))


def sine_terms():
    square = (np.cos(np.linspace(0.0, math.pi, 200)) + 1.0) / 32.0
    y = np.sqrt(np.maximum(square, 1e-12))
    return [float(v) for v in np.polynomial.polynomial.polyfit(square, np.sin(2.0 * math.pi * y) / y, 6)]


def phase_tables(onsets, places, freq_devs, per_dev, samples, rows=None, first=0, half_rows=0):
    terms = sine_terms()
    count = rows or onsets[0].shape[0]
    widths = [v.shape[1] for v in onsets]

    def sine(y):
        square = y * y
        total = jnp.full_like(y, terms[-1])
        for term in terms[-2::-1]:
            total = total * square + term
        return total * y

    def body(freq, _, sblk, *refs):
        cosines, sines, fraction = refs[-3:]
        at = 0
        for ref, width in zip(refs, widths):
            if rows:
                value = ref[pl.ds(pl.multiple_of(sblk[0] * half_rows + first, ROWS), rows), :]
            else:
                value = ref[...]
            part = value.astype(F32) * (1.0 / samples)
            to = slice(at, at + width)
            fraction[:, to] = part
            for step, way in enumerate(ways(freq_devs)):
                for j in range(per_dev):
                    order = ((freq[0] ^ way) * per_dev + j + 1).astype(F32)
                    turn = part * order
                    turn = turn - jnp.floor(turn + 0.5)
                    size = jnp.abs(turn)
                    folded = jnp.where(size > 0.25, jnp.where(turn > 0.0, 0.5, -0.5) - turn, turn)
                    cosines[step, j, :, to] = sine(0.25 - size)
                    sines[step, j, :, to] = sine(folded)
            at += width

    table = jax.ShapeDtypeStruct((freq_devs, per_dev, count, sum(widths)), F32)
    shapes = [table, table, jax.ShapeDtypeStruct((count, sum(widths)), F32)]
    return call(body, places, [(v, whole(v)) for v in onsets], [(v, whole(v)) for v in shapes], (1,))


def down_products(near, far, responses, freq_place, freq_devs):
    _, per_dev, rows, rcv = near.shape
    flat = [v for by_half in responses for pair in by_half for v in pair]
    width = flat[0].shape[0]
    tile = min(width, 256)
    share = rows // freq_devs

    def body(place_ref, n_ref, f_ref, *rest):
        resp, outs, held = rest[: len(flat)], rest[len(flat) : -1], rest[-1]
        for j in range(per_dev):
            sides = []
            for ref in (n_ref, f_ref):
                real, imag = ref[0, j], ref[1, j]
                sides.append(jnp.concatenate([jnp.concatenate([real, -imag], 1), jnp.concatenate([imag, real], 1)], 0))
            for half in range(2):
                pair = resp[(j * 2 + half) * 2 : (j * 2 + half) * 2 + 2]
                for at in range(width // tile):
                    cut = slice(at * tile, (at + 1) * tile)
                    total = sum(
                        lax.dot_general(lhs, ref[cut], (((1,), (1,)), ((), ())), preferred_element_type=F32)
                        for lhs, ref in zip(sides, pair)
                    )
                    to = slice(half * width + at * tile, half * width + (at + 1) * tile)
                    held[0, j, :, to] = total[:rows]
                    held[1, j, :, to] = total[rows:]
        for way, out in zip(ways(freq_devs), outs):
            start = pl.multiple_of((place_ref[0] ^ way) * share, share)
            out[...] = held[:, :, pl.ds(start, share), :].astype(BF16)

    shape = jax.ShapeDtypeStruct((2, per_dev, share, 2 * width), BF16)
    return call(
        body,
        (freq_place,),
        [(v, whole(v)) for v in (near, far, *flat)],
        [(shape, whole(shape))] * freq_devs,
        (1,),
        scratch=[pltpu.VMEM((2, per_dev, rows, 2 * width), F32)],
        flops=2 * 8 * per_dev * rows * 2 * width * rcv,
    )


def mixed_fields(plain, cos, sin, matrix):
    tile = plain[0].shape[-1]
    turned = [
        jnp.stack([v[0] * c - v[1] * s, v[0] * s + v[1] * c]) for v, c, s in zip(plain, cos, sin)
    ]
    flat = [jnp.stack(v).reshape(matrix.shape[1], tile).astype(BF16) for v in (turned, plain)]
    mixed = jnp.dot(matrix, jnp.concatenate(flat, 1), preferred_element_type=F32)
    shape = (-1, 2) + plain[0].shape[1:]
    return mixed[:, :tile].reshape(shape), mixed[:, tile:].reshape(shape)


def unturned(up, low, value, cos, sin, part):
    real = cos * up[0] + sin * up[1] - low[0] + part * value[0]
    imag = cos * up[1] - sin * up[0] - low[1] + part * value[1]
    return jnp.stack([real, imag])


def tiles(width, body):
    def at(step, carry):
        body(pl.ds(pl.multiple_of(step * BLOCK, BLOCK), BLOCK))
        return carry

    lax.fori_loop(0, width // BLOCK, at, 0, unroll=2)


def windowed(messages, tables, matrix, freq_place, per_dev, share):
    cosines, sines, fraction = tables
    freq_devs = len(messages)
    width = messages[0].shape[-1]
    count = freq_devs * 2 * per_dev * ROWS

    def body(place_ref, c_ref, s_ref, f_ref, g_ref, *rest):
        refs, outs = rest[:freq_devs], rest[freq_devs:]
        matrix_here = g_ref[place_ref[0]]

        def one(at):
            data = [ref[:, :, :, at].astype(F32) for ref in refs]
            made = [[] for _ in outs]
            for first in range(0, share, ROWS):
                cut = slice(first, first + ROWS)
                plain = [value[:, :, cut] for value in data]
                cos = [c_ref[step, :, cut, at] for step in range(freq_devs)]
                sin = [s_ref[step, :, cut, at] for step in range(freq_devs)]
                up, low = mixed_fields(plain, cos, sin, matrix_here)
                part = f_ref[cut, at]
                for step in range(freq_devs):
                    made[step].append(unturned(up[step], low[step], plain[step], cos[step], sin[step], part))
            for out, value in zip(outs, made):
                out[:, :, :, at] = jnp.concatenate(value, 2).astype(BF16)

        tiles(width, one)

    inputs = (cosines, sines, fraction, matrix, *messages)
    return call(
        body,
        (freq_place,),
        [(v, whole(v)) for v in inputs],
        [(jax.ShapeDtypeStruct(v.shape, BF16), whole(v)) for v in messages],
        (1,),
        flops=2 * count * count * 2 * width * share // ROWS,
    )


def up_products(messages, responses, freq_place, rows):
    freq_devs = len(messages)
    flat = [v for by_half in responses for pair in by_half for v in pair]
    src, rcv = flat[0].shape[0], flat[0].shape[1] // 2
    _, per_dev, share, _ = messages[0].shape

    def body(place_ref, *rest):
        resp, refs = rest[: len(flat)], rest[len(flat) : len(flat) + freq_devs]
        keep, send, held = rest[len(flat) + freq_devs :]
        for way, ref in zip(ways(freq_devs), refs):
            for part in range(2):
                start = pl.multiple_of(part * rows + (place_ref[0] ^ way) * share, share)
                held[:, pl.ds(start, share), :] = ref[part]
        for j in range(per_dev):
            for side, out in ((1, send), (0, keep)):
                total = sum(
                    jnp.dot(
                        held[j, :, half * src : (half + 1) * src],
                        resp[(j * 2 + half) * 2 + side][...],
                        preferred_element_type=F32,
                    )
                    for half in range(2)
                )
                out[0, j] = (total[:rows, :rcv] + total[rows:, rcv:]).astype(out.dtype)
                out[1, j] = (total[rows:, :rcv] - total[:rows, rcv:]).astype(out.dtype)

    shapes = [jax.ShapeDtypeStruct((2, per_dev, rows, rcv), kind) for kind in (F32, BF16)]
    return call(
        body,
        (freq_place,),
        [(v, whole(v)) for v in (*flat, *messages)],
        [(v, whole(v)) for v in shapes],
        (1,),
        scratch=[pltpu.VMEM((per_dev, 2 * rows, 2 * src), BF16)],
        flops=2 * 8 * per_dev * rows * 2 * src * rcv,
    )


def next_spectra(sums, messages, tables, matrix, freq_place):
    cosines, sines, fraction = tables
    freq_devs = len(messages)
    _, per_dev, rows, rcv = sums.shape
    count = freq_devs * 2 * per_dev * ROWS
    own = 2 * per_dev * ROWS

    def body(place_ref, u_ref, c_ref, s_ref, f_ref, g_ref, *rest):
        refs, out = rest[:freq_devs], rest[freq_devs]
        matrix_here = g_ref[place_ref[0], :own]

        def one(at):
            for base in range(0, rows, 2 * ROWS):
                pair = slice(base, base + 2 * ROWS)
                data = [ref[:, :, pair, at].astype(F32) for ref in refs]
                made = []
                for half in range(2):
                    plain = [value[:, :, half * ROWS : (half + 1) * ROWS] for value in data]
                    cut = slice(base + half * ROWS, base + (half + 1) * ROWS)
                    cos = [c_ref[step, :, cut, at] for step in range(freq_devs)]
                    sin = [s_ref[step, :, cut, at] for step in range(freq_devs)]
                    up, low = mixed_fields(plain, cos, sin, matrix_here)
                    made.append(unturned(up[0], low[0], plain[0], cos[0], sin[0], f_ref[cut, at]))
                out[:, :, pair, at] = (u_ref[:, :, pair, at] - jnp.concatenate(made, 2)).astype(BF16)

        tiles(rcv, one)

    inputs = (sums, cosines, sines, fraction, matrix, *messages)
    (out,) = call(
        body,
        (freq_place,),
        [(v, whole(v)) for v in inputs],
        [(jax.ShapeDtypeStruct(sums.shape, BF16), whole(sums))],
        (1,),
        flops=2 * own * count * 2 * rcv * rows // ROWS,
    )
    return out


def updated(initial, onset, messages, table, places, first, rows, target):
    freq_devs = len(messages)
    half_rows, own, rcv = initial.shape
    per_dev = messages[0].shape[1]
    tile = 2 * ROWS
    count = table.shape[2]

    def body(place_ref, _, sblk, x_ref, o_ref, t_ref, *rest):
        refs = rest[:freq_devs]
        out, spread_ref = rest[-2:]
        step = pl.program_id(0)

        @pl.when(step == 0)
        def _():
            base = t_ref[place_ref[0]].astype(F32)
            lane = lax.broadcasted_iota(jnp.int32, (own, count), 1) % ROWS
            for row in range(ROWS):
                spread_ref[row * own : (row + 1) * own] = jnp.where(lane == row, base, 0.0).astype(BF16)

        here = pl.ds(pl.multiple_of(step * tile, tile), tile)
        data = [ref[:, :, here, :].astype(F32) for ref in refs]
        onsets = o_ref[pl.ds(pl.multiple_of(sblk[0] * half_rows + first + step * tile, tile), tile), :]
        time = lax.broadcasted_iota(jnp.int32, (own, rcv), 0) + place_ref[0] * own
        for half in range(2):
            cut = slice(half * ROWS, (half + 1) * ROWS)
            flat = jnp.stack([v[:, :, cut] for v in data]).reshape(count, rcv).astype(BF16)
            change = jnp.dot(spread_ref[...], flat, preferred_element_type=F32)
            for row in range(ROWS):
                spot = half * ROWS + row
                on = time < onsets[spot : spot + 1, :]
                moved = jnp.where(on, change[row * own : (row + 1) * own], 0.0)
                out[spot] = (x_ref[first + step * tile + spot].astype(F32) - moved).astype(BF16)

    inputs = [(v, whole(v)) for v in (initial, onset, table, *messages)]
    aliases = {}
    if target is not None:
        inputs.append((target, pl.BlockSpec(memory_space=pl.ANY)))
        aliases = {len(places) + len(inputs) - 1: 0}
    (out,) = call(
        body,
        places,
        inputs,
        [(jax.ShapeDtypeStruct(initial.shape, BF16), pl.BlockSpec((tile, own, rcv), lambda i, *_: (first // tile + i, 0, 0)))],
        (rows // tile,),
        scratch=[pltpu.VMEM((ROWS * own, count), BF16)],
        aliases=aliases,
        flops=2 * 2 * freq_devs * per_dev * own * rows * rcv,
    )
    return out


def exchanged(value, axis, step):
    return lax.ppermute(value, axis, [(i, i ^ step) for i in range(lax.axis_size(axis))])


def dealt_out(parts):
    return [exchanged(part, "freq", step) if step else part for part, step in zip(parts, ways(len(parts)))]


def spread(value, count):
    return dealt_out([value] * count)


def on_device(initial, response, aperture, onset_rcv, onset_src):
    freq_devs = lax.axis_size("freq")
    per_dev = response.shape[0]
    samples = initial.shape[1] * freq_devs
    half_rows = initial.shape[0]
    src_width = response.shape[2] // 2
    rows = half_rows // CHUNKS
    share = rows // freq_devs
    freq_index = lax.axis_index("freq")
    rblk_index = lax.axis_index("rblk")
    sblk_index = lax.axis_index("sblk")
    places = tuple(index.reshape(1) for index in (freq_index, rblk_index, sblk_index))
    freq_place = places[0]

    kept, moved = masked_halves(response, aperture, places)
    moved = [exchanged(v, "rblk", 1) for v in moved]
    kept_pair = [exchanged(v, "sblk", 1) for v in kept]
    responses = None
    forward = jnp.asarray(forward_tables(samples, freq_devs, per_dev))
    inverse = jnp.asarray(inverse_tables(samples, freq_devs, per_dev))
    matrix = jnp.asarray(window_tables(samples, freq_devs, per_dev))

    result = None
    for chunk in range(CHUNKS):
        first = chunk * rows
        parts = first_spectra(initial, forward, freq_place, freq_devs, per_dev, first, rows)
        sums, spectra = summed(dealt_out(parts))
        far = exchanged(spectra, "rblk", 1)
        if responses is None:
            before, moved_pair = spectra, []
            for at in range(per_dev):
                moved[at], before = lax.optimization_barrier((moved[at], before))
                spectra, far = (spectra, before) if at else (before, far)
                moved_pair.append(exchanged(moved[at], "sblk", 1))
                before = far
            responses = [((kept[j], moved[j]), (kept_pair[j], moved_pair[j])) for j in range(per_dev)]

        own, other = src_onsets(onset_src, places, half_rows, first, share, src_width)
        src_tables = phase_tables((own, exchanged(other, "sblk", 1)), places, freq_devs, per_dev, samples)
        rcv_tables = phase_tables((onset_rcv,), places, freq_devs, per_dev, samples, rows, first, half_rows)

        for step in range(ITERS):
            far = far if step == 0 else exchanged(spectra, "rblk", 1)
            messages = dealt_out(down_products(spectra, far, responses, freq_place, freq_devs))
            messages = windowed(messages, src_tables, matrix, freq_place, per_dev, share)
            keep, send = up_products(dealt_out(messages), responses, freq_place, rows)
            back = added(keep, exchanged(send, "rblk", 1))
            messages = spread(back, freq_devs)
            if step < ITERS - 1:
                spectra = next_spectra(sums, messages, rcv_tables, matrix, freq_place)
            else:
                result = updated(initial, onset_rcv, messages, inverse, places, first, rows, result)
    return result


def transform_tables(length, count):
    table = fields(length, count).reshape(2 * count, length)
    forward_table = jnp.asarray(table.astype(np.float32).astype(BF16))
    inverse_table = jnp.asarray((table.T * (2.0 / length)).astype(np.float32).astype(BF16))
    return forward_table, inverse_table


def settle(values):
    return lax.optimization_barrier(values.astype(BF16)).astype(F32)


def samples_into_spectra(values, forward_table, freq_total):
    out = jnp.einsum("kt,ptn->pkn", forward_table, values, preferred_element_type=F32)
    return out.reshape(values.shape[0], 2, freq_total, values.shape[2]).astype(BF16)


def spectra_into_samples(trace_spectra, inverse_table):
    flat = trace_spectra.reshape(trace_spectra.shape[0], -1, trace_spectra.shape[3])
    return jnp.einsum("tk,pkn->ptn", inverse_table, flat, preferred_element_type=F32)


def dense(spec, gated, real, imag, sign):
    dot = functools.partial(jnp.einsum, spec, preferred_element_type=F32)
    return jnp.stack(
        [dot(gated[:, 0], real) - sign * dot(gated[:, 1], imag), dot(gated[:, 0], imag) + sign * dot(gated[:, 1], real)], 1
    )


def general_device(initial, response, aperture, onset_rcv, onset_src):
    freq_devs, rblk_devs, sblk_devs = (lax.axis_size(a) for a in ("freq", "rblk", "sblk"))
    freq_index, rblk_index, sblk_index = (lax.axis_index(a) for a in ("freq", "rblk", "sblk"))
    freq_total = response.shape[0] * freq_devs
    samples = initial.shape[1] * freq_devs
    focal_all = onset_rcv.shape[0]
    forward_table, inverse_table = transform_tables(samples, freq_total)
    steps_axis = lax.iota(jnp.int32, samples)
    own_axis = freq_index * initial.shape[1] + lax.iota(jnp.int32, initial.shape[1])
    half_rows = focal_all // sblk_devs
    own_onsets = lax.dynamic_slice_in_dim(onset_rcv, sblk_index * half_rows, half_rows, 0)
    rcv_gate = (own_axis[None, :, None] < own_onsets[:, None, :]).astype(F32)
    src_rows = focal_all // (rblk_devs * freq_devs)
    src_first = rblk_index * (focal_all // rblk_devs) + freq_index * src_rows
    src_onsets = lax.dynamic_slice_in_dim(onset_src, src_first, src_rows, 0)
    src_gate = (steps_axis[None, :, None] < src_onsets[:, None, :]).astype(F32)
    mask_full = jnp.repeat(jnp.repeat(aperture, BLOCK, 1), BLOCK, 2).astype(BF16)
    gated = response * mask_full[:, None]
    own_forward = lax.dynamic_slice_in_dim(forward_table, freq_index * initial.shape[1], initial.shape[1], 1)
    own_inverse = lax.dynamic_slice_in_dim(inverse_table, freq_index * initial.shape[1], initial.shape[1], 0)
    current = initial
    for _ in range(ITERS):
        partial = samples_into_spectra(current, own_forward, freq_total)
        spec_back = lax.psum_scatter(partial.astype(F32), "freq", scatter_dimension=2, tiled=True).astype(BF16)
        spec_all = lax.all_gather(spec_back, "sblk", axis=0, tiled=True)
        down = lax.psum_scatter(
            settle(dense("euk,bek->beu", gated, spec_all[:, 0], spec_all[:, 1], 1.0)).astype(BF16),
            "rblk",
            scatter_dimension=0,
            tiled=True,
        )
        src_traces = lax.all_to_all(down, "freq", split_axis=0, concat_axis=2, tiled=True)
        upgoing = (src_gate * spectra_into_samples(src_traces, inverse_table)).astype(BF16)
        upspec = samples_into_spectra(upgoing, forward_table, freq_total)
        up_back = lax.all_to_all(upspec, "freq", split_axis=2, concat_axis=0, tiled=True)
        up_all = lax.all_gather(up_back, "rblk", axis=0, tiled=True)
        sums = dense("qao,bqa->bqo", gated, up_all[:, 0], up_all[:, 1], -1.0).astype(BF16)
        back = lax.psum_scatter(sums, "sblk", scatter_dimension=0, tiled=True)
        traces = lax.all_gather(back, "freq", axis=2, tiled=True)
        update = rcv_gate * spectra_into_samples(traces, own_inverse)
        current = (initial.astype(F32) - update).astype(BF16)
    return current


def fits(initial, response, aperture, onset_rcv, onset_src):
    freq_devs = lax.axis_size("freq")
    if lax.axis_size("rblk") != 2 or lax.axis_size("sblk") != 2 or freq_devs & (freq_devs - 1):
        return False
    rows = initial.shape[0] // CHUNKS
    whole_rows = initial.shape[0] % CHUNKS == 0 and rows % (2 * ROWS * freq_devs) == 0
    whole_width = response.shape[2] % (4 * BLOCK) == 0 and response.shape[3] % BLOCK == 0
    return whole_rows and whole_width and onset_rcv.shape[0] == 2 * initial.shape[0]


def chosen(*arrays):
    return on_device(*arrays) if fits(*arrays) else general_device(*arrays)


def solution(mesh):
    in_specs = (
        P(("group", "sblk"), "freq", "rblk"),
        P(("group", "freq"), None, "sblk", "rblk"),
        P(("group", "freq"), "sblk", "rblk"),
        P("group", "rblk"),
        P("group", "sblk"),
    )
    out_specs = P(("group", "sblk"), "freq", "rblk")
    return jax.shard_map(chosen, mesh=mesh, in_specs=in_specs, out_specs=out_specs, check_vma=False)
```

```python
import functools
import math

import jax
import jax.numpy as jnp
import numpy as np
from jax import lax
from jax.experimental import pallas as pl
from jax.experimental.pallas import tpu as pltpu
from jax.sharding import PartitionSpec as P

BLOCK = 128
ITERS = 2
ROWS = 8
CHUNKS = 2
PARTS = 2
VMEM_BYTES = 6 * 1024 * 1024

BF16 = jnp.bfloat16
F32 = jnp.float32


def ways(count):
    far = sorted(range(1, count), key=lambda step: (step.bit_length() < count.bit_length() - 1, step))
    return [0] + far


def field_rows(place, freq_devs, per_dev):
    rows = []
    for step in ways(freq_devs):
        first = (place ^ step) * per_dev
        for part in range(2):
            rows.extend((part, first + local) for local in range(per_dev))
    return rows


def fields(samples, freq_total):
    phase = (np.arange(1, freq_total + 1)[:, None] * np.arange(samples)[None, :]) % samples
    angle = phase * (2.0 * math.pi / samples)
    return np.stack([np.cos(angle), -np.sin(angle)])


def inverse_tables(samples, freq_devs, per_dev):
    exact = fields(samples, freq_devs * per_dev) * (2.0 / samples)
    own = samples // freq_devs
    out = []
    for place in range(freq_devs):
        part = [exact[c, j, place * own : (place + 1) * own] for c, j in field_rows(place, freq_devs, per_dev)]
        out.append(np.repeat(np.stack(part), ROWS, 0).T)
    return np.stack(out).astype(np.float32).astype(BF16)


def window_tables(samples, freq_devs, per_dev):
    freq_total = freq_devs * per_dev
    order = np.arange(1, freq_total + 1)
    unit = 2j * math.pi / samples
    diff = order[None, :] - order[:, None]
    total = order[None, :] + order[:, None]
    same = np.where(diff == 0, 0.0, 1.0 / (samples * (np.exp(unit * np.where(diff == 0, 1, diff)) - 1.0)))
    mixed = 1.0 / (samples * (np.exp(-unit * total) - 1.0))
    full = np.zeros((2, freq_total, 2, freq_total))
    full[0, :, 0, :] = same.real + mixed.real
    full[0, :, 1, :] = mixed.imag - same.imag
    full[1, :, 0, :] = same.imag + mixed.imag
    full[1, :, 1, :] = same.real - mixed.real
    out = []
    for place in range(freq_devs):
        rows = [c * freq_total + j for c, j in field_rows(place, freq_devs, per_dev)]
        flat = full.reshape(2 * freq_total, 2 * freq_total)[np.ix_(rows, rows)]
        out.append(np.kron(flat, np.eye(ROWS)))
    return np.stack(out).astype(np.float32).astype(BF16)


def call(body, scalars, inputs, outputs, grid, scratch=(), aliases=None, flops=0):
    in_arrays = [value for value, _ in inputs]
    bytes_all = sum(v.size * v.dtype.itemsize for v in in_arrays)
    bytes_all += sum(math.prod(s.shape) * s.dtype.itemsize for s, _ in outputs)
    return pl.pallas_call(
        body,
        grid_spec=pltpu.PrefetchScalarGridSpec(
            num_scalar_prefetch=len(scalars),
            grid=grid,
            in_specs=[spec for _, spec in inputs],
            out_specs=[spec for _, spec in outputs],
            scratch_shapes=list(scratch),
        ),
        out_shape=[shape for shape, _ in outputs],
        input_output_aliases=aliases or {},
        compiler_params=pltpu.CompilerParams(vmem_limit_bytes=VMEM_BYTES),
        cost_estimate=pl.CostEstimate(flops=flops, bytes_accessed=bytes_all, transcendentals=0),
    )(*scalars, *in_arrays)


def whole(array):
    zeros = (0,) * array.ndim
    return pl.BlockSpec(array.shape, lambda *_: zeros)


def sine_terms():
    square = (np.cos(np.linspace(0.0, math.pi, 200)) + 1.0) / 32.0
    y = np.sqrt(np.maximum(square, 1e-12))
    return [float(v) for v in np.polynomial.polynomial.polyfit(square, np.sin(2.0 * math.pi * y) / y, 6)]


def turned(turn):
    terms = sine_terms()

    def sine(y):
        square = y * y
        total = jnp.full_like(y, terms[-1])
        for term in terms[-2::-1]:
            total = total * square + term
        return total * y

    turn = turn - jnp.floor(turn + 0.5)
    size = jnp.abs(turn)
    folded = jnp.where(size > 0.25, jnp.where(turn > 0.0, 0.5, -0.5) - turn, turn)
    return sine(0.25 - size), sine(folded)


def first_spectra(initial, places, freq_devs, per_dev):
    rows, own, rcv = initial.shape
    samples = own * freq_devs
    tile = 2 * ROWS
    count = freq_devs * 2 * per_dev * ROWS

    def body(freq, rblk, sblk, x_ref, *rest):
        outs, spread_ref = rest[:freq_devs], rest[freq_devs]
        time = lax.broadcasted_iota(jnp.int32, (ROWS, own), 1) + freq[0] * own
        time = time.astype(F32) * (1.0 / samples)
        table = []
        for way in ways(freq_devs):
            waves = [turned(time * ((freq[0] ^ way) * per_dev + j + 1).astype(F32)) for j in range(per_dev)]
            table += [cosine for cosine, _ in waves] + [-sine for _, sine in waves]
        table = jnp.concatenate(table, 0)
        lane = lax.broadcasted_iota(jnp.int32, (count, own), 0) % ROWS
        for row in range(ROWS):
            spread_ref[:, row * own : (row + 1) * own] = jnp.where(lane == row, table, 0.0).astype(BF16)
        for at in range(rows // tile):
            parts = []
            for half in range(2):
                start = at * tile + half * ROWS
                flat = x_ref[start : start + ROWS].reshape(ROWS * own, rcv)
                value = jnp.dot(spread_ref[...], flat, preferred_element_type=F32)
                parts.append(value.reshape(freq_devs, 2, per_dev, ROWS, rcv))
            both = jnp.concatenate(parts, 3).astype(BF16)
            for step, out in enumerate(outs):
                out[:, :, at * tile : (at + 1) * tile, :] = both[step]

    shape = jax.ShapeDtypeStruct((2, per_dev, rows, rcv), BF16)
    return call(
        body,
        places,
        [(initial, whole(initial))],
        [(shape, whole(shape))] * freq_devs,
        (1,),
        scratch=[pltpu.VMEM((count, ROWS * own), BF16)],
        flops=2 * 2 * freq_devs * per_dev * own * rows * rcv,
    )


def masked_halves(response, aperture, places, after):
    per_dev, _, src, rcv = response.shape
    half = src // 2
    width = half // PARTS

    def body(_, rblk, __, flags, x_ref, ___, *outs):
        lane = lax.broadcasted_iota(jnp.int32, (1, rcv), 1) // BLOCK
        for flip in (1, 0):
            for j in range(per_dev):
                for step in range(half // BLOCK):
                    block = (rblk[0] ^ flip) * (half // BLOCK) + step
                    on = flags[j, pl.ds(block, 1), :].astype(F32)
                    row = sum(jnp.where(lane == r, on[:, r : r + 1], 0.0) for r in range(rcv // BLOCK))
                    gate = jnp.broadcast_to(row, (BLOCK, rcv)).astype(BF16)
                    rows = pl.ds(pl.multiple_of(block * BLOCK, BLOCK), BLOCK)
                    part, at = divmod(step * BLOCK, width)
                    out = outs[flip * PARTS + part]
                    for c in range(2):
                        out[j, at : at + BLOCK, c * rcv : (c + 1) * rcv] = x_ref[j, c, rows, :] * gate

    shape = jax.ShapeDtypeStruct((per_dev, width, 2 * rcv), BF16)
    inputs = [(v, whole(v)) for v in (aperture, response)] + [(after, pl.BlockSpec(memory_space=pl.ANY))]
    outs = call(body, places, inputs, [(shape, whole(shape))] * (2 * PARTS), (1,))
    return list(outs[:PARTS]), list(outs[PARTS:])


def summed(parts):
    def body(*refs):
        total = sum(ref[...].astype(F32) for ref in refs[:-2])
        refs[-2][...] = total
        refs[-1][...] = total.astype(BF16)

    shapes = [jax.ShapeDtypeStruct(parts[0].shape, kind) for kind in (F32, BF16)]
    return call(body, (), [(v, whole(v)) for v in parts], [(v, whole(v)) for v in shapes], (1,))


def added(keep, received):
    def body(k_ref, r_ref, out):
        out[...] = (k_ref[...] + r_ref[...].astype(F32)).astype(BF16)

    shape = jax.ShapeDtypeStruct(keep.shape, BF16)
    (out,) = call(body, (), [(v, whole(v)) for v in (keep, received)], [(shape, whole(shape))], (1,))
    return out


def src_onsets(onset, places, half_rows, share, width):
    group = half_rows // CHUNKS

    def body(freq, rblk, sblk, o_ref, own, other):
        lanes = pl.ds(pl.multiple_of(rblk[0] * width, BLOCK), width)
        for core, out in ((sblk[0], own), (1 - sblk[0], other)):
            for chunk in range(CHUNKS):
                spot = pl.multiple_of(core * half_rows + chunk * group + freq[0] * share, ROWS)
                out[chunk * share : (chunk + 1) * share] = o_ref[pl.ds(spot, share), lanes]

    shape = jax.ShapeDtypeStruct((CHUNKS * share, width), onset.dtype)
    return call(body, places, [(onset, whole(onset))], [(shape, whole(shape))] * 2, (1,))


def phase_tables(onsets, places, freq_devs, per_dev, samples, parts=1, rows=None):
    count = rows or onsets[0].shape[0]
    width = onsets[0].shape[1] // parts

    def body(freq, _, sblk, *refs):
        cosines, sines, fraction = refs[-3:]
        for part in range(parts):
            for spot, ref in enumerate(refs[: len(onsets)]):
                here = slice(part * width, (part + 1) * width)
                if rows:
                    value = ref[pl.ds(pl.multiple_of(sblk[0] * rows, ROWS), rows), here]
                else:
                    value = ref[:, here]
                value = value.astype(F32) * (1.0 / samples)
                at = (part * len(onsets) + spot) * width
                to = slice(at, at + width)
                fraction[:, to] = value
                for step, way in enumerate(ways(freq_devs)):
                    for j in range(per_dev):
                        order = ((freq[0] ^ way) * per_dev + j + 1).astype(F32)
                        cosines[step, j, :, to], sines[step, j, :, to] = turned(value * order)

    table = jax.ShapeDtypeStruct((freq_devs, per_dev, count, width * parts * len(onsets)), F32)
    shapes = [table, table, jax.ShapeDtypeStruct(table.shape[2:], F32)]
    return call(body, places, [(v, whole(v)) for v in onsets], [(v, whole(v)) for v in shapes], (1,))


def down_products(near, far, parts, freq_place, freq_devs, groups):
    _, per_dev, rows, rcv = near.shape
    flat = [v for part in parts for pair in part for v in pair]
    width = flat[0].shape[1]
    total_width = width * len(flat) // 2
    group = rows // groups
    share = group // freq_devs

    def body(place_ref, n_ref, f_ref, *rest):
        resp, outs, held = rest[: len(flat)], rest[len(flat) : -1], rest[-1]
        for j in range(per_dev):
            sides = []
            for ref in (n_ref, f_ref):
                real, imag = ref[0, j], ref[1, j]
                sides.append(jnp.concatenate([jnp.concatenate([real, -imag], 1), jnp.concatenate([imag, real], 1)], 0))
            for at in range(len(flat) // 2):
                total = sum(
                    lax.dot_general(lhs, ref[j], (((1,), (1,)), ((), ())), preferred_element_type=F32)
                    for lhs, ref in zip(sides, resp[2 * at : 2 * at + 2])
                )
                to = slice(at * width, (at + 1) * width)
                held[0, j, :, to] = total[:rows]
                held[1, j, :, to] = total[rows:]
        for way, out in zip(ways(freq_devs), outs):
            pieces = []
            for index in range(groups):
                start = pl.multiple_of(index * group + (place_ref[0] ^ way) * share, ROWS)
                pieces.append(held[:, :, pl.ds(start, share), :])
            out[...] = jnp.concatenate(pieces, 2).reshape(out.shape).astype(BF16)

    shape = jax.ShapeDtypeStruct((2 * per_dev * groups * share, total_width), BF16)
    return call(
        body,
        (freq_place,),
        [(v, whole(v)) for v in (near, far, *flat)],
        [(shape, whole(shape))] * freq_devs,
        (1,),
        scratch=[pltpu.VMEM((2, per_dev, rows, total_width), F32)],
        flops=2 * 8 * per_dev * rows * total_width * rcv,
    )


def mixed_fields(plain, cos, sin, matrix):
    tile = plain[0].shape[-1]
    turned = [
        jnp.stack([v[0] * c - v[1] * s, v[0] * s + v[1] * c]) for v, c, s in zip(plain, cos, sin)
    ]
    flat = [jnp.stack(v).reshape(matrix.shape[1], tile).astype(BF16) for v in (turned, plain)]
    mixed = jnp.dot(matrix, jnp.concatenate(flat, 1), preferred_element_type=F32)
    shape = (-1, 2) + plain[0].shape[1:]
    return mixed[:, :tile].reshape(shape), mixed[:, tile:].reshape(shape)


def unturned(up, low, value, cos, sin, part):
    real = cos * up[0] + sin * up[1] - low[0] + part * value[0]
    imag = cos * up[1] - sin * up[0] - low[1] + part * value[1]
    return jnp.stack([real, imag])


def tiles(width, body, first=0):
    def at(step, carry):
        here = pl.multiple_of(step * BLOCK, BLOCK)
        body(pl.ds(here, BLOCK), pl.ds(pl.multiple_of(here + first, BLOCK), BLOCK))
        return carry

    lax.fori_loop(0, width // BLOCK, at, 0, unroll=2)


def windowed(messages, tables, matrix, freq_place, per_dev, share, first_row, first_lane):
    cosines, sines, fraction = tables
    freq_devs = len(messages)
    width = messages[0].shape[-1]
    count = freq_devs * 2 * per_dev * ROWS

    def body(place_ref, c_ref, s_ref, f_ref, g_ref, *rest):
        refs, outs = rest[:freq_devs], rest[freq_devs:]
        matrix_here = g_ref[place_ref[0]]

        def one(at, there):
            data = [ref[:, at].astype(F32).reshape(2, per_dev, share, BLOCK) for ref in refs]
            made = [[] for _ in outs]
            for first in range(0, share, ROWS):
                cut = slice(first_row + first, first_row + first + ROWS)
                plain = [value[:, :, first : first + ROWS] for value in data]
                cos = [c_ref[step, :, cut, there] for step in range(freq_devs)]
                sin = [s_ref[step, :, cut, there] for step in range(freq_devs)]
                up, low = mixed_fields(plain, cos, sin, matrix_here)
                part = f_ref[cut, there]
                for step in range(freq_devs):
                    made[step].append(unturned(up[step], low[step], plain[step], cos[step], sin[step], part))
            for out, value in zip(outs, made):
                out[:, at] = jnp.concatenate(value, 2).reshape(out.shape[0], BLOCK).astype(BF16)

        tiles(width, one, first_lane)

    inputs = (cosines, sines, fraction, matrix, *messages)
    return call(
        body,
        (freq_place,),
        [(v, whole(v)) for v in inputs],
        [(jax.ShapeDtypeStruct(v.shape, BF16), whole(v)) for v in messages],
        (1,),
        flops=2 * count * count * 2 * width * share // ROWS,
    )


def up_products(by_part, parts, freq_place, rows, groups):
    freq_devs = len(by_part[0])
    flat = [v for part in parts for pair in part for v in pair]
    per_dev, src, rcv = flat[0].shape[0], flat[0].shape[1], flat[0].shape[2] // 2
    messages = [v for part in by_part for v in part]
    group = rows // groups
    share = group // freq_devs
    total_width = src * len(flat) // 2

    def body(place_ref, *rest):
        resp, refs = rest[: len(flat)], rest[len(flat) : len(flat) + len(messages)]
        outs, held = rest[len(flat) + len(messages) : -1], rest[-1]
        lane = 0
        for part in range(len(by_part)):
            to = slice(lane, lane + refs[part * freq_devs].shape[1])
            lane = to.stop
            for step, way in enumerate(ways(freq_devs)):
                value = refs[part * freq_devs + step][...].astype(F32)
                value = value.reshape(2, per_dev, groups, share, value.shape[1])
                for index in range(groups):
                    start = pl.multiple_of(index * group + (place_ref[0] ^ way) * share, ROWS)
                    held[:, :, pl.ds(start, share), to] = value[:, :, index]
        for j in range(per_dev):
            both = [jnp.concatenate([held[0, j], held[1, j]], 0).astype(BF16)]
            for side in (1, 0):
                total = sum(
                    jnp.dot(both[0][:, at * src : (at + 1) * src], resp[2 * at + side][j], preferred_element_type=F32)
                    for at in range(len(flat) // 2)
                )
                real = total[:rows, :rcv] + total[rows:, rcv:]
                imag = total[rows:, :rcv] - total[:rows, rcv:]
                for index in range(groups):
                    out = outs[2 * index + side]
                    cut = slice(index * group, (index + 1) * group)
                    out[0, j] = real[cut].astype(out.dtype)
                    out[1, j] = imag[cut].astype(out.dtype)

    shapes = [jax.ShapeDtypeStruct((2, per_dev, group, rcv), kind) for kind in (F32, BF16)] * groups
    outs = call(
        body,
        (freq_place,),
        [(v, whole(v)) for v in (*flat, *messages)],
        [(v, whole(v)) for v in shapes],
        (1,),
        scratch=[pltpu.VMEM((2, per_dev, rows, total_width), F32)],
        flops=2 * 8 * per_dev * rows * total_width * rcv,
    )
    return [tuple(outs[2 * index : 2 * index + 2]) for index in range(groups)]


def next_spectra(sums, messages, tables, matrix, freq_place, first_row):
    cosines, sines, fraction = tables
    freq_devs = len(messages)
    _, per_dev, rows, rcv = messages[0].shape
    count = freq_devs * 2 * per_dev * ROWS
    own = 2 * per_dev * ROWS

    def body(place_ref, u_ref, c_ref, s_ref, f_ref, g_ref, *rest):
        refs, out = rest[:freq_devs], rest[freq_devs]
        matrix_here = g_ref[place_ref[0], :own]

        def one(at, _):
            for base in range(0, rows, 2 * ROWS):
                pair = slice(base, base + 2 * ROWS)
                data = [ref[:, :, pair, at].astype(F32) for ref in refs]
                made = []
                for half in range(2):
                    plain = [value[:, :, half * ROWS : (half + 1) * ROWS] for value in data]
                    cut = slice(first_row + base + half * ROWS, first_row + base + (half + 1) * ROWS)
                    cos = [c_ref[step, :, cut, at] for step in range(freq_devs)]
                    sin = [s_ref[step, :, cut, at] for step in range(freq_devs)]
                    up, low = mixed_fields(plain, cos, sin, matrix_here)
                    change = unturned(up[0], low[0], plain[0], cos[0], sin[0], f_ref[cut, at])
                    made.append(u_ref[:, :, cut, at] - change)
                out[:, :, pair, at] = jnp.concatenate(made, 2).astype(BF16)

        tiles(rcv, one)

    inputs = (sums, cosines, sines, fraction, matrix, *messages)
    shape = jax.ShapeDtypeStruct(messages[0].shape, BF16)
    (out,) = call(
        body,
        (freq_place,),
        [(v, whole(v)) for v in inputs],
        [(shape, whole(shape))],
        (1,),
        flops=2 * own * count * 2 * rcv * rows // ROWS,
    )
    return out


def updated(initial, onset, messages, table, places, first, rows, target):
    freq_devs = len(messages)
    half_rows, own, rcv = initial.shape
    per_dev = messages[0].shape[1]
    tile = 2 * ROWS
    count = table.shape[2]

    def body(place_ref, _, sblk, x_ref, o_ref, t_ref, *rest):
        refs = rest[:freq_devs]
        out, spread_ref = rest[-2:]
        step = pl.program_id(0)

        @pl.when(step == 0)
        def _():
            base = t_ref[place_ref[0]].astype(F32)
            lane = lax.broadcasted_iota(jnp.int32, (own, count), 1) % ROWS
            for row in range(ROWS):
                spread_ref[row * own : (row + 1) * own] = jnp.where(lane == row, base, 0.0).astype(BF16)

        here = pl.ds(pl.multiple_of(step * tile, tile), tile)
        data = [ref[:, :, here, :].astype(F32) for ref in refs]
        onsets = o_ref[pl.ds(pl.multiple_of(sblk[0] * half_rows + first + step * tile, tile), tile), :]
        time = lax.broadcasted_iota(jnp.int32, (own, rcv), 0) + place_ref[0] * own
        for half in range(2):
            cut = slice(half * ROWS, (half + 1) * ROWS)
            flat = jnp.stack([v[:, :, cut] for v in data]).reshape(count, rcv).astype(BF16)
            change = jnp.dot(spread_ref[...], flat, preferred_element_type=F32)
            for row in range(ROWS):
                spot = half * ROWS + row
                on = time < onsets[spot : spot + 1, :]
                moved = jnp.where(on, change[row * own : (row + 1) * own], 0.0)
                out[spot] = (x_ref[first + step * tile + spot].astype(F32) - moved).astype(BF16)

    inputs = [(v, whole(v)) for v in (initial, onset, table, *messages)]
    aliases = {}
    if target is not None:
        inputs.append((target, pl.BlockSpec(memory_space=pl.ANY)))
        aliases = {len(places) + len(inputs) - 1: 0}
    (out,) = call(
        body,
        places,
        inputs,
        [(jax.ShapeDtypeStruct(initial.shape, BF16), pl.BlockSpec((tile, own, rcv), lambda i, *_: (first // tile + i, 0, 0)))],
        (rows // tile,),
        scratch=[pltpu.VMEM((ROWS * own, count), BF16)],
        aliases=aliases,
        flops=2 * 2 * freq_devs * per_dev * own * rows * rcv,
    )
    return out


def exchanged(value, axis, step):
    return lax.ppermute(value, axis, [(i, i ^ step) for i in range(lax.axis_size(axis))])


def dealt_out(parts):
    return [exchanged(part, "freq", step) if step else part for part, step in zip(parts, ways(len(parts)))]


def spread(value, count):
    return dealt_out([value] * count)


def on_device(initial, response, aperture, onset_rcv, onset_src):
    freq_devs = lax.axis_size("freq")
    per_dev = response.shape[0]
    samples = initial.shape[1] * freq_devs
    half_rows = initial.shape[0]
    src_width = response.shape[2] // 2
    rows = half_rows // CHUNKS
    share = rows // freq_devs
    places = tuple(lax.axis_index(axis).reshape(1) for axis in ("freq", "rblk", "sblk"))
    freq_place = places[0]
    inverse = jnp.asarray(inverse_tables(samples, freq_devs, per_dev))
    matrix = jnp.asarray(window_tables(samples, freq_devs, per_dev))

    partial = first_spectra(initial, places, freq_devs, per_dev)
    kept, sent = masked_halves(response, aperture, places, partial[0])
    moved = exchanged(sent[0], "rblk", 1)
    moved, partial = lax.optimization_barrier((moved, dealt_out(partial)))
    sums, spectra = summed(partial)
    far = exchanged(spectra, "rblk", 1)

    own, other = src_onsets(onset_src, places, half_rows, share, src_width)
    src_tables = phase_tables((own, exchanged(other, "sblk", 1)), places, freq_devs, per_dev, samples, PARTS)
    rcv_tables = phase_tables((onset_rcv,), places, freq_devs, per_dev, samples, rows=half_rows)

    parts, by_part = [], []
    for index in range(PARTS):
        if index:
            sent[index], far = lax.optimization_barrier((sent[index], far))
            moved = exchanged(sent[index], "rblk", 1)
            received = dealt_out(messages)
            moved, received[1:-1] = lax.optimization_barrier((moved, received[1:-1]))
            by_part.append(received)
        pair = tuple(exchanged(v, "sblk", 1) for v in (kept[index], moved))
        parts.append(((kept[index], moved), pair))
        messages = dealt_out(down_products(spectra, far, parts[index:], freq_place, freq_devs, CHUNKS))
        lane = index * messages[0].shape[-1]
        messages = windowed(messages, src_tables, matrix, freq_place, per_dev, share * CHUNKS, 0, lane)
    by_part.append(dealt_out(messages))
    sums_of = up_products(by_part, parts, freq_place, half_rows, CHUNKS)

    result = None
    for chunk, (keep, send) in enumerate(sums_of):
        first = chunk * rows
        for _ in range(1, ITERS):
            messages = spread(added(keep, exchanged(send, "rblk", 1)), freq_devs)
            near = next_spectra(sums, messages, rcv_tables, matrix, freq_place, first)
            messages = down_products(near, exchanged(near, "rblk", 1), parts, freq_place, freq_devs, 1)
            messages = windowed(
                dealt_out(messages), src_tables, matrix, freq_place, per_dev, share, chunk * share, 0
            )
            ((keep, send),) = up_products([dealt_out(messages)], parts, freq_place, rows, 1)
        messages = spread(added(keep, exchanged(send, "rblk", 1)), freq_devs)
        result = updated(initial, onset_rcv, messages, inverse, places, first, rows, result)
    return result


def transform_tables(length, count):
    table = fields(length, count).reshape(2 * count, length)
    forward_table = jnp.asarray(table.astype(np.float32).astype(BF16))
    inverse_table = jnp.asarray((table.T * (2.0 / length)).astype(np.float32).astype(BF16))
    return forward_table, inverse_table


def settle(values):
    return lax.optimization_barrier(values.astype(BF16)).astype(F32)


def samples_into_spectra(values, forward_table, freq_total):
    out = jnp.einsum("kt,ptn->pkn", forward_table, values, preferred_element_type=F32)
    return out.reshape(values.shape[0], 2, freq_total, values.shape[2]).astype(BF16)


def spectra_into_samples(trace_spectra, inverse_table):
    flat = trace_spectra.reshape(trace_spectra.shape[0], -1, trace_spectra.shape[3])
    return jnp.einsum("tk,pkn->ptn", inverse_table, flat, preferred_element_type=F32)


def dense(spec, gated, real, imag, sign):
    dot = functools.partial(jnp.einsum, spec, preferred_element_type=F32)
    return jnp.stack(
        [dot(gated[:, 0], real) - sign * dot(gated[:, 1], imag), dot(gated[:, 0], imag) + sign * dot(gated[:, 1], real)], 1
    )


def general_device(initial, response, aperture, onset_rcv, onset_src):
    freq_devs, rblk_devs, sblk_devs = (lax.axis_size(a) for a in ("freq", "rblk", "sblk"))
    freq_index, rblk_index, sblk_index = (lax.axis_index(a) for a in ("freq", "rblk", "sblk"))
    freq_total = response.shape[0] * freq_devs
    samples = initial.shape[1] * freq_devs
    focal_all = onset_rcv.shape[0]
    forward_table, inverse_table = transform_tables(samples, freq_total)
    steps_axis = lax.iota(jnp.int32, samples)
    own_axis = freq_index * initial.shape[1] + lax.iota(jnp.int32, initial.shape[1])
    half_rows = focal_all // sblk_devs
    own_onsets = lax.dynamic_slice_in_dim(onset_rcv, sblk_index * half_rows, half_rows, 0)
    rcv_gate = (own_axis[None, :, None] < own_onsets[:, None, :]).astype(F32)
    src_rows = focal_all // (rblk_devs * freq_devs)
    src_first = rblk_index * (focal_all // rblk_devs) + freq_index * src_rows
    src_onsets = lax.dynamic_slice_in_dim(onset_src, src_first, src_rows, 0)
    src_gate = (steps_axis[None, :, None] < src_onsets[:, None, :]).astype(F32)
    mask_full = jnp.repeat(jnp.repeat(aperture, BLOCK, 1), BLOCK, 2).astype(BF16)
    gated = response * mask_full[:, None]
    own_forward = lax.dynamic_slice_in_dim(forward_table, freq_index * initial.shape[1], initial.shape[1], 1)
    own_inverse = lax.dynamic_slice_in_dim(inverse_table, freq_index * initial.shape[1], initial.shape[1], 0)
    current = initial
    for _ in range(ITERS):
        partial = samples_into_spectra(current, own_forward, freq_total)
        spec_back = lax.psum_scatter(partial.astype(F32), "freq", scatter_dimension=2, tiled=True).astype(BF16)
        spec_all = lax.all_gather(spec_back, "sblk", axis=0, tiled=True)
        down = lax.psum_scatter(
            settle(dense("euk,bek->beu", gated, spec_all[:, 0], spec_all[:, 1], 1.0)).astype(BF16),
            "rblk",
            scatter_dimension=0,
            tiled=True,
        )
        src_traces = lax.all_to_all(down, "freq", split_axis=0, concat_axis=2, tiled=True)
        upgoing = (src_gate * spectra_into_samples(src_traces, inverse_table)).astype(BF16)
        upspec = samples_into_spectra(upgoing, forward_table, freq_total)
        up_back = lax.all_to_all(upspec, "freq", split_axis=2, concat_axis=0, tiled=True)
        up_all = lax.all_gather(up_back, "rblk", axis=0, tiled=True)
        sums = dense("qao,bqa->bqo", gated, up_all[:, 0], up_all[:, 1], -1.0).astype(BF16)
        back = lax.psum_scatter(sums, "sblk", scatter_dimension=0, tiled=True)
        traces = lax.all_gather(back, "freq", axis=2, tiled=True)
        update = rcv_gate * spectra_into_samples(traces, own_inverse)
        current = (initial.astype(F32) - update).astype(BF16)
    return current


def fits(initial, response, aperture, onset_rcv, onset_src):
    freq_devs = lax.axis_size("freq")
    if lax.axis_size("rblk") != 2 or lax.axis_size("sblk") != 2 or freq_devs & (freq_devs - 1):
        return False
    whole_rows = initial.shape[0] % (max(2, CHUNKS) * ROWS * freq_devs) == 0
    whole_width = response.shape[2] % (2 * PARTS * BLOCK) == 0 and response.shape[3] % BLOCK == 0
    return whole_rows and whole_width and onset_rcv.shape[0] == 2 * initial.shape[0]


def chosen(*arrays):
    return on_device(*arrays) if fits(*arrays) else general_device(*arrays)


def solution(mesh):
    in_specs = (
        P(("group", "sblk"), "freq", "rblk"),
        P(("group", "freq"), None, "sblk", "rblk"),
        P(("group", "freq"), "sblk", "rblk"),
        P("group", "rblk"),
        P("group", "sblk"),
    )
    out_specs = P(("group", "sblk"), "freq", "rblk")
    return jax.shard_map(chosen, mesh=mesh, in_specs=in_specs, out_specs=out_specs, check_vma=False)
```

```python
import functools
import math

import jax
import jax.numpy as jnp
import numpy as np
from jax import lax
from jax.experimental import pallas as pl
from jax.experimental.pallas import tpu as pltpu
from jax.sharding import PartitionSpec as P

BLOCK = 128
ITERS = 2
ROWS = 8
CHUNKS = 2
PARTS = 2
VMEM_BYTES = 6 * 1024 * 1024

BF16 = jnp.bfloat16
F32 = jnp.float32


def ways(count):
    far = sorted(range(1, count), key=lambda step: (step.bit_length() < count.bit_length() - 1, step))
    return [0] + far


def field_rows(place, freq_devs, per_dev):
    rows = []
    for step in ways(freq_devs):
        first = (place ^ step) * per_dev
        for part in range(2):
            rows.extend((part, first + local) for local in range(per_dev))
    return rows


def fields(samples, freq_total):
    phase = (np.arange(1, freq_total + 1)[:, None] * np.arange(samples)[None, :]) % samples
    angle = phase * (2.0 * math.pi / samples)
    return np.stack([np.cos(angle), -np.sin(angle)])


def inverse_tables(samples, freq_devs, per_dev):
    exact = fields(samples, freq_devs * per_dev) * (2.0 / samples)
    own = samples // freq_devs
    out = []
    for place in range(freq_devs):
        part = [exact[c, j, place * own : (place + 1) * own] for c, j in field_rows(place, freq_devs, per_dev)]
        out.append(np.repeat(np.stack(part), ROWS, 0).T)
    return np.stack(out).astype(np.float32).astype(BF16)


def window_tables(samples, freq_devs, per_dev):
    freq_total = freq_devs * per_dev
    order = np.arange(1, freq_total + 1)
    unit = 2j * math.pi / samples
    diff = order[None, :] - order[:, None]
    total = order[None, :] + order[:, None]
    same = np.where(diff == 0, 0.0, 1.0 / (samples * (np.exp(unit * np.where(diff == 0, 1, diff)) - 1.0)))
    mixed = 1.0 / (samples * (np.exp(-unit * total) - 1.0))
    full = np.zeros((2, freq_total, 2, freq_total))
    full[0, :, 0, :] = same.real + mixed.real
    full[0, :, 1, :] = mixed.imag - same.imag
    full[1, :, 0, :] = same.imag + mixed.imag
    full[1, :, 1, :] = same.real - mixed.real
    out = []
    for place in range(freq_devs):
        rows = [c * freq_total + j for c, j in field_rows(place, freq_devs, per_dev)]
        flat = full.reshape(2 * freq_total, 2 * freq_total)[np.ix_(rows, rows)]
        out.append(np.kron(flat, np.eye(ROWS)))
    return np.stack(out).astype(np.float32).astype(BF16)


def call(body, scalars, inputs, outputs, grid, scratch=(), aliases=None, flops=0):
    in_arrays = [value for value, _ in inputs]
    bytes_all = sum(v.size * v.dtype.itemsize for v in in_arrays)
    bytes_all += sum(math.prod(s.shape) * s.dtype.itemsize for s, _ in outputs)
    return pl.pallas_call(
        body,
        grid_spec=pltpu.PrefetchScalarGridSpec(
            num_scalar_prefetch=len(scalars),
            grid=grid,
            in_specs=[spec for _, spec in inputs],
            out_specs=[spec for _, spec in outputs],
            scratch_shapes=list(scratch),
        ),
        out_shape=[shape for shape, _ in outputs],
        input_output_aliases=aliases or {},
        compiler_params=pltpu.CompilerParams(vmem_limit_bytes=VMEM_BYTES),
        cost_estimate=pl.CostEstimate(flops=flops, bytes_accessed=bytes_all, transcendentals=0),
    )(*scalars, *in_arrays)


def whole(array):
    zeros = (0,) * array.ndim
    return pl.BlockSpec(array.shape, lambda *_: zeros)


def sine_terms():
    square = (np.cos(np.linspace(0.0, math.pi, 200)) + 1.0) / 32.0
    y = np.sqrt(np.maximum(square, 1e-12))
    return [float(v) for v in np.polynomial.polynomial.polyfit(square, np.sin(2.0 * math.pi * y) / y, 6)]


def turned(turn):
    terms = sine_terms()

    def sine(y):
        square = y * y
        total = jnp.full_like(y, terms[-1])
        for term in terms[-2::-1]:
            total = total * square + term
        return total * y

    turn = turn - jnp.floor(turn + 0.5)
    size = jnp.abs(turn)
    folded = jnp.where(size > 0.25, jnp.where(turn > 0.0, 0.5, -0.5) - turn, turn)
    return sine(0.25 - size), sine(folded)


def first_spectra(initial, places, freq_devs, per_dev):
    rows, own, rcv = initial.shape
    samples = own * freq_devs
    tile = 2 * ROWS
    count = freq_devs * 2 * per_dev * ROWS

    def body(freq, rblk, sblk, x_ref, *rest):
        outs, spread_ref = rest[:freq_devs], rest[freq_devs]
        time = lax.broadcasted_iota(jnp.int32, (ROWS, own), 1) + freq[0] * own
        time = time.astype(F32) * (1.0 / samples)
        table = []
        for way in ways(freq_devs):
            waves = [turned(time * ((freq[0] ^ way) * per_dev + j + 1).astype(F32)) for j in range(per_dev)]
            table += [cosine for cosine, _ in waves] + [-sine for _, sine in waves]
        table = jnp.concatenate(table, 0)
        lane = lax.broadcasted_iota(jnp.int32, (count, own), 0) % ROWS
        for row in range(ROWS):
            spread_ref[:, row * own : (row + 1) * own] = jnp.where(lane == row, table, 0.0).astype(BF16)
        for at in range(rows // tile):
            parts = []
            for half in range(2):
                start = at * tile + half * ROWS
                flat = x_ref[start : start + ROWS].reshape(ROWS * own, rcv)
                value = jnp.dot(spread_ref[...], flat, preferred_element_type=F32)
                parts.append(value.reshape(freq_devs, 2, per_dev, ROWS, rcv))
            both = jnp.concatenate(parts, 3).astype(BF16)
            for step, out in enumerate(outs):
                out[:, :, at * tile : (at + 1) * tile, :] = both[step]

    shape = jax.ShapeDtypeStruct((2, per_dev, rows, rcv), BF16)
    return call(
        body,
        places,
        [(initial, whole(initial))],
        [(shape, whole(shape))] * freq_devs,
        (1,),
        scratch=[pltpu.VMEM((count, ROWS * own), BF16)],
        flops=2 * 2 * freq_devs * per_dev * own * rows * rcv,
    )


def masked_halves(response, aperture, places):
    per_dev, _, src, rcv = response.shape
    half = src // 2
    width = half // PARTS

    def body(_, rblk, __, flags, x_ref, *outs):
        lane = lax.broadcasted_iota(jnp.int32, (1, rcv), 1) // BLOCK
        for flip in (1, 0):
            for j in range(per_dev):
                for step in range(half // BLOCK):
                    block = (rblk[0] ^ flip) * (half // BLOCK) + step
                    on = flags[j, pl.ds(block, 1), :].astype(F32)
                    row = sum(jnp.where(lane == r, on[:, r : r + 1], 0.0) for r in range(rcv // BLOCK))
                    gate = jnp.broadcast_to(row, (BLOCK, rcv)).astype(BF16)
                    rows = pl.ds(pl.multiple_of(block * BLOCK, BLOCK), BLOCK)
                    part, at = divmod(step * BLOCK, width)
                    out = outs[flip * PARTS + part]
                    for c in range(2):
                        out[j, at : at + BLOCK, c * rcv : (c + 1) * rcv] = x_ref[j, c, rows, :] * gate

    shape = jax.ShapeDtypeStruct((per_dev, width, 2 * rcv), BF16)
    inputs = [(v, whole(v)) for v in (aperture, response)]
    outs = call(body, places, inputs, [(shape, whole(shape))] * (2 * PARTS), (1,))
    return list(outs[:PARTS]), list(outs[PARTS:])


def summed(parts):
    def body(*refs):
        total = sum(ref[...].astype(F32) for ref in refs[:-2])
        refs[-2][...] = total
        refs[-1][...] = total.astype(BF16)

    shapes = [jax.ShapeDtypeStruct(parts[0].shape, kind) for kind in (F32, BF16)]
    return call(body, (), [(v, whole(v)) for v in parts], [(v, whole(v)) for v in shapes], (1,))


def added(keep, received):
    def body(k_ref, r_ref, out):
        out[...] = (k_ref[...] + r_ref[...].astype(F32)).astype(BF16)

    shape = jax.ShapeDtypeStruct(keep.shape, BF16)
    (out,) = call(body, (), [(v, whole(v)) for v in (keep, received)], [(shape, whole(shape))], (1,))
    return out


def src_onsets(onset, places, half_rows, share, width):

    def body(freq, rblk, sblk, o_ref, own, other):
        lanes = pl.ds(pl.multiple_of(rblk[0] * width, BLOCK), width)
        for core, out in ((sblk[0], own), (1 - sblk[0], other)):
            spot = pl.multiple_of(core * half_rows + freq[0] * share, ROWS)
            out[...] = o_ref[pl.ds(spot, share), lanes]

    shape = jax.ShapeDtypeStruct((share, width), onset.dtype)
    return call(body, places, [(onset, whole(onset))], [(shape, whole(shape))] * 2, (1,))


def phase_tables(onsets, places, freq_devs, per_dev, samples, parts=1, rows=None):
    count = rows or onsets[0].shape[0]
    width = onsets[0].shape[1] // parts

    def body(freq, _, sblk, *refs):
        cosines, sines, fraction = refs[-3:]
        for part in range(parts):
            for spot, ref in enumerate(refs[: len(onsets)]):
                here = slice(part * width, (part + 1) * width)
                if rows:
                    value = ref[pl.ds(pl.multiple_of(sblk[0] * rows, ROWS), rows), here]
                else:
                    value = ref[:, here]
                value = value.astype(F32) * (1.0 / samples)
                at = (part * len(onsets) + spot) * width
                to = slice(at, at + width)
                fraction[:, to] = value
                for step, way in enumerate(ways(freq_devs)):
                    for j in range(per_dev):
                        order = ((freq[0] ^ way) * per_dev + j + 1).astype(F32)
                        cosines[step, j, :, to], sines[step, j, :, to] = turned(value * order)

    table = jax.ShapeDtypeStruct((freq_devs, per_dev, count, width * parts * len(onsets)), F32)
    shapes = [table, table, jax.ShapeDtypeStruct(table.shape[2:], F32)]
    return call(body, places, [(v, whole(v)) for v in onsets], [(v, whole(v)) for v in shapes], (1,))


def down_products(near, far, parts, freq_place, freq_devs):
    _, per_dev, _, rcv = near[0].shape
    rows = sum(v.shape[2] for v in near)
    flat = [v for part in parts for pair in part for v in pair]
    width = flat[0].shape[1]
    total_width = width * len(flat) // 2
    share = rows // freq_devs

    def body(place_ref, *rest):
        spectra, rest = rest[: 2 * len(near)], rest[2 * len(near) :]
        resp, outs, held = rest[: len(flat)], rest[len(flat) : -1], rest[-1]
        for j in range(per_dev):
            sides = []
            for refs in (spectra[: len(near)], spectra[len(near) :]):
                real = jnp.concatenate([ref[0, j] for ref in refs], 0)
                imag = jnp.concatenate([ref[1, j] for ref in refs], 0)
                sides.append(jnp.concatenate([jnp.concatenate([real, -imag], 1), jnp.concatenate([imag, real], 1)], 0))
            for at in range(len(flat) // 2):
                total = sum(
                    lax.dot_general(lhs, ref[j], (((1,), (1,)), ((), ())), preferred_element_type=F32)
                    for lhs, ref in zip(sides, resp[2 * at : 2 * at + 2])
                )
                to = slice(at * width, (at + 1) * width)
                held[0, j, :, to] = total[:rows]
                held[1, j, :, to] = total[rows:]
        for way, out in zip(ways(freq_devs), outs):
            start = pl.multiple_of((place_ref[0] ^ way) * share, share)
            out[...] = held[:, :, pl.ds(start, share), :].reshape(out.shape).astype(BF16)

    shape = jax.ShapeDtypeStruct((2 * per_dev * share, total_width), BF16)
    return call(
        body,
        (freq_place,),
        [(v, whole(v)) for v in (*near, *far, *flat)],
        [(shape, whole(shape))] * freq_devs,
        (1,),
        scratch=[pltpu.VMEM((2, per_dev, rows, total_width), F32)],
        flops=2 * 8 * per_dev * rows * total_width * rcv,
    )


def mixed_fields(plain, cos, sin, matrix):
    tile = plain[0].shape[-1]
    turned = [
        jnp.stack([v[0] * c - v[1] * s, v[0] * s + v[1] * c]) for v, c, s in zip(plain, cos, sin)
    ]
    flat = [jnp.stack(v).reshape(matrix.shape[1], tile).astype(BF16) for v in (turned, plain)]
    mixed = jnp.dot(matrix, jnp.concatenate(flat, 1), preferred_element_type=F32)
    shape = (-1, 2) + plain[0].shape[1:]
    return mixed[:, :tile].reshape(shape), mixed[:, tile:].reshape(shape)


def unturned(up, low, value, cos, sin, part):
    real = cos * up[0] + sin * up[1] - low[0] + part * value[0]
    imag = cos * up[1] - sin * up[0] - low[1] + part * value[1]
    return jnp.stack([real, imag])


def tiles(width, body):
    def at(step, carry):
        body(pl.ds(pl.multiple_of(step * BLOCK, BLOCK), BLOCK))
        return carry

    lax.fori_loop(0, width // BLOCK, at, 0, unroll=2)


def windowed(messages, tables, matrix, freq_place, per_dev, share):
    cosines, sines, fraction = tables
    freq_devs = len(messages)
    width = messages[0].shape[-1]
    count = freq_devs * 2 * per_dev * ROWS

    def body(place_ref, c_ref, s_ref, f_ref, g_ref, *rest):
        refs, outs = rest[:freq_devs], rest[freq_devs:]
        matrix_here = g_ref[place_ref[0]]

        def one(at):
            data = [ref[:, at].astype(F32).reshape(2, per_dev, share, BLOCK) for ref in refs]
            made = [[] for _ in outs]
            for first in range(0, share, ROWS):
                cut = slice(first, first + ROWS)
                plain = [value[:, :, cut] for value in data]
                cos = [c_ref[step, :, cut, at] for step in range(freq_devs)]
                sin = [s_ref[step, :, cut, at] for step in range(freq_devs)]
                up, low = mixed_fields(plain, cos, sin, matrix_here)
                part = f_ref[cut, at]
                for step in range(freq_devs):
                    made[step].append(unturned(up[step], low[step], plain[step], cos[step], sin[step], part))
            for out, value in zip(outs, made):
                out[:, at] = jnp.concatenate(value, 2).reshape(out.shape[0], BLOCK).astype(BF16)

        tiles(width, one)

    inputs = (cosines, sines, fraction, matrix, *messages)
    return call(
        body,
        (freq_place,),
        [(v, whole(v)) for v in inputs],
        [(jax.ShapeDtypeStruct(v.shape, BF16), whole(v)) for v in messages],
        (1,),
        flops=2 * count * count * 2 * width * share // ROWS,
    )


def up_products(messages, parts, freq_place, rows, side):
    freq_devs = len(messages)
    flat = [pair[side] for part in parts for pair in part]
    per_dev, src, rcv = flat[0].shape[0], flat[0].shape[1], flat[0].shape[2] // 2
    group = rows // CHUNKS
    share = rows // freq_devs
    total_width = src * len(flat)
    kind = BF16 if side else F32

    def body(place_ref, *rest):
        resp, refs = rest[: len(flat)], rest[len(flat) : len(flat) + freq_devs]
        outs, held = rest[len(flat) + freq_devs : -1], rest[-1]
        for way, ref in zip(ways(freq_devs), refs):
            start = pl.multiple_of((place_ref[0] ^ way) * share, share)
            value = ref[...].reshape(2, per_dev, share, total_width)
            for part in range(2):
                for j in range(per_dev):
                    held[part, j, pl.ds(start, share), :] = value[part, j]
        for j in range(per_dev):
            both = jnp.concatenate([held[0, j], held[1, j]], 0)
            total = sum(
                jnp.dot(both[:, at * src : (at + 1) * src], ref[j], preferred_element_type=F32)
                for at, ref in enumerate(resp)
            )
            real = total[:rows, :rcv] + total[rows:, rcv:]
            imag = total[rows:, :rcv] - total[:rows, rcv:]
            for index, out in enumerate(outs):
                cut = slice(index * group, (index + 1) * group)
                out[0, j] = real[cut].astype(kind)
                out[1, j] = imag[cut].astype(kind)

    shape = jax.ShapeDtypeStruct((2, per_dev, group, rcv), kind)
    return call(
        body,
        (freq_place,),
        [(v, whole(v)) for v in (*flat, *messages)],
        [(shape, whole(shape))] * CHUNKS,
        (1,),
        scratch=[pltpu.VMEM((2, per_dev, rows, total_width), BF16)],
        flops=2 * 4 * per_dev * rows * total_width * rcv,
    )


def next_spectra(sums, messages, tables, matrix, freq_place, first_row):
    cosines, sines, fraction = tables
    freq_devs = len(messages)
    _, per_dev, rows, rcv = messages[0].shape
    count = freq_devs * 2 * per_dev * ROWS
    own = 2 * per_dev * ROWS

    def body(place_ref, u_ref, c_ref, s_ref, f_ref, g_ref, *rest):
        refs, out = rest[:freq_devs], rest[freq_devs]
        matrix_here = g_ref[place_ref[0], :own]

        def one(at):
            for base in range(0, rows, 2 * ROWS):
                pair = slice(base, base + 2 * ROWS)
                data = [ref[:, :, pair, at].astype(F32) for ref in refs]
                made = []
                for half in range(2):
                    plain = [value[:, :, half * ROWS : (half + 1) * ROWS] for value in data]
                    cut = slice(first_row + base + half * ROWS, first_row + base + (half + 1) * ROWS)
                    cos = [c_ref[step, :, cut, at] for step in range(freq_devs)]
                    sin = [s_ref[step, :, cut, at] for step in range(freq_devs)]
                    up, low = mixed_fields(plain, cos, sin, matrix_here)
                    change = unturned(up[0], low[0], plain[0], cos[0], sin[0], f_ref[cut, at])
                    made.append(u_ref[:, :, cut, at] - change)
                out[:, :, pair, at] = jnp.concatenate(made, 2).astype(BF16)

        tiles(rcv, one)

    inputs = (sums, cosines, sines, fraction, matrix, *messages)
    shape = jax.ShapeDtypeStruct(messages[0].shape, BF16)
    (out,) = call(
        body,
        (freq_place,),
        [(v, whole(v)) for v in inputs],
        [(shape, whole(shape))],
        (1,),
        flops=2 * own * count * 2 * rcv * rows // ROWS,
    )
    return out


def updated(initial, onset, messages, table, places, first, rows, target):
    freq_devs = len(messages)
    half_rows, own, rcv = initial.shape
    per_dev = messages[0].shape[1]
    tile = 2 * ROWS
    count = table.shape[2]

    def body(place_ref, _, sblk, x_ref, o_ref, t_ref, *rest):
        refs = rest[:freq_devs]
        out, spread_ref = rest[-2:]
        step = pl.program_id(0)

        @pl.when(step == 0)
        def _():
            base = t_ref[place_ref[0]].astype(F32)
            lane = lax.broadcasted_iota(jnp.int32, (own, count), 1) % ROWS
            for row in range(ROWS):
                spread_ref[row * own : (row + 1) * own] = jnp.where(lane == row, base, 0.0).astype(BF16)

        here = pl.ds(pl.multiple_of(step * tile, tile), tile)
        data = [ref[:, :, here, :].astype(F32) for ref in refs]
        onsets = o_ref[pl.ds(pl.multiple_of(sblk[0] * half_rows + first + step * tile, tile), tile), :]
        time = lax.broadcasted_iota(jnp.int32, (own, rcv), 0) + place_ref[0] * own
        for half in range(2):
            cut = slice(half * ROWS, (half + 1) * ROWS)
            flat = jnp.stack([v[:, :, cut] for v in data]).reshape(count, rcv).astype(BF16)
            change = jnp.dot(spread_ref[...], flat, preferred_element_type=F32)
            for row in range(ROWS):
                spot = half * ROWS + row
                on = time < onsets[spot : spot + 1, :]
                moved = jnp.where(on, change[row * own : (row + 1) * own], 0.0)
                out[spot] = (x_ref[first + step * tile + spot].astype(F32) - moved).astype(BF16)

    inputs = [(v, whole(v)) for v in (initial, onset, table, *messages)]
    aliases = {}
    if target is not None:
        inputs.append((target, pl.BlockSpec(memory_space=pl.ANY)))
        aliases = {len(places) + len(inputs) - 1: 0}
    (out,) = call(
        body,
        places,
        inputs,
        [(jax.ShapeDtypeStruct(initial.shape, BF16), pl.BlockSpec((tile, own, rcv), lambda i, *_: (first // tile + i, 0, 0)))],
        (rows // tile,),
        scratch=[pltpu.VMEM((ROWS * own, count), BF16)],
        aliases=aliases,
        flops=2 * 2 * freq_devs * per_dev * own * rows * rcv,
    )
    return out


def exchanged(value, axis, step):
    return lax.ppermute(value, axis, [(i, i ^ step) for i in range(lax.axis_size(axis))])


def dealt_out(parts):
    return [exchanged(part, "freq", step) if step else part for part, step in zip(parts, ways(len(parts)))]


def spread(value, count):
    return dealt_out([value] * count)


def on_device(initial, response, aperture, onset_rcv, onset_src):
    freq_devs = lax.axis_size("freq")
    per_dev = response.shape[0]
    samples = initial.shape[1] * freq_devs
    half_rows = initial.shape[0]
    src_width = response.shape[2] // 2
    rows = half_rows // CHUNKS
    share = half_rows // freq_devs
    places = tuple(lax.axis_index(axis).reshape(1) for axis in ("freq", "rblk", "sblk"))
    freq_place = places[0]
    inverse = jnp.asarray(inverse_tables(samples, freq_devs, per_dev))
    matrix = jnp.asarray(window_tables(samples, freq_devs, per_dev))

    kept, sent = masked_halves(response, aperture, places)
    moved = [exchanged(v, "rblk", 1) for v in sent]
    kept_pair = [exchanged(v, "sblk", 1) for v in kept]
    sums, spectra = summed(dealt_out(first_spectra(initial, places, freq_devs, per_dev)))
    far = exchanged(spectra, "rblk", 1)
    moved_pair = []
    for index in range(PARTS):
        if index:
            moved[index], far = lax.optimization_barrier((moved[index], far))
        else:
            moved[index], spectra = lax.optimization_barrier((moved[index], spectra))
        moved_pair.append(exchanged(moved[index], "sblk", 1))
    parts = [((kept[i], moved[i]), (kept_pair[i], moved_pair[i])) for i in range(PARTS)]

    own, other = src_onsets(onset_src, places, half_rows, share, src_width)
    src_tables = phase_tables((own, exchanged(other, "sblk", 1)), places, freq_devs, per_dev, samples, PARTS)
    rcv_tables = phase_tables((onset_rcv,), places, freq_devs, per_dev, samples, rows=half_rows)

    near, far, result = [spectra], [far], None
    for step in range(ITERS):
        messages = dealt_out(down_products(near, far, parts, freq_place, freq_devs))
        messages = dealt_out(windowed(messages, src_tables, matrix, freq_place, per_dev, share))
        received = [exchanged(v, "rblk", 1) for v in up_products(messages, parts, freq_place, half_rows, 1)]
        keep = up_products(messages, parts, freq_place, half_rows, 0)
        near, far = [], []
        for chunk in range(CHUNKS):
            back = spread(added(keep[chunk], received[chunk]), freq_devs)
            if step < ITERS - 1:
                near.append(next_spectra(sums, back, rcv_tables, matrix, freq_place, chunk * rows))
                far.append(exchanged(near[chunk], "rblk", 1))
            else:
                result = updated(initial, onset_rcv, back, inverse, places, chunk * rows, rows, result)
    return result


def transform_tables(length, count):
    table = fields(length, count).reshape(2 * count, length)
    forward_table = jnp.asarray(table.astype(np.float32).astype(BF16))
    inverse_table = jnp.asarray((table.T * (2.0 / length)).astype(np.float32).astype(BF16))
    return forward_table, inverse_table


def settle(values):
    return lax.optimization_barrier(values.astype(BF16)).astype(F32)


def samples_into_spectra(values, forward_table, freq_total):
    out = jnp.einsum("kt,ptn->pkn", forward_table, values, preferred_element_type=F32)
    return out.reshape(values.shape[0], 2, freq_total, values.shape[2]).astype(BF16)


def spectra_into_samples(trace_spectra, inverse_table):
    flat = trace_spectra.reshape(trace_spectra.shape[0], -1, trace_spectra.shape[3])
    return jnp.einsum("tk,pkn->ptn", inverse_table, flat, preferred_element_type=F32)


def dense(spec, gated, real, imag, sign):
    dot = functools.partial(jnp.einsum, spec, preferred_element_type=F32)
    return jnp.stack(
        [dot(gated[:, 0], real) - sign * dot(gated[:, 1], imag), dot(gated[:, 0], imag) + sign * dot(gated[:, 1], real)], 1
    )


def general_device(initial, response, aperture, onset_rcv, onset_src):
    freq_devs, rblk_devs, sblk_devs = (lax.axis_size(a) for a in ("freq", "rblk", "sblk"))
    freq_index, rblk_index, sblk_index = (lax.axis_index(a) for a in ("freq", "rblk", "sblk"))
    freq_total = response.shape[0] * freq_devs
    samples = initial.shape[1] * freq_devs
    focal_all = onset_rcv.shape[0]
    forward_table, inverse_table = transform_tables(samples, freq_total)
    steps_axis = lax.iota(jnp.int32, samples)
    own_axis = freq_index * initial.shape[1] + lax.iota(jnp.int32, initial.shape[1])
    half_rows = focal_all // sblk_devs
    own_onsets = lax.dynamic_slice_in_dim(onset_rcv, sblk_index * half_rows, half_rows, 0)
    rcv_gate = (own_axis[None, :, None] < own_onsets[:, None, :]).astype(F32)
    src_rows = focal_all // (rblk_devs * freq_devs)
    src_first = rblk_index * (focal_all // rblk_devs) + freq_index * src_rows
    src_onsets = lax.dynamic_slice_in_dim(onset_src, src_first, src_rows, 0)
    src_gate = (steps_axis[None, :, None] < src_onsets[:, None, :]).astype(F32)
    mask_full = jnp.repeat(jnp.repeat(aperture, BLOCK, 1), BLOCK, 2).astype(BF16)
    gated = response * mask_full[:, None]
    own_forward = lax.dynamic_slice_in_dim(forward_table, freq_index * initial.shape[1], initial.shape[1], 1)
    own_inverse = lax.dynamic_slice_in_dim(inverse_table, freq_index * initial.shape[1], initial.shape[1], 0)
    current = initial
    for _ in range(ITERS):
        partial = samples_into_spectra(current, own_forward, freq_total)
        spec_back = lax.psum_scatter(partial.astype(F32), "freq", scatter_dimension=2, tiled=True).astype(BF16)
        spec_all = lax.all_gather(spec_back, "sblk", axis=0, tiled=True)
        down = lax.psum_scatter(
            settle(dense("euk,bek->beu", gated, spec_all[:, 0], spec_all[:, 1], 1.0)).astype(BF16),
            "rblk",
            scatter_dimension=0,
            tiled=True,
        )
        src_traces = lax.all_to_all(down, "freq", split_axis=0, concat_axis=2, tiled=True)
        upgoing = (src_gate * spectra_into_samples(src_traces, inverse_table)).astype(BF16)
        upspec = samples_into_spectra(upgoing, forward_table, freq_total)
        up_back = lax.all_to_all(upspec, "freq", split_axis=2, concat_axis=0, tiled=True)
        up_all = lax.all_gather(up_back, "rblk", axis=0, tiled=True)
        sums = dense("qao,bqa->bqo", gated, up_all[:, 0], up_all[:, 1], -1.0).astype(BF16)
        back = lax.psum_scatter(sums, "sblk", scatter_dimension=0, tiled=True)
        traces = lax.all_gather(back, "freq", axis=2, tiled=True)
        update = rcv_gate * spectra_into_samples(traces, own_inverse)
        current = (initial.astype(F32) - update).astype(BF16)
    return current


def fits(initial, response, aperture, onset_rcv, onset_src):
    freq_devs = lax.axis_size("freq")
    if lax.axis_size("rblk") != 2 or lax.axis_size("sblk") != 2 or freq_devs & (freq_devs - 1):
        return False
    whole_rows = initial.shape[0] % (max(2, CHUNKS) * ROWS * freq_devs) == 0
    whole_width = response.shape[2] % (2 * PARTS * BLOCK) == 0 and response.shape[3] % BLOCK == 0
    return whole_rows and whole_width and onset_rcv.shape[0] == 2 * initial.shape[0]


def chosen(*arrays):
    return on_device(*arrays) if fits(*arrays) else general_device(*arrays)


def solution(mesh):
    in_specs = (
        P(("group", "sblk"), "freq", "rblk"),
        P(("group", "freq"), None, "sblk", "rblk"),
        P(("group", "freq"), "sblk", "rblk"),
        P("group", "rblk"),
        P("group", "sblk"),
    )
    out_specs = P(("group", "sblk"), "freq", "rblk")
    return jax.shard_map(chosen, mesh=mesh, in_specs=in_specs, out_specs=out_specs, check_vma=False)
```

```python
import functools
import math

import jax
import jax.numpy as jnp
import numpy as np
from jax import lax
from jax.experimental import pallas as pl
from jax.experimental.pallas import tpu as pltpu
from jax.sharding import PartitionSpec as P

BLOCK = 128
ITERS = 2
ROWS = 8
CHUNKS = 2
PARTS = 2
VMEM_BYTES = 6 * 1024 * 1024

BF16 = jnp.bfloat16
F32 = jnp.float32


def ways(count):
    far = sorted(range(1, count), key=lambda step: (step.bit_length() < count.bit_length() - 1, step))
    return [0] + far


def field_rows(place, freq_devs, per_dev):
    rows = []
    for step in ways(freq_devs):
        first = (place ^ step) * per_dev
        for part in range(2):
            rows.extend((part, first + local) for local in range(per_dev))
    return rows


def fields(samples, freq_total):
    phase = (np.arange(1, freq_total + 1)[:, None] * np.arange(samples)[None, :]) % samples
    angle = phase * (2.0 * math.pi / samples)
    return np.stack([np.cos(angle), -np.sin(angle)])


def inverse_tables(samples, freq_devs, per_dev):
    exact = fields(samples, freq_devs * per_dev) * (2.0 / samples)
    own = samples // freq_devs
    out = []
    for place in range(freq_devs):
        part = [exact[c, j, place * own : (place + 1) * own] for c, j in field_rows(place, freq_devs, per_dev)]
        out.append(np.repeat(np.stack(part), ROWS, 0).T)
    return np.stack(out).astype(np.float32).astype(BF16)


def window_tables(samples, freq_devs, per_dev):
    freq_total = freq_devs * per_dev
    order = np.arange(1, freq_total + 1)
    unit = 2j * math.pi / samples
    diff = order[None, :] - order[:, None]
    total = order[None, :] + order[:, None]
    same = np.where(diff == 0, 0.0, 1.0 / (samples * (np.exp(unit * np.where(diff == 0, 1, diff)) - 1.0)))
    mixed = 1.0 / (samples * (np.exp(-unit * total) - 1.0))
    full = np.zeros((2, freq_total, 2, freq_total))
    full[0, :, 0, :] = same.real + mixed.real
    full[0, :, 1, :] = mixed.imag - same.imag
    full[1, :, 0, :] = same.imag + mixed.imag
    full[1, :, 1, :] = same.real - mixed.real
    out = []
    for place in range(freq_devs):
        rows = [c * freq_total + j for c, j in field_rows(place, freq_devs, per_dev)]
        flat = full.reshape(2 * freq_total, 2 * freq_total)[np.ix_(rows, rows)]
        out.append(np.kron(flat, np.eye(ROWS)))
    return np.stack(out).astype(np.float32).astype(BF16)


def call(body, scalars, inputs, outputs, grid, scratch=(), aliases=None, flops=0):
    in_arrays = [value for value, _ in inputs]
    bytes_all = sum(v.size * v.dtype.itemsize for v in in_arrays)
    bytes_all += sum(math.prod(s.shape) * s.dtype.itemsize for s, _ in outputs)
    return pl.pallas_call(
        body,
        grid_spec=pltpu.PrefetchScalarGridSpec(
            num_scalar_prefetch=len(scalars),
            grid=grid,
            in_specs=[spec for _, spec in inputs],
            out_specs=[spec for _, spec in outputs],
            scratch_shapes=list(scratch),
        ),
        out_shape=[shape for shape, _ in outputs],
        input_output_aliases=aliases or {},
        compiler_params=pltpu.CompilerParams(vmem_limit_bytes=VMEM_BYTES),
        cost_estimate=pl.CostEstimate(flops=flops, bytes_accessed=bytes_all, transcendentals=0),
    )(*scalars, *in_arrays)


def whole(array):
    zeros = (0,) * array.ndim
    return pl.BlockSpec(array.shape, lambda *_: zeros)


def sine_terms():
    square = (np.cos(np.linspace(0.0, math.pi, 200)) + 1.0) / 32.0
    y = np.sqrt(np.maximum(square, 1e-12))
    return [float(v) for v in np.polynomial.polynomial.polyfit(square, np.sin(2.0 * math.pi * y) / y, 6)]


def turned(turn):
    terms = sine_terms()

    def sine(y):
        square = y * y
        total = jnp.full_like(y, terms[-1])
        for term in terms[-2::-1]:
            total = total * square + term
        return total * y

    turn = turn - jnp.floor(turn + 0.5)
    size = jnp.abs(turn)
    folded = jnp.where(size > 0.25, jnp.where(turn > 0.0, 0.5, -0.5) - turn, turn)
    return sine(0.25 - size), sine(folded)


def first_spectra(initial, places, freq_devs, per_dev):
    rows, own, rcv = initial.shape
    samples = own * freq_devs
    tile = 2 * ROWS
    count = freq_devs * 2 * per_dev * ROWS

    def body(freq, rblk, sblk, x_ref, *rest):
        outs, spread_ref = rest[:freq_devs], rest[freq_devs]
        time = lax.broadcasted_iota(jnp.int32, (ROWS, own), 1) + freq[0] * own
        time = time.astype(F32) * (1.0 / samples)
        table = []
        for way in ways(freq_devs):
            waves = [turned(time * ((freq[0] ^ way) * per_dev + j + 1).astype(F32)) for j in range(per_dev)]
            table += [cosine for cosine, _ in waves] + [-sine for _, sine in waves]
        table = jnp.concatenate(table, 0)
        lane = lax.broadcasted_iota(jnp.int32, (count, own), 0) % ROWS
        for row in range(ROWS):
            spread_ref[:, row * own : (row + 1) * own] = jnp.where(lane == row, table, 0.0).astype(BF16)
        for at in range(rows // tile):
            parts = []
            for half in range(2):
                start = at * tile + half * ROWS
                flat = x_ref[start : start + ROWS].reshape(ROWS * own, rcv)
                value = jnp.dot(spread_ref[...], flat, preferred_element_type=F32)
                parts.append(value.reshape(freq_devs, 2, per_dev, ROWS, rcv))
            both = jnp.concatenate(parts, 3).astype(BF16)
            for step, out in enumerate(outs):
                out[:, :, at * tile : (at + 1) * tile, :] = both[step]

    shape = jax.ShapeDtypeStruct((2, per_dev, rows, rcv), BF16)
    return call(
        body,
        places,
        [(initial, whole(initial))],
        [(shape, whole(shape))] * freq_devs,
        (1,),
        scratch=[pltpu.VMEM((count, ROWS * own), BF16)],
        flops=2 * 2 * freq_devs * per_dev * own * rows * rcv,
    )


def masked_halves(response, aperture, places):
    per_dev, _, src, rcv = response.shape
    half = src // 2
    width = half // PARTS

    def body(_, rblk, __, flags, x_ref, *outs):
        lane = lax.broadcasted_iota(jnp.int32, (1, rcv), 1) // BLOCK
        for flip in (1, 0):
            for j in range(per_dev):
                for step in range(half // BLOCK):
                    block = (rblk[0] ^ flip) * (half // BLOCK) + step
                    on = flags[j, pl.ds(block, 1), :].astype(F32)
                    row = sum(jnp.where(lane == r, on[:, r : r + 1], 0.0) for r in range(rcv // BLOCK))
                    gate = jnp.broadcast_to(row, (BLOCK, rcv)).astype(BF16)
                    rows = pl.ds(pl.multiple_of(block * BLOCK, BLOCK), BLOCK)
                    part, at = divmod(step * BLOCK, width)
                    out = outs[flip * PARTS + part]
                    for c in range(2):
                        out[j, at : at + BLOCK, c * rcv : (c + 1) * rcv] = x_ref[j, c, rows, :] * gate

    shape = jax.ShapeDtypeStruct((per_dev, width, 2 * rcv), BF16)
    inputs = [(v, whole(v)) for v in (aperture, response)]
    outs = call(body, places, inputs, [(shape, whole(shape))] * (2 * PARTS), (1,))
    return list(outs[:PARTS]), list(outs[PARTS:])


def summed(parts):
    def body(*refs):
        total = sum(ref[...].astype(F32) for ref in refs[:-2])
        refs[-2][...] = total
        refs[-1][...] = total.astype(BF16)

    shapes = [jax.ShapeDtypeStruct(parts[0].shape, kind) for kind in (F32, BF16)]
    return call(body, (), [(v, whole(v)) for v in parts], [(v, whole(v)) for v in shapes], (1,))


def added(keep, received):
    def body(k_ref, r_ref, out):
        out[...] = (k_ref[...] + r_ref[...].astype(F32)).astype(BF16)

    shape = jax.ShapeDtypeStruct(keep.shape, BF16)
    (out,) = call(body, (), [(v, whole(v)) for v in (keep, received)], [(shape, whole(shape))], (1,))
    return out


def src_onsets(onset, places, half_rows, share, width):

    def body(freq, rblk, sblk, o_ref, own, other):
        lanes = pl.ds(pl.multiple_of(rblk[0] * width, BLOCK), width)
        for core, out in ((sblk[0], own), (1 - sblk[0], other)):
            spot = pl.multiple_of(core * half_rows + freq[0] * share, ROWS)
            out[...] = o_ref[pl.ds(spot, share), lanes]

    shape = jax.ShapeDtypeStruct((share, width), onset.dtype)
    return call(body, places, [(onset, whole(onset))], [(shape, whole(shape))] * 2, (1,))


def phase_tables(onsets, places, freq_devs, per_dev, samples, parts=1, rows=None):
    count = rows or onsets[0].shape[0]
    width = onsets[0].shape[1] // parts

    def body(freq, _, sblk, *refs):
        cosines, sines, fraction = refs[-3:]
        for part in range(parts):
            for spot, ref in enumerate(refs[: len(onsets)]):
                here = slice(part * width, (part + 1) * width)
                if rows:
                    value = ref[pl.ds(pl.multiple_of(sblk[0] * rows, ROWS), rows), here]
                else:
                    value = ref[:, here]
                value = value.astype(F32) * (1.0 / samples)
                at = (part * len(onsets) + spot) * width
                to = slice(at, at + width)
                fraction[:, to] = value
                for step, way in enumerate(ways(freq_devs)):
                    for j in range(per_dev):
                        order = ((freq[0] ^ way) * per_dev + j + 1).astype(F32)
                        cosines[step, j, :, to], sines[step, j, :, to] = turned(value * order)

    table = jax.ShapeDtypeStruct((freq_devs, per_dev, count, width * parts * len(onsets)), F32)
    shapes = [table, table, jax.ShapeDtypeStruct(table.shape[2:], F32)]
    return call(body, places, [(v, whole(v)) for v in onsets], [(v, whole(v)) for v in shapes], (1,))


def down_products(near, far, parts, freq_place, freq_devs):
    _, per_dev, _, rcv = near[0].shape
    rows = sum(v.shape[2] for v in near)
    flat = [v for part in parts for pair in part for v in pair]
    width = flat[0].shape[1]
    total_width = width * len(flat) // 2
    share = rows // freq_devs

    def body(place_ref, *rest):
        spectra, rest = rest[: 2 * len(near)], rest[2 * len(near) :]
        resp, outs, held = rest[: len(flat)], rest[len(flat) : -1], rest[-1]
        for j in range(per_dev):
            sides = []
            for refs in (spectra[: len(near)], spectra[len(near) :]):
                real = jnp.concatenate([ref[0, j] for ref in refs], 0)
                imag = jnp.concatenate([ref[1, j] for ref in refs], 0)
                sides.append(jnp.concatenate([jnp.concatenate([real, -imag], 1), jnp.concatenate([imag, real], 1)], 0))
            for at in range(len(flat) // 2):
                total = sum(
                    lax.dot_general(lhs, ref[j], (((1,), (1,)), ((), ())), preferred_element_type=F32)
                    for lhs, ref in zip(sides, resp[2 * at : 2 * at + 2])
                )
                to = slice(at * width, (at + 1) * width)
                held[0, j, :, to] = total[:rows]
                held[1, j, :, to] = total[rows:]
        for way, out in zip(ways(freq_devs), outs):
            start = pl.multiple_of((place_ref[0] ^ way) * share, share)
            out[...] = held[:, :, pl.ds(start, share), :].reshape(out.shape).astype(BF16)

    shape = jax.ShapeDtypeStruct((2 * per_dev * share, total_width), BF16)
    return call(
        body,
        (freq_place,),
        [(v, whole(v)) for v in (*near, *far, *flat)],
        [(shape, whole(shape))] * freq_devs,
        (1,),
        scratch=[pltpu.VMEM((2, per_dev, rows, total_width), F32)],
        flops=2 * 8 * per_dev * rows * total_width * rcv,
    )


def mixed_fields(plain, cos, sin, matrix):
    tile = plain[0].shape[-1]
    turned = [
        jnp.stack([v[0] * c - v[1] * s, v[0] * s + v[1] * c]) for v, c, s in zip(plain, cos, sin)
    ]
    flat = [jnp.stack(v).reshape(matrix.shape[1], tile).astype(BF16) for v in (turned, plain)]
    mixed = jnp.dot(matrix, jnp.concatenate(flat, 1), preferred_element_type=F32)
    shape = (-1, 2) + plain[0].shape[1:]
    return mixed[:, :tile].reshape(shape), mixed[:, tile:].reshape(shape)


def unturned(up, low, value, cos, sin, part):
    real = cos * up[0] + sin * up[1] - low[0] + part * value[0]
    imag = cos * up[1] - sin * up[0] - low[1] + part * value[1]
    return jnp.stack([real, imag])


def tiles(width, body):
    def at(step, carry):
        body(pl.ds(pl.multiple_of(step * BLOCK, BLOCK), BLOCK))
        return carry

    lax.fori_loop(0, width // BLOCK, at, 0, unroll=2)


def windowed(messages, tables, matrix, freq_place, per_dev, share):
    cosines, sines, fraction = tables
    freq_devs = len(messages)
    width = messages[0].shape[-1]
    count = freq_devs * 2 * per_dev * ROWS

    def body(place_ref, c_ref, s_ref, f_ref, g_ref, *rest):
        refs, outs = rest[:freq_devs], rest[freq_devs:]
        matrix_here = g_ref[place_ref[0]]

        def one(at):
            data = [ref[:, at].astype(F32).reshape(2, per_dev, share, BLOCK) for ref in refs]
            made = [[] for _ in outs]
            for first in range(0, share, ROWS):
                cut = slice(first, first + ROWS)
                plain = [value[:, :, cut] for value in data]
                cos = [c_ref[step, :, cut, at] for step in range(freq_devs)]
                sin = [s_ref[step, :, cut, at] for step in range(freq_devs)]
                up, low = mixed_fields(plain, cos, sin, matrix_here)
                part = f_ref[cut, at]
                for step in range(freq_devs):
                    made[step].append(unturned(up[step], low[step], plain[step], cos[step], sin[step], part))
            for out, value in zip(outs, made):
                out[:, at] = jnp.concatenate(value, 2).reshape(out.shape[0], BLOCK).astype(BF16)

        tiles(width, one)

    inputs = (cosines, sines, fraction, matrix, *messages)
    return call(
        body,
        (freq_place,),
        [(v, whole(v)) for v in inputs],
        [(jax.ShapeDtypeStruct(v.shape, BF16), whole(v)) for v in messages],
        (1,),
        flops=2 * count * count * 2 * width * share // ROWS,
    )


def up_products(messages, parts, freq_place, rows, side):
    freq_devs = len(messages)
    flat = [pair[side] for part in parts for pair in part]
    per_dev, src, rcv = flat[0].shape[0], flat[0].shape[1], flat[0].shape[2] // 2
    group = rows // CHUNKS
    share = rows // freq_devs
    total_width = src * len(flat)
    kind = BF16 if side else F32

    def body(place_ref, *rest):
        resp, refs = rest[: len(flat)], rest[len(flat) : len(flat) + freq_devs]
        outs, held = rest[len(flat) + freq_devs : -1], rest[-1]
        for way, ref in zip(ways(freq_devs), refs):
            start = pl.multiple_of((place_ref[0] ^ way) * share, share)
            value = ref[...].reshape(2, per_dev, share, total_width)
            for part in range(2):
                for j in range(per_dev):
                    held[part, j, pl.ds(start, share), :] = value[part, j]
        for j in range(per_dev):
            both = jnp.concatenate([held[0, j], held[1, j]], 0)
            total = sum(
                jnp.dot(both[:, at * src : (at + 1) * src], ref[j], preferred_element_type=F32)
                for at, ref in enumerate(resp)
            )
            real = total[:rows, :rcv] + total[rows:, rcv:]
            imag = total[rows:, :rcv] - total[:rows, rcv:]
            for index, out in enumerate(outs):
                cut = slice(index * group, (index + 1) * group)
                out[0, j] = real[cut].astype(kind)
                out[1, j] = imag[cut].astype(kind)

    shape = jax.ShapeDtypeStruct((2, per_dev, group, rcv), kind)
    return call(
        body,
        (freq_place,),
        [(v, whole(v)) for v in (*flat, *messages)],
        [(shape, whole(shape))] * CHUNKS,
        (1,),
        scratch=[pltpu.VMEM((2, per_dev, rows, total_width), BF16)],
        flops=2 * 4 * per_dev * rows * total_width * rcv,
    )


def next_spectra(sums, messages, tables, matrix, freq_place, first_row):
    cosines, sines, fraction = tables
    freq_devs = len(messages)
    _, per_dev, rows, rcv = messages[0].shape
    count = freq_devs * 2 * per_dev * ROWS
    own = 2 * per_dev * ROWS

    def body(place_ref, u_ref, c_ref, s_ref, f_ref, g_ref, *rest):
        refs, out = rest[:freq_devs], rest[freq_devs]
        matrix_here = g_ref[place_ref[0], :own]

        def one(at):
            for base in range(0, rows, 2 * ROWS):
                pair = slice(base, base + 2 * ROWS)
                data = [ref[:, :, pair, at].astype(F32) for ref in refs]
                made = []
                for half in range(2):
                    plain = [value[:, :, half * ROWS : (half + 1) * ROWS] for value in data]
                    cut = slice(first_row + base + half * ROWS, first_row + base + (half + 1) * ROWS)
                    cos = [c_ref[step, :, cut, at] for step in range(freq_devs)]
                    sin = [s_ref[step, :, cut, at] for step in range(freq_devs)]
                    up, low = mixed_fields(plain, cos, sin, matrix_here)
                    change = unturned(up[0], low[0], plain[0], cos[0], sin[0], f_ref[cut, at])
                    made.append(u_ref[:, :, cut, at] - change)
                out[:, :, pair, at] = jnp.concatenate(made, 2).astype(BF16)

        tiles(rcv, one)

    inputs = (sums, cosines, sines, fraction, matrix, *messages)
    shape = jax.ShapeDtypeStruct(messages[0].shape, BF16)
    (out,) = call(
        body,
        (freq_place,),
        [(v, whole(v)) for v in inputs],
        [(shape, whole(shape))],
        (1,),
        flops=2 * own * count * 2 * rcv * rows // ROWS,
    )
    return out


def updated(initial, onset, messages, table, places, first, rows, target):
    freq_devs = len(messages)
    half_rows, own, rcv = initial.shape
    per_dev = messages[0].shape[1]
    tile = 2 * ROWS
    count = table.shape[2]

    def body(place_ref, _, sblk, x_ref, o_ref, t_ref, *rest):
        refs = rest[:freq_devs]
        out, spread_ref = rest[-2:]
        step = pl.program_id(0)

        @pl.when(step == 0)
        def _():
            base = t_ref[place_ref[0]].astype(F32)
            lane = lax.broadcasted_iota(jnp.int32, (own, count), 1) % ROWS
            for row in range(ROWS):
                spread_ref[row * own : (row + 1) * own] = jnp.where(lane == row, base, 0.0).astype(BF16)

        here = pl.ds(pl.multiple_of(step * tile, tile), tile)
        data = [ref[:, :, here, :].astype(F32) for ref in refs]
        onsets = o_ref[pl.ds(pl.multiple_of(sblk[0] * half_rows + first + step * tile, tile), tile), :]
        time = lax.broadcasted_iota(jnp.int32, (own, rcv), 0) + place_ref[0] * own
        for half in range(2):
            cut = slice(half * ROWS, (half + 1) * ROWS)
            flat = jnp.stack([v[:, :, cut] for v in data]).reshape(count, rcv).astype(BF16)
            change = jnp.dot(spread_ref[...], flat, preferred_element_type=F32)
            for row in range(ROWS):
                spot = half * ROWS + row
                on = time < onsets[spot : spot + 1, :]
                moved = jnp.where(on, change[row * own : (row + 1) * own], 0.0)
                out[spot] = (x_ref[first + step * tile + spot].astype(F32) - moved).astype(BF16)

    inputs = [(v, whole(v)) for v in (initial, onset, table, *messages)]
    aliases = {}
    if target is not None:
        inputs.append((target, pl.BlockSpec(memory_space=pl.ANY)))
        aliases = {len(places) + len(inputs) - 1: 0}
    (out,) = call(
        body,
        places,
        inputs,
        [(jax.ShapeDtypeStruct(initial.shape, BF16), pl.BlockSpec((tile, own, rcv), lambda i, *_: (first // tile + i, 0, 0)))],
        (rows // tile,),
        scratch=[pltpu.VMEM((ROWS * own, count), BF16)],
        aliases=aliases,
        flops=2 * 2 * freq_devs * per_dev * own * rows * rcv,
    )
    return out


def exchanged(value, axis, step):
    return lax.ppermute(value, axis, [(i, i ^ step) for i in range(lax.axis_size(axis))])


def dealt_out(parts):
    return [exchanged(part, "freq", step) if step else part for part, step in zip(parts, ways(len(parts)))]


def spread(value, count):
    held = {0: value}
    bit = count // 2
    while bit:
        held.update({way | bit: exchanged(held[way], "freq", bit) for way in sorted(held)})
        bit //= 2
    return [held[way] for way in ways(count)]


def on_device(initial, response, aperture, onset_rcv, onset_src):
    freq_devs = lax.axis_size("freq")
    per_dev = response.shape[0]
    samples = initial.shape[1] * freq_devs
    half_rows = initial.shape[0]
    src_width = response.shape[2] // 2
    rows = half_rows // CHUNKS
    share = half_rows // freq_devs
    places = tuple(lax.axis_index(axis).reshape(1) for axis in ("freq", "rblk", "sblk"))
    freq_place = places[0]
    inverse = jnp.asarray(inverse_tables(samples, freq_devs, per_dev))
    matrix = jnp.asarray(window_tables(samples, freq_devs, per_dev))

    kept, sent = masked_halves(response, aperture, places)
    moved = [exchanged(v, "rblk", 1) for v in sent]
    kept_pair = [exchanged(v, "sblk", 1) for v in kept]
    sums, spectra = summed(dealt_out(first_spectra(initial, places, freq_devs, per_dev)))
    far = exchanged(spectra, "rblk", 1)
    moved_pair = []
    for index in range(PARTS):
        if index:
            moved[index], far = lax.optimization_barrier((moved[index], far))
        else:
            moved[index], spectra = lax.optimization_barrier((moved[index], spectra))
        moved_pair.append(exchanged(moved[index], "sblk", 1))
    parts = [((kept[i], moved[i]), (kept_pair[i], moved_pair[i])) for i in range(PARTS)]

    own, other = src_onsets(onset_src, places, half_rows, share, src_width)
    src_tables = phase_tables((own, exchanged(other, "sblk", 1)), places, freq_devs, per_dev, samples, PARTS)
    rcv_tables = phase_tables((onset_rcv,), places, freq_devs, per_dev, samples, rows=half_rows)

    near, far, result = [spectra], [far], None
    for step in range(ITERS):
        messages = dealt_out(down_products(near, far, parts, freq_place, freq_devs))
        messages = dealt_out(windowed(messages, src_tables, matrix, freq_place, per_dev, share))
        received = [exchanged(v, "rblk", 1) for v in up_products(messages, parts, freq_place, half_rows, 1)]
        keep = up_products(messages, parts, freq_place, half_rows, 0)
        near, far = [], []
        for chunk in range(CHUNKS):
            back = spread(added(keep[chunk], received[chunk]), freq_devs)
            if step < ITERS - 1:
                near.append(next_spectra(sums, back, rcv_tables, matrix, freq_place, chunk * rows))
                far.append(exchanged(near[chunk], "rblk", 1))
            else:
                result = updated(initial, onset_rcv, back, inverse, places, chunk * rows, rows, result)
    return result


def transform_tables(length, count):
    table = fields(length, count).reshape(2 * count, length)
    forward_table = jnp.asarray(table.astype(np.float32).astype(BF16))
    inverse_table = jnp.asarray((table.T * (2.0 / length)).astype(np.float32).astype(BF16))
    return forward_table, inverse_table


def settle(values):
    return lax.optimization_barrier(values.astype(BF16)).astype(F32)


def samples_into_spectra(values, forward_table, freq_total):
    out = jnp.einsum("kt,ptn->pkn", forward_table, values, preferred_element_type=F32)
    return out.reshape(values.shape[0], 2, freq_total, values.shape[2]).astype(BF16)


def spectra_into_samples(trace_spectra, inverse_table):
    flat = trace_spectra.reshape(trace_spectra.shape[0], -1, trace_spectra.shape[3])
    return jnp.einsum("tk,pkn->ptn", inverse_table, flat, preferred_element_type=F32)


def dense(spec, gated, real, imag, sign):
    dot = functools.partial(jnp.einsum, spec, preferred_element_type=F32)
    return jnp.stack(
        [dot(gated[:, 0], real) - sign * dot(gated[:, 1], imag), dot(gated[:, 0], imag) + sign * dot(gated[:, 1], real)], 1
    )


def general_device(initial, response, aperture, onset_rcv, onset_src):
    freq_devs, rblk_devs, sblk_devs = (lax.axis_size(a) for a in ("freq", "rblk", "sblk"))
    freq_index, rblk_index, sblk_index = (lax.axis_index(a) for a in ("freq", "rblk", "sblk"))
    freq_total = response.shape[0] * freq_devs
    samples = initial.shape[1] * freq_devs
    focal_all = onset_rcv.shape[0]
    forward_table, inverse_table = transform_tables(samples, freq_total)
    steps_axis = lax.iota(jnp.int32, samples)
    own_axis = freq_index * initial.shape[1] + lax.iota(jnp.int32, initial.shape[1])
    half_rows = focal_all // sblk_devs
    own_onsets = lax.dynamic_slice_in_dim(onset_rcv, sblk_index * half_rows, half_rows, 0)
    rcv_gate = (own_axis[None, :, None] < own_onsets[:, None, :]).astype(F32)
    src_rows = focal_all // (rblk_devs * freq_devs)
    src_first = rblk_index * (focal_all // rblk_devs) + freq_index * src_rows
    src_onsets = lax.dynamic_slice_in_dim(onset_src, src_first, src_rows, 0)
    src_gate = (steps_axis[None, :, None] < src_onsets[:, None, :]).astype(F32)
    mask_full = jnp.repeat(jnp.repeat(aperture, BLOCK, 1), BLOCK, 2).astype(BF16)
    gated = response * mask_full[:, None]
    own_forward = lax.dynamic_slice_in_dim(forward_table, freq_index * initial.shape[1], initial.shape[1], 1)
    own_inverse = lax.dynamic_slice_in_dim(inverse_table, freq_index * initial.shape[1], initial.shape[1], 0)
    current = initial
    for _ in range(ITERS):
        partial = samples_into_spectra(current, own_forward, freq_total)
        spec_back = lax.psum_scatter(partial.astype(F32), "freq", scatter_dimension=2, tiled=True).astype(BF16)
        spec_all = lax.all_gather(spec_back, "sblk", axis=0, tiled=True)
        down = lax.psum_scatter(
            settle(dense("euk,bek->beu", gated, spec_all[:, 0], spec_all[:, 1], 1.0)).astype(BF16),
            "rblk",
            scatter_dimension=0,
            tiled=True,
        )
        src_traces = lax.all_to_all(down, "freq", split_axis=0, concat_axis=2, tiled=True)
        upgoing = (src_gate * spectra_into_samples(src_traces, inverse_table)).astype(BF16)
        upspec = samples_into_spectra(upgoing, forward_table, freq_total)
        up_back = lax.all_to_all(upspec, "freq", split_axis=2, concat_axis=0, tiled=True)
        up_all = lax.all_gather(up_back, "rblk", axis=0, tiled=True)
        sums = dense("qao,bqa->bqo", gated, up_all[:, 0], up_all[:, 1], -1.0).astype(BF16)
        back = lax.psum_scatter(sums, "sblk", scatter_dimension=0, tiled=True)
        traces = lax.all_gather(back, "freq", axis=2, tiled=True)
        update = rcv_gate * spectra_into_samples(traces, own_inverse)
        current = (initial.astype(F32) - update).astype(BF16)
    return current


def fits(initial, response, aperture, onset_rcv, onset_src):
    freq_devs = lax.axis_size("freq")
    if lax.axis_size("rblk") != 2 or lax.axis_size("sblk") != 2 or freq_devs & (freq_devs - 1):
        return False
    whole_rows = initial.shape[0] % (max(2, CHUNKS) * ROWS * freq_devs) == 0
    whole_width = response.shape[2] % (2 * PARTS * BLOCK) == 0 and response.shape[3] % BLOCK == 0
    return whole_rows and whole_width and onset_rcv.shape[0] == 2 * initial.shape[0]


def chosen(*arrays):
    return on_device(*arrays) if fits(*arrays) else general_device(*arrays)


def solution(mesh):
    in_specs = (
        P(("group", "sblk"), "freq", "rblk"),
        P(("group", "freq"), None, "sblk", "rblk"),
        P(("group", "freq"), "sblk", "rblk"),
        P("group", "rblk"),
        P("group", "sblk"),
    )
    out_specs = P(("group", "sblk"), "freq", "rblk")
    return jax.shard_map(chosen, mesh=mesh, in_specs=in_specs, out_specs=out_specs, check_vma=False)
```

```python
import functools
import math

import jax
import jax.numpy as jnp
import numpy as np
from jax import lax
from jax.experimental import pallas as pl
from jax.experimental.pallas import tpu as pltpu
from jax.sharding import PartitionSpec as P

BLOCK = 128
ITERS = 2
ROWS = 8
CHUNKS = 2
PARTS = 2
VMEM_BYTES = 6 * 1024 * 1024

BF16 = jnp.bfloat16
F32 = jnp.float32


def ways(count):
    far = sorted(range(1, count), key=lambda step: (step.bit_length() < count.bit_length() - 1, step))
    return [0] + far


def field_rows(place, freq_devs, per_dev):
    rows = []
    for step in ways(freq_devs):
        first = (place ^ step) * per_dev
        for part in range(2):
            rows.extend((part, first + local) for local in range(per_dev))
    return rows


def fields(samples, freq_total):
    phase = (np.arange(1, freq_total + 1)[:, None] * np.arange(samples)[None, :]) % samples
    angle = phase * (2.0 * math.pi / samples)
    return np.stack([np.cos(angle), -np.sin(angle)])


def inverse_tables(samples, freq_devs, per_dev):
    exact = fields(samples, freq_devs * per_dev) * (2.0 / samples)
    own = samples // freq_devs
    out = []
    for place in range(freq_devs):
        part = [exact[c, j, place * own : (place + 1) * own] for c, j in field_rows(place, freq_devs, per_dev)]
        out.append(np.repeat(np.stack(part), ROWS, 0).T)
    return np.stack(out).astype(np.float32).astype(BF16)


def window_tables(samples, freq_devs, per_dev):
    freq_total = freq_devs * per_dev
    order = np.arange(1, freq_total + 1)
    unit = 2j * math.pi / samples
    diff = order[None, :] - order[:, None]
    total = order[None, :] + order[:, None]
    same = np.where(diff == 0, 0.0, 1.0 / (samples * (np.exp(unit * np.where(diff == 0, 1, diff)) - 1.0)))
    mixed = 1.0 / (samples * (np.exp(-unit * total) - 1.0))
    full = np.zeros((2, freq_total, 2, freq_total))
    full[0, :, 0, :] = same.real + mixed.real
    full[0, :, 1, :] = mixed.imag - same.imag
    full[1, :, 0, :] = same.imag + mixed.imag
    full[1, :, 1, :] = same.real - mixed.real
    out = []
    for place in range(freq_devs):
        rows = [c * freq_total + j for c, j in field_rows(place, freq_devs, per_dev)]
        flat = full.reshape(2 * freq_total, 2 * freq_total)[np.ix_(rows, rows)]
        out.append(np.kron(flat, np.eye(ROWS)))
    return np.stack(out).astype(np.float32).astype(BF16)


def call(body, scalars, inputs, outputs, grid, scratch=(), aliases=None, flops=0):
    in_arrays = [value for value, _ in inputs]
    bytes_all = sum(v.size * v.dtype.itemsize for v in in_arrays)
    bytes_all += sum(math.prod(s.shape) * s.dtype.itemsize for s, _ in outputs)
    return pl.pallas_call(
        body,
        grid_spec=pltpu.PrefetchScalarGridSpec(
            num_scalar_prefetch=len(scalars),
            grid=grid,
            in_specs=[spec for _, spec in inputs],
            out_specs=[spec for _, spec in outputs],
            scratch_shapes=list(scratch),
        ),
        out_shape=[shape for shape, _ in outputs],
        input_output_aliases=aliases or {},
        compiler_params=pltpu.CompilerParams(vmem_limit_bytes=VMEM_BYTES),
        cost_estimate=pl.CostEstimate(flops=flops, bytes_accessed=bytes_all, transcendentals=0),
    )(*scalars, *in_arrays)


def whole(array):
    zeros = (0,) * array.ndim
    return pl.BlockSpec(array.shape, lambda *_: zeros)


def sine_terms():
    square = (np.cos(np.linspace(0.0, math.pi, 200)) + 1.0) / 32.0
    y = np.sqrt(np.maximum(square, 1e-12))
    return [float(v) for v in np.polynomial.polynomial.polyfit(square, np.sin(2.0 * math.pi * y) / y, 6)]


def turned(turn):
    terms = sine_terms()

    def sine(y):
        square = y * y
        total = jnp.full_like(y, terms[-1])
        for term in terms[-2::-1]:
            total = total * square + term
        return total * y

    turn = turn - jnp.floor(turn + 0.5)
    size = jnp.abs(turn)
    folded = jnp.where(size > 0.25, jnp.where(turn > 0.0, 0.5, -0.5) - turn, turn)
    return sine(0.25 - size), sine(folded)


def first_spectra(initial, places, freq_devs, per_dev):
    rows, own, rcv = initial.shape
    samples = own * freq_devs
    tile = 2 * ROWS
    count = freq_devs * 2 * per_dev * ROWS

    def body(freq, rblk, sblk, x_ref, *rest):
        outs, spread_ref = rest[:freq_devs], rest[freq_devs]
        time = lax.broadcasted_iota(jnp.int32, (ROWS, own), 1) + freq[0] * own
        time = time.astype(F32) * (1.0 / samples)
        table = []
        for way in ways(freq_devs):
            waves = [turned(time * ((freq[0] ^ way) * per_dev + j + 1).astype(F32)) for j in range(per_dev)]
            table += [cosine for cosine, _ in waves] + [-sine for _, sine in waves]
        table = jnp.concatenate(table, 0)
        lane = lax.broadcasted_iota(jnp.int32, (count, own), 0) % ROWS
        for row in range(ROWS):
            spread_ref[:, row * own : (row + 1) * own] = jnp.where(lane == row, table, 0.0).astype(BF16)
        for at in range(rows // tile):
            parts = []
            for half in range(2):
                start = at * tile + half * ROWS
                flat = x_ref[start : start + ROWS].reshape(ROWS * own, rcv)
                value = jnp.dot(spread_ref[...], flat, preferred_element_type=F32)
                parts.append(value.reshape(freq_devs, 2, per_dev, ROWS, rcv))
            both = jnp.concatenate(parts, 3).astype(BF16)
            for step, out in enumerate(outs):
                out[:, :, at * tile : (at + 1) * tile, :] = both[step]

    shape = jax.ShapeDtypeStruct((2, per_dev, rows, rcv), BF16)
    return call(
        body,
        places,
        [(initial, whole(initial))],
        [(shape, whole(shape))] * freq_devs,
        (1,),
        scratch=[pltpu.VMEM((count, ROWS * own), BF16)],
        flops=2 * 2 * freq_devs * per_dev * own * rows * rcv,
    )


def masked_halves(response, aperture, places):
    per_dev, _, src, rcv = response.shape
    half = src // 2
    width = half // PARTS

    def body(_, rblk, __, flags, x_ref, *outs):
        lane = lax.broadcasted_iota(jnp.int32, (1, rcv), 1) // BLOCK
        for flip in (1, 0):
            for j in range(per_dev):
                for step in range(half // BLOCK):
                    block = (rblk[0] ^ flip) * (half // BLOCK) + step
                    on = flags[j, pl.ds(block, 1), :].astype(F32)
                    row = sum(jnp.where(lane == r, on[:, r : r + 1], 0.0) for r in range(rcv // BLOCK))
                    gate = jnp.broadcast_to(row, (BLOCK, rcv)).astype(BF16)
                    rows = pl.ds(pl.multiple_of(block * BLOCK, BLOCK), BLOCK)
                    part, at = divmod(step * BLOCK, width)
                    out = outs[flip * PARTS + part]
                    for c in range(2):
                        out[j, at : at + BLOCK, c * rcv : (c + 1) * rcv] = x_ref[j, c, rows, :] * gate

    shape = jax.ShapeDtypeStruct((per_dev, width, 2 * rcv), BF16)
    inputs = [(v, whole(v)) for v in (aperture, response)]
    outs = call(body, places, inputs, [(shape, whole(shape))] * (2 * PARTS), (1,))
    return list(outs[:PARTS]), list(outs[PARTS:])


def summed(parts):
    def body(*refs):
        total = sum(ref[...].astype(F32) for ref in refs[:-2])
        refs[-2][...] = total
        refs[-1][...] = total.astype(BF16)

    shapes = [jax.ShapeDtypeStruct(parts[0].shape, kind) for kind in (F32, BF16)]
    return call(body, (), [(v, whole(v)) for v in parts], [(v, whole(v)) for v in shapes], (1,))


def added(keep, received):
    def body(k_ref, r_ref, out):
        out[...] = (k_ref[...] + r_ref[...].astype(F32)).astype(BF16)

    shape = jax.ShapeDtypeStruct(keep.shape, BF16)
    (out,) = call(body, (), [(v, whole(v)) for v in (keep, received)], [(shape, whole(shape))], (1,))
    return out


def src_onsets(onset, places, half_rows, share, width):

    def body(freq, rblk, sblk, o_ref, own, other):
        lanes = pl.ds(pl.multiple_of(rblk[0] * width, BLOCK), width)
        for core, out in ((sblk[0], own), (1 - sblk[0], other)):
            spot = pl.multiple_of(core * half_rows + freq[0] * share, ROWS)
            out[...] = o_ref[pl.ds(spot, share), lanes]

    shape = jax.ShapeDtypeStruct((share, width), onset.dtype)
    return call(body, places, [(onset, whole(onset))], [(shape, whole(shape))] * 2, (1,))


def phase_tables(src, rcv, places, freq_devs, per_dev, samples, parts, rows):
    width = src[0].shape[1] // parts

    def fill(outs, value, to, freq):
        cosines, sines, fraction = outs
        value = value.astype(F32) * (1.0 / samples)
        fraction[:, to] = value
        for step, way in enumerate(ways(freq_devs)):
            for j in range(per_dev):
                order = ((freq[0] ^ way) * per_dev + j + 1).astype(F32)
                cosines[step, j, :, to], sines[step, j, :, to] = turned(value * order)

    def body(freq, _, sblk, own, other, r_ref, *outs):
        for part in range(parts):
            for spot, ref in enumerate((own, other)):
                at = (part * 2 + spot) * width
                fill(outs[:3], ref[:, part * width : (part + 1) * width], slice(at, at + width), freq)
        value = r_ref[pl.ds(pl.multiple_of(sblk[0] * rows, ROWS), rows), :]
        fill(outs[3:], value, slice(0, value.shape[1]), freq)

    shapes = []
    for count, total in ((src[0].shape[0], 2 * src[0].shape[1]), (rows, rcv.shape[1])):
        table = jax.ShapeDtypeStruct((freq_devs, per_dev, count, total), F32)
        shapes += [table, table, jax.ShapeDtypeStruct(table.shape[2:], F32)]
    outs = call(body, places, [(v, whole(v)) for v in (*src, rcv)], [(v, whole(v)) for v in shapes], (1,))
    return tuple(outs[:3]), tuple(outs[3:])


def down_products(before, spectra, parts, side, first, freq_place, freq_devs=0):
    _, per_dev, _, rcv = spectra[0].shape
    rows = sum(v.shape[2] for v in spectra)
    flat = [pair[side] for part in parts for pair in part]
    width = flat[0].shape[1]
    total_width = before.shape[-1] if before is not None else first + width * len(flat)
    share = rows // freq_devs if freq_devs else 0
    old = [] if before is None else [before]

    def body(place_ref, *rest):
        held_ref, rest = (rest[0], rest[1:]) if old else (None, rest)
        refs, resp, outs = rest[: len(spectra)], rest[len(spectra) : len(spectra) + len(flat)], rest[len(spectra) + len(flat) :]
        held = outs[-1]
        for j in range(per_dev):
            real = jnp.concatenate([ref[0, j] for ref in refs], 0)
            imag = jnp.concatenate([ref[1, j] for ref in refs], 0)
            lhs = jnp.concatenate([jnp.concatenate([real, -imag], 1), jnp.concatenate([imag, real], 1)], 0)
            for at, ref in enumerate(resp):
                total = lax.dot_general(lhs, ref[j], (((1,), (1,)), ((), ())), preferred_element_type=F32)
                to = slice(first + at * width, first + (at + 1) * width)
                for part in range(2):
                    value = total[part * rows : (part + 1) * rows]
                    held[part, j, :, to] = value + held_ref[part, j, :, to] if old else value
        if old:
            for to in (slice(0, first), slice(first + len(flat) * width, total_width)):
                if to.start < to.stop:
                    held[:, :, :, to] = held_ref[:, :, :, to]
        if freq_devs:
            for way, out in zip(ways(freq_devs), outs):
                start = pl.multiple_of((place_ref[0] ^ way) * share, share)
                out[...] = held[:, :, pl.ds(start, share), :].reshape(out.shape).astype(BF16)

    sums = (2, per_dev, rows, total_width)
    if freq_devs:
        shapes = [jax.ShapeDtypeStruct((2 * per_dev * share, total_width), BF16)] * freq_devs
    else:
        shapes = [jax.ShapeDtypeStruct(sums, F32)]
    outs = call(
        body,
        (freq_place,),
        [(v, whole(v)) for v in (*old, *spectra, *flat)],
        [(v, whole(v)) for v in shapes],
        (1,),
        scratch=[pltpu.VMEM(sums, F32)] if freq_devs else [],
        flops=2 * 4 * per_dev * rows * len(flat) * width * rcv,
    )
    return outs if freq_devs else outs[0]


def mixed_fields(plain, cos, sin, matrix):
    tile = plain[0].shape[-1]
    turned = [
        jnp.stack([v[0] * c - v[1] * s, v[0] * s + v[1] * c]) for v, c, s in zip(plain, cos, sin)
    ]
    flat = [jnp.stack(v).reshape(matrix.shape[1], tile).astype(BF16) for v in (turned, plain)]
    mixed = jnp.dot(matrix, jnp.concatenate(flat, 1), preferred_element_type=F32)
    shape = (-1, 2) + plain[0].shape[1:]
    return mixed[:, :tile].reshape(shape), mixed[:, tile:].reshape(shape)


def unturned(up, low, value, cos, sin, part):
    real = cos * up[0] + sin * up[1] - low[0] + part * value[0]
    imag = cos * up[1] - sin * up[0] - low[1] + part * value[1]
    return jnp.stack([real, imag])


def tiles(width, body):
    def at(step, carry):
        body(pl.ds(pl.multiple_of(step * BLOCK, BLOCK), BLOCK))
        return carry

    lax.fori_loop(0, width // BLOCK, at, 0, unroll=2)


def windowed(messages, tables, matrix, freq_place, per_dev, share):
    cosines, sines, fraction = tables
    freq_devs = len(messages)
    width = messages[0].shape[-1]
    count = freq_devs * 2 * per_dev * ROWS

    def body(place_ref, c_ref, s_ref, f_ref, g_ref, *rest):
        refs, outs = rest[:freq_devs], rest[freq_devs:]
        matrix_here = g_ref[place_ref[0]]

        def one(at):
            data = [ref[:, at].astype(F32).reshape(2, per_dev, share, BLOCK) for ref in refs]
            made = [[] for _ in outs]
            for first in range(0, share, ROWS):
                cut = slice(first, first + ROWS)
                plain = [value[:, :, cut] for value in data]
                cos = [c_ref[step, :, cut, at] for step in range(freq_devs)]
                sin = [s_ref[step, :, cut, at] for step in range(freq_devs)]
                up, low = mixed_fields(plain, cos, sin, matrix_here)
                part = f_ref[cut, at]
                for step in range(freq_devs):
                    made[step].append(unturned(up[step], low[step], plain[step], cos[step], sin[step], part))
            for out, value in zip(outs, made):
                out[:, at] = jnp.concatenate(value, 2).reshape(out.shape[0], BLOCK).astype(BF16)

        tiles(width, one)

    inputs = (cosines, sines, fraction, matrix, *messages)
    return call(
        body,
        (freq_place,),
        [(v, whole(v)) for v in inputs],
        [(jax.ShapeDtypeStruct(v.shape, BF16), whole(v)) for v in messages],
        (1,),
        flops=2 * count * count * 2 * width * share // ROWS,
    )


def up_products(messages, parts, freq_place, rows, side):
    freq_devs = len(messages)
    flat = [pair[side] for part in parts for pair in part]
    per_dev, src, rcv = flat[0].shape[0], flat[0].shape[1], flat[0].shape[2] // 2
    group = rows // CHUNKS
    share = rows // freq_devs
    total_width = src * len(flat)
    kind = BF16 if side else F32

    def body(place_ref, *rest):
        resp, refs = rest[: len(flat)], rest[len(flat) : len(flat) + freq_devs]
        outs, held = rest[len(flat) + freq_devs : -1], rest[-1]
        for way, ref in zip(ways(freq_devs), refs):
            start = pl.multiple_of((place_ref[0] ^ way) * share, share)
            value = ref[...].reshape(2, per_dev, share, total_width)
            for part in range(2):
                for j in range(per_dev):
                    held[part, j, pl.ds(start, share), :] = value[part, j]
        for j in range(per_dev):
            both = jnp.concatenate([held[0, j], held[1, j]], 0)
            total = sum(
                jnp.dot(both[:, at * src : (at + 1) * src], ref[j], preferred_element_type=F32)
                for at, ref in enumerate(resp)
            )
            real = total[:rows, :rcv] + total[rows:, rcv:]
            imag = total[rows:, :rcv] - total[:rows, rcv:]
            for index, out in enumerate(outs):
                cut = slice(index * group, (index + 1) * group)
                out[0, j] = real[cut].astype(kind)
                out[1, j] = imag[cut].astype(kind)

    shape = jax.ShapeDtypeStruct((2, per_dev, group, rcv), kind)
    return call(
        body,
        (freq_place,),
        [(v, whole(v)) for v in (*flat, *messages)],
        [(shape, whole(shape))] * CHUNKS,
        (1,),
        scratch=[pltpu.VMEM((2, per_dev, rows, total_width), BF16)],
        flops=2 * 4 * per_dev * rows * total_width * rcv,
    )


def next_spectra(sums, messages, tables, matrix, freq_place, first_row):
    cosines, sines, fraction = tables
    freq_devs = len(messages)
    _, per_dev, rows, rcv = messages[0].shape
    count = freq_devs * 2 * per_dev * ROWS
    own = 2 * per_dev * ROWS

    def body(place_ref, u_ref, c_ref, s_ref, f_ref, g_ref, *rest):
        refs, out = rest[:freq_devs], rest[freq_devs]
        matrix_here = g_ref[place_ref[0], :own]

        def one(at):
            for base in range(0, rows, 2 * ROWS):
                pair = slice(base, base + 2 * ROWS)
                data = [ref[:, :, pair, at].astype(F32) for ref in refs]
                made = []
                for half in range(2):
                    plain = [value[:, :, half * ROWS : (half + 1) * ROWS] for value in data]
                    cut = slice(first_row + base + half * ROWS, first_row + base + (half + 1) * ROWS)
                    cos = [c_ref[step, :, cut, at] for step in range(freq_devs)]
                    sin = [s_ref[step, :, cut, at] for step in range(freq_devs)]
                    up, low = mixed_fields(plain, cos, sin, matrix_here)
                    change = unturned(up[0], low[0], plain[0], cos[0], sin[0], f_ref[cut, at])
                    made.append(u_ref[:, :, cut, at] - change)
                out[:, :, pair, at] = jnp.concatenate(made, 2).astype(BF16)

        tiles(rcv, one)

    inputs = (sums, cosines, sines, fraction, matrix, *messages)
    shape = jax.ShapeDtypeStruct(messages[0].shape, BF16)
    (out,) = call(
        body,
        (freq_place,),
        [(v, whole(v)) for v in inputs],
        [(shape, whole(shape))],
        (1,),
        flops=2 * own * count * 2 * rcv * rows // ROWS,
    )
    return out


def updated(initial, onset, messages, table, places, first, rows, target):
    freq_devs = len(messages)
    half_rows, own, rcv = initial.shape
    per_dev = messages[0].shape[1]
    tile = 2 * ROWS
    count = table.shape[2]

    def body(place_ref, _, sblk, x_ref, o_ref, t_ref, *rest):
        refs = rest[:freq_devs]
        out, spread_ref = rest[-2:]
        step = pl.program_id(0)

        @pl.when(step == 0)
        def _():
            base = t_ref[place_ref[0]].astype(F32)
            lane = lax.broadcasted_iota(jnp.int32, (own, count), 1) % ROWS
            for row in range(ROWS):
                spread_ref[row * own : (row + 1) * own] = jnp.where(lane == row, base, 0.0).astype(BF16)

        here = pl.ds(pl.multiple_of(step * tile, tile), tile)
        data = [ref[:, :, here, :].astype(F32) for ref in refs]
        onsets = o_ref[pl.ds(pl.multiple_of(sblk[0] * half_rows + first + step * tile, tile), tile), :]
        time = lax.broadcasted_iota(jnp.int32, (own, rcv), 0) + place_ref[0] * own
        for half in range(2):
            cut = slice(half * ROWS, (half + 1) * ROWS)
            flat = jnp.stack([v[:, :, cut] for v in data]).reshape(count, rcv).astype(BF16)
            change = jnp.dot(spread_ref[...], flat, preferred_element_type=F32)
            for row in range(ROWS):
                spot = half * ROWS + row
                on = time < onsets[spot : spot + 1, :]
                moved = jnp.where(on, change[row * own : (row + 1) * own], 0.0)
                out[spot] = (x_ref[first + step * tile + spot].astype(F32) - moved).astype(BF16)

    inputs = [(v, whole(v)) for v in (initial, onset, table, *messages)]
    aliases = {}
    if target is not None:
        inputs.append((target, pl.BlockSpec(memory_space=pl.ANY)))
        aliases = {len(places) + len(inputs) - 1: 0}
    (out,) = call(
        body,
        places,
        inputs,
        [(jax.ShapeDtypeStruct(initial.shape, BF16), pl.BlockSpec((tile, own, rcv), lambda i, *_: (first // tile + i, 0, 0)))],
        (rows // tile,),
        scratch=[pltpu.VMEM((ROWS * own, count), BF16)],
        aliases=aliases,
        flops=2 * 2 * freq_devs * per_dev * own * rows * rcv,
    )
    return out


def exchanged(value, axis, step):
    return lax.ppermute(value, axis, [(i, i ^ step) for i in range(lax.axis_size(axis))])


def dealt_out(parts):
    return [exchanged(part, "freq", step) if step else part for part, step in zip(parts, ways(len(parts)))]


def spread(value, count):
    held = {0: value}
    bit = count // 2
    while bit:
        held.update({way | bit: exchanged(held[way], "freq", bit) for way in sorted(held)})
        bit //= 2
    return [held[way] for way in ways(count)]


def on_device(initial, response, aperture, onset_rcv, onset_src):
    freq_devs = lax.axis_size("freq")
    per_dev = response.shape[0]
    samples = initial.shape[1] * freq_devs
    half_rows = initial.shape[0]
    src_width = response.shape[2] // 2
    rows = half_rows // CHUNKS
    share = half_rows // freq_devs
    places = tuple(lax.axis_index(axis).reshape(1) for axis in ("freq", "rblk", "sblk"))
    freq_place = places[0]
    inverse = jnp.asarray(inverse_tables(samples, freq_devs, per_dev))
    matrix = jnp.asarray(window_tables(samples, freq_devs, per_dev))

    kept, sent = masked_halves(response, aperture, places)
    moved = [exchanged(v, "rblk", 1) for v in sent]
    kept_pair = [exchanged(v, "sblk", 1) for v in kept]
    sums, spectra = summed(dealt_out(first_spectra(initial, places, freq_devs, per_dev)))
    far = exchanged(spectra, "rblk", 1)
    moved_pair = []
    for index in range(PARTS):
        if index:
            moved[index], far = lax.optimization_barrier((moved[index], far))
        else:
            moved[index], spectra = lax.optimization_barrier((moved[index], spectra))
        moved_pair.append(exchanged(moved[index], "sblk", 1))
    parts = [((kept[i], moved[i]), (kept_pair[i], moved_pair[i])) for i in range(PARTS)]

    own, other = src_onsets(onset_src, places, half_rows, share, src_width)
    onsets = (own, exchanged(other, "sblk", 1))
    src_tables, rcv_tables = phase_tables(onsets, onset_rcv, places, freq_devs, per_dev, samples, PARTS, half_rows)

    near, far, result = [spectra], [far], None
    for step in range(ITERS):
        held = down_products(None, near, parts, 0, 0, freq_place)
        at = 0 if step else PARTS - 1
        if at:
            held = down_products(held, far, parts[:at], 1, 0, freq_place)
        first = at * 2 * kept[0].shape[1]
        messages = dealt_out(down_products(held, far, parts[at:], 1, first, freq_place, freq_devs))
        messages = dealt_out(windowed(messages, src_tables, matrix, freq_place, per_dev, share))
        received = [exchanged(v, "rblk", 1) for v in up_products(messages, parts, freq_place, half_rows, 1)]
        keep = up_products(messages, parts, freq_place, half_rows, 0)
        near, far = [], []
        for chunk in range(CHUNKS):
            back = spread(added(keep[chunk], received[chunk]), freq_devs)
            if step < ITERS - 1:
                near.append(next_spectra(sums, back, rcv_tables, matrix, freq_place, chunk * rows))
                far.append(exchanged(near[chunk], "rblk", 1))
            else:
                result = updated(initial, onset_rcv, back, inverse, places, chunk * rows, rows, result)
    return result


def transform_tables(length, count):
    table = fields(length, count).reshape(2 * count, length)
    forward_table = jnp.asarray(table.astype(np.float32).astype(BF16))
    inverse_table = jnp.asarray((table.T * (2.0 / length)).astype(np.float32).astype(BF16))
    return forward_table, inverse_table


def settle(values):
    return lax.optimization_barrier(values.astype(BF16)).astype(F32)


def samples_into_spectra(values, forward_table, freq_total):
    out = jnp.einsum("kt,ptn->pkn", forward_table, values, preferred_element_type=F32)
    return out.reshape(values.shape[0], 2, freq_total, values.shape[2]).astype(BF16)


def spectra_into_samples(trace_spectra, inverse_table):
    flat = trace_spectra.reshape(trace_spectra.shape[0], -1, trace_spectra.shape[3])
    return jnp.einsum("tk,pkn->ptn", inverse_table, flat, preferred_element_type=F32)


def dense(spec, gated, real, imag, sign):
    dot = functools.partial(jnp.einsum, spec, preferred_element_type=F32)
    return jnp.stack(
        [dot(gated[:, 0], real) - sign * dot(gated[:, 1], imag), dot(gated[:, 0], imag) + sign * dot(gated[:, 1], real)], 1
    )


def general_device(initial, response, aperture, onset_rcv, onset_src):
    freq_devs, rblk_devs, sblk_devs = (lax.axis_size(a) for a in ("freq", "rblk", "sblk"))
    freq_index, rblk_index, sblk_index = (lax.axis_index(a) for a in ("freq", "rblk", "sblk"))
    freq_total = response.shape[0] * freq_devs
    samples = initial.shape[1] * freq_devs
    focal_all = onset_rcv.shape[0]
    forward_table, inverse_table = transform_tables(samples, freq_total)
    steps_axis = lax.iota(jnp.int32, samples)
    own_axis = freq_index * initial.shape[1] + lax.iota(jnp.int32, initial.shape[1])
    half_rows = focal_all // sblk_devs
    own_onsets = lax.dynamic_slice_in_dim(onset_rcv, sblk_index * half_rows, half_rows, 0)
    rcv_gate = (own_axis[None, :, None] < own_onsets[:, None, :]).astype(F32)
    src_rows = focal_all // (rblk_devs * freq_devs)
    src_first = rblk_index * (focal_all // rblk_devs) + freq_index * src_rows
    src_onsets = lax.dynamic_slice_in_dim(onset_src, src_first, src_rows, 0)
    src_gate = (steps_axis[None, :, None] < src_onsets[:, None, :]).astype(F32)
    mask_full = jnp.repeat(jnp.repeat(aperture, BLOCK, 1), BLOCK, 2).astype(BF16)
    gated = response * mask_full[:, None]
    own_forward = lax.dynamic_slice_in_dim(forward_table, freq_index * initial.shape[1], initial.shape[1], 1)
    own_inverse = lax.dynamic_slice_in_dim(inverse_table, freq_index * initial.shape[1], initial.shape[1], 0)
    current = initial
    for _ in range(ITERS):
        partial = samples_into_spectra(current, own_forward, freq_total)
        spec_back = lax.psum_scatter(partial.astype(F32), "freq", scatter_dimension=2, tiled=True).astype(BF16)
        spec_all = lax.all_gather(spec_back, "sblk", axis=0, tiled=True)
        down = lax.psum_scatter(
            settle(dense("euk,bek->beu", gated, spec_all[:, 0], spec_all[:, 1], 1.0)).astype(BF16),
            "rblk",
            scatter_dimension=0,
            tiled=True,
        )
        src_traces = lax.all_to_all(down, "freq", split_axis=0, concat_axis=2, tiled=True)
        upgoing = (src_gate * spectra_into_samples(src_traces, inverse_table)).astype(BF16)
        upspec = samples_into_spectra(upgoing, forward_table, freq_total)
        up_back = lax.all_to_all(upspec, "freq", split_axis=2, concat_axis=0, tiled=True)
        up_all = lax.all_gather(up_back, "rblk", axis=0, tiled=True)
        sums = dense("qao,bqa->bqo", gated, up_all[:, 0], up_all[:, 1], -1.0).astype(BF16)
        back = lax.psum_scatter(sums, "sblk", scatter_dimension=0, tiled=True)
        traces = lax.all_gather(back, "freq", axis=2, tiled=True)
        update = rcv_gate * spectra_into_samples(traces, own_inverse)
        current = (initial.astype(F32) - update).astype(BF16)
    return current


def fits(initial, response, aperture, onset_rcv, onset_src):
    freq_devs = lax.axis_size("freq")
    if lax.axis_size("rblk") != 2 or lax.axis_size("sblk") != 2 or freq_devs & (freq_devs - 1):
        return False
    whole_rows = initial.shape[0] % (max(2, CHUNKS) * ROWS * freq_devs) == 0
    whole_width = response.shape[2] % (2 * PARTS * BLOCK) == 0 and response.shape[3] % BLOCK == 0
    return whole_rows and whole_width and onset_rcv.shape[0] == 2 * initial.shape[0]


def chosen(*arrays):
    return on_device(*arrays) if fits(*arrays) else general_device(*arrays)


def solution(mesh):
    in_specs = (
        P(("group", "sblk"), "freq", "rblk"),
        P(("group", "freq"), None, "sblk", "rblk"),
        P(("group", "freq"), "sblk", "rblk"),
        P("group", "rblk"),
        P("group", "sblk"),
    )
    out_specs = P(("group", "sblk"), "freq", "rblk")
    return jax.shard_map(chosen, mesh=mesh, in_specs=in_specs, out_specs=out_specs, check_vma=False)
```

```python
import functools
import math

import jax
import jax.numpy as jnp
import numpy as np
from jax import lax
from jax.experimental import pallas as pl
from jax.experimental.pallas import tpu as pltpu
from jax.sharding import PartitionSpec as P

BLOCK = 128
ITERS = 2
ROWS = 8
CHUNKS = 1
PARTS = 2
VMEM_BYTES = 6 * 1024 * 1024

BF16 = jnp.bfloat16
F32 = jnp.float32


def ways(count):
    far = sorted(range(1, count), key=lambda step: (step.bit_length() < count.bit_length() - 1, step))
    return [0] + far


def field_rows(place, freq_devs, per_dev):
    rows = []
    for step in ways(freq_devs):
        first = (place ^ step) * per_dev
        for part in range(2):
            rows.extend((part, first + local) for local in range(per_dev))
    return rows


def fields(samples, freq_total):
    phase = (np.arange(1, freq_total + 1)[:, None] * np.arange(samples)[None, :]) % samples
    angle = phase * (2.0 * math.pi / samples)
    return np.stack([np.cos(angle), -np.sin(angle)])


def inverse_tables(samples, freq_devs, per_dev):
    exact = fields(samples, freq_devs * per_dev) * (2.0 / samples)
    own = samples // freq_devs
    out = []
    for place in range(freq_devs):
        part = [exact[c, j, place * own : (place + 1) * own] for c, j in field_rows(place, freq_devs, per_dev)]
        out.append(np.repeat(np.stack(part), ROWS, 0).T)
    return np.stack(out).astype(np.float32).astype(BF16)


def window_tables(samples, freq_devs, per_dev):
    freq_total = freq_devs * per_dev
    order = np.arange(1, freq_total + 1)
    unit = 2j * math.pi / samples
    diff = order[None, :] - order[:, None]
    total = order[None, :] + order[:, None]
    same = np.where(diff == 0, 0.0, 1.0 / (samples * (np.exp(unit * np.where(diff == 0, 1, diff)) - 1.0)))
    mixed = 1.0 / (samples * (np.exp(-unit * total) - 1.0))
    full = np.zeros((2, freq_total, 2, freq_total))
    full[0, :, 0, :] = same.real + mixed.real
    full[0, :, 1, :] = mixed.imag - same.imag
    full[1, :, 0, :] = same.imag + mixed.imag
    full[1, :, 1, :] = same.real - mixed.real
    out = []
    for place in range(freq_devs):
        rows = [c * freq_total + j for c, j in field_rows(place, freq_devs, per_dev)]
        flat = full.reshape(2 * freq_total, 2 * freq_total)[np.ix_(rows, rows)]
        out.append(np.kron(flat, np.eye(ROWS)))
    return np.stack(out).astype(np.float32).astype(BF16)


def call(body, scalars, inputs, outputs, grid, scratch=(), aliases=None, flops=0):
    in_arrays = [value for value, _ in inputs]
    bytes_all = sum(v.size * v.dtype.itemsize for v in in_arrays)
    bytes_all += sum(math.prod(s.shape) * s.dtype.itemsize for s, _ in outputs)
    return pl.pallas_call(
        body,
        grid_spec=pltpu.PrefetchScalarGridSpec(
            num_scalar_prefetch=len(scalars),
            grid=grid,
            in_specs=[spec for _, spec in inputs],
            out_specs=[spec for _, spec in outputs],
            scratch_shapes=list(scratch),
        ),
        out_shape=[shape for shape, _ in outputs],
        input_output_aliases=aliases or {},
        compiler_params=pltpu.CompilerParams(vmem_limit_bytes=VMEM_BYTES),
        cost_estimate=pl.CostEstimate(flops=flops, bytes_accessed=bytes_all, transcendentals=0),
    )(*scalars, *in_arrays)


def whole(array):
    zeros = (0,) * array.ndim
    return pl.BlockSpec(array.shape, lambda *_: zeros)


def sine_terms():
    square = (np.cos(np.linspace(0.0, math.pi, 200)) + 1.0) / 32.0
    y = np.sqrt(np.maximum(square, 1e-12))
    return [float(v) for v in np.polynomial.polynomial.polyfit(square, np.sin(2.0 * math.pi * y) / y, 6)]


def turned(turn):
    terms = sine_terms()

    def sine(y):
        square = y * y
        total = jnp.full_like(y, terms[-1])
        for term in terms[-2::-1]:
            total = total * square + term
        return total * y

    turn = turn - jnp.floor(turn + 0.5)
    size = jnp.abs(turn)
    folded = jnp.where(size > 0.25, jnp.where(turn > 0.0, 0.5, -0.5) - turn, turn)
    return sine(0.25 - size), sine(folded)


def first_spectra(initial, places, freq_devs, per_dev):
    rows, own, rcv = initial.shape
    samples = own * freq_devs
    tile = 2 * ROWS
    count = freq_devs * 2 * per_dev * ROWS

    def body(freq, rblk, sblk, x_ref, *rest):
        outs, spread_ref = rest[:freq_devs], rest[freq_devs]
        time = lax.broadcasted_iota(jnp.int32, (ROWS, own), 1) + freq[0] * own
        time = time.astype(F32) * (1.0 / samples)
        table = []
        for way in ways(freq_devs):
            waves = [turned(time * ((freq[0] ^ way) * per_dev + j + 1).astype(F32)) for j in range(per_dev)]
            table += [cosine for cosine, _ in waves] + [-sine for _, sine in waves]
        table = jnp.concatenate(table, 0)
        lane = lax.broadcasted_iota(jnp.int32, (count, own), 0) % ROWS
        for row in range(ROWS):
            spread_ref[:, row * own : (row + 1) * own] = jnp.where(lane == row, table, 0.0).astype(BF16)
        for at in range(rows // tile):
            parts = []
            for half in range(2):
                start = at * tile + half * ROWS
                flat = x_ref[start : start + ROWS].reshape(ROWS * own, rcv)
                value = jnp.dot(spread_ref[...], flat, preferred_element_type=F32)
                parts.append(value.reshape(freq_devs, 2, per_dev, ROWS, rcv))
            both = jnp.concatenate(parts, 3).astype(BF16)
            for step, out in enumerate(outs):
                out[:, :, at * tile : (at + 1) * tile, :] = both[step]

    shape = jax.ShapeDtypeStruct((2, per_dev, rows, rcv), BF16)
    return call(
        body,
        places,
        [(initial, whole(initial))],
        [(shape, whole(shape))] * freq_devs,
        (1,),
        scratch=[pltpu.VMEM((count, ROWS * own), BF16)],
        flops=2 * 2 * freq_devs * per_dev * own * rows * rcv,
    )


def masked_halves(response, aperture, places):
    per_dev, _, src, rcv = response.shape
    half = src // 2
    width = half // PARTS

    def body(_, rblk, __, flags, x_ref, *outs):
        lane = lax.broadcasted_iota(jnp.int32, (1, rcv), 1) // BLOCK
        for flip in (1, 0):
            for j in range(per_dev):
                for step in range(half // BLOCK):
                    block = (rblk[0] ^ flip) * (half // BLOCK) + step
                    on = flags[j, pl.ds(block, 1), :].astype(F32)
                    row = sum(jnp.where(lane == r, on[:, r : r + 1], 0.0) for r in range(rcv // BLOCK))
                    gate = jnp.broadcast_to(row, (BLOCK, rcv)).astype(BF16)
                    rows = pl.ds(pl.multiple_of(block * BLOCK, BLOCK), BLOCK)
                    part, at = divmod(step * BLOCK, width)
                    out = outs[flip * PARTS + part]
                    for c in range(2):
                        out[j, at : at + BLOCK, c * rcv : (c + 1) * rcv] = x_ref[j, c, rows, :] * gate

    shape = jax.ShapeDtypeStruct((per_dev, width, 2 * rcv), BF16)
    inputs = [(v, whole(v)) for v in (aperture, response)]
    outs = call(body, places, inputs, [(shape, whole(shape))] * (2 * PARTS), (1,))
    return list(outs[:PARTS]), list(outs[PARTS:])


def summed(parts):
    def body(*refs):
        total = sum(ref[...].astype(F32) for ref in refs[:-2])
        refs[-2][...] = total
        refs[-1][...] = total.astype(BF16)

    shapes = [jax.ShapeDtypeStruct(parts[0].shape, kind) for kind in (F32, BF16)]
    return call(body, (), [(v, whole(v)) for v in parts], [(v, whole(v)) for v in shapes], (1,))


def added(keep, received):
    def body(k_ref, r_ref, out):
        out[...] = (k_ref[...] + r_ref[...].astype(F32)).astype(BF16)

    shape = jax.ShapeDtypeStruct(keep.shape, BF16)
    (out,) = call(body, (), [(v, whole(v)) for v in (keep, received)], [(shape, whole(shape))], (1,))
    return out


def src_onsets(onset, places, half_rows, share, width):

    def body(freq, rblk, sblk, o_ref, own, other):
        lanes = pl.ds(pl.multiple_of(rblk[0] * width, BLOCK), width)
        for core, out in ((sblk[0], own), (1 - sblk[0], other)):
            spot = pl.multiple_of(core * half_rows + freq[0] * share, ROWS)
            out[...] = o_ref[pl.ds(spot, share), lanes]

    shape = jax.ShapeDtypeStruct((share, width), onset.dtype)
    return call(body, places, [(onset, whole(onset))], [(shape, whole(shape))] * 2, (1,))


def phase_tables(src, rcv, places, freq_devs, per_dev, samples, parts, rows):
    width = src[0].shape[1] // parts

    def fill(outs, value, to, freq):
        cosines, sines, fraction = outs
        value = value.astype(F32) * (1.0 / samples)
        fraction[:, to] = value
        for step, way in enumerate(ways(freq_devs)):
            for j in range(per_dev):
                order = ((freq[0] ^ way) * per_dev + j + 1).astype(F32)
                cosines[step, j, :, to], sines[step, j, :, to] = turned(value * order)

    def body(freq, _, sblk, own, other, r_ref, *outs):
        for part in range(parts):
            for spot, ref in enumerate((own, other)):
                at = (part * 2 + spot) * width
                fill(outs[:3], ref[:, part * width : (part + 1) * width], slice(at, at + width), freq)
        value = r_ref[pl.ds(pl.multiple_of(sblk[0] * rows, ROWS), rows), :]
        fill(outs[3:], value, slice(0, value.shape[1]), freq)

    shapes = []
    for count, total in ((src[0].shape[0], 2 * src[0].shape[1]), (rows, rcv.shape[1])):
        table = jax.ShapeDtypeStruct((freq_devs, per_dev, count, total), F32)
        shapes += [table, table, jax.ShapeDtypeStruct(table.shape[2:], F32)]
    outs = call(body, places, [(v, whole(v)) for v in (*src, rcv)], [(v, whole(v)) for v in shapes], (1,))
    return tuple(outs[:3]), tuple(outs[3:])


def down_products(before, spectra, parts, side, first, freq_place, freq_devs=0):
    _, per_dev, _, rcv = spectra[0].shape
    rows = sum(v.shape[2] for v in spectra)
    flat = [pair[side] for part in parts for pair in part]
    width = flat[0].shape[1]
    total_width = before.shape[-1] if before is not None else first + width * len(flat)
    share = rows // freq_devs if freq_devs else 0
    old = [] if before is None else [before]

    def body(place_ref, *rest):
        held_ref, rest = (rest[0], rest[1:]) if old else (None, rest)
        refs, resp, outs = rest[: len(spectra)], rest[len(spectra) : len(spectra) + len(flat)], rest[len(spectra) + len(flat) :]
        held = outs[-1]
        for j in range(per_dev):
            real = jnp.concatenate([ref[0, j] for ref in refs], 0)
            imag = jnp.concatenate([ref[1, j] for ref in refs], 0)
            lhs = jnp.concatenate([jnp.concatenate([real, -imag], 1), jnp.concatenate([imag, real], 1)], 0)
            for at, ref in enumerate(resp):
                total = lax.dot_general(lhs, ref[j], (((1,), (1,)), ((), ())), preferred_element_type=F32)
                to = slice(first + at * width, first + (at + 1) * width)
                for part in range(2):
                    value = total[part * rows : (part + 1) * rows]
                    held[part, j, :, to] = value + held_ref[part, j, :, to] if old else value
        if old:
            for to in (slice(0, first), slice(first + len(flat) * width, total_width)):
                if to.start < to.stop:
                    held[:, :, :, to] = held_ref[:, :, :, to]
        if freq_devs:
            for way, out in zip(ways(freq_devs), outs):
                start = pl.multiple_of((place_ref[0] ^ way) * share, share)
                out[...] = held[:, :, pl.ds(start, share), :].reshape(out.shape).astype(BF16)

    sums = (2, per_dev, rows, total_width)
    if freq_devs:
        shapes = [jax.ShapeDtypeStruct((2 * per_dev * share, total_width), BF16)] * freq_devs
    else:
        shapes = [jax.ShapeDtypeStruct(sums, F32)]
    outs = call(
        body,
        (freq_place,),
        [(v, whole(v)) for v in (*old, *spectra, *flat)],
        [(v, whole(v)) for v in shapes],
        (1,),
        scratch=[pltpu.VMEM(sums, F32)] if freq_devs else [],
        flops=2 * 4 * per_dev * rows * len(flat) * width * rcv,
    )
    return outs if freq_devs else outs[0]


def mixed_fields(plain, cos, sin, matrix):
    tile = plain[0].shape[-1]
    turned = [
        jnp.stack([v[0] * c - v[1] * s, v[0] * s + v[1] * c]) for v, c, s in zip(plain, cos, sin)
    ]
    flat = [jnp.stack(v).reshape(matrix.shape[1], tile).astype(BF16) for v in (turned, plain)]
    mixed = jnp.dot(matrix, jnp.concatenate(flat, 1), preferred_element_type=F32)
    shape = (-1, 2) + plain[0].shape[1:]
    return mixed[:, :tile].reshape(shape), mixed[:, tile:].reshape(shape)


def unturned(up, low, value, cos, sin, part):
    real = cos * up[0] + sin * up[1] - low[0] + part * value[0]
    imag = cos * up[1] - sin * up[0] - low[1] + part * value[1]
    return jnp.stack([real, imag])


def tiles(width, body):
    def at(step, carry):
        body(pl.ds(pl.multiple_of(step * BLOCK, BLOCK), BLOCK))
        return carry

    lax.fori_loop(0, width // BLOCK, at, 0, unroll=2)


def windowed(messages, tables, matrix, freq_place, per_dev, share):
    cosines, sines, fraction = tables
    freq_devs = len(messages)
    width = messages[0].shape[-1]
    count = freq_devs * 2 * per_dev * ROWS

    def body(place_ref, c_ref, s_ref, f_ref, g_ref, *rest):
        refs, outs = rest[:freq_devs], rest[freq_devs:]
        matrix_here = g_ref[place_ref[0]]

        def one(at):
            data = [ref[:, at].astype(F32).reshape(2, per_dev, share, BLOCK) for ref in refs]
            made = [[] for _ in outs]
            for first in range(0, share, ROWS):
                cut = slice(first, first + ROWS)
                plain = [value[:, :, cut] for value in data]
                cos = [c_ref[step, :, cut, at] for step in range(freq_devs)]
                sin = [s_ref[step, :, cut, at] for step in range(freq_devs)]
                up, low = mixed_fields(plain, cos, sin, matrix_here)
                part = f_ref[cut, at]
                for step in range(freq_devs):
                    made[step].append(unturned(up[step], low[step], plain[step], cos[step], sin[step], part))
            for out, value in zip(outs, made):
                out[:, at] = jnp.concatenate(value, 2).reshape(out.shape[0], BLOCK).astype(BF16)

        tiles(width, one)

    inputs = (cosines, sines, fraction, matrix, *messages)
    return call(
        body,
        (freq_place,),
        [(v, whole(v)) for v in inputs],
        [(jax.ShapeDtypeStruct(v.shape, BF16), whole(v)) for v in messages],
        (1,),
        flops=2 * count * count * 2 * width * share // ROWS,
    )


def up_products(messages, parts, freq_place, rows, side):
    freq_devs = len(messages)
    flat = [pair[side] for part in parts for pair in part]
    per_dev, src, rcv = flat[0].shape[0], flat[0].shape[1], flat[0].shape[2] // 2
    group = rows // CHUNKS
    share = rows // freq_devs
    total_width = src * len(flat)
    kind = BF16 if side else F32

    def body(place_ref, *rest):
        resp, refs = rest[: len(flat)], rest[len(flat) : len(flat) + freq_devs]
        outs, held = rest[len(flat) + freq_devs : -1], rest[-1]
        for way, ref in zip(ways(freq_devs), refs):
            start = pl.multiple_of((place_ref[0] ^ way) * share, share)
            value = ref[...].reshape(2, per_dev, share, total_width)
            for part in range(2):
                for j in range(per_dev):
                    held[part, j, pl.ds(start, share), :] = value[part, j]
        for j in range(per_dev):
            both = jnp.concatenate([held[0, j], held[1, j]], 0)
            total = sum(
                jnp.dot(both[:, at * src : (at + 1) * src], ref[j], preferred_element_type=F32)
                for at, ref in enumerate(resp)
            )
            real = total[:rows, :rcv] + total[rows:, rcv:]
            imag = total[rows:, :rcv] - total[:rows, rcv:]
            for index, out in enumerate(outs):
                cut = slice(index * group, (index + 1) * group)
                out[0, j] = real[cut].astype(kind)
                out[1, j] = imag[cut].astype(kind)

    shape = jax.ShapeDtypeStruct((2, per_dev, group, rcv), kind)
    return call(
        body,
        (freq_place,),
        [(v, whole(v)) for v in (*flat, *messages)],
        [(shape, whole(shape))] * CHUNKS,
        (1,),
        scratch=[pltpu.VMEM((2, per_dev, rows, total_width), BF16)],
        flops=2 * 4 * per_dev * rows * total_width * rcv,
    )


def next_spectra(sums, messages, tables, matrix, freq_place, first_row):
    cosines, sines, fraction = tables
    freq_devs = len(messages)
    _, per_dev, rows, rcv = messages[0].shape
    count = freq_devs * 2 * per_dev * ROWS
    own = 2 * per_dev * ROWS

    def body(place_ref, u_ref, c_ref, s_ref, f_ref, g_ref, *rest):
        refs, out = rest[:freq_devs], rest[freq_devs]
        matrix_here = g_ref[place_ref[0], :own]

        def one(at):
            for base in range(0, rows, 2 * ROWS):
                pair = slice(base, base + 2 * ROWS)
                data = [ref[:, :, pair, at].astype(F32) for ref in refs]
                made = []
                for half in range(2):
                    plain = [value[:, :, half * ROWS : (half + 1) * ROWS] for value in data]
                    cut = slice(first_row + base + half * ROWS, first_row + base + (half + 1) * ROWS)
                    cos = [c_ref[step, :, cut, at] for step in range(freq_devs)]
                    sin = [s_ref[step, :, cut, at] for step in range(freq_devs)]
                    up, low = mixed_fields(plain, cos, sin, matrix_here)
                    change = unturned(up[0], low[0], plain[0], cos[0], sin[0], f_ref[cut, at])
                    made.append(u_ref[:, :, cut, at] - change)
                out[:, :, pair, at] = jnp.concatenate(made, 2).astype(BF16)

        tiles(rcv, one)

    inputs = (sums, cosines, sines, fraction, matrix, *messages)
    shape = jax.ShapeDtypeStruct(messages[0].shape, BF16)
    (out,) = call(
        body,
        (freq_place,),
        [(v, whole(v)) for v in inputs],
        [(shape, whole(shape))],
        (1,),
        flops=2 * own * count * 2 * rcv * rows // ROWS,
    )
    return out


def updated(initial, onset, messages, table, places, first, rows, target):
    freq_devs = len(messages)
    half_rows, own, rcv = initial.shape
    per_dev = messages[0].shape[1]
    tile = 2 * ROWS
    count = table.shape[2]

    def body(place_ref, _, sblk, x_ref, o_ref, t_ref, *rest):
        refs = rest[:freq_devs]
        out, spread_ref = rest[-2:]
        step = pl.program_id(0)

        @pl.when(step == 0)
        def _():
            base = t_ref[place_ref[0]].astype(F32)
            lane = lax.broadcasted_iota(jnp.int32, (own, count), 1) % ROWS
            for row in range(ROWS):
                spread_ref[row * own : (row + 1) * own] = jnp.where(lane == row, base, 0.0).astype(BF16)

        here = pl.ds(pl.multiple_of(step * tile, tile), tile)
        data = [ref[:, :, here, :].astype(F32) for ref in refs]
        onsets = o_ref[pl.ds(pl.multiple_of(sblk[0] * half_rows + first + step * tile, tile), tile), :]
        time = lax.broadcasted_iota(jnp.int32, (own, rcv), 0) + place_ref[0] * own
        for half in range(2):
            cut = slice(half * ROWS, (half + 1) * ROWS)
            flat = jnp.stack([v[:, :, cut] for v in data]).reshape(count, rcv).astype(BF16)
            change = jnp.dot(spread_ref[...], flat, preferred_element_type=F32)
            for row in range(ROWS):
                spot = half * ROWS + row
                on = time < onsets[spot : spot + 1, :]
                moved = jnp.where(on, change[row * own : (row + 1) * own], 0.0)
                out[spot] = (x_ref[first + step * tile + spot].astype(F32) - moved).astype(BF16)

    inputs = [(v, whole(v)) for v in (initial, onset, table, *messages)]
    aliases = {}
    if target is not None:
        inputs.append((target, pl.BlockSpec(memory_space=pl.ANY)))
        aliases = {len(places) + len(inputs) - 1: 0}
    (out,) = call(
        body,
        places,
        inputs,
        [(jax.ShapeDtypeStruct(initial.shape, BF16), pl.BlockSpec((tile, own, rcv), lambda i, *_: (first // tile + i, 0, 0)))],
        (rows // tile,),
        scratch=[pltpu.VMEM((ROWS * own, count), BF16)],
        aliases=aliases,
        flops=2 * 2 * freq_devs * per_dev * own * rows * rcv,
    )
    return out


def exchanged(value, axis, step):
    return lax.ppermute(value, axis, [(i, i ^ step) for i in range(lax.axis_size(axis))])


def dealt_out(parts):
    return [exchanged(part, "freq", step) if step else part for part, step in zip(parts, ways(len(parts)))]


def spread(value, count):
    held = {0: value}
    bit = count // 2
    while bit:
        held.update({way | bit: exchanged(held[way], "freq", bit) for way in sorted(held)})
        bit //= 2
    return [held[way] for way in ways(count)]


def on_device(initial, response, aperture, onset_rcv, onset_src):
    freq_devs = lax.axis_size("freq")
    per_dev = response.shape[0]
    samples = initial.shape[1] * freq_devs
    half_rows = initial.shape[0]
    src_width = response.shape[2] // 2
    rows = half_rows // CHUNKS
    share = half_rows // freq_devs
    places = tuple(lax.axis_index(axis).reshape(1) for axis in ("freq", "rblk", "sblk"))
    freq_place = places[0]
    inverse = jnp.asarray(inverse_tables(samples, freq_devs, per_dev))
    matrix = jnp.asarray(window_tables(samples, freq_devs, per_dev))

    kept, sent = masked_halves(response, aperture, places)
    moved = [exchanged(v, "rblk", 1) for v in sent]
    kept_pair = [exchanged(v, "sblk", 1) for v in kept]
    sums, spectra = summed(dealt_out(first_spectra(initial, places, freq_devs, per_dev)))
    far = exchanged(spectra, "rblk", 1)
    moved_pair = []
    for index in range(PARTS):
        if index:
            moved[index], far = lax.optimization_barrier((moved[index], far))
        else:
            moved[index], spectra = lax.optimization_barrier((moved[index], spectra))
        moved_pair.append(exchanged(moved[index], "sblk", 1))
    parts = [((kept[i], moved[i]), (kept_pair[i], moved_pair[i])) for i in range(PARTS)]

    own, other = src_onsets(onset_src, places, half_rows, share, src_width)
    onsets = (own, exchanged(other, "sblk", 1))
    src_tables, rcv_tables = phase_tables(onsets, onset_rcv, places, freq_devs, per_dev, samples, PARTS, half_rows)

    near, far, result = [spectra], [far], None
    for step in range(ITERS):
        held = down_products(None, near, parts, 0, 0, freq_place)
        at = 0 if step else PARTS - 1
        if at:
            held = down_products(held, far, parts[:at], 1, 0, freq_place)
        first = at * 2 * kept[0].shape[1]
        messages = dealt_out(down_products(held, far, parts[at:], 1, first, freq_place, freq_devs))
        messages = dealt_out(windowed(messages, src_tables, matrix, freq_place, per_dev, share))
        received = [exchanged(v, "rblk", 1) for v in up_products(messages, parts, freq_place, half_rows, 1)]
        keep = up_products(messages, parts, freq_place, half_rows, 0)
        near, far = [], []
        for chunk in range(CHUNKS):
            back = spread(added(keep[chunk], received[chunk]), freq_devs)
            if step < ITERS - 1:
                near.append(next_spectra(sums, back, rcv_tables, matrix, freq_place, chunk * rows))
                far.append(exchanged(near[chunk], "rblk", 1))
            else:
                result = updated(initial, onset_rcv, back, inverse, places, chunk * rows, rows, result)
    return result


def transform_tables(length, count):
    table = fields(length, count).reshape(2 * count, length)
    forward_table = jnp.asarray(table.astype(np.float32).astype(BF16))
    inverse_table = jnp.asarray((table.T * (2.0 / length)).astype(np.float32).astype(BF16))
    return forward_table, inverse_table


def settle(values):
    return lax.optimization_barrier(values.astype(BF16)).astype(F32)


def samples_into_spectra(values, forward_table, freq_total):
    out = jnp.einsum("kt,ptn->pkn", forward_table, values, preferred_element_type=F32)
    return out.reshape(values.shape[0], 2, freq_total, values.shape[2]).astype(BF16)


def spectra_into_samples(trace_spectra, inverse_table):
    flat = trace_spectra.reshape(trace_spectra.shape[0], -1, trace_spectra.shape[3])
    return jnp.einsum("tk,pkn->ptn", inverse_table, flat, preferred_element_type=F32)


def dense(spec, gated, real, imag, sign):
    dot = functools.partial(jnp.einsum, spec, preferred_element_type=F32)
    return jnp.stack(
        [dot(gated[:, 0], real) - sign * dot(gated[:, 1], imag), dot(gated[:, 0], imag) + sign * dot(gated[:, 1], real)], 1
    )


def general_device(initial, response, aperture, onset_rcv, onset_src):
    freq_devs, rblk_devs, sblk_devs = (lax.axis_size(a) for a in ("freq", "rblk", "sblk"))
    freq_index, rblk_index, sblk_index = (lax.axis_index(a) for a in ("freq", "rblk", "sblk"))
    freq_total = response.shape[0] * freq_devs
    samples = initial.shape[1] * freq_devs
    focal_all = onset_rcv.shape[0]
    forward_table, inverse_table = transform_tables(samples, freq_total)
    steps_axis = lax.iota(jnp.int32, samples)
    own_axis = freq_index * initial.shape[1] + lax.iota(jnp.int32, initial.shape[1])
    half_rows = focal_all // sblk_devs
    own_onsets = lax.dynamic_slice_in_dim(onset_rcv, sblk_index * half_rows, half_rows, 0)
    rcv_gate = (own_axis[None, :, None] < own_onsets[:, None, :]).astype(F32)
    src_rows = focal_all // (rblk_devs * freq_devs)
    src_first = rblk_index * (focal_all // rblk_devs) + freq_index * src_rows
    src_onsets = lax.dynamic_slice_in_dim(onset_src, src_first, src_rows, 0)
    src_gate = (steps_axis[None, :, None] < src_onsets[:, None, :]).astype(F32)
    mask_full = jnp.repeat(jnp.repeat(aperture, BLOCK, 1), BLOCK, 2).astype(BF16)
    gated = response * mask_full[:, None]
    own_forward = lax.dynamic_slice_in_dim(forward_table, freq_index * initial.shape[1], initial.shape[1], 1)
    own_inverse = lax.dynamic_slice_in_dim(inverse_table, freq_index * initial.shape[1], initial.shape[1], 0)
    current = initial
    for _ in range(ITERS):
        partial = samples_into_spectra(current, own_forward, freq_total)
        spec_back = lax.psum_scatter(partial.astype(F32), "freq", scatter_dimension=2, tiled=True).astype(BF16)
        spec_all = lax.all_gather(spec_back, "sblk", axis=0, tiled=True)
        down = lax.psum_scatter(
            settle(dense("euk,bek->beu", gated, spec_all[:, 0], spec_all[:, 1], 1.0)).astype(BF16),
            "rblk",
            scatter_dimension=0,
            tiled=True,
        )
        src_traces = lax.all_to_all(down, "freq", split_axis=0, concat_axis=2, tiled=True)
        upgoing = (src_gate * spectra_into_samples(src_traces, inverse_table)).astype(BF16)
        upspec = samples_into_spectra(upgoing, forward_table, freq_total)
        up_back = lax.all_to_all(upspec, "freq", split_axis=2, concat_axis=0, tiled=True)
        up_all = lax.all_gather(up_back, "rblk", axis=0, tiled=True)
        sums = dense("qao,bqa->bqo", gated, up_all[:, 0], up_all[:, 1], -1.0).astype(BF16)
        back = lax.psum_scatter(sums, "sblk", scatter_dimension=0, tiled=True)
        traces = lax.all_gather(back, "freq", axis=2, tiled=True)
        update = rcv_gate * spectra_into_samples(traces, own_inverse)
        current = (initial.astype(F32) - update).astype(BF16)
    return current


def fits(initial, response, aperture, onset_rcv, onset_src):
    freq_devs = lax.axis_size("freq")
    if lax.axis_size("rblk") != 2 or lax.axis_size("sblk") != 2 or freq_devs & (freq_devs - 1):
        return False
    whole_rows = initial.shape[0] % (max(2, CHUNKS) * ROWS * freq_devs) == 0
    whole_width = response.shape[2] % (2 * PARTS * BLOCK) == 0 and response.shape[3] % BLOCK == 0
    return whole_rows and whole_width and onset_rcv.shape[0] == 2 * initial.shape[0]


def chosen(*arrays):
    return on_device(*arrays) if fits(*arrays) else general_device(*arrays)


def solution(mesh):
    in_specs = (
        P(("group", "sblk"), "freq", "rblk"),
        P(("group", "freq"), None, "sblk", "rblk"),
        P(("group", "freq"), "sblk", "rblk"),
        P("group", "rblk"),
        P("group", "sblk"),
    )
    out_specs = P(("group", "sblk"), "freq", "rblk")
    return jax.shard_map(chosen, mesh=mesh, in_specs=in_specs, out_specs=out_specs, check_vma=False)
```

```python
import functools
import math

import jax
import jax.numpy as jnp
import numpy as np
from jax import lax
from jax.experimental import pallas as pl
from jax.experimental.pallas import tpu as pltpu
from jax.sharding import PartitionSpec as P

BLOCK = 128
ITERS = 2
ROWS = 8
CHUNKS = 2
PARTS = 2
VMEM_BYTES = 6 * 1024 * 1024

BF16 = jnp.bfloat16
F32 = jnp.float32


def ways(count):
    far = sorted(range(1, count), key=lambda step: (step.bit_length() < count.bit_length() - 1, step))
    return [0] + far


def field_rows(place, freq_devs, per_dev):
    rows = []
    for step in ways(freq_devs):
        first = (place ^ step) * per_dev
        for part in range(2):
            rows.extend((part, first + local) for local in range(per_dev))
    return rows


def fields(samples, freq_total):
    phase = (np.arange(1, freq_total + 1)[:, None] * np.arange(samples)[None, :]) % samples
    angle = phase * (2.0 * math.pi / samples)
    return np.stack([np.cos(angle), -np.sin(angle)])


def inverse_tables(samples, freq_devs, per_dev):
    exact = fields(samples, freq_devs * per_dev) * (2.0 / samples)
    own = samples // freq_devs
    out = []
    for place in range(freq_devs):
        part = [exact[c, j, place * own : (place + 1) * own] for c, j in field_rows(place, freq_devs, per_dev)]
        out.append(np.repeat(np.stack(part), ROWS, 0).T)
    return np.stack(out).astype(np.float32).astype(BF16)


def window_tables(samples, freq_devs, per_dev):
    freq_total = freq_devs * per_dev
    order = np.arange(1, freq_total + 1)
    unit = 2j * math.pi / samples
    diff = order[None, :] - order[:, None]
    total = order[None, :] + order[:, None]
    same = np.where(diff == 0, 0.0, 1.0 / (samples * (np.exp(unit * np.where(diff == 0, 1, diff)) - 1.0)))
    mixed = 1.0 / (samples * (np.exp(-unit * total) - 1.0))
    full = np.zeros((2, freq_total, 2, freq_total))
    full[0, :, 0, :] = same.real + mixed.real
    full[0, :, 1, :] = mixed.imag - same.imag
    full[1, :, 0, :] = same.imag + mixed.imag
    full[1, :, 1, :] = same.real - mixed.real
    out = []
    for place in range(freq_devs):
        rows = [c * freq_total + j for c, j in field_rows(place, freq_devs, per_dev)]
        flat = full.reshape(2 * freq_total, 2 * freq_total)[np.ix_(rows, rows)]
        out.append(np.kron(flat, np.eye(ROWS)))
    return np.stack(out).astype(np.float32).astype(BF16)


def call(body, scalars, inputs, outputs, grid, scratch=(), aliases=None, flops=0):
    in_arrays = [value for value, _ in inputs]
    bytes_all = sum(v.size * v.dtype.itemsize for v in in_arrays)
    bytes_all += sum(math.prod(s.shape) * s.dtype.itemsize for s, _ in outputs)
    return pl.pallas_call(
        body,
        grid_spec=pltpu.PrefetchScalarGridSpec(
            num_scalar_prefetch=len(scalars),
            grid=grid,
            in_specs=[spec for _, spec in inputs],
            out_specs=[spec for _, spec in outputs],
            scratch_shapes=list(scratch),
        ),
        out_shape=[shape for shape, _ in outputs],
        input_output_aliases=aliases or {},
        compiler_params=pltpu.CompilerParams(vmem_limit_bytes=VMEM_BYTES),
        cost_estimate=pl.CostEstimate(flops=flops, bytes_accessed=bytes_all, transcendentals=0),
    )(*scalars, *in_arrays)


def whole(array):
    zeros = (0,) * array.ndim
    return pl.BlockSpec(array.shape, lambda *_: zeros)


def sine_terms():
    square = (np.cos(np.linspace(0.0, math.pi, 200)) + 1.0) / 32.0
    y = np.sqrt(np.maximum(square, 1e-12))
    return [float(v) for v in np.polynomial.polynomial.polyfit(square, np.sin(2.0 * math.pi * y) / y, 6)]


def turned(turn):
    terms = sine_terms()

    def sine(y):
        square = y * y
        total = jnp.full_like(y, terms[-1])
        for term in terms[-2::-1]:
            total = total * square + term
        return total * y

    turn = turn - jnp.floor(turn + 0.5)
    size = jnp.abs(turn)
    folded = jnp.where(size > 0.25, jnp.where(turn > 0.0, 0.5, -0.5) - turn, turn)
    return sine(0.25 - size), sine(folded)


def first_spectra(initial, places, freq_devs, per_dev):
    rows, own, rcv = initial.shape
    samples = own * freq_devs
    tile = 2 * ROWS
    count = freq_devs * 2 * per_dev * ROWS

    def body(freq, rblk, sblk, x_ref, *rest):
        outs, spread_ref = rest[:freq_devs], rest[freq_devs]
        time = lax.broadcasted_iota(jnp.int32, (ROWS, own), 1) + freq[0] * own
        time = time.astype(F32) * (1.0 / samples)
        table = []
        for way in ways(freq_devs):
            waves = [turned(time * ((freq[0] ^ way) * per_dev + j + 1).astype(F32)) for j in range(per_dev)]
            table += [cosine for cosine, _ in waves] + [-sine for _, sine in waves]
        table = jnp.concatenate(table, 0)
        lane = lax.broadcasted_iota(jnp.int32, (count, own), 0) % ROWS
        for row in range(ROWS):
            spread_ref[:, row * own : (row + 1) * own] = jnp.where(lane == row, table, 0.0).astype(BF16)
        for at in range(rows // tile):
            parts = []
            for half in range(2):
                start = at * tile + half * ROWS
                flat = x_ref[start : start + ROWS].reshape(ROWS * own, rcv)
                value = jnp.dot(spread_ref[...], flat, preferred_element_type=F32)
                parts.append(value.reshape(freq_devs, 2, per_dev, ROWS, rcv))
            both = jnp.concatenate(parts, 3).astype(BF16)
            for step, out in enumerate(outs):
                out[:, :, at * tile : (at + 1) * tile, :] = both[step]

    shape = jax.ShapeDtypeStruct((2, per_dev, rows, rcv), BF16)
    return call(
        body,
        places,
        [(initial, whole(initial))],
        [(shape, whole(shape))] * freq_devs,
        (1,),
        scratch=[pltpu.VMEM((count, ROWS * own), BF16)],
        flops=2 * 2 * freq_devs * per_dev * own * rows * rcv,
    )


def masked_halves(response, aperture, places):
    per_dev, _, src, rcv = response.shape
    half = src // 2
    width = half // PARTS

    def body(_, rblk, __, flags, x_ref, *outs):
        lane = lax.broadcasted_iota(jnp.int32, (1, rcv), 1) // BLOCK
        for flip in (1, 0):
            for j in range(per_dev):
                for step in range(half // BLOCK):
                    block = (rblk[0] ^ flip) * (half // BLOCK) + step
                    on = flags[j, pl.ds(block, 1), :].astype(F32)
                    row = sum(jnp.where(lane == r, on[:, r : r + 1], 0.0) for r in range(rcv // BLOCK))
                    gate = jnp.broadcast_to(row, (BLOCK, rcv)).astype(BF16)
                    rows = pl.ds(pl.multiple_of(block * BLOCK, BLOCK), BLOCK)
                    part, at = divmod(step * BLOCK, width)
                    out = outs[flip * PARTS + part]
                    for c in range(2):
                        out[j, at : at + BLOCK, c * rcv : (c + 1) * rcv] = x_ref[j, c, rows, :] * gate

    shape = jax.ShapeDtypeStruct((per_dev, width, 2 * rcv), BF16)
    inputs = [(v, whole(v)) for v in (aperture, response)]
    outs = call(body, places, inputs, [(shape, whole(shape))] * (2 * PARTS), (1,))
    return list(outs[:PARTS]), list(outs[PARTS:])


def summed(parts):
    def body(*refs):
        total = sum(ref[...].astype(F32) for ref in refs[:-2])
        refs[-2][...] = total
        refs[-1][...] = total.astype(BF16)

    shapes = [jax.ShapeDtypeStruct(parts[0].shape, kind) for kind in (F32, BF16)]
    return call(body, (), [(v, whole(v)) for v in parts], [(v, whole(v)) for v in shapes], (1,))


def added(keep, received):
    lead, rows, rcv = keep.shape[:2], keep.shape[2], keep.shape[3]
    group = rows // CHUNKS

    def body(k_ref, r_ref, out, *groups):
        total = (k_ref[...] + r_ref[...].astype(F32)).astype(BF16)
        out[...] = total
        for index, ref in enumerate(groups):
            ref[...] = total[:, :, index * group : (index + 1) * group]

    shapes = [jax.ShapeDtypeStruct(lead + (count, rcv), BF16) for count in [rows] + [group] * CHUNKS]
    inputs = [(v, whole(v)) for v in (keep, received)]
    outs = call(body, (), inputs, [(v, whole(v)) for v in shapes], (1,))
    return outs[0], outs[1:]


def src_onsets(onset, places, half_rows, share, width):

    def body(freq, rblk, sblk, o_ref, own, other):
        lanes = pl.ds(pl.multiple_of(rblk[0] * width, BLOCK), width)
        for core, out in ((sblk[0], own), (1 - sblk[0], other)):
            spot = pl.multiple_of(core * half_rows + freq[0] * share, ROWS)
            out[...] = o_ref[pl.ds(spot, share), lanes]

    shape = jax.ShapeDtypeStruct((share, width), onset.dtype)
    return call(body, places, [(onset, whole(onset))], [(shape, whole(shape))] * 2, (1,))


def phase_tables(src, rcv, places, freq_devs, per_dev, samples, parts, rows):
    width = src[0].shape[1] // parts

    def fill(outs, value, to, freq):
        cosines, sines, fraction = outs
        value = value.astype(F32) * (1.0 / samples)
        fraction[:, to] = value
        for step, way in enumerate(ways(freq_devs)):
            for j in range(per_dev):
                order = ((freq[0] ^ way) * per_dev + j + 1).astype(F32)
                cosines[step, j, :, to], sines[step, j, :, to] = turned(value * order)

    def body(freq, _, sblk, own, other, r_ref, *outs):
        for part in range(parts):
            for spot, ref in enumerate((own, other)):
                at = (part * 2 + spot) * width
                fill(outs[:3], ref[:, part * width : (part + 1) * width], slice(at, at + width), freq)
        value = r_ref[pl.ds(pl.multiple_of(sblk[0] * rows, ROWS), rows), :]
        fill(outs[3:], value, slice(0, value.shape[1]), freq)

    shapes = []
    for count, total in ((src[0].shape[0], 2 * src[0].shape[1]), (rows, rcv.shape[1])):
        table = jax.ShapeDtypeStruct((freq_devs, per_dev, count, total), F32)
        shapes += [table, table, jax.ShapeDtypeStruct(table.shape[2:], F32)]
    outs = call(body, places, [(v, whole(v)) for v in (*src, rcv)], [(v, whole(v)) for v in shapes], (1,))
    return tuple(outs[:3]), tuple(outs[3:])


def down_products(before, spectra, parts, side, first, freq_place, freq_devs=0):
    _, per_dev, rows, rcv = spectra.shape
    flat = [pair[side] for part in parts for pair in part]
    width = flat[0].shape[1]
    total_width = before.shape[-1] if before is not None else first + width * len(flat)
    share = rows // freq_devs if freq_devs else 0
    old = [] if before is None else [before]

    def body(place_ref, *rest):
        held_ref, rest = (rest[0], rest[1:]) if old else (None, rest)
        ref, resp, outs = rest[0], rest[1 : 1 + len(flat)], rest[1 + len(flat) :]
        held = outs[-1]
        for j in range(per_dev):
            real, imag = ref[0, j], ref[1, j]
            lhs = jnp.concatenate([jnp.concatenate([real, -imag], 1), jnp.concatenate([imag, real], 1)], 0)
            for at, block in enumerate(resp):
                total = lax.dot_general(lhs, block[j], (((1,), (1,)), ((), ())), preferred_element_type=F32)
                to = slice(first + at * width, first + (at + 1) * width)
                for part in range(2):
                    value = total[part * rows : (part + 1) * rows]
                    held[part, j, :, to] = value + held_ref[part, j, :, to] if old else value
        if old:
            for to in (slice(0, first), slice(first + len(flat) * width, total_width)):
                if to.start < to.stop:
                    held[:, :, :, to] = held_ref[:, :, :, to]
        if freq_devs:
            for way, out in zip(ways(freq_devs), outs):
                start = pl.multiple_of((place_ref[0] ^ way) * share, share)
                out[...] = held[:, :, pl.ds(start, share), :].reshape(out.shape).astype(BF16)

    sums = (2, per_dev, rows, total_width)
    if freq_devs:
        shapes = [jax.ShapeDtypeStruct((2 * per_dev * share, total_width), BF16)] * freq_devs
    else:
        shapes = [jax.ShapeDtypeStruct(sums, F32)]
    outs = call(
        body,
        (freq_place,),
        [(v, whole(v)) for v in (*old, spectra, *flat)],
        [(v, whole(v)) for v in shapes],
        (1,),
        scratch=[pltpu.VMEM(sums, F32)] if freq_devs else [],
        flops=2 * 4 * per_dev * rows * len(flat) * width * rcv,
    )
    return outs if freq_devs else outs[0]


def mixed_fields(plain, cos, sin, matrix):
    tile = plain[0].shape[-1]
    turned = [
        jnp.stack([v[0] * c - v[1] * s, v[0] * s + v[1] * c]) for v, c, s in zip(plain, cos, sin)
    ]
    flat = [jnp.stack(v).reshape(matrix.shape[1], tile).astype(BF16) for v in (turned, plain)]
    mixed = jnp.dot(matrix, jnp.concatenate(flat, 1), preferred_element_type=F32)
    shape = (-1, 2) + plain[0].shape[1:]
    return mixed[:, :tile].reshape(shape), mixed[:, tile:].reshape(shape)


def unturned(up, low, value, cos, sin, part):
    real = cos * up[0] + sin * up[1] - low[0] + part * value[0]
    imag = cos * up[1] - sin * up[0] - low[1] + part * value[1]
    return jnp.stack([real, imag])


def tiles(width, body):
    def at(step, carry):
        body(pl.ds(pl.multiple_of(step * BLOCK, BLOCK), BLOCK))
        return carry

    lax.fori_loop(0, width // BLOCK, at, 0, unroll=2)


def windowed(messages, tables, matrix, freq_place, per_dev, share):
    cosines, sines, fraction = tables
    freq_devs = len(messages)
    width = messages[0].shape[-1]
    count = freq_devs * 2 * per_dev * ROWS

    def body(place_ref, c_ref, s_ref, f_ref, g_ref, *rest):
        refs, outs = rest[:freq_devs], rest[freq_devs:]
        matrix_here = g_ref[place_ref[0]]

        def one(at):
            data = [ref[:, at].astype(F32).reshape(2, per_dev, share, BLOCK) for ref in refs]
            made = [[] for _ in outs]
            for first in range(0, share, ROWS):
                cut = slice(first, first + ROWS)
                plain = [value[:, :, cut] for value in data]
                cos = [c_ref[step, :, cut, at] for step in range(freq_devs)]
                sin = [s_ref[step, :, cut, at] for step in range(freq_devs)]
                up, low = mixed_fields(plain, cos, sin, matrix_here)
                part = f_ref[cut, at]
                for step in range(freq_devs):
                    made[step].append(unturned(up[step], low[step], plain[step], cos[step], sin[step], part))
            for out, value in zip(outs, made):
                out[:, at] = jnp.concatenate(value, 2).reshape(out.shape[0], BLOCK).astype(BF16)

        tiles(width, one)

    inputs = (cosines, sines, fraction, matrix, *messages)
    return call(
        body,
        (freq_place,),
        [(v, whole(v)) for v in inputs],
        [(jax.ShapeDtypeStruct(v.shape, BF16), whole(v)) for v in messages],
        (1,),
        flops=2 * count * count * 2 * width * share // ROWS,
    )


def up_products(messages, parts, freq_place, rows, side):
    freq_devs = len(messages)
    flat = [pair[side] for part in parts for pair in part]
    per_dev, src, rcv = flat[0].shape[0], flat[0].shape[1], flat[0].shape[2] // 2
    share = rows // freq_devs
    total_width = src * len(flat)
    kind = BF16 if side else F32

    def body(place_ref, *rest):
        resp, refs = rest[: len(flat)], rest[len(flat) : len(flat) + freq_devs]
        out, held = rest[len(flat) + freq_devs :]
        for way, ref in zip(ways(freq_devs), refs):
            start = pl.multiple_of((place_ref[0] ^ way) * share, share)
            value = ref[...].reshape(2, per_dev, share, total_width)
            for part in range(2):
                for j in range(per_dev):
                    held[part, j, pl.ds(start, share), :] = value[part, j]
        for j in range(per_dev):
            both = jnp.concatenate([held[0, j], held[1, j]], 0)
            total = sum(
                jnp.dot(both[:, at * src : (at + 1) * src], ref[j], preferred_element_type=F32)
                for at, ref in enumerate(resp)
            )
            out[0, j] = (total[:rows, :rcv] + total[rows:, rcv:]).astype(kind)
            out[1, j] = (total[rows:, :rcv] - total[:rows, rcv:]).astype(kind)

    shape = jax.ShapeDtypeStruct((2, per_dev, rows, rcv), kind)
    (out,) = call(
        body,
        (freq_place,),
        [(v, whole(v)) for v in (*flat, *messages)],
        [(shape, whole(shape))],
        (1,),
        scratch=[pltpu.VMEM((2, per_dev, rows, total_width), BF16)],
        flops=2 * 4 * per_dev * rows * total_width * rcv,
    )
    return out


def piece(ref, index, group, cut):
    first = index * group if ref.shape[2] > group else 0
    return slice(first + cut.start, first + cut.stop)


def next_spectra(sums, by_group, tables, matrix, freq_place):
    cosines, sines, fraction = tables
    freq_devs = len(by_group[0])
    _, per_dev, rows, rcv = sums.shape
    group = rows // len(by_group)
    flat = [v for messages in by_group for v in messages]
    count = freq_devs * 2 * per_dev * ROWS
    own = 2 * per_dev * ROWS

    def body(place_ref, u_ref, c_ref, s_ref, f_ref, g_ref, *rest):
        out = rest[-1]
        matrix_here = g_ref[place_ref[0], :own]

        def one(at):
            for base in range(0, rows, 2 * ROWS):
                pair = slice(base, base + 2 * ROWS)
                index = base // group
                refs = rest[index * freq_devs : (index + 1) * freq_devs]
                local = slice(base - index * group, base - index * group + 2 * ROWS)
                data = [ref[:, :, piece(ref, index, group, local), at].astype(F32) for ref in refs]
                made = []
                for half in range(2):
                    plain = [value[:, :, half * ROWS : (half + 1) * ROWS] for value in data]
                    cut = slice(base + half * ROWS, base + (half + 1) * ROWS)
                    cos = [c_ref[step, :, cut, at] for step in range(freq_devs)]
                    sin = [s_ref[step, :, cut, at] for step in range(freq_devs)]
                    up, low = mixed_fields(plain, cos, sin, matrix_here)
                    change = unturned(up[0], low[0], plain[0], cos[0], sin[0], f_ref[cut, at])
                    made.append(u_ref[:, :, cut, at] - change)
                out[:, :, pair, at] = jnp.concatenate(made, 2).astype(BF16)

        tiles(rcv, one)

    inputs = (sums, cosines, sines, fraction, matrix, *flat)
    shape = jax.ShapeDtypeStruct(sums.shape, BF16)
    (out,) = call(
        body,
        (freq_place,),
        [(v, whole(v)) for v in inputs],
        [(shape, whole(shape))],
        (1,),
        flops=2 * own * count * 2 * rcv * rows // ROWS,
    )
    return out


def updated(initial, onset, messages, table, places, first, rows, target):
    freq_devs = len(messages)
    half_rows, own, rcv = initial.shape
    per_dev = messages[0].shape[1]
    tile = 2 * ROWS
    count = table.shape[2]

    def body(place_ref, _, sblk, x_ref, o_ref, t_ref, *rest):
        refs = rest[:freq_devs]
        out, spread_ref = rest[-2:]
        step = pl.program_id(0)

        @pl.when(step == 0)
        def _():
            base = t_ref[place_ref[0]].astype(F32)
            lane = lax.broadcasted_iota(jnp.int32, (own, count), 1) % ROWS
            for row in range(ROWS):
                spread_ref[row * own : (row + 1) * own] = jnp.where(lane == row, base, 0.0).astype(BF16)

        data = []
        for ref in refs:
            skip = first if ref.shape[2] > rows else 0
            here = pl.ds(pl.multiple_of(skip + step * tile, tile), tile)
            data.append(ref[:, :, here, :].astype(F32))
        onsets = o_ref[pl.ds(pl.multiple_of(sblk[0] * half_rows + first + step * tile, tile), tile), :]
        time = lax.broadcasted_iota(jnp.int32, (own, rcv), 0) + place_ref[0] * own
        for half in range(2):
            cut = slice(half * ROWS, (half + 1) * ROWS)
            flat = jnp.stack([v[:, :, cut] for v in data]).reshape(count, rcv).astype(BF16)
            change = jnp.dot(spread_ref[...], flat, preferred_element_type=F32)
            for row in range(ROWS):
                spot = half * ROWS + row
                on = time < onsets[spot : spot + 1, :]
                moved = jnp.where(on, change[row * own : (row + 1) * own], 0.0)
                out[spot] = (x_ref[first + step * tile + spot].astype(F32) - moved).astype(BF16)

    inputs = [(v, whole(v)) for v in (initial, onset, table, *messages)]
    aliases = {}
    if target is not None:
        inputs.append((target, pl.BlockSpec(memory_space=pl.ANY)))
        aliases = {len(places) + len(inputs) - 1: 0}
    (out,) = call(
        body,
        places,
        inputs,
        [(jax.ShapeDtypeStruct(initial.shape, BF16), pl.BlockSpec((tile, own, rcv), lambda i, *_: (first // tile + i, 0, 0)))],
        (rows // tile,),
        scratch=[pltpu.VMEM((ROWS * own, count), BF16)],
        aliases=aliases,
        flops=2 * 2 * freq_devs * per_dev * own * rows * rcv,
    )
    return out


def exchanged(value, axis, step):
    return lax.ppermute(value, axis, [(i, i ^ step) for i in range(lax.axis_size(axis))])


def dealt_out(parts):
    return [exchanged(part, "freq", step) if step else part for part, step in zip(parts, ways(len(parts)))]


def spread(value, groups, count):
    top = count // 2
    far = [{top: exchanged(group, "freq", top)} for group in groups]
    near = {0: value}
    bit = top // 2
    while bit:
        for held in (near, *far):
            held.update({way | bit: exchanged(held[way], "freq", bit) for way in sorted(held)})
        bit //= 2
    return [[{**near, **held}[way] for way in ways(count)] for held in far]


def on_device(initial, response, aperture, onset_rcv, onset_src):
    freq_devs = lax.axis_size("freq")
    per_dev = response.shape[0]
    samples = initial.shape[1] * freq_devs
    half_rows = initial.shape[0]
    src_width = response.shape[2] // 2
    rows = half_rows // CHUNKS
    share = half_rows // freq_devs
    places = tuple(lax.axis_index(axis).reshape(1) for axis in ("freq", "rblk", "sblk"))
    freq_place = places[0]
    inverse = jnp.asarray(inverse_tables(samples, freq_devs, per_dev))
    matrix = jnp.asarray(window_tables(samples, freq_devs, per_dev))

    kept, sent = masked_halves(response, aperture, places)
    moved = [exchanged(v, "rblk", 1) for v in sent]
    kept_pair = [exchanged(v, "sblk", 1) for v in kept]
    sums, spectra = summed(dealt_out(first_spectra(initial, places, freq_devs, per_dev)))
    far = exchanged(spectra, "rblk", 1)
    moved_pair = []
    for index in range(PARTS):
        if index:
            moved[index], far = lax.optimization_barrier((moved[index], far))
        else:
            moved[index], spectra = lax.optimization_barrier((moved[index], spectra))
        moved_pair.append(exchanged(moved[index], "sblk", 1))
    parts = [((kept[i], moved[i]), (kept_pair[i], moved_pair[i])) for i in range(PARTS)]

    own, other = src_onsets(onset_src, places, half_rows, share, src_width)
    onsets = (own, exchanged(other, "sblk", 1))
    src_tables, rcv_tables = phase_tables(onsets, onset_rcv, places, freq_devs, per_dev, samples, PARTS, half_rows)

    near, result = spectra, None
    for step in range(ITERS):
        held = down_products(None, near, parts, 0, 0, freq_place)
        at = 0 if step else PARTS - 1
        if at:
            held = down_products(held, far, parts[:at], 1, 0, freq_place)
        first = at * 2 * kept[0].shape[1]
        messages = dealt_out(down_products(held, far, parts[at:], 1, first, freq_place, freq_devs))
        messages = dealt_out(windowed(messages, src_tables, matrix, freq_place, per_dev, share))
        received = exchanged(up_products(messages, parts, freq_place, half_rows, 1), "rblk", 1)
        keep = up_products(messages, parts, freq_place, half_rows, 0)
        back = spread(*added(keep, received), freq_devs)
        if step < ITERS - 1:
            near = next_spectra(sums, back, rcv_tables, matrix, freq_place)
            far = exchanged(near, "rblk", 1)
        else:
            for chunk, messages in enumerate(back):
                result = updated(initial, onset_rcv, messages, inverse, places, chunk * rows, rows, result)
    return result


def transform_tables(length, count):
    table = fields(length, count).reshape(2 * count, length)
    forward_table = jnp.asarray(table.astype(np.float32).astype(BF16))
    inverse_table = jnp.asarray((table.T * (2.0 / length)).astype(np.float32).astype(BF16))
    return forward_table, inverse_table


def settle(values):
    return lax.optimization_barrier(values.astype(BF16)).astype(F32)


def samples_into_spectra(values, forward_table, freq_total):
    out = jnp.einsum("kt,ptn->pkn", forward_table, values, preferred_element_type=F32)
    return out.reshape(values.shape[0], 2, freq_total, values.shape[2]).astype(BF16)


def spectra_into_samples(trace_spectra, inverse_table):
    flat = trace_spectra.reshape(trace_spectra.shape[0], -1, trace_spectra.shape[3])
    return jnp.einsum("tk,pkn->ptn", inverse_table, flat, preferred_element_type=F32)


def dense(spec, gated, real, imag, sign):
    dot = functools.partial(jnp.einsum, spec, preferred_element_type=F32)
    return jnp.stack(
        [dot(gated[:, 0], real) - sign * dot(gated[:, 1], imag), dot(gated[:, 0], imag) + sign * dot(gated[:, 1], real)], 1
    )


def general_device(initial, response, aperture, onset_rcv, onset_src):
    freq_devs, rblk_devs, sblk_devs = (lax.axis_size(a) for a in ("freq", "rblk", "sblk"))
    freq_index, rblk_index, sblk_index = (lax.axis_index(a) for a in ("freq", "rblk", "sblk"))
    freq_total = response.shape[0] * freq_devs
    samples = initial.shape[1] * freq_devs
    focal_all = onset_rcv.shape[0]
    forward_table, inverse_table = transform_tables(samples, freq_total)
    steps_axis = lax.iota(jnp.int32, samples)
    own_axis = freq_index * initial.shape[1] + lax.iota(jnp.int32, initial.shape[1])
    half_rows = focal_all // sblk_devs
    own_onsets = lax.dynamic_slice_in_dim(onset_rcv, sblk_index * half_rows, half_rows, 0)
    rcv_gate = (own_axis[None, :, None] < own_onsets[:, None, :]).astype(F32)
    src_rows = focal_all // (rblk_devs * freq_devs)
    src_first = rblk_index * (focal_all // rblk_devs) + freq_index * src_rows
    src_onsets = lax.dynamic_slice_in_dim(onset_src, src_first, src_rows, 0)
    src_gate = (steps_axis[None, :, None] < src_onsets[:, None, :]).astype(F32)
    mask_full = jnp.repeat(jnp.repeat(aperture, BLOCK, 1), BLOCK, 2).astype(BF16)
    gated = response * mask_full[:, None]
    own_forward = lax.dynamic_slice_in_dim(forward_table, freq_index * initial.shape[1], initial.shape[1], 1)
    own_inverse = lax.dynamic_slice_in_dim(inverse_table, freq_index * initial.shape[1], initial.shape[1], 0)
    current = initial
    for _ in range(ITERS):
        partial = samples_into_spectra(current, own_forward, freq_total)
        spec_back = lax.psum_scatter(partial.astype(F32), "freq", scatter_dimension=2, tiled=True).astype(BF16)
        spec_all = lax.all_gather(spec_back, "sblk", axis=0, tiled=True)
        down = lax.psum_scatter(
            settle(dense("euk,bek->beu", gated, spec_all[:, 0], spec_all[:, 1], 1.0)).astype(BF16),
            "rblk",
            scatter_dimension=0,
            tiled=True,
        )
        src_traces = lax.all_to_all(down, "freq", split_axis=0, concat_axis=2, tiled=True)
        upgoing = (src_gate * spectra_into_samples(src_traces, inverse_table)).astype(BF16)
        upspec = samples_into_spectra(upgoing, forward_table, freq_total)
        up_back = lax.all_to_all(upspec, "freq", split_axis=2, concat_axis=0, tiled=True)
        up_all = lax.all_gather(up_back, "rblk", axis=0, tiled=True)
        sums = dense("qao,bqa->bqo", gated, up_all[:, 0], up_all[:, 1], -1.0).astype(BF16)
        back = lax.psum_scatter(sums, "sblk", scatter_dimension=0, tiled=True)
        traces = lax.all_gather(back, "freq", axis=2, tiled=True)
        update = rcv_gate * spectra_into_samples(traces, own_inverse)
        current = (initial.astype(F32) - update).astype(BF16)
    return current


def fits(initial, response, aperture, onset_rcv, onset_src):
    freq_devs = lax.axis_size("freq")
    if lax.axis_size("rblk") != 2 or lax.axis_size("sblk") != 2 or freq_devs & (freq_devs - 1):
        return False
    whole_rows = initial.shape[0] % (max(2, CHUNKS) * ROWS * freq_devs) == 0
    whole_width = response.shape[2] % (2 * PARTS * BLOCK) == 0 and response.shape[3] % BLOCK == 0
    return whole_rows and whole_width and onset_rcv.shape[0] == 2 * initial.shape[0]


def chosen(*arrays):
    return on_device(*arrays) if fits(*arrays) else general_device(*arrays)


def solution(mesh):
    in_specs = (
        P(("group", "sblk"), "freq", "rblk"),
        P(("group", "freq"), None, "sblk", "rblk"),
        P(("group", "freq"), "sblk", "rblk"),
        P("group", "rblk"),
        P("group", "sblk"),
    )
    out_specs = P(("group", "sblk"), "freq", "rblk")
    return jax.shard_map(chosen, mesh=mesh, in_specs=in_specs, out_specs=out_specs, check_vma=False)
```

```python
import functools
import math

import jax
import jax.numpy as jnp
import numpy as np
from jax import lax
from jax.experimental import pallas as pl
from jax.experimental.pallas import tpu as pltpu
from jax.sharding import PartitionSpec as P

BLOCK = 128
ITERS = 2
ROWS = 8
CHUNKS = 2
PARTS = 2
VMEM_BYTES = 6 * 1024 * 1024

BF16 = jnp.bfloat16
F32 = jnp.float32


def ways(count):
    far = sorted(range(1, count), key=lambda step: (step.bit_length() < count.bit_length() - 1, step))
    return [0] + far


def field_rows(place, freq_devs, per_dev):
    rows = []
    for step in ways(freq_devs):
        first = (place ^ step) * per_dev
        for part in range(2):
            rows.extend((part, first + local) for local in range(per_dev))
    return rows


def fields(samples, freq_total):
    phase = (np.arange(1, freq_total + 1)[:, None] * np.arange(samples)[None, :]) % samples
    angle = phase * (2.0 * math.pi / samples)
    return np.stack([np.cos(angle), -np.sin(angle)])


def inverse_tables(samples, freq_devs, per_dev):
    exact = fields(samples, freq_devs * per_dev) * (2.0 / samples)
    own = samples // freq_devs
    out = []
    for place in range(freq_devs):
        part = [exact[c, j, place * own : (place + 1) * own] for c, j in field_rows(place, freq_devs, per_dev)]
        out.append(np.repeat(np.stack(part), ROWS, 0).T)
    return np.stack(out).astype(np.float32).astype(BF16)


def window_tables(samples, freq_devs, per_dev):
    freq_total = freq_devs * per_dev
    order = np.arange(1, freq_total + 1)
    unit = 2j * math.pi / samples
    diff = order[None, :] - order[:, None]
    total = order[None, :] + order[:, None]
    same = np.where(diff == 0, 0.0, 1.0 / (samples * (np.exp(unit * np.where(diff == 0, 1, diff)) - 1.0)))
    mixed = 1.0 / (samples * (np.exp(-unit * total) - 1.0))
    full = np.zeros((2, freq_total, 2, freq_total))
    full[0, :, 0, :] = same.real + mixed.real
    full[0, :, 1, :] = mixed.imag - same.imag
    full[1, :, 0, :] = same.imag + mixed.imag
    full[1, :, 1, :] = same.real - mixed.real
    out = []
    for place in range(freq_devs):
        rows = [c * freq_total + j for c, j in field_rows(place, freq_devs, per_dev)]
        flat = full.reshape(2 * freq_total, 2 * freq_total)[np.ix_(rows, rows)]
        out.append(np.kron(flat, np.eye(ROWS)))
    return np.stack(out).astype(np.float32).astype(BF16)


def call(body, scalars, inputs, outputs, grid, scratch=(), aliases=None, flops=0):
    in_arrays = [value for value, _ in inputs]
    bytes_all = sum(v.size * v.dtype.itemsize for v in in_arrays)
    bytes_all += sum(math.prod(s.shape) * s.dtype.itemsize for s, _ in outputs)
    return pl.pallas_call(
        body,
        grid_spec=pltpu.PrefetchScalarGridSpec(
            num_scalar_prefetch=len(scalars),
            grid=grid,
            in_specs=[spec for _, spec in inputs],
            out_specs=[spec for _, spec in outputs],
            scratch_shapes=list(scratch),
        ),
        out_shape=[shape for shape, _ in outputs],
        input_output_aliases=aliases or {},
        compiler_params=pltpu.CompilerParams(vmem_limit_bytes=VMEM_BYTES),
        cost_estimate=pl.CostEstimate(flops=flops, bytes_accessed=bytes_all, transcendentals=0),
    )(*scalars, *in_arrays)


def whole(array):
    zeros = (0,) * array.ndim
    return pl.BlockSpec(array.shape, lambda *_: zeros)


def sine_terms():
    square = (np.cos(np.linspace(0.0, math.pi, 200)) + 1.0) / 32.0
    y = np.sqrt(np.maximum(square, 1e-12))
    return [float(v) for v in np.polynomial.polynomial.polyfit(square, np.sin(2.0 * math.pi * y) / y, 6)]


def turned(turn):
    terms = sine_terms()

    def sine(y):
        square = y * y
        total = jnp.full_like(y, terms[-1])
        for term in terms[-2::-1]:
            total = total * square + term
        return total * y

    turn = turn - jnp.floor(turn + 0.5)
    size = jnp.abs(turn)
    folded = jnp.where(size > 0.25, jnp.where(turn > 0.0, 0.5, -0.5) - turn, turn)
    return sine(0.25 - size), sine(folded)


def first_spectra(initial, places, freq_devs, per_dev):
    rows, own, rcv = initial.shape
    samples = own * freq_devs
    tile = 2 * ROWS
    count = freq_devs * 2 * per_dev * ROWS

    def body(freq, rblk, sblk, x_ref, *rest):
        outs, spread_ref = rest[:freq_devs], rest[freq_devs]
        time = lax.broadcasted_iota(jnp.int32, (ROWS, own), 1) + freq[0] * own
        time = time.astype(F32) * (1.0 / samples)
        table = []
        for way in ways(freq_devs):
            waves = [turned(time * ((freq[0] ^ way) * per_dev + j + 1).astype(F32)) for j in range(per_dev)]
            table += [cosine for cosine, _ in waves] + [-sine for _, sine in waves]
        table = jnp.concatenate(table, 0)
        lane = lax.broadcasted_iota(jnp.int32, (count, own), 0) % ROWS
        for row in range(ROWS):
            spread_ref[:, row * own : (row + 1) * own] = jnp.where(lane == row, table, 0.0).astype(BF16)
        for at in range(rows // tile):
            parts = []
            for half in range(2):
                start = at * tile + half * ROWS
                flat = x_ref[start : start + ROWS].reshape(ROWS * own, rcv)
                value = jnp.dot(spread_ref[...], flat, preferred_element_type=F32)
                parts.append(value.reshape(freq_devs, 2, per_dev, ROWS, rcv))
            both = jnp.concatenate(parts, 3).astype(BF16)
            for step, out in enumerate(outs):
                out[:, :, at * tile : (at + 1) * tile, :] = both[step]

    shape = jax.ShapeDtypeStruct((2, per_dev, rows, rcv), BF16)
    return call(
        body,
        places,
        [(initial, whole(initial))],
        [(shape, whole(shape))] * freq_devs,
        (1,),
        scratch=[pltpu.VMEM((count, ROWS * own), BF16)],
        flops=2 * 2 * freq_devs * per_dev * own * rows * rcv,
    )


def masked_halves(response, aperture, places):
    per_dev, _, src, rcv = response.shape
    half = src // 2
    width = half // PARTS

    def body(_, rblk, __, flags, x_ref, *outs):
        lane = lax.broadcasted_iota(jnp.int32, (1, rcv), 1) // BLOCK
        for flip in (1, 0):
            for j in range(per_dev):
                for step in range(half // BLOCK):
                    block = (rblk[0] ^ flip) * (half // BLOCK) + step
                    on = flags[j, pl.ds(block, 1), :].astype(F32)
                    row = sum(jnp.where(lane == r, on[:, r : r + 1], 0.0) for r in range(rcv // BLOCK))
                    gate = jnp.broadcast_to(row, (BLOCK, rcv)).astype(BF16)
                    rows = pl.ds(pl.multiple_of(block * BLOCK, BLOCK), BLOCK)
                    part, at = divmod(step * BLOCK, width)
                    out = outs[flip * PARTS + part]
                    for c in range(2):
                        out[j, at : at + BLOCK, c * rcv : (c + 1) * rcv] = x_ref[j, c, rows, :] * gate

    shape = jax.ShapeDtypeStruct((per_dev, width, 2 * rcv), BF16)
    inputs = [(v, whole(v)) for v in (aperture, response)]
    outs = call(body, places, inputs, [(shape, whole(shape))] * (2 * PARTS), (1,))
    return list(outs[:PARTS]), list(outs[PARTS:])


def summed(parts):
    def body(*refs):
        total = sum(ref[...].astype(F32) for ref in refs[:-2])
        refs[-2][...] = total
        refs[-1][...] = total.astype(BF16)

    shapes = [jax.ShapeDtypeStruct(parts[0].shape, kind) for kind in (F32, BF16)]
    return call(body, (), [(v, whole(v)) for v in parts], [(v, whole(v)) for v in shapes], (1,))


def added(keep, received):
    def body(k_ref, r_ref, out):
        out[...] = (k_ref[...] + r_ref[...].astype(F32)).astype(BF16)

    shape = jax.ShapeDtypeStruct(keep.shape, BF16)
    (out,) = call(body, (), [(v, whole(v)) for v in (keep, received)], [(shape, whole(shape))], (1,))
    return out


def added_to(keep, received, before):
    group, rcv = received.shape[2:]
    rows = group * (len(before) + 1)

    def body(k_ref, r_ref, *rest):
        refs, (out, together) = rest[: len(before)], rest[len(before) :]
        total = (k_ref[...] + r_ref[...].astype(F32)).astype(BF16)
        out[...] = total
        for at, ref in enumerate(refs):
            together[:, :, at * group : (at + 1) * group] = ref[...]
        together[:, :, rows - group :] = total

    shapes = [jax.ShapeDtypeStruct(keep.shape[:2] + (count, rcv), BF16) for count in (group, rows)]
    inputs = [(v, whole(v)) for v in (keep, received, *before)]
    return call(body, (), inputs, [(v, whole(v)) for v in shapes], (1,))


def src_onsets(onset, places, half_rows, share, width):

    def body(freq, rblk, sblk, o_ref, own, other):
        lanes = pl.ds(pl.multiple_of(rblk[0] * width, BLOCK), width)
        for core, out in ((sblk[0], own), (1 - sblk[0], other)):
            spot = pl.multiple_of(core * half_rows + freq[0] * share, ROWS)
            out[...] = o_ref[pl.ds(spot, share), lanes]

    shape = jax.ShapeDtypeStruct((share, width), onset.dtype)
    return call(body, places, [(onset, whole(onset))], [(shape, whole(shape))] * 2, (1,))


def phase_tables(src, rcv, places, freq_devs, per_dev, samples, parts, rows):
    width = src[0].shape[1] // parts

    def fill(outs, value, to, freq):
        cosines, sines, fraction = outs
        value = value.astype(F32) * (1.0 / samples)
        fraction[:, to] = value
        for step, way in enumerate(ways(freq_devs)):
            for j in range(per_dev):
                order = ((freq[0] ^ way) * per_dev + j + 1).astype(F32)
                cosines[step, j, :, to], sines[step, j, :, to] = turned(value * order)

    def body(freq, _, sblk, own, other, r_ref, *outs):
        for part in range(parts):
            for spot, ref in enumerate((own, other)):
                at = (part * 2 + spot) * width
                fill(outs[:3], ref[:, part * width : (part + 1) * width], slice(at, at + width), freq)
        value = r_ref[pl.ds(pl.multiple_of(sblk[0] * rows, ROWS), rows), :]
        fill(outs[3:], value, slice(0, value.shape[1]), freq)

    shapes = []
    for count, total in ((src[0].shape[0], 2 * src[0].shape[1]), (rows, rcv.shape[1])):
        table = jax.ShapeDtypeStruct((freq_devs, per_dev, count, total), F32)
        shapes += [table, table, jax.ShapeDtypeStruct(table.shape[2:], F32)]
    outs = call(body, places, [(v, whole(v)) for v in (*src, rcv)], [(v, whole(v)) for v in shapes], (1,))
    return tuple(outs[:3]), tuple(outs[3:])


def down_products(before, spectra, parts, side, first, freq_place, freq_devs=0):
    _, per_dev, _, rcv = spectra[0].shape
    rows = sum(v.shape[2] for v in spectra)
    flat = [pair[side] for part in parts for pair in part]
    width = flat[0].shape[1]
    total_width = before.shape[-1] if before is not None else first + width * len(flat)
    share = rows // freq_devs if freq_devs else 0
    old = [] if before is None else [before]

    def body(place_ref, *rest):
        held_ref, rest = (rest[0], rest[1:]) if old else (None, rest)
        refs, resp, outs = rest[: len(spectra)], rest[len(spectra) : len(spectra) + len(flat)], rest[len(spectra) + len(flat) :]
        held = outs[-1]
        for j in range(per_dev):
            real = jnp.concatenate([ref[0, j] for ref in refs], 0)
            imag = jnp.concatenate([ref[1, j] for ref in refs], 0)
            lhs = jnp.concatenate([jnp.concatenate([real, -imag], 1), jnp.concatenate([imag, real], 1)], 0)
            for at, ref in enumerate(resp):
                total = lax.dot_general(lhs, ref[j], (((1,), (1,)), ((), ())), preferred_element_type=F32)
                to = slice(first + at * width, first + (at + 1) * width)
                for part in range(2):
                    value = total[part * rows : (part + 1) * rows]
                    held[part, j, :, to] = value + held_ref[part, j, :, to] if old else value
        if old:
            for to in (slice(0, first), slice(first + len(flat) * width, total_width)):
                if to.start < to.stop:
                    held[:, :, :, to] = held_ref[:, :, :, to]
        if freq_devs:
            for way, out in zip(ways(freq_devs), outs):
                start = pl.multiple_of((place_ref[0] ^ way) * share, share)
                out[...] = held[:, :, pl.ds(start, share), :].reshape(out.shape).astype(BF16)

    sums = (2, per_dev, rows, total_width)
    if freq_devs:
        shapes = [jax.ShapeDtypeStruct((2 * per_dev * share, total_width), BF16)] * freq_devs
    else:
        shapes = [jax.ShapeDtypeStruct(sums, F32)]
    outs = call(
        body,
        (freq_place,),
        [(v, whole(v)) for v in (*old, *spectra, *flat)],
        [(v, whole(v)) for v in shapes],
        (1,),
        scratch=[pltpu.VMEM(sums, F32)] if freq_devs else [],
        flops=2 * 4 * per_dev * rows * len(flat) * width * rcv,
    )
    return outs if freq_devs else outs[0]


def mixed_fields(plain, cos, sin, matrix):
    tile = plain[0].shape[-1]
    turned = [
        jnp.stack([v[0] * c - v[1] * s, v[0] * s + v[1] * c]) for v, c, s in zip(plain, cos, sin)
    ]
    flat = [jnp.stack(v).reshape(matrix.shape[1], tile).astype(BF16) for v in (turned, plain)]
    mixed = jnp.dot(matrix, jnp.concatenate(flat, 1), preferred_element_type=F32)
    shape = (-1, 2) + plain[0].shape[1:]
    return mixed[:, :tile].reshape(shape), mixed[:, tile:].reshape(shape)


def unturned(up, low, value, cos, sin, part):
    real = cos * up[0] + sin * up[1] - low[0] + part * value[0]
    imag = cos * up[1] - sin * up[0] - low[1] + part * value[1]
    return jnp.stack([real, imag])


def tiles(width, body):
    def at(step, carry):
        body(pl.ds(pl.multiple_of(step * BLOCK, BLOCK), BLOCK))
        return carry

    lax.fori_loop(0, width // BLOCK, at, 0, unroll=4)


def windowed(messages, tables, matrix, freq_place, per_dev, share):
    cosines, sines, fraction = tables
    freq_devs = len(messages)
    width = messages[0].shape[-1]
    count = freq_devs * 2 * per_dev * ROWS

    def body(place_ref, c_ref, s_ref, f_ref, g_ref, *rest):
        refs, outs = rest[:freq_devs], rest[freq_devs:]
        matrix_here = g_ref[place_ref[0]]

        def one(at):
            data = [ref[:, at].astype(F32).reshape(2, per_dev, share, BLOCK) for ref in refs]
            made = [[] for _ in outs]
            for first in range(0, share, ROWS):
                cut = slice(first, first + ROWS)
                plain = [value[:, :, cut] for value in data]
                cos = [c_ref[step, :, cut, at] for step in range(freq_devs)]
                sin = [s_ref[step, :, cut, at] for step in range(freq_devs)]
                up, low = mixed_fields(plain, cos, sin, matrix_here)
                part = f_ref[cut, at]
                for step in range(freq_devs):
                    made[step].append(unturned(up[step], low[step], plain[step], cos[step], sin[step], part))
            for out, value in zip(outs, made):
                out[:, at] = jnp.concatenate(value, 2).reshape(out.shape[0], BLOCK).astype(BF16)

        tiles(width, one)

    inputs = (cosines, sines, fraction, matrix, *messages)
    return call(
        body,
        (freq_place,),
        [(v, whole(v)) for v in inputs],
        [(jax.ShapeDtypeStruct(v.shape, BF16), whole(v)) for v in messages],
        (1,),
        flops=2 * count * count * 2 * width * share // ROWS,
    )


def up_products(messages, parts, freq_place, rows, side):
    freq_devs = len(messages)
    flat = [pair[side] for part in parts for pair in part]
    per_dev, src, rcv = flat[0].shape[0], flat[0].shape[1], flat[0].shape[2] // 2
    group = rows // CHUNKS
    share = rows // freq_devs
    total_width = src * len(flat)
    kind = BF16 if side else F32

    def body(place_ref, *rest):
        resp, refs = rest[: len(flat)], rest[len(flat) : len(flat) + freq_devs]
        outs, held = rest[len(flat) + freq_devs : -1], rest[-1]
        for way, ref in zip(ways(freq_devs), refs):
            start = pl.multiple_of((place_ref[0] ^ way) * share, share)
            value = ref[...].reshape(2, per_dev, share, total_width)
            for part in range(2):
                for j in range(per_dev):
                    held[part, j, pl.ds(start, share), :] = value[part, j]
        for j in range(per_dev):
            both = jnp.concatenate([held[0, j], held[1, j]], 0)
            total = sum(
                jnp.dot(both[:, at * src : (at + 1) * src], ref[j], preferred_element_type=F32)
                for at, ref in enumerate(resp)
            )
            real = total[:rows, :rcv] + total[rows:, rcv:]
            imag = total[rows:, :rcv] - total[:rows, rcv:]
            for index, out in enumerate(outs):
                cut = slice(index * group, (index + 1) * group)
                out[0, j] = real[cut].astype(kind)
                out[1, j] = imag[cut].astype(kind)

    shape = jax.ShapeDtypeStruct((2, per_dev, group, rcv), kind)
    return call(
        body,
        (freq_place,),
        [(v, whole(v)) for v in (*flat, *messages)],
        [(shape, whole(shape))] * CHUNKS,
        (1,),
        scratch=[pltpu.VMEM((2, per_dev, rows, total_width), BF16)],
        flops=2 * 4 * per_dev * rows * total_width * rcv,
    )


def next_spectra(sums, messages, tables, matrix, freq_place, first_row):
    cosines, sines, fraction = tables
    freq_devs = len(messages)
    _, per_dev, rows, rcv = messages[0].shape
    count = freq_devs * 2 * per_dev * ROWS
    own = 2 * per_dev * ROWS

    def body(place_ref, u_ref, c_ref, s_ref, f_ref, g_ref, *rest):
        refs, out = rest[:freq_devs], rest[freq_devs]
        matrix_here = g_ref[place_ref[0], :own]

        def one(at):
            for base in range(0, rows, 2 * ROWS):
                pair = slice(base, base + 2 * ROWS)
                data = [ref[:, :, pair, at].astype(F32) for ref in refs]
                made = []
                for half in range(2):
                    plain = [value[:, :, half * ROWS : (half + 1) * ROWS] for value in data]
                    cut = slice(first_row + base + half * ROWS, first_row + base + (half + 1) * ROWS)
                    cos = [c_ref[step, :, cut, at] for step in range(freq_devs)]
                    sin = [s_ref[step, :, cut, at] for step in range(freq_devs)]
                    up, low = mixed_fields(plain, cos, sin, matrix_here)
                    change = unturned(up[0], low[0], plain[0], cos[0], sin[0], f_ref[cut, at])
                    made.append(u_ref[:, :, cut, at] - change)
                out[:, :, pair, at] = jnp.concatenate(made, 2).astype(BF16)

        tiles(rcv, one)

    inputs = (sums, cosines, sines, fraction, matrix, *messages)
    shape = jax.ShapeDtypeStruct(messages[0].shape, BF16)
    (out,) = call(
        body,
        (freq_place,),
        [(v, whole(v)) for v in inputs],
        [(shape, whole(shape))],
        (1,),
        flops=2 * own * count * 2 * rcv * rows // ROWS,
    )
    return out


def updated(initial, onset, messages, table, places, first, rows, target):
    freq_devs = len(messages)
    half_rows, own, rcv = initial.shape
    per_dev = messages[0].shape[1]
    tile = 2 * ROWS
    count = table.shape[2]

    def body(place_ref, _, sblk, x_ref, o_ref, t_ref, *rest):
        refs = rest[:freq_devs]
        out, spread_ref = rest[-2:]
        step = pl.program_id(0)

        @pl.when(step == 0)
        def _():
            base = t_ref[place_ref[0]].astype(F32)
            lane = lax.broadcasted_iota(jnp.int32, (own, count), 1) % ROWS
            for row in range(ROWS):
                spread_ref[row * own : (row + 1) * own] = jnp.where(lane == row, base, 0.0).astype(BF16)

        data = []
        for ref in refs:
            skip = first if ref.shape[2] > rows else 0
            here = pl.ds(pl.multiple_of(skip + step * tile, tile), tile)
            data.append(ref[:, :, here, :].astype(F32))
        onsets = o_ref[pl.ds(pl.multiple_of(sblk[0] * half_rows + first + step * tile, tile), tile), :]
        time = lax.broadcasted_iota(jnp.int32, (own, rcv), 0) + place_ref[0] * own
        for half in range(2):
            cut = slice(half * ROWS, (half + 1) * ROWS)
            flat = jnp.stack([v[:, :, cut] for v in data]).reshape(count, rcv).astype(BF16)
            change = jnp.dot(spread_ref[...], flat, preferred_element_type=F32)
            for row in range(ROWS):
                spot = half * ROWS + row
                on = time < onsets[spot : spot + 1, :]
                moved = jnp.where(on, change[row * own : (row + 1) * own], 0.0)
                out[spot] = (x_ref[first + step * tile + spot].astype(F32) - moved).astype(BF16)

    inputs = [(v, whole(v)) for v in (initial, onset, table, *messages)]
    aliases = {}
    if target is not None:
        inputs.append((target, pl.BlockSpec(memory_space=pl.ANY)))
        aliases = {len(places) + len(inputs) - 1: 0}
    (out,) = call(
        body,
        places,
        inputs,
        [(jax.ShapeDtypeStruct(initial.shape, BF16), pl.BlockSpec((tile, own, rcv), lambda i, *_: (first // tile + i, 0, 0)))],
        (rows // tile,),
        scratch=[pltpu.VMEM((ROWS * own, count), BF16)],
        aliases=aliases,
        flops=2 * 2 * freq_devs * per_dev * own * rows * rcv,
    )
    return out


def exchanged(value, axis, step):
    return lax.ppermute(value, axis, [(i, i ^ step) for i in range(lax.axis_size(axis))])


def dealt_out(parts):
    return [exchanged(part, "freq", step) if step else part for part, step in zip(parts, ways(len(parts)))]


def spread(value, count):
    held = {0: value}
    bit = count // 2
    while bit:
        held.update({way | bit: exchanged(held[way], "freq", bit) for way in sorted(held)})
        bit //= 2
    return [held[way] for way in ways(count)]


def spread_groups(value, groups, count):
    top = count // 2
    far = [{top: exchanged(group, "freq", top)} for group in groups]
    near = {0: value}
    bit = top // 2
    while bit:
        for held in (near, *far):
            held.update({way | bit: exchanged(held[way], "freq", bit) for way in sorted(held)})
        bit //= 2
    return [[{**near, **held}[way] for way in ways(count)] for held in far]


def on_device(initial, response, aperture, onset_rcv, onset_src):
    freq_devs = lax.axis_size("freq")
    per_dev = response.shape[0]
    samples = initial.shape[1] * freq_devs
    half_rows = initial.shape[0]
    src_width = response.shape[2] // 2
    rows = half_rows // CHUNKS
    share = half_rows // freq_devs
    places = tuple(lax.axis_index(axis).reshape(1) for axis in ("freq", "rblk", "sblk"))
    freq_place = places[0]
    inverse = jnp.asarray(inverse_tables(samples, freq_devs, per_dev))
    matrix = jnp.asarray(window_tables(samples, freq_devs, per_dev))

    kept, sent = masked_halves(response, aperture, places)
    moved = [exchanged(v, "rblk", 1) for v in sent]
    kept_pair = [exchanged(v, "sblk", 1) for v in kept]
    sums, spectra = summed(dealt_out(first_spectra(initial, places, freq_devs, per_dev)))
    far = exchanged(spectra, "rblk", 1)
    moved_pair = []
    for index in range(PARTS):
        if index:
            moved[index], far = lax.optimization_barrier((moved[index], far))
        else:
            moved[index], spectra = lax.optimization_barrier((moved[index], spectra))
        moved_pair.append(exchanged(moved[index], "sblk", 1))
    parts = [((kept[i], moved[i]), (kept_pair[i], moved_pair[i])) for i in range(PARTS)]

    own, other = src_onsets(onset_src, places, half_rows, share, src_width)
    onsets = (own, exchanged(other, "sblk", 1))
    src_tables, rcv_tables = phase_tables(onsets, onset_rcv, places, freq_devs, per_dev, samples, PARTS, half_rows)

    near, far, result = [spectra], [far], None
    for step in range(ITERS):
        held = down_products(None, near, parts, 0, 0, freq_place)
        at = 0 if step else PARTS - 1
        if at:
            held = down_products(held, far, parts[:at], 1, 0, freq_place)
        first = at * 2 * kept[0].shape[1]
        messages = dealt_out(down_products(held, far, parts[at:], 1, first, freq_place, freq_devs))
        messages = dealt_out(windowed(messages, src_tables, matrix, freq_place, per_dev, share))
        received = [exchanged(v, "rblk", 1) for v in up_products(messages, parts, freq_place, half_rows, 1)]
        keep = up_products(messages, parts, freq_place, half_rows, 0)
        near, far = [], []
        if step < ITERS - 1:
            for chunk in range(CHUNKS):
                back = spread(added(keep[chunk], received[chunk]), freq_devs)
                near.append(next_spectra(sums, back, rcv_tables, matrix, freq_place, chunk * rows))
                far.append(exchanged(near[chunk], "rblk", 1))
            continue
        back = [added(*pair) for pair in zip(keep[:-1], received)]
        last, together = added_to(keep[-1], received[-1], back)
        for chunk, messages in enumerate(spread_groups(together, back + [last], freq_devs)):
            result = updated(initial, onset_rcv, messages, inverse, places, chunk * rows, rows, result)
    return result


def transform_tables(length, count):
    table = fields(length, count).reshape(2 * count, length)
    forward_table = jnp.asarray(table.astype(np.float32).astype(BF16))
    inverse_table = jnp.asarray((table.T * (2.0 / length)).astype(np.float32).astype(BF16))
    return forward_table, inverse_table


def settle(values):
    return lax.optimization_barrier(values.astype(BF16)).astype(F32)


def samples_into_spectra(values, forward_table, freq_total):
    out = jnp.einsum("kt,ptn->pkn", forward_table, values, preferred_element_type=F32)
    return out.reshape(values.shape[0], 2, freq_total, values.shape[2]).astype(BF16)


def spectra_into_samples(trace_spectra, inverse_table):
    flat = trace_spectra.reshape(trace_spectra.shape[0], -1, trace_spectra.shape[3])
    return jnp.einsum("tk,pkn->ptn", inverse_table, flat, preferred_element_type=F32)


def dense(spec, gated, real, imag, sign):
    dot = functools.partial(jnp.einsum, spec, preferred_element_type=F32)
    return jnp.stack(
        [dot(gated[:, 0], real) - sign * dot(gated[:, 1], imag), dot(gated[:, 0], imag) + sign * dot(gated[:, 1], real)], 1
    )


def general_device(initial, response, aperture, onset_rcv, onset_src):
    freq_devs, rblk_devs, sblk_devs = (lax.axis_size(a) for a in ("freq", "rblk", "sblk"))
    freq_index, rblk_index, sblk_index = (lax.axis_index(a) for a in ("freq", "rblk", "sblk"))
    freq_total = response.shape[0] * freq_devs
    samples = initial.shape[1] * freq_devs
    focal_all = onset_rcv.shape[0]
    forward_table, inverse_table = transform_tables(samples, freq_total)
    steps_axis = lax.iota(jnp.int32, samples)
    own_axis = freq_index * initial.shape[1] + lax.iota(jnp.int32, initial.shape[1])
    half_rows = focal_all // sblk_devs
    own_onsets = lax.dynamic_slice_in_dim(onset_rcv, sblk_index * half_rows, half_rows, 0)
    rcv_gate = (own_axis[None, :, None] < own_onsets[:, None, :]).astype(F32)
    src_rows = focal_all // (rblk_devs * freq_devs)
    src_first = rblk_index * (focal_all // rblk_devs) + freq_index * src_rows
    src_onsets = lax.dynamic_slice_in_dim(onset_src, src_first, src_rows, 0)
    src_gate = (steps_axis[None, :, None] < src_onsets[:, None, :]).astype(F32)
    mask_full = jnp.repeat(jnp.repeat(aperture, BLOCK, 1), BLOCK, 2).astype(BF16)
    gated = response * mask_full[:, None]
    own_forward = lax.dynamic_slice_in_dim(forward_table, freq_index * initial.shape[1], initial.shape[1], 1)
    own_inverse = lax.dynamic_slice_in_dim(inverse_table, freq_index * initial.shape[1], initial.shape[1], 0)
    current = initial
    for _ in range(ITERS):
        partial = samples_into_spectra(current, own_forward, freq_total)
        spec_back = lax.psum_scatter(partial.astype(F32), "freq", scatter_dimension=2, tiled=True).astype(BF16)
        spec_all = lax.all_gather(spec_back, "sblk", axis=0, tiled=True)
        down = lax.psum_scatter(
            settle(dense("euk,bek->beu", gated, spec_all[:, 0], spec_all[:, 1], 1.0)).astype(BF16),
            "rblk",
            scatter_dimension=0,
            tiled=True,
        )
        src_traces = lax.all_to_all(down, "freq", split_axis=0, concat_axis=2, tiled=True)
        upgoing = (src_gate * spectra_into_samples(src_traces, inverse_table)).astype(BF16)
        upspec = samples_into_spectra(upgoing, forward_table, freq_total)
        up_back = lax.all_to_all(upspec, "freq", split_axis=2, concat_axis=0, tiled=True)
        up_all = lax.all_gather(up_back, "rblk", axis=0, tiled=True)
        sums = dense("qao,bqa->bqo", gated, up_all[:, 0], up_all[:, 1], -1.0).astype(BF16)
        back = lax.psum_scatter(sums, "sblk", scatter_dimension=0, tiled=True)
        traces = lax.all_gather(back, "freq", axis=2, tiled=True)
        update = rcv_gate * spectra_into_samples(traces, own_inverse)
        current = (initial.astype(F32) - update).astype(BF16)
    return current


def fits(initial, response, aperture, onset_rcv, onset_src):
    freq_devs = lax.axis_size("freq")
    if lax.axis_size("rblk") != 2 or lax.axis_size("sblk") != 2 or freq_devs & (freq_devs - 1):
        return False
    whole_rows = initial.shape[0] % (max(2, CHUNKS) * ROWS * freq_devs) == 0
    whole_width = response.shape[2] % (2 * PARTS * BLOCK) == 0 and response.shape[3] % BLOCK == 0
    return whole_rows and whole_width and onset_rcv.shape[0] == 2 * initial.shape[0]


def chosen(*arrays):
    return on_device(*arrays) if fits(*arrays) else general_device(*arrays)


def solution(mesh):
    in_specs = (
        P(("group", "sblk"), "freq", "rblk"),
        P(("group", "freq"), None, "sblk", "rblk"),
        P(("group", "freq"), "sblk", "rblk"),
        P("group", "rblk"),
        P("group", "sblk"),
    )
    out_specs = P(("group", "sblk"), "freq", "rblk")
    return jax.shard_map(chosen, mesh=mesh, in_specs=in_specs, out_specs=out_specs, check_vma=False)
```

```python
import functools
import math

import jax
import jax.numpy as jnp
import numpy as np
from jax import lax
from jax.experimental import pallas as pl
from jax.experimental.pallas import tpu as pltpu
from jax.sharding import PartitionSpec as P

BLOCK = 128
ITERS = 2
ROWS = 8
CHUNKS = 2
PARTS = 2
VMEM_BYTES = 6 * 1024 * 1024

BF16 = jnp.bfloat16
F32 = jnp.float32


def ways(count):
    far = sorted(range(1, count), key=lambda step: (step.bit_length() < count.bit_length() - 1, step))
    return [0] + far


def field_rows(place, freq_devs, per_dev):
    rows = []
    for step in ways(freq_devs):
        first = (place ^ step) * per_dev
        for part in range(2):
            rows.extend((part, first + local) for local in range(per_dev))
    return rows


def fields(samples, freq_total):
    phase = (np.arange(1, freq_total + 1)[:, None] * np.arange(samples)[None, :]) % samples
    angle = phase * (2.0 * math.pi / samples)
    return np.stack([np.cos(angle), -np.sin(angle)])


def inverse_tables(samples, freq_devs, per_dev):
    exact = fields(samples, freq_devs * per_dev) * (2.0 / samples)
    own = samples // freq_devs
    out = []
    for place in range(freq_devs):
        part = [exact[c, j, place * own : (place + 1) * own] for c, j in field_rows(place, freq_devs, per_dev)]
        out.append(np.repeat(np.stack(part), ROWS, 0).T)
    return np.stack(out).astype(np.float32).astype(BF16)


def window_tables(samples, freq_devs, per_dev):
    freq_total = freq_devs * per_dev
    order = np.arange(1, freq_total + 1)
    unit = 2j * math.pi / samples
    diff = order[None, :] - order[:, None]
    total = order[None, :] + order[:, None]
    same = np.where(diff == 0, 0.0, 1.0 / (samples * (np.exp(unit * np.where(diff == 0, 1, diff)) - 1.0)))
    mixed = 1.0 / (samples * (np.exp(-unit * total) - 1.0))
    full = np.zeros((2, freq_total, 2, freq_total))
    full[0, :, 0, :] = same.real + mixed.real
    full[0, :, 1, :] = mixed.imag - same.imag
    full[1, :, 0, :] = same.imag + mixed.imag
    full[1, :, 1, :] = same.real - mixed.real
    out = []
    for place in range(freq_devs):
        rows = [c * freq_total + j for c, j in field_rows(place, freq_devs, per_dev)]
        flat = full.reshape(2 * freq_total, 2 * freq_total)[np.ix_(rows, rows)]
        out.append(np.kron(flat, np.eye(ROWS)))
    return np.stack(out).astype(np.float32).astype(BF16)


def call(body, scalars, inputs, outputs, grid, scratch=(), aliases=None, flops=0):
    in_arrays = [value for value, _ in inputs]
    bytes_all = sum(v.size * v.dtype.itemsize for v in in_arrays)
    bytes_all += sum(math.prod(s.shape) * s.dtype.itemsize for s, _ in outputs)
    return pl.pallas_call(
        body,
        grid_spec=pltpu.PrefetchScalarGridSpec(
            num_scalar_prefetch=len(scalars),
            grid=grid,
            in_specs=[spec for _, spec in inputs],
            out_specs=[spec for _, spec in outputs],
            scratch_shapes=list(scratch),
        ),
        out_shape=[shape for shape, _ in outputs],
        input_output_aliases=aliases or {},
        compiler_params=pltpu.CompilerParams(vmem_limit_bytes=VMEM_BYTES),
        cost_estimate=pl.CostEstimate(flops=flops, bytes_accessed=bytes_all, transcendentals=0),
    )(*scalars, *in_arrays)


def whole(array):
    zeros = (0,) * array.ndim
    return pl.BlockSpec(array.shape, lambda *_: zeros)


def sine_terms():
    square = (np.cos(np.linspace(0.0, math.pi, 200)) + 1.0) / 32.0
    y = np.sqrt(np.maximum(square, 1e-12))
    return [float(v) for v in np.polynomial.polynomial.polyfit(square, np.sin(2.0 * math.pi * y) / y, 6)]


def turned(turn):
    terms = sine_terms()

    def sine(y):
        square = y * y
        total = jnp.full_like(y, terms[-1])
        for term in terms[-2::-1]:
            total = total * square + term
        return total * y

    turn = turn - jnp.floor(turn + 0.5)
    size = jnp.abs(turn)
    folded = jnp.where(size > 0.25, jnp.where(turn > 0.0, 0.5, -0.5) - turn, turn)
    return sine(0.25 - size), sine(folded)


def first_spectra(initial, places, freq_devs, per_dev):
    rows, own, rcv = initial.shape
    samples = own * freq_devs
    tile = 2 * ROWS
    count = freq_devs * 2 * per_dev * ROWS

    def body(freq, rblk, sblk, x_ref, *rest):
        outs, spread_ref = rest[:freq_devs], rest[freq_devs]
        time = lax.broadcasted_iota(jnp.int32, (ROWS, own), 1) + freq[0] * own
        time = time.astype(F32) * (1.0 / samples)
        table = []
        for way in ways(freq_devs):
            waves = [turned(time * ((freq[0] ^ way) * per_dev + j + 1).astype(F32)) for j in range(per_dev)]
            table += [cosine for cosine, _ in waves] + [-sine for _, sine in waves]
        table = jnp.concatenate(table, 0)
        lane = lax.broadcasted_iota(jnp.int32, (count, own), 0) % ROWS
        for row in range(ROWS):
            spread_ref[:, row * own : (row + 1) * own] = jnp.where(lane == row, table, 0.0).astype(BF16)
        for at in range(rows // tile):
            parts = []
            for half in range(2):
                start = at * tile + half * ROWS
                flat = x_ref[start : start + ROWS].reshape(ROWS * own, rcv)
                value = jnp.dot(spread_ref[...], flat, preferred_element_type=F32)
                parts.append(value.reshape(freq_devs, 2, per_dev, ROWS, rcv))
            both = jnp.concatenate(parts, 3).astype(BF16)
            for step, out in enumerate(outs):
                out[:, :, at * tile : (at + 1) * tile, :] = both[step]

    shape = jax.ShapeDtypeStruct((2, per_dev, rows, rcv), BF16)
    return call(
        body,
        places,
        [(initial, whole(initial))],
        [(shape, whole(shape))] * freq_devs,
        (1,),
        scratch=[pltpu.VMEM((count, ROWS * own), BF16)],
        flops=2 * 2 * freq_devs * per_dev * own * rows * rcv,
    )


def masked_halves(response, aperture, places):
    per_dev, _, src, rcv = response.shape
    half = src // 2
    width = half // PARTS

    def body(_, rblk, __, flags, x_ref, *outs):
        lane = lax.broadcasted_iota(jnp.int32, (1, rcv), 1) // BLOCK
        for flip in (1, 0):
            for j in range(per_dev):
                for step in range(half // BLOCK):
                    block = (rblk[0] ^ flip) * (half // BLOCK) + step
                    on = flags[j, pl.ds(block, 1), :].astype(F32)
                    row = sum(jnp.where(lane == r, on[:, r : r + 1], 0.0) for r in range(rcv // BLOCK))
                    gate = jnp.broadcast_to(row, (BLOCK, rcv)).astype(BF16)
                    rows = pl.ds(pl.multiple_of(block * BLOCK, BLOCK), BLOCK)
                    part, at = divmod(step * BLOCK, width)
                    out = outs[flip * PARTS + part]
                    for c in range(2):
                        out[j, at : at + BLOCK, c * rcv : (c + 1) * rcv] = x_ref[j, c, rows, :] * gate

    shape = jax.ShapeDtypeStruct((per_dev, width, 2 * rcv), BF16)
    inputs = [(v, whole(v)) for v in (aperture, response)]
    outs = call(body, places, inputs, [(shape, whole(shape))] * (2 * PARTS), (1,))
    return list(outs[:PARTS]), list(outs[PARTS:])


def summed(parts):
    def body(*refs):
        total = sum(ref[...].astype(F32) for ref in refs[:-2])
        refs[-2][...] = total
        refs[-1][...] = total.astype(BF16)

    shapes = [jax.ShapeDtypeStruct(parts[0].shape, kind) for kind in (F32, BF16)]
    return call(body, (), [(v, whole(v)) for v in parts], [(v, whole(v)) for v in shapes], (1,))


def added(keep, received):
    def body(k_ref, r_ref, out):
        out[...] = (k_ref[...] + r_ref[...].astype(F32)).astype(BF16)

    shape = jax.ShapeDtypeStruct(keep.shape, BF16)
    (out,) = call(body, (), [(v, whole(v)) for v in (keep, received)], [(shape, whole(shape))], (1,))
    return out


def src_onsets(onset, places, half_rows, share, width):

    def body(freq, rblk, sblk, o_ref, own, other):
        lanes = pl.ds(pl.multiple_of(rblk[0] * width, BLOCK), width)
        for core, out in ((sblk[0], own), (1 - sblk[0], other)):
            spot = pl.multiple_of(core * half_rows + freq[0] * share, ROWS)
            out[...] = o_ref[pl.ds(spot, share), lanes]

    shape = jax.ShapeDtypeStruct((share, width), onset.dtype)
    return call(body, places, [(onset, whole(onset))], [(shape, whole(shape))] * 2, (1,))


def phase_tables(src, rcv, places, freq_devs, per_dev, samples, parts, rows):
    width = src[0].shape[1] // parts

    def fill(outs, value, to, freq):
        cosines, sines, fraction = outs
        value = value.astype(F32) * (1.0 / samples)
        fraction[:, to] = value
        for step, way in enumerate(ways(freq_devs)):
            for j in range(per_dev):
                order = ((freq[0] ^ way) * per_dev + j + 1).astype(F32)
                cosines[step, j, :, to], sines[step, j, :, to] = turned(value * order)

    def body(freq, _, sblk, own, other, r_ref, *outs):
        for part in range(parts):
            for spot, ref in enumerate((own, other)):
                at = (part * 2 + spot) * width
                fill(outs[:3], ref[:, part * width : (part + 1) * width], slice(at, at + width), freq)
        value = r_ref[pl.ds(pl.multiple_of(sblk[0] * rows, ROWS), rows), :]
        fill(outs[3:], value, slice(0, value.shape[1]), freq)

    shapes = []
    for count, total in ((src[0].shape[0], 2 * src[0].shape[1]), (rows, rcv.shape[1])):
        table = jax.ShapeDtypeStruct((freq_devs, per_dev, count, total), F32)
        shapes += [table, table, jax.ShapeDtypeStruct(table.shape[2:], F32)]
    outs = call(body, places, [(v, whole(v)) for v in (*src, rcv)], [(v, whole(v)) for v in shapes], (1,))
    return tuple(outs[:3]), tuple(outs[3:])


def down_products(before, spectra, parts, side, first, freq_place, freq_devs=0):
    _, per_dev, _, rcv = spectra[0].shape
    rows = sum(v.shape[2] for v in spectra)
    flat = [pair[side] for part in parts for pair in part]
    width = flat[0].shape[1]
    total_width = before.shape[-1] if before is not None else first + width * len(flat)
    share = rows // freq_devs if freq_devs else 0
    old = [] if before is None else [before]

    def body(place_ref, *rest):
        held_ref, rest = (rest[0], rest[1:]) if old else (None, rest)
        refs, resp, outs = rest[: len(spectra)], rest[len(spectra) : len(spectra) + len(flat)], rest[len(spectra) + len(flat) :]
        held = outs[-1]
        for j in range(per_dev):
            real = jnp.concatenate([ref[0, j] for ref in refs], 0)
            imag = jnp.concatenate([ref[1, j] for ref in refs], 0)
            lhs = jnp.concatenate([jnp.concatenate([real, -imag], 1), jnp.concatenate([imag, real], 1)], 0)
            for at, ref in enumerate(resp):
                total = lax.dot_general(lhs, ref[j], (((1,), (1,)), ((), ())), preferred_element_type=F32)
                to = slice(first + at * width, first + (at + 1) * width)
                for part in range(2):
                    value = total[part * rows : (part + 1) * rows]
                    held[part, j, :, to] = value + held_ref[part, j, :, to] if old else value
        if old:
            for to in (slice(0, first), slice(first + len(flat) * width, total_width)):
                if to.start < to.stop:
                    held[:, :, :, to] = held_ref[:, :, :, to]
        if freq_devs:
            for way, out in zip(ways(freq_devs), outs):
                start = pl.multiple_of((place_ref[0] ^ way) * share, share)
                out[...] = held[:, :, pl.ds(start, share), :].reshape(out.shape).astype(BF16)

    sums = (2, per_dev, rows, total_width)
    if freq_devs:
        shapes = [jax.ShapeDtypeStruct((2 * per_dev * share, total_width), BF16)] * freq_devs
    else:
        shapes = [jax.ShapeDtypeStruct(sums, F32)]
    outs = call(
        body,
        (freq_place,),
        [(v, whole(v)) for v in (*old, *spectra, *flat)],
        [(v, whole(v)) for v in shapes],
        (1,),
        scratch=[pltpu.VMEM(sums, F32)] if freq_devs else [],
        flops=2 * 4 * per_dev * rows * len(flat) * width * rcv,
    )
    return outs if freq_devs else outs[0]


def mixed_fields(plain, cos, sin, matrix):
    tile = plain[0].shape[-1]
    turned = [
        jnp.stack([v[0] * c - v[1] * s, v[0] * s + v[1] * c]) for v, c, s in zip(plain, cos, sin)
    ]
    flat = [jnp.stack(v).reshape(matrix.shape[1], tile).astype(BF16) for v in (turned, plain)]
    mixed = jnp.dot(matrix, jnp.concatenate(flat, 1), preferred_element_type=F32)
    shape = (-1, 2) + plain[0].shape[1:]
    return mixed[:, :tile].reshape(shape), mixed[:, tile:].reshape(shape)


def unturned(up, low, value, cos, sin, part):
    real = cos * up[0] + sin * up[1] - low[0] + part * value[0]
    imag = cos * up[1] - sin * up[0] - low[1] + part * value[1]
    return jnp.stack([real, imag])


def tiles(width, body, unroll):
    def at(step, carry):
        body(pl.ds(pl.multiple_of(step * BLOCK, BLOCK), BLOCK))
        return carry

    lax.fori_loop(0, width // BLOCK, at, 0, unroll=unroll)


def windowed(messages, tables, matrix, freq_place, per_dev, share):
    cosines, sines, fraction = tables
    freq_devs = len(messages)
    width = messages[0].shape[-1]
    count = freq_devs * 2 * per_dev * ROWS

    def body(place_ref, c_ref, s_ref, f_ref, g_ref, *rest):
        refs, outs = rest[:freq_devs], rest[freq_devs:]
        matrix_here = g_ref[place_ref[0]]

        def one(at):
            data = [ref[:, at].astype(F32).reshape(2, per_dev, share, BLOCK) for ref in refs]
            made = [[] for _ in outs]
            for first in range(0, share, ROWS):
                cut = slice(first, first + ROWS)
                plain = [value[:, :, cut] for value in data]
                cos = [c_ref[step, :, cut, at] for step in range(freq_devs)]
                sin = [s_ref[step, :, cut, at] for step in range(freq_devs)]
                up, low = mixed_fields(plain, cos, sin, matrix_here)
                part = f_ref[cut, at]
                for step in range(freq_devs):
                    made[step].append(unturned(up[step], low[step], plain[step], cos[step], sin[step], part))
            for out, value in zip(outs, made):
                out[:, at] = jnp.concatenate(value, 2).reshape(out.shape[0], BLOCK).astype(BF16)

        tiles(width, one, 4)

    inputs = (cosines, sines, fraction, matrix, *messages)
    return call(
        body,
        (freq_place,),
        [(v, whole(v)) for v in inputs],
        [(jax.ShapeDtypeStruct(v.shape, BF16), whole(v)) for v in messages],
        (1,),
        flops=2 * count * count * 2 * width * share // ROWS,
    )


def up_products(messages, parts, freq_place, rows, side):
    freq_devs = len(messages)
    flat = [pair[side] for part in parts for pair in part]
    per_dev, src, rcv = flat[0].shape[0], flat[0].shape[1], flat[0].shape[2] // 2
    group = rows // CHUNKS
    share = rows // freq_devs
    total_width = src * len(flat)
    kind = BF16 if side else F32

    def body(place_ref, *rest):
        resp, refs = rest[: len(flat)], rest[len(flat) : len(flat) + freq_devs]
        outs, held = rest[len(flat) + freq_devs : -1], rest[-1]
        for way, ref in zip(ways(freq_devs), refs):
            start = pl.multiple_of((place_ref[0] ^ way) * share, share)
            value = ref[...].reshape(2, per_dev, share, total_width)
            for part in range(2):
                for j in range(per_dev):
                    held[part, j, pl.ds(start, share), :] = value[part, j]
        for j in range(per_dev):
            both = jnp.concatenate([held[0, j], held[1, j]], 0)
            total = sum(
                jnp.dot(both[:, at * src : (at + 1) * src], ref[j], preferred_element_type=F32)
                for at, ref in enumerate(resp)
            )
            real = total[:rows, :rcv] + total[rows:, rcv:]
            imag = total[rows:, :rcv] - total[:rows, rcv:]
            for index, out in enumerate(outs):
                cut = slice(index * group, (index + 1) * group)
                out[0, j] = real[cut].astype(kind)
                out[1, j] = imag[cut].astype(kind)

    shape = jax.ShapeDtypeStruct((2, per_dev, group, rcv), kind)
    return call(
        body,
        (freq_place,),
        [(v, whole(v)) for v in (*flat, *messages)],
        [(shape, whole(shape))] * CHUNKS,
        (1,),
        scratch=[pltpu.VMEM((2, per_dev, rows, total_width), BF16)],
        flops=2 * 4 * per_dev * rows * total_width * rcv,
    )


def next_spectra(sums, messages, tables, matrix, freq_place, first_row):
    cosines, sines, fraction = tables
    freq_devs = len(messages)
    _, per_dev, rows, rcv = messages[0].shape
    count = freq_devs * 2 * per_dev * ROWS
    own = 2 * per_dev * ROWS

    def body(place_ref, u_ref, c_ref, s_ref, f_ref, g_ref, *rest):
        refs, out = rest[:freq_devs], rest[freq_devs]
        matrix_here = g_ref[place_ref[0], :own]

        def one(at):
            for base in range(0, rows, 2 * ROWS):
                pair = slice(base, base + 2 * ROWS)
                data = [ref[:, :, pair, at].astype(F32) for ref in refs]
                made = []
                for half in range(2):
                    plain = [value[:, :, half * ROWS : (half + 1) * ROWS] for value in data]
                    cut = slice(first_row + base + half * ROWS, first_row + base + (half + 1) * ROWS)
                    cos = [c_ref[step, :, cut, at] for step in range(freq_devs)]
                    sin = [s_ref[step, :, cut, at] for step in range(freq_devs)]
                    up, low = mixed_fields(plain, cos, sin, matrix_here)
                    change = unturned(up[0], low[0], plain[0], cos[0], sin[0], f_ref[cut, at])
                    made.append(u_ref[:, :, cut, at] - change)
                out[:, :, pair, at] = jnp.concatenate(made, 2).astype(BF16)

        tiles(rcv, one, 2)

    inputs = (sums, cosines, sines, fraction, matrix, *messages)
    shape = jax.ShapeDtypeStruct(messages[0].shape, BF16)
    (out,) = call(
        body,
        (freq_place,),
        [(v, whole(v)) for v in inputs],
        [(shape, whole(shape))],
        (1,),
        flops=2 * own * count * 2 * rcv * rows // ROWS,
    )
    return out


def updated(initial, onset, messages, table, places, first, rows, target):
    freq_devs = len(messages)
    half_rows, own, rcv = initial.shape
    per_dev = messages[0].shape[1]
    tile = 2 * ROWS
    count = table.shape[2]

    def body(place_ref, _, sblk, x_ref, o_ref, t_ref, *rest):
        refs = rest[:freq_devs]
        out, spread_ref = rest[-2:]
        step = pl.program_id(0)

        @pl.when(step == 0)
        def _():
            base = t_ref[place_ref[0]].astype(F32)
            lane = lax.broadcasted_iota(jnp.int32, (own, count), 1) % ROWS
            for row in range(ROWS):
                spread_ref[row * own : (row + 1) * own] = jnp.where(lane == row, base, 0.0).astype(BF16)

        here = pl.ds(pl.multiple_of(step * tile, tile), tile)
        data = [ref[:, :, here, :].astype(F32) for ref in refs]
        onsets = o_ref[pl.ds(pl.multiple_of(sblk[0] * half_rows + first + step * tile, tile), tile), :]
        time = lax.broadcasted_iota(jnp.int32, (own, rcv), 0) + place_ref[0] * own
        for half in range(2):
            cut = slice(half * ROWS, (half + 1) * ROWS)
            flat = jnp.stack([v[:, :, cut] for v in data]).reshape(count, rcv).astype(BF16)
            change = jnp.dot(spread_ref[...], flat, preferred_element_type=F32)
            for row in range(ROWS):
                spot = half * ROWS + row
                on = time < onsets[spot : spot + 1, :]
                moved = jnp.where(on, change[row * own : (row + 1) * own], 0.0)
                out[spot] = (x_ref[first + step * tile + spot].astype(F32) - moved).astype(BF16)

    inputs = [(v, whole(v)) for v in (initial, onset, table, *messages)]
    aliases = {}
    if target is not None:
        inputs.append((target, pl.BlockSpec(memory_space=pl.ANY)))
        aliases = {len(places) + len(inputs) - 1: 0}
    (out,) = call(
        body,
        places,
        inputs,
        [(jax.ShapeDtypeStruct(initial.shape, BF16), pl.BlockSpec((tile, own, rcv), lambda i, *_: (first // tile + i, 0, 0)))],
        (rows // tile,),
        scratch=[pltpu.VMEM((ROWS * own, count), BF16)],
        aliases=aliases,
        flops=2 * 2 * freq_devs * per_dev * own * rows * rcv,
    )
    return out


def exchanged(value, axis, step):
    return lax.ppermute(value, axis, [(i, i ^ step) for i in range(lax.axis_size(axis))])


def dealt_out(parts):
    return [exchanged(part, "freq", step) if step else part for part, step in zip(parts, ways(len(parts)))]


def spread(value, count):
    held = {0: value}
    bit = count // 2
    while bit:
        held.update({way | bit: exchanged(held[way], "freq", bit) for way in sorted(held)})
        bit //= 2
    return [held[way] for way in ways(count)]


def on_device(initial, response, aperture, onset_rcv, onset_src):
    freq_devs = lax.axis_size("freq")
    per_dev = response.shape[0]
    samples = initial.shape[1] * freq_devs
    half_rows = initial.shape[0]
    src_width = response.shape[2] // 2
    rows = half_rows // CHUNKS
    share = half_rows // freq_devs
    places = tuple(lax.axis_index(axis).reshape(1) for axis in ("freq", "rblk", "sblk"))
    freq_place = places[0]
    inverse = jnp.asarray(inverse_tables(samples, freq_devs, per_dev))
    matrix = jnp.asarray(window_tables(samples, freq_devs, per_dev))

    kept, sent = masked_halves(response, aperture, places)
    moved = [exchanged(v, "rblk", 1) for v in sent]
    kept_pair = [exchanged(v, "sblk", 1) for v in kept]
    sums, spectra = summed(dealt_out(first_spectra(initial, places, freq_devs, per_dev)))
    far = exchanged(spectra, "rblk", 1)
    moved_pair = []
    for index in range(PARTS):
        if index:
            moved[index], far = lax.optimization_barrier((moved[index], far))
        else:
            moved[index], spectra = lax.optimization_barrier((moved[index], spectra))
        moved_pair.append(exchanged(moved[index], "sblk", 1))
    parts = [((kept[i], moved[i]), (kept_pair[i], moved_pair[i])) for i in range(PARTS)]

    own, other = src_onsets(onset_src, places, half_rows, share, src_width)
    onsets = (own, exchanged(other, "sblk", 1))
    src_tables, rcv_tables = phase_tables(onsets, onset_rcv, places, freq_devs, per_dev, samples, PARTS, half_rows)

    near, far, result = [spectra], [far], None
    for step in range(ITERS):
        held = down_products(None, near, parts, 0, 0, freq_place)
        at = 0 if step else PARTS - 1
        if at:
            held = down_products(held, far, parts[:at], 1, 0, freq_place)
        first = at * 2 * kept[0].shape[1]
        messages = dealt_out(down_products(held, far, parts[at:], 1, first, freq_place, freq_devs))
        messages = dealt_out(windowed(messages, src_tables, matrix, freq_place, per_dev, share))
        received = [exchanged(v, "rblk", 1) for v in up_products(messages, parts, freq_place, half_rows, 1)]
        keep = up_products(messages, parts, freq_place, half_rows, 0)
        near, far = [], []
        for chunk in range(CHUNKS):
            back = spread(added(keep[chunk], received[chunk]), freq_devs)
            if step < ITERS - 1:
                near.append(next_spectra(sums, back, rcv_tables, matrix, freq_place, chunk * rows))
                far.append(exchanged(near[chunk], "rblk", 1))
            else:
                result = updated(initial, onset_rcv, back, inverse, places, chunk * rows, rows, result)
    return result


def transform_tables(length, count):
    table = fields(length, count).reshape(2 * count, length)
    forward_table = jnp.asarray(table.astype(np.float32).astype(BF16))
    inverse_table = jnp.asarray((table.T * (2.0 / length)).astype(np.float32).astype(BF16))
    return forward_table, inverse_table


def settle(values):
    return lax.optimization_barrier(values.astype(BF16)).astype(F32)


def samples_into_spectra(values, forward_table, freq_total):
    out = jnp.einsum("kt,ptn->pkn", forward_table, values, preferred_element_type=F32)
    return out.reshape(values.shape[0], 2, freq_total, values.shape[2]).astype(BF16)


def spectra_into_samples(trace_spectra, inverse_table):
    flat = trace_spectra.reshape(trace_spectra.shape[0], -1, trace_spectra.shape[3])
    return jnp.einsum("tk,pkn->ptn", inverse_table, flat, preferred_element_type=F32)


def dense(spec, gated, real, imag, sign):
    dot = functools.partial(jnp.einsum, spec, preferred_element_type=F32)
    return jnp.stack(
        [dot(gated[:, 0], real) - sign * dot(gated[:, 1], imag), dot(gated[:, 0], imag) + sign * dot(gated[:, 1], real)], 1
    )


def general_device(initial, response, aperture, onset_rcv, onset_src):
    freq_devs, rblk_devs, sblk_devs = (lax.axis_size(a) for a in ("freq", "rblk", "sblk"))
    freq_index, rblk_index, sblk_index = (lax.axis_index(a) for a in ("freq", "rblk", "sblk"))
    freq_total = response.shape[0] * freq_devs
    samples = initial.shape[1] * freq_devs
    focal_all = onset_rcv.shape[0]
    forward_table, inverse_table = transform_tables(samples, freq_total)
    steps_axis = lax.iota(jnp.int32, samples)
    own_axis = freq_index * initial.shape[1] + lax.iota(jnp.int32, initial.shape[1])
    half_rows = focal_all // sblk_devs
    own_onsets = lax.dynamic_slice_in_dim(onset_rcv, sblk_index * half_rows, half_rows, 0)
    rcv_gate = (own_axis[None, :, None] < own_onsets[:, None, :]).astype(F32)
    src_rows = focal_all // (rblk_devs * freq_devs)
    src_first = rblk_index * (focal_all // rblk_devs) + freq_index * src_rows
    src_onsets = lax.dynamic_slice_in_dim(onset_src, src_first, src_rows, 0)
    src_gate = (steps_axis[None, :, None] < src_onsets[:, None, :]).astype(F32)
    mask_full = jnp.repeat(jnp.repeat(aperture, BLOCK, 1), BLOCK, 2).astype(BF16)
    gated = response * mask_full[:, None]
    own_forward = lax.dynamic_slice_in_dim(forward_table, freq_index * initial.shape[1], initial.shape[1], 1)
    own_inverse = lax.dynamic_slice_in_dim(inverse_table, freq_index * initial.shape[1], initial.shape[1], 0)
    current = initial
    for _ in range(ITERS):
        partial = samples_into_spectra(current, own_forward, freq_total)
        spec_back = lax.psum_scatter(partial.astype(F32), "freq", scatter_dimension=2, tiled=True).astype(BF16)
        spec_all = lax.all_gather(spec_back, "sblk", axis=0, tiled=True)
        down = lax.psum_scatter(
            settle(dense("euk,bek->beu", gated, spec_all[:, 0], spec_all[:, 1], 1.0)).astype(BF16),
            "rblk",
            scatter_dimension=0,
            tiled=True,
        )
        src_traces = lax.all_to_all(down, "freq", split_axis=0, concat_axis=2, tiled=True)
        upgoing = (src_gate * spectra_into_samples(src_traces, inverse_table)).astype(BF16)
        upspec = samples_into_spectra(upgoing, forward_table, freq_total)
        up_back = lax.all_to_all(upspec, "freq", split_axis=2, concat_axis=0, tiled=True)
        up_all = lax.all_gather(up_back, "rblk", axis=0, tiled=True)
        sums = dense("qao,bqa->bqo", gated, up_all[:, 0], up_all[:, 1], -1.0).astype(BF16)
        back = lax.psum_scatter(sums, "sblk", scatter_dimension=0, tiled=True)
        traces = lax.all_gather(back, "freq", axis=2, tiled=True)
        update = rcv_gate * spectra_into_samples(traces, own_inverse)
        current = (initial.astype(F32) - update).astype(BF16)
    return current


def fits(initial, response, aperture, onset_rcv, onset_src):
    freq_devs = lax.axis_size("freq")
    if lax.axis_size("rblk") != 2 or lax.axis_size("sblk") != 2 or freq_devs & (freq_devs - 1):
        return False
    whole_rows = initial.shape[0] % (max(2, CHUNKS) * ROWS * freq_devs) == 0
    whole_width = response.shape[2] % (2 * PARTS * BLOCK) == 0 and response.shape[3] % BLOCK == 0
    return whole_rows and whole_width and onset_rcv.shape[0] == 2 * initial.shape[0]


def chosen(*arrays):
    return on_device(*arrays) if fits(*arrays) else general_device(*arrays)


def solution(mesh):
    in_specs = (
        P(("group", "sblk"), "freq", "rblk"),
        P(("group", "freq"), None, "sblk", "rblk"),
        P(("group", "freq"), "sblk", "rblk"),
        P("group", "rblk"),
        P("group", "sblk"),
    )
    out_specs = P(("group", "sblk"), "freq", "rblk")
    return jax.shard_map(chosen, mesh=mesh, in_specs=in_specs, out_specs=out_specs, check_vma=False)
```

```python
import functools
import itertools
import math

import jax
import jax.numpy as jnp
import numpy as np
from jax import lax
from jax.experimental import pallas as pl
from jax.experimental.pallas import tpu as pltpu
from jax.sharding import PartitionSpec as P

BLOCK = 128
ITERS = 2
ROWS = 8
CHUNKS = 2
PARTS = 2
VMEM_BYTES = 6 * 1024 * 1024

BF16 = jnp.bfloat16
F32 = jnp.float32


def ways(count):
    far = sorted(range(1, count), key=lambda step: (step.bit_length() < count.bit_length() - 1, step))
    return [0] + far


def slot_ways(count):
    lead = ways(count)
    return [[0] + lead[:0:-1], lead]


def way_of(slot, core, count):
    first, second = (order[slot] for order in slot_ways(count))
    return first + core * (second - first) if first != second else first


def field_rows(place, freq_devs, per_dev, order=None):
    rows = []
    for step in order or ways(freq_devs):
        first = (place ^ step) * per_dev
        for part in range(2):
            rows.extend((part, first + local) for local in range(per_dev))
    return rows


def fields(samples, freq_total):
    phase = (np.arange(1, freq_total + 1)[:, None] * np.arange(samples)[None, :]) % samples
    angle = phase * (2.0 * math.pi / samples)
    return np.stack([np.cos(angle), -np.sin(angle)])


def inverse_tables(samples, freq_devs, per_dev):
    exact = fields(samples, freq_devs * per_dev) * (2.0 / samples)
    own = samples // freq_devs
    out = []
    for place in range(freq_devs):
        part = [exact[c, j, place * own : (place + 1) * own] for c, j in field_rows(place, freq_devs, per_dev)]
        out.append(np.repeat(np.stack(part), ROWS, 0).T)
    return np.stack(out).astype(np.float32).astype(BF16)


def window_tables(samples, freq_devs, per_dev):
    freq_total = freq_devs * per_dev
    order = np.arange(1, freq_total + 1)
    unit = 2j * math.pi / samples
    diff = order[None, :] - order[:, None]
    total = order[None, :] + order[:, None]
    same = np.where(diff == 0, 0.0, 1.0 / (samples * (np.exp(unit * np.where(diff == 0, 1, diff)) - 1.0)))
    mixed = 1.0 / (samples * (np.exp(-unit * total) - 1.0))
    full = np.zeros((2, freq_total, 2, freq_total))
    full[0, :, 0, :] = same.real + mixed.real
    full[0, :, 1, :] = mixed.imag - same.imag
    full[1, :, 0, :] = same.imag + mixed.imag
    full[1, :, 1, :] = same.real - mixed.real
    out = []
    for place, order in itertools.product(range(freq_devs), slot_ways(freq_devs)):
        rows = [c * freq_total + j for c, j in field_rows(place, freq_devs, per_dev, order)]
        flat = full.reshape(2 * freq_total, 2 * freq_total)[np.ix_(rows, rows)]
        out.append(np.kron(flat, np.eye(ROWS)))
    return np.stack(out).astype(np.float32).astype(BF16)


def call(body, scalars, inputs, outputs, grid, scratch=(), aliases=None, flops=0):
    in_arrays = [value for value, _ in inputs]
    bytes_all = sum(v.size * v.dtype.itemsize for v in in_arrays)
    bytes_all += sum(math.prod(s.shape) * s.dtype.itemsize for s, _ in outputs)
    return pl.pallas_call(
        body,
        grid_spec=pltpu.PrefetchScalarGridSpec(
            num_scalar_prefetch=len(scalars),
            grid=grid,
            in_specs=[spec for _, spec in inputs],
            out_specs=[spec for _, spec in outputs],
            scratch_shapes=list(scratch),
        ),
        out_shape=[shape for shape, _ in outputs],
        input_output_aliases=aliases or {},
        compiler_params=pltpu.CompilerParams(vmem_limit_bytes=VMEM_BYTES),
        cost_estimate=pl.CostEstimate(flops=flops, bytes_accessed=bytes_all, transcendentals=0),
    )(*scalars, *in_arrays)


def whole(array):
    zeros = (0,) * array.ndim
    return pl.BlockSpec(array.shape, lambda *_: zeros)


def sine_terms():
    square = (np.cos(np.linspace(0.0, math.pi, 200)) + 1.0) / 32.0
    y = np.sqrt(np.maximum(square, 1e-12))
    return [float(v) for v in np.polynomial.polynomial.polyfit(square, np.sin(2.0 * math.pi * y) / y, 6)]


def turned(turn):
    terms = sine_terms()

    def sine(y):
        square = y * y
        total = jnp.full_like(y, terms[-1])
        for term in terms[-2::-1]:
            total = total * square + term
        return total * y

    turn = turn - jnp.floor(turn + 0.5)
    size = jnp.abs(turn)
    folded = jnp.where(size > 0.25, jnp.where(turn > 0.0, 0.5, -0.5) - turn, turn)
    return sine(0.25 - size), sine(folded)


def first_spectra(initial, places, freq_devs, per_dev):
    rows, own, rcv = initial.shape
    samples = own * freq_devs
    tile = 2 * ROWS
    count = freq_devs * 2 * per_dev * ROWS

    def body(freq, rblk, sblk, x_ref, *rest):
        outs, spread_ref = rest[:freq_devs], rest[freq_devs]
        time = lax.broadcasted_iota(jnp.int32, (ROWS, own), 1) + freq[0] * own
        time = time.astype(F32) * (1.0 / samples)
        table = []
        for way in ways(freq_devs):
            waves = [turned(time * ((freq[0] ^ way) * per_dev + j + 1).astype(F32)) for j in range(per_dev)]
            table += [cosine for cosine, _ in waves] + [-sine for _, sine in waves]
        table = jnp.concatenate(table, 0)
        lane = lax.broadcasted_iota(jnp.int32, (count, own), 0) % ROWS
        for row in range(ROWS):
            spread_ref[:, row * own : (row + 1) * own] = jnp.where(lane == row, table, 0.0).astype(BF16)
        for at in range(rows // tile):
            parts = []
            for half in range(2):
                start = at * tile + half * ROWS
                flat = x_ref[start : start + ROWS].reshape(ROWS * own, rcv)
                value = jnp.dot(spread_ref[...], flat, preferred_element_type=F32)
                parts.append(value.reshape(freq_devs, 2, per_dev, ROWS, rcv))
            both = jnp.concatenate(parts, 3).astype(BF16)
            for step, out in enumerate(outs):
                out[:, :, at * tile : (at + 1) * tile, :] = both[step]

    shape = jax.ShapeDtypeStruct((2, per_dev, rows, rcv), BF16)
    return call(
        body,
        places,
        [(initial, whole(initial))],
        [(shape, whole(shape))] * freq_devs,
        (1,),
        scratch=[pltpu.VMEM((count, ROWS * own), BF16)],
        flops=2 * 2 * freq_devs * per_dev * own * rows * rcv,
    )


def masked_halves(response, aperture, places):
    per_dev, _, src, rcv = response.shape
    half = src // 2
    width = half // PARTS

    def body(_, rblk, __, flags, x_ref, *outs):
        lane = lax.broadcasted_iota(jnp.int32, (1, rcv), 1) // BLOCK
        for flip in (1, 0):
            for j in range(per_dev):
                for step in range(half // BLOCK):
                    block = (rblk[0] ^ flip) * (half // BLOCK) + step
                    on = flags[j, pl.ds(block, 1), :].astype(F32)
                    row = sum(jnp.where(lane == r, on[:, r : r + 1], 0.0) for r in range(rcv // BLOCK))
                    gate = jnp.broadcast_to(row, (BLOCK, rcv)).astype(BF16)
                    rows = pl.ds(pl.multiple_of(block * BLOCK, BLOCK), BLOCK)
                    part, at = divmod(step * BLOCK, width)
                    out = outs[flip * PARTS + part]
                    for c in range(2):
                        out[j, at : at + BLOCK, c * rcv : (c + 1) * rcv] = x_ref[j, c, rows, :] * gate

    shape = jax.ShapeDtypeStruct((per_dev, width, 2 * rcv), BF16)
    inputs = [(v, whole(v)) for v in (aperture, response)]
    outs = call(body, places, inputs, [(shape, whole(shape))] * (2 * PARTS), (1,))
    return list(outs[:PARTS]), list(outs[PARTS:])


def summed(parts):
    def body(*refs):
        total = sum(ref[...].astype(F32) for ref in refs[:-2])
        refs[-2][...] = total
        refs[-1][...] = total.astype(BF16)

    shapes = [jax.ShapeDtypeStruct(parts[0].shape, kind) for kind in (F32, BF16)]
    return call(body, (), [(v, whole(v)) for v in parts], [(v, whole(v)) for v in shapes], (1,))


def added(keep, received):
    def body(k_ref, r_ref, out):
        out[...] = (k_ref[...] + r_ref[...].astype(F32)).astype(BF16)

    shape = jax.ShapeDtypeStruct(keep.shape, BF16)
    (out,) = call(body, (), [(v, whole(v)) for v in (keep, received)], [(shape, whole(shape))], (1,))
    return out


def src_onsets(onset, places, half_rows, share, width):

    def body(freq, rblk, sblk, o_ref, own, other):
        lanes = pl.ds(pl.multiple_of(rblk[0] * width, BLOCK), width)
        for core, out in ((sblk[0], own), (1 - sblk[0], other)):
            spot = pl.multiple_of(core * half_rows + freq[0] * share, ROWS)
            out[...] = o_ref[pl.ds(spot, share), lanes]

    shape = jax.ShapeDtypeStruct((share, width), onset.dtype)
    return call(body, places, [(onset, whole(onset))], [(shape, whole(shape))] * 2, (1,))


def phase_tables(src, rcv, places, freq_devs, per_dev, samples, parts, rows):
    width = src[0].shape[1] // parts

    def fill(outs, value, to, freq, order_of):
        cosines, sines, fraction = outs
        value = value.astype(F32) * (1.0 / samples)
        fraction[:, to] = value
        for step, way in enumerate(order_of):
            for j in range(per_dev):
                order = ((freq[0] ^ way) * per_dev + j + 1).astype(F32)
                cosines[step, j, :, to], sines[step, j, :, to] = turned(value * order)

    def body(freq, _, sblk, own, other, r_ref, *outs):
        slots = [way_of(slot, sblk[0], freq_devs) for slot in range(freq_devs)]
        for part in range(parts):
            for spot, ref in enumerate((own, other)):
                at = (part * 2 + spot) * width
                fill(outs[:3], ref[:, part * width : (part + 1) * width], slice(at, at + width), freq, slots)
        value = r_ref[pl.ds(pl.multiple_of(sblk[0] * rows, ROWS), rows), :]
        fill(outs[3:], value, slice(0, value.shape[1]), freq, ways(freq_devs))

    shapes = []
    for count, total in ((src[0].shape[0], 2 * src[0].shape[1]), (rows, rcv.shape[1])):
        table = jax.ShapeDtypeStruct((freq_devs, per_dev, count, total), F32)
        shapes += [table, table, jax.ShapeDtypeStruct(table.shape[2:], F32)]
    outs = call(body, places, [(v, whole(v)) for v in (*src, rcv)], [(v, whole(v)) for v in shapes], (1,))
    return tuple(outs[:3]), tuple(outs[3:])


def down_products(before, spectra, parts, side, first, places, freq_devs=0):
    _, per_dev, _, rcv = spectra[0].shape
    rows = sum(v.shape[2] for v in spectra)
    flat = [pair[side] for part in parts for pair in part]
    width = flat[0].shape[1]
    total_width = before.shape[-1] if before is not None else first + width * len(flat)
    share = rows // freq_devs if freq_devs else 0
    old = [] if before is None else [before]

    def body(freq, _, sblk, *rest):
        held_ref, rest = (rest[0], rest[1:]) if old else (None, rest)
        refs, resp, outs = rest[: len(spectra)], rest[len(spectra) : len(spectra) + len(flat)], rest[len(spectra) + len(flat) :]
        held = outs[-1]
        for j in range(per_dev):
            real = jnp.concatenate([ref[0, j] for ref in refs], 0)
            imag = jnp.concatenate([ref[1, j] for ref in refs], 0)
            lhs = jnp.concatenate([jnp.concatenate([real, -imag], 1), jnp.concatenate([imag, real], 1)], 0)
            for at, ref in enumerate(resp):
                total = lax.dot_general(lhs, ref[j], (((1,), (1,)), ((), ())), preferred_element_type=F32)
                to = slice(first + at * width, first + (at + 1) * width)
                for part in range(2):
                    value = total[part * rows : (part + 1) * rows]
                    held[part, j, :, to] = value + held_ref[part, j, :, to] if old else value
        if old:
            for to in (slice(0, first), slice(first + len(flat) * width, total_width)):
                if to.start < to.stop:
                    held[:, :, :, to] = held_ref[:, :, :, to]
        if freq_devs:
            for slot, out in enumerate(outs[:freq_devs]):
                start = pl.multiple_of((freq[0] ^ way_of(slot, sblk[0], freq_devs)) * share, share)
                out[...] = held[:, :, pl.ds(start, share), :].reshape(out.shape).astype(BF16)

    sums = (2, per_dev, rows, total_width)
    if freq_devs:
        shapes = [jax.ShapeDtypeStruct((2 * per_dev * share, total_width), BF16)] * freq_devs
    else:
        shapes = [jax.ShapeDtypeStruct(sums, F32)]
    outs = call(
        body,
        places,
        [(v, whole(v)) for v in (*old, *spectra, *flat)],
        [(v, whole(v)) for v in shapes],
        (1,),
        scratch=[pltpu.VMEM(sums, F32)] if freq_devs else [],
        flops=2 * 4 * per_dev * rows * len(flat) * width * rcv,
    )
    return outs if freq_devs else outs[0]


def mixed_fields(plain, cos, sin, matrix):
    tile = plain[0].shape[-1]
    turned = [
        jnp.stack([v[0] * c - v[1] * s, v[0] * s + v[1] * c]) for v, c, s in zip(plain, cos, sin)
    ]
    flat = [jnp.stack(v).reshape(matrix.shape[1], tile).astype(BF16) for v in (turned, plain)]
    mixed = jnp.dot(matrix, jnp.concatenate(flat, 1), preferred_element_type=F32)
    shape = (-1, 2) + plain[0].shape[1:]
    return mixed[:, :tile].reshape(shape), mixed[:, tile:].reshape(shape)


def unturned(up, low, value, cos, sin, part):
    real = cos * up[0] + sin * up[1] - low[0] + part * value[0]
    imag = cos * up[1] - sin * up[0] - low[1] + part * value[1]
    return jnp.stack([real, imag])


def tiles(width, body):
    def at(step, carry):
        body(pl.ds(pl.multiple_of(step * BLOCK, BLOCK), BLOCK))
        return carry

    lax.fori_loop(0, width // BLOCK, at, 0, unroll=2)


def windowed(messages, tables, matrix, places, per_dev, share):
    cosines, sines, fraction = tables
    freq_devs = len(messages)
    width = messages[0].shape[-1]
    count = freq_devs * 2 * per_dev * ROWS

    def body(freq, _, sblk, c_ref, s_ref, f_ref, g_ref, *rest):
        refs, outs = rest[:freq_devs], rest[freq_devs:]
        matrix_here = g_ref[freq[0] * 2 + sblk[0]]

        def one(at):
            data = [ref[:, at].astype(F32).reshape(2, per_dev, share, BLOCK) for ref in refs]
            made = [[] for _ in outs]
            for first in range(0, share, ROWS):
                cut = slice(first, first + ROWS)
                plain = [value[:, :, cut] for value in data]
                cos = [c_ref[step, :, cut, at] for step in range(freq_devs)]
                sin = [s_ref[step, :, cut, at] for step in range(freq_devs)]
                up, low = mixed_fields(plain, cos, sin, matrix_here)
                part = f_ref[cut, at]
                for step in range(freq_devs):
                    made[step].append(unturned(up[step], low[step], plain[step], cos[step], sin[step], part))
            for out, value in zip(outs, made):
                out[:, at] = jnp.concatenate(value, 2).reshape(out.shape[0], BLOCK).astype(BF16)

        tiles(width, one)

    inputs = (cosines, sines, fraction, matrix, *messages)
    return call(
        body,
        places,
        [(v, whole(v)) for v in inputs],
        [(jax.ShapeDtypeStruct(v.shape, BF16), whole(v)) for v in messages],
        (1,),
        flops=2 * count * count * 2 * width * share // ROWS,
    )


def up_products(messages, parts, places, rows, side):
    freq_devs = len(messages)
    flat = [pair[side] for part in parts for pair in part]
    per_dev, src, rcv = flat[0].shape[0], flat[0].shape[1], flat[0].shape[2] // 2
    group = rows // CHUNKS
    share = rows // freq_devs
    total_width = src * len(flat)
    kind = BF16 if side else F32

    def body(freq, _, sblk, *rest):
        resp, refs = rest[: len(flat)], rest[len(flat) : len(flat) + freq_devs]
        outs, held = rest[len(flat) + freq_devs : -1], rest[-1]
        for slot, ref in enumerate(refs):
            start = pl.multiple_of((freq[0] ^ way_of(slot, sblk[0], freq_devs)) * share, share)
            value = ref[...].reshape(2, per_dev, share, total_width)
            for part in range(2):
                for j in range(per_dev):
                    held[part, j, pl.ds(start, share), :] = value[part, j]
        for j in range(per_dev):
            both = jnp.concatenate([held[0, j], held[1, j]], 0)
            total = sum(
                jnp.dot(both[:, at * src : (at + 1) * src], ref[j], preferred_element_type=F32)
                for at, ref in enumerate(resp)
            )
            real = total[:rows, :rcv] + total[rows:, rcv:]
            imag = total[rows:, :rcv] - total[:rows, rcv:]
            for index, out in enumerate(outs):
                cut = slice(index * group, (index + 1) * group)
                out[0, j] = real[cut].astype(kind)
                out[1, j] = imag[cut].astype(kind)

    shape = jax.ShapeDtypeStruct((2, per_dev, group, rcv), kind)
    return call(
        body,
        places,
        [(v, whole(v)) for v in (*flat, *messages)],
        [(shape, whole(shape))] * CHUNKS,
        (1,),
        scratch=[pltpu.VMEM((2, per_dev, rows, total_width), BF16)],
        flops=2 * 4 * per_dev * rows * total_width * rcv,
    )


def next_spectra(sums, messages, tables, matrix, freq_place, first_row):
    cosines, sines, fraction = tables
    freq_devs = len(messages)
    _, per_dev, rows, rcv = messages[0].shape
    count = freq_devs * 2 * per_dev * ROWS
    own = 2 * per_dev * ROWS

    def body(place_ref, u_ref, c_ref, s_ref, f_ref, g_ref, *rest):
        refs, out = rest[:freq_devs], rest[freq_devs]
        matrix_here = g_ref[place_ref[0] * 2 + 1, :own]

        def one(at):
            for base in range(0, rows, 2 * ROWS):
                pair = slice(base, base + 2 * ROWS)
                data = [ref[:, :, pair, at].astype(F32) for ref in refs]
                made = []
                for half in range(2):
                    plain = [value[:, :, half * ROWS : (half + 1) * ROWS] for value in data]
                    cut = slice(first_row + base + half * ROWS, first_row + base + (half + 1) * ROWS)
                    cos = [c_ref[step, :, cut, at] for step in range(freq_devs)]
                    sin = [s_ref[step, :, cut, at] for step in range(freq_devs)]
                    up, low = mixed_fields(plain, cos, sin, matrix_here)
                    change = unturned(up[0], low[0], plain[0], cos[0], sin[0], f_ref[cut, at])
                    made.append(u_ref[:, :, cut, at] - change)
                out[:, :, pair, at] = jnp.concatenate(made, 2).astype(BF16)

        tiles(rcv, one)

    inputs = (sums, cosines, sines, fraction, matrix, *messages)
    shape = jax.ShapeDtypeStruct(messages[0].shape, BF16)
    (out,) = call(
        body,
        (freq_place,),
        [(v, whole(v)) for v in inputs],
        [(shape, whole(shape))],
        (1,),
        flops=2 * own * count * 2 * rcv * rows // ROWS,
    )
    return out


def updated(initial, onset, messages, table, places, first, rows, target):
    freq_devs = len(messages)
    half_rows, own, rcv = initial.shape
    per_dev = messages[0].shape[1]
    tile = 2 * ROWS
    count = table.shape[2]

    def body(place_ref, _, sblk, x_ref, o_ref, t_ref, *rest):
        refs = rest[:freq_devs]
        out, spread_ref = rest[-2:]
        step = pl.program_id(0)

        @pl.when(step == 0)
        def _():
            base = t_ref[place_ref[0]].astype(F32)
            lane = lax.broadcasted_iota(jnp.int32, (own, count), 1) % ROWS
            for row in range(ROWS):
                spread_ref[row * own : (row + 1) * own] = jnp.where(lane == row, base, 0.0).astype(BF16)

        here = pl.ds(pl.multiple_of(step * tile, tile), tile)
        data = [ref[:, :, here, :].astype(F32) for ref in refs]
        onsets = o_ref[pl.ds(pl.multiple_of(sblk[0] * half_rows + first + step * tile, tile), tile), :]
        time = lax.broadcasted_iota(jnp.int32, (own, rcv), 0) + place_ref[0] * own
        for half in range(2):
            cut = slice(half * ROWS, (half + 1) * ROWS)
            flat = jnp.stack([v[:, :, cut] for v in data]).reshape(count, rcv).astype(BF16)
            change = jnp.dot(spread_ref[...], flat, preferred_element_type=F32)
            for row in range(ROWS):
                spot = half * ROWS + row
                on = time < onsets[spot : spot + 1, :]
                moved = jnp.where(on, change[row * own : (row + 1) * own], 0.0)
                out[spot] = (x_ref[first + step * tile + spot].astype(F32) - moved).astype(BF16)

    inputs = [(v, whole(v)) for v in (initial, onset, table, *messages)]
    aliases = {}
    if target is not None:
        inputs.append((target, pl.BlockSpec(memory_space=pl.ANY)))
        aliases = {len(places) + len(inputs) - 1: 0}
    (out,) = call(
        body,
        places,
        inputs,
        [(jax.ShapeDtypeStruct(initial.shape, BF16), pl.BlockSpec((tile, own, rcv), lambda i, *_: (first // tile + i, 0, 0)))],
        (rows // tile,),
        scratch=[pltpu.VMEM((ROWS * own, count), BF16)],
        aliases=aliases,
        flops=2 * 2 * freq_devs * per_dev * own * rows * rcv,
    )
    return out


def exchanged(value, axis, step):
    return lax.ppermute(value, axis, [(i, i ^ step) for i in range(lax.axis_size(axis))])


def dealt_out(parts):
    return [exchanged(part, "freq", step) if step else part for part, step in zip(parts, ways(len(parts)))]


def dealt_by_core(parts):
    count = len(parts)
    out = [parts[0]]
    for slot in range(1, count):
        steps = [order[slot] for order in slot_ways(count)]
        pairs = [(f * 2 + core, (f ^ steps[core]) * 2 + core) for f in range(count) for core in range(2)]
        out.append(lax.ppermute(parts[slot], ("freq", "sblk"), pairs))
    return out


def spread(value, count):
    held = {0: value}
    bit = count // 2
    while bit:
        held.update({way | bit: exchanged(held[way], "freq", bit) for way in sorted(held)})
        bit //= 2
    return [held[way] for way in ways(count)]


def on_device(initial, response, aperture, onset_rcv, onset_src):
    freq_devs = lax.axis_size("freq")
    per_dev = response.shape[0]
    samples = initial.shape[1] * freq_devs
    half_rows = initial.shape[0]
    src_width = response.shape[2] // 2
    rows = half_rows // CHUNKS
    share = half_rows // freq_devs
    places = tuple(lax.axis_index(axis).reshape(1) for axis in ("freq", "rblk", "sblk"))
    freq_place = places[0]
    inverse = jnp.asarray(inverse_tables(samples, freq_devs, per_dev))
    matrix = jnp.asarray(window_tables(samples, freq_devs, per_dev))

    kept, sent = masked_halves(response, aperture, places)
    moved = [exchanged(v, "rblk", 1) for v in sent]
    kept_pair = [exchanged(v, "sblk", 1) for v in kept]
    sums, spectra = summed(dealt_out(first_spectra(initial, places, freq_devs, per_dev)))
    far = exchanged(spectra, "rblk", 1)
    moved_pair = []
    for index in range(PARTS):
        if index:
            moved[index], far = lax.optimization_barrier((moved[index], far))
        else:
            moved[index], spectra = lax.optimization_barrier((moved[index], spectra))
        moved_pair.append(exchanged(moved[index], "sblk", 1))
    parts = [((kept[i], moved[i]), (kept_pair[i], moved_pair[i])) for i in range(PARTS)]

    own, other = src_onsets(onset_src, places, half_rows, share, src_width)
    onsets = (own, exchanged(other, "sblk", 1))
    src_tables, rcv_tables = phase_tables(onsets, onset_rcv, places, freq_devs, per_dev, samples, PARTS, half_rows)

    near, far, result = [spectra], [far], None
    for step in range(ITERS):
        held = down_products(None, near, parts, 0, 0, places)
        at = 0 if step else PARTS - 1
        if at:
            held = down_products(held, far, parts[:at], 1, 0, places)
        first = at * 2 * kept[0].shape[1]
        messages = dealt_by_core(down_products(held, far, parts[at:], 1, first, places, freq_devs))
        messages = dealt_by_core(windowed(messages, src_tables, matrix, places, per_dev, share))
        received = [exchanged(v, "rblk", 1) for v in up_products(messages, parts, places, half_rows, 1)]
        keep = up_products(messages, parts, places, half_rows, 0)
        near, far = [], []
        for chunk in range(CHUNKS):
            back = spread(added(keep[chunk], received[chunk]), freq_devs)
            if step < ITERS - 1:
                near.append(next_spectra(sums, back, rcv_tables, matrix, freq_place, chunk * rows))
                far.append(exchanged(near[chunk], "rblk", 1))
            else:
                result = updated(initial, onset_rcv, back, inverse, places, chunk * rows, rows, result)
    return result


def transform_tables(length, count):
    table = fields(length, count).reshape(2 * count, length)
    forward_table = jnp.asarray(table.astype(np.float32).astype(BF16))
    inverse_table = jnp.asarray((table.T * (2.0 / length)).astype(np.float32).astype(BF16))
    return forward_table, inverse_table


def settle(values):
    return lax.optimization_barrier(values.astype(BF16)).astype(F32)


def samples_into_spectra(values, forward_table, freq_total):
    out = jnp.einsum("kt,ptn->pkn", forward_table, values, preferred_element_type=F32)
    return out.reshape(values.shape[0], 2, freq_total, values.shape[2]).astype(BF16)


def spectra_into_samples(trace_spectra, inverse_table):
    flat = trace_spectra.reshape(trace_spectra.shape[0], -1, trace_spectra.shape[3])
    return jnp.einsum("tk,pkn->ptn", inverse_table, flat, preferred_element_type=F32)


def dense(spec, gated, real, imag, sign):
    dot = functools.partial(jnp.einsum, spec, preferred_element_type=F32)
    return jnp.stack(
        [dot(gated[:, 0], real) - sign * dot(gated[:, 1], imag), dot(gated[:, 0], imag) + sign * dot(gated[:, 1], real)], 1
    )


def general_device(initial, response, aperture, onset_rcv, onset_src):
    freq_devs, rblk_devs, sblk_devs = (lax.axis_size(a) for a in ("freq", "rblk", "sblk"))
    freq_index, rblk_index, sblk_index = (lax.axis_index(a) for a in ("freq", "rblk", "sblk"))
    freq_total = response.shape[0] * freq_devs
    samples = initial.shape[1] * freq_devs
    focal_all = onset_rcv.shape[0]
    forward_table, inverse_table = transform_tables(samples, freq_total)
    steps_axis = lax.iota(jnp.int32, samples)
    own_axis = freq_index * initial.shape[1] + lax.iota(jnp.int32, initial.shape[1])
    half_rows = focal_all // sblk_devs
    own_onsets = lax.dynamic_slice_in_dim(onset_rcv, sblk_index * half_rows, half_rows, 0)
    rcv_gate = (own_axis[None, :, None] < own_onsets[:, None, :]).astype(F32)
    src_rows = focal_all // (rblk_devs * freq_devs)
    src_first = rblk_index * (focal_all // rblk_devs) + freq_index * src_rows
    src_onsets = lax.dynamic_slice_in_dim(onset_src, src_first, src_rows, 0)
    src_gate = (steps_axis[None, :, None] < src_onsets[:, None, :]).astype(F32)
    mask_full = jnp.repeat(jnp.repeat(aperture, BLOCK, 1), BLOCK, 2).astype(BF16)
    gated = response * mask_full[:, None]
    own_forward = lax.dynamic_slice_in_dim(forward_table, freq_index * initial.shape[1], initial.shape[1], 1)
    own_inverse = lax.dynamic_slice_in_dim(inverse_table, freq_index * initial.shape[1], initial.shape[1], 0)
    current = initial
    for _ in range(ITERS):
        partial = samples_into_spectra(current, own_forward, freq_total)
        spec_back = lax.psum_scatter(partial.astype(F32), "freq", scatter_dimension=2, tiled=True).astype(BF16)
        spec_all = lax.all_gather(spec_back, "sblk", axis=0, tiled=True)
        down = lax.psum_scatter(
            settle(dense("euk,bek->beu", gated, spec_all[:, 0], spec_all[:, 1], 1.0)).astype(BF16),
            "rblk",
            scatter_dimension=0,
            tiled=True,
        )
        src_traces = lax.all_to_all(down, "freq", split_axis=0, concat_axis=2, tiled=True)
        upgoing = (src_gate * spectra_into_samples(src_traces, inverse_table)).astype(BF16)
        upspec = samples_into_spectra(upgoing, forward_table, freq_total)
        up_back = lax.all_to_all(upspec, "freq", split_axis=2, concat_axis=0, tiled=True)
        up_all = lax.all_gather(up_back, "rblk", axis=0, tiled=True)
        sums = dense("qao,bqa->bqo", gated, up_all[:, 0], up_all[:, 1], -1.0).astype(BF16)
        back = lax.psum_scatter(sums, "sblk", scatter_dimension=0, tiled=True)
        traces = lax.all_gather(back, "freq", axis=2, tiled=True)
        update = rcv_gate * spectra_into_samples(traces, own_inverse)
        current = (initial.astype(F32) - update).astype(BF16)
    return current


def fits(initial, response, aperture, onset_rcv, onset_src):
    freq_devs = lax.axis_size("freq")
    if lax.axis_size("rblk") != 2 or lax.axis_size("sblk") != 2 or freq_devs & (freq_devs - 1):
        return False
    whole_rows = initial.shape[0] % (max(2, CHUNKS) * ROWS * freq_devs) == 0
    whole_width = response.shape[2] % (2 * PARTS * BLOCK) == 0 and response.shape[3] % BLOCK == 0
    return whole_rows and whole_width and onset_rcv.shape[0] == 2 * initial.shape[0]


def chosen(*arrays):
    return on_device(*arrays) if fits(*arrays) else general_device(*arrays)


def solution(mesh):
    in_specs = (
        P(("group", "sblk"), "freq", "rblk"),
        P(("group", "freq"), None, "sblk", "rblk"),
        P(("group", "freq"), "sblk", "rblk"),
        P("group", "rblk"),
        P("group", "sblk"),
    )
    out_specs = P(("group", "sblk"), "freq", "rblk")
    return jax.shard_map(chosen, mesh=mesh, in_specs=in_specs, out_specs=out_specs, check_vma=False)
```

```python
import functools
import itertools
import math

import jax
import jax.numpy as jnp
import numpy as np
from jax import lax
from jax.experimental import pallas as pl
from jax.experimental.pallas import tpu as pltpu
from jax.sharding import PartitionSpec as P

BLOCK = 128
ITERS = 2
ROWS = 8
CHUNKS = 2
PARTS = 2
VMEM_BYTES = 6 * 1024 * 1024

BF16 = jnp.bfloat16
F32 = jnp.float32


def ways(count):
    far = sorted(range(1, count), key=lambda step: (step.bit_length() < count.bit_length() - 1, step))
    return [0] + far


def slot_ways(count):
    lead = ways(count)
    return [[0] + lead[:0:-1], lead]


def way_of(slot, core, count):
    first, second = (order[slot] for order in slot_ways(count))
    return first + core * (second - first) if first != second else first


def field_rows(place, freq_devs, per_dev, order=None):
    rows = []
    for step in order or ways(freq_devs):
        first = (place ^ step) * per_dev
        for part in range(2):
            rows.extend((part, first + local) for local in range(per_dev))
    return rows


def fields(samples, freq_total):
    phase = (np.arange(1, freq_total + 1)[:, None] * np.arange(samples)[None, :]) % samples
    angle = phase * (2.0 * math.pi / samples)
    return np.stack([np.cos(angle), -np.sin(angle)])


def inverse_tables(samples, freq_devs, per_dev):
    exact = fields(samples, freq_devs * per_dev) * (2.0 / samples)
    own = samples // freq_devs
    out = []
    for place in range(freq_devs):
        part = [exact[c, j, place * own : (place + 1) * own] for c, j in field_rows(place, freq_devs, per_dev)]
        out.append(np.repeat(np.stack(part), ROWS, 0).T)
    return np.stack(out).astype(np.float32).astype(BF16)


def window_tables(samples, freq_devs, per_dev):
    freq_total = freq_devs * per_dev
    order = np.arange(1, freq_total + 1)
    unit = 2j * math.pi / samples
    diff = order[None, :] - order[:, None]
    total = order[None, :] + order[:, None]
    same = np.where(diff == 0, 0.0, 1.0 / (samples * (np.exp(unit * np.where(diff == 0, 1, diff)) - 1.0)))
    mixed = 1.0 / (samples * (np.exp(-unit * total) - 1.0))
    full = np.zeros((2, freq_total, 2, freq_total))
    full[0, :, 0, :] = same.real + mixed.real
    full[0, :, 1, :] = mixed.imag - same.imag
    full[1, :, 0, :] = same.imag + mixed.imag
    full[1, :, 1, :] = same.real - mixed.real
    out = []
    for place, order in itertools.product(range(freq_devs), slot_ways(freq_devs)):
        rows = [c * freq_total + j for c, j in field_rows(place, freq_devs, per_dev, order)]
        flat = full.reshape(2 * freq_total, 2 * freq_total)[np.ix_(rows, rows)]
        out.append(np.kron(flat, np.eye(ROWS)))
    return np.stack(out).astype(np.float32).astype(BF16)


def call(body, scalars, inputs, outputs, grid, scratch=(), aliases=None, flops=0):
    in_arrays = [value for value, _ in inputs]
    bytes_all = sum(v.size * v.dtype.itemsize for v in in_arrays)
    bytes_all += sum(math.prod(s.shape) * s.dtype.itemsize for s, _ in outputs)
    return pl.pallas_call(
        body,
        grid_spec=pltpu.PrefetchScalarGridSpec(
            num_scalar_prefetch=len(scalars),
            grid=grid,
            in_specs=[spec for _, spec in inputs],
            out_specs=[spec for _, spec in outputs],
            scratch_shapes=list(scratch),
        ),
        out_shape=[shape for shape, _ in outputs],
        input_output_aliases=aliases or {},
        compiler_params=pltpu.CompilerParams(vmem_limit_bytes=VMEM_BYTES),
        cost_estimate=pl.CostEstimate(flops=flops, bytes_accessed=bytes_all, transcendentals=0),
    )(*scalars, *in_arrays)


def whole(array):
    zeros = (0,) * array.ndim
    return pl.BlockSpec(array.shape, lambda *_: zeros)


def sine_terms():
    square = (np.cos(np.linspace(0.0, math.pi, 200)) + 1.0) / 32.0
    y = np.sqrt(np.maximum(square, 1e-12))
    return [float(v) for v in np.polynomial.polynomial.polyfit(square, np.sin(2.0 * math.pi * y) / y, 6)]


def turned(turn):
    terms = sine_terms()

    def sine(y):
        square = y * y
        total = jnp.full_like(y, terms[-1])
        for term in terms[-2::-1]:
            total = total * square + term
        return total * y

    turn = turn - jnp.floor(turn + 0.5)
    size = jnp.abs(turn)
    folded = jnp.where(size > 0.25, jnp.where(turn > 0.0, 0.5, -0.5) - turn, turn)
    return sine(0.25 - size), sine(folded)


def first_spectra(initial, places, freq_devs, per_dev):
    rows, own, rcv = initial.shape
    samples = own * freq_devs
    tile = 2 * ROWS
    count = freq_devs * 2 * per_dev * ROWS

    def body(freq, rblk, sblk, x_ref, *rest):
        outs, spread_ref = rest[:freq_devs], rest[freq_devs]
        time = lax.broadcasted_iota(jnp.int32, (ROWS, own), 1) + freq[0] * own
        time = time.astype(F32) * (1.0 / samples)
        table = []
        for way in ways(freq_devs):
            waves = [turned(time * ((freq[0] ^ way) * per_dev + j + 1).astype(F32)) for j in range(per_dev)]
            table += [cosine for cosine, _ in waves] + [-sine for _, sine in waves]
        table = jnp.concatenate(table, 0)
        lane = lax.broadcasted_iota(jnp.int32, (count, own), 0) % ROWS
        for row in range(ROWS):
            spread_ref[:, row * own : (row + 1) * own] = jnp.where(lane == row, table, 0.0).astype(BF16)
        for at in range(rows // tile):
            parts = []
            for half in range(2):
                start = at * tile + half * ROWS
                flat = x_ref[start : start + ROWS].reshape(ROWS * own, rcv)
                value = jnp.dot(spread_ref[...], flat, preferred_element_type=F32)
                parts.append(value.reshape(freq_devs, 2, per_dev, ROWS, rcv))
            both = jnp.concatenate(parts, 3).astype(BF16)
            for step, out in enumerate(outs):
                out[:, :, at * tile : (at + 1) * tile, :] = both[step]

    shape = jax.ShapeDtypeStruct((2, per_dev, rows, rcv), BF16)
    return call(
        body,
        places,
        [(initial, whole(initial))],
        [(shape, whole(shape))] * freq_devs,
        (1,),
        scratch=[pltpu.VMEM((count, ROWS * own), BF16)],
        flops=2 * 2 * freq_devs * per_dev * own * rows * rcv,
    )


def masked_halves(response, aperture, places):
    per_dev, _, src, rcv = response.shape
    half = src // 2
    width = half // PARTS

    def body(_, rblk, __, flags, x_ref, *outs):
        lane = lax.broadcasted_iota(jnp.int32, (1, rcv), 1) // BLOCK
        for flip in (1, 0):
            for j in range(per_dev):
                for step in range(half // BLOCK):
                    block = (rblk[0] ^ flip) * (half // BLOCK) + step
                    on = flags[j, pl.ds(block, 1), :].astype(F32)
                    row = sum(jnp.where(lane == r, on[:, r : r + 1], 0.0) for r in range(rcv // BLOCK))
                    gate = jnp.broadcast_to(row, (BLOCK, rcv)).astype(BF16)
                    rows = pl.ds(pl.multiple_of(block * BLOCK, BLOCK), BLOCK)
                    part, at = divmod(step * BLOCK, width)
                    out = outs[flip * PARTS + part]
                    for c in range(2):
                        out[j, at : at + BLOCK, c * rcv : (c + 1) * rcv] = x_ref[j, c, rows, :] * gate

    shape = jax.ShapeDtypeStruct((per_dev, width, 2 * rcv), BF16)
    inputs = [(v, whole(v)) for v in (aperture, response)]
    outs = call(body, places, inputs, [(shape, whole(shape))] * (2 * PARTS), (1,))
    return list(outs[:PARTS]), list(outs[PARTS:])


def summed(parts):
    def body(*refs):
        total = sum(ref[...].astype(F32) for ref in refs[:-2])
        refs[-2][...] = total
        refs[-1][...] = total.astype(BF16)

    shapes = [jax.ShapeDtypeStruct(parts[0].shape, kind) for kind in (F32, BF16)]
    return call(body, (), [(v, whole(v)) for v in parts], [(v, whole(v)) for v in shapes], (1,))


def added(keep, received):
    def body(k_ref, r_ref, out):
        out[...] = (k_ref[...] + r_ref[...].astype(F32)).astype(BF16)

    shape = jax.ShapeDtypeStruct(keep.shape, BF16)
    (out,) = call(body, (), [(v, whole(v)) for v in (keep, received)], [(shape, whole(shape))], (1,))
    return out


def src_onsets(onset, places, half_rows, share, width):

    def body(freq, rblk, sblk, o_ref, own, other):
        lanes = pl.ds(pl.multiple_of(rblk[0] * width, BLOCK), width)
        for core, out in ((sblk[0], own), (1 - sblk[0], other)):
            spot = pl.multiple_of(core * half_rows + freq[0] * share, ROWS)
            out[...] = o_ref[pl.ds(spot, share), lanes]

    shape = jax.ShapeDtypeStruct((share, width), onset.dtype)
    return call(body, places, [(onset, whole(onset))], [(shape, whole(shape))] * 2, (1,))


def phase_tables(src, rcv, places, freq_devs, per_dev, samples, parts, rows):
    width = src[0].shape[1] // parts

    def fill(outs, value, to, freq, order_of):
        cosines, sines, fraction = outs
        value = value.astype(F32) * (1.0 / samples)
        fraction[:, to] = value
        for step, way in enumerate(order_of):
            for j in range(per_dev):
                order = ((freq[0] ^ way) * per_dev + j + 1).astype(F32)
                cosines[step, j, :, to], sines[step, j, :, to] = turned(value * order)

    def body(freq, _, sblk, own, other, r_ref, *outs):
        slots = [way_of(slot, sblk[0], freq_devs) for slot in range(freq_devs)]
        for part in range(parts):
            for spot, ref in enumerate((own, other)):
                at = (part * 2 + spot) * width
                fill(outs[:3], ref[:, part * width : (part + 1) * width], slice(at, at + width), freq, slots)
        value = r_ref[pl.ds(pl.multiple_of(sblk[0] * rows, ROWS), rows), :]
        fill(outs[3:], value, slice(0, value.shape[1]), freq, ways(freq_devs))

    shapes = []
    for count, total in ((src[0].shape[0], 2 * src[0].shape[1]), (rows, rcv.shape[1])):
        table = jax.ShapeDtypeStruct((freq_devs, per_dev, count, total), F32)
        shapes += [table, table, jax.ShapeDtypeStruct(table.shape[2:], F32)]
    outs = call(body, places, [(v, whole(v)) for v in (*src, rcv)], [(v, whole(v)) for v in shapes], (1,))
    return tuple(outs[:3]), tuple(outs[3:])


def down_products(before, spectra, parts, side, first, places, freq_devs=0, by_core=False):
    _, per_dev, _, rcv = spectra[0].shape
    rows = sum(v.shape[2] for v in spectra)
    flat = [pair[side] for part in parts for pair in part]
    width = flat[0].shape[1]
    total_width = before.shape[-1] if before is not None else first + width * len(flat)
    share = rows // freq_devs if freq_devs else 0
    old = [] if before is None else [before]

    def body(freq, _, sblk, *rest):
        held_ref, rest = (rest[0], rest[1:]) if old else (None, rest)
        refs, resp, outs = rest[: len(spectra)], rest[len(spectra) : len(spectra) + len(flat)], rest[len(spectra) + len(flat) :]
        held = outs[-1]
        for j in range(per_dev):
            real = jnp.concatenate([ref[0, j] for ref in refs], 0)
            imag = jnp.concatenate([ref[1, j] for ref in refs], 0)
            lhs = jnp.concatenate([jnp.concatenate([real, -imag], 1), jnp.concatenate([imag, real], 1)], 0)
            for at, ref in enumerate(resp):
                total = lax.dot_general(lhs, ref[j], (((1,), (1,)), ((), ())), preferred_element_type=F32)
                to = slice(first + at * width, first + (at + 1) * width)
                for part in range(2):
                    value = total[part * rows : (part + 1) * rows]
                    held[part, j, :, to] = value + held_ref[part, j, :, to] if old else value
        if old:
            for to in (slice(0, first), slice(first + len(flat) * width, total_width)):
                if to.start < to.stop:
                    held[:, :, :, to] = held_ref[:, :, :, to]
        if freq_devs:
            for slot, out in enumerate(outs[:freq_devs]):
                way = way_of(slot, sblk[0] if by_core else 1, freq_devs)
                start = pl.multiple_of((freq[0] ^ way) * share, share)
                out[...] = held[:, :, pl.ds(start, share), :].reshape(out.shape).astype(BF16)

    sums = (2, per_dev, rows, total_width)
    if freq_devs:
        shapes = [jax.ShapeDtypeStruct((2 * per_dev * share, total_width), BF16)] * freq_devs
    else:
        shapes = [jax.ShapeDtypeStruct(sums, F32)]
    outs = call(
        body,
        places,
        [(v, whole(v)) for v in (*old, *spectra, *flat)],
        [(v, whole(v)) for v in shapes],
        (1,),
        scratch=[pltpu.VMEM(sums, F32)] if freq_devs else [],
        flops=2 * 4 * per_dev * rows * len(flat) * width * rcv,
    )
    return outs if freq_devs else outs[0]


def mixed_fields(plain, cos, sin, matrix):
    tile = plain[0].shape[-1]
    turned = [
        jnp.stack([v[0] * c - v[1] * s, v[0] * s + v[1] * c]) for v, c, s in zip(plain, cos, sin)
    ]
    flat = [jnp.stack(v).reshape(matrix.shape[1], tile).astype(BF16) for v in (turned, plain)]
    mixed = jnp.dot(matrix, jnp.concatenate(flat, 1), preferred_element_type=F32)
    shape = (-1, 2) + plain[0].shape[1:]
    return mixed[:, :tile].reshape(shape), mixed[:, tile:].reshape(shape)


def unturned(up, low, value, cos, sin, part):
    real = cos * up[0] + sin * up[1] - low[0] + part * value[0]
    imag = cos * up[1] - sin * up[0] - low[1] + part * value[1]
    return jnp.stack([real, imag])


def tiles(width, body):
    def at(step, carry):
        body(pl.ds(pl.multiple_of(step * BLOCK, BLOCK), BLOCK))
        return carry

    lax.fori_loop(0, width // BLOCK, at, 0, unroll=2)


def windowed(messages, tables, matrix, places, per_dev, share, by_core):
    cosines, sines, fraction = tables
    freq_devs = len(messages)
    width = messages[0].shape[-1]
    count = freq_devs * 2 * per_dev * ROWS

    def body(freq, _, sblk, c_ref, s_ref, f_ref, g_ref, *rest):
        refs, outs = rest[:freq_devs], rest[freq_devs:]
        matrix_here = g_ref[freq[0] * 2 + (sblk[0] if by_core else 1)]
        spots = list(range(freq_devs))
        if not by_core:
            first, second = slot_ways(freq_devs)
            spots = [first.index(way) + sblk[0] * (slot - first.index(way)) for slot, way in enumerate(second)]

        def one(at):
            data = [ref[:, at].astype(F32).reshape(2, per_dev, share, BLOCK) for ref in refs]
            made = [[] for _ in outs]
            for first in range(0, share, ROWS):
                cut = slice(first, first + ROWS)
                plain = [value[:, :, cut] for value in data]
                cos = [c_ref[spot, :, cut, at] for spot in spots]
                sin = [s_ref[spot, :, cut, at] for spot in spots]
                up, low = mixed_fields(plain, cos, sin, matrix_here)
                part = f_ref[cut, at]
                for step in range(freq_devs):
                    made[step].append(unturned(up[step], low[step], plain[step], cos[step], sin[step], part))
            for out, value in zip(outs, made):
                out[:, at] = jnp.concatenate(value, 2).reshape(out.shape[0], BLOCK).astype(BF16)

        tiles(width, one)

    inputs = (cosines, sines, fraction, matrix, *messages)
    return call(
        body,
        places,
        [(v, whole(v)) for v in inputs],
        [(jax.ShapeDtypeStruct(v.shape, BF16), whole(v)) for v in messages],
        (1,),
        flops=2 * count * count * 2 * width * share // ROWS,
    )


def up_products(messages, parts, places, rows, side, by_core):
    freq_devs = len(messages)
    flat = [pair[side] for part in parts for pair in part]
    per_dev, src, rcv = flat[0].shape[0], flat[0].shape[1], flat[0].shape[2] // 2
    group = rows // CHUNKS
    share = rows // freq_devs
    total_width = src * len(flat)
    kind = BF16 if side else F32

    def body(freq, _, sblk, *rest):
        resp, refs = rest[: len(flat)], rest[len(flat) : len(flat) + freq_devs]
        outs, held = rest[len(flat) + freq_devs : -1], rest[-1]
        for slot, ref in enumerate(refs):
            way = way_of(slot, sblk[0] if by_core else 1, freq_devs)
            start = pl.multiple_of((freq[0] ^ way) * share, share)
            value = ref[...].reshape(2, per_dev, share, total_width)
            for part in range(2):
                for j in range(per_dev):
                    held[part, j, pl.ds(start, share), :] = value[part, j]
        for j in range(per_dev):
            both = jnp.concatenate([held[0, j], held[1, j]], 0)
            total = sum(
                jnp.dot(both[:, at * src : (at + 1) * src], ref[j], preferred_element_type=F32)
                for at, ref in enumerate(resp)
            )
            real = total[:rows, :rcv] + total[rows:, rcv:]
            imag = total[rows:, :rcv] - total[:rows, rcv:]
            for index, out in enumerate(outs):
                cut = slice(index * group, (index + 1) * group)
                out[0, j] = real[cut].astype(kind)
                out[1, j] = imag[cut].astype(kind)

    shape = jax.ShapeDtypeStruct((2, per_dev, group, rcv), kind)
    return call(
        body,
        places,
        [(v, whole(v)) for v in (*flat, *messages)],
        [(shape, whole(shape))] * CHUNKS,
        (1,),
        scratch=[pltpu.VMEM((2, per_dev, rows, total_width), BF16)],
        flops=2 * 4 * per_dev * rows * total_width * rcv,
    )


def next_spectra(sums, messages, tables, matrix, freq_place, first_row):
    cosines, sines, fraction = tables
    freq_devs = len(messages)
    _, per_dev, rows, rcv = messages[0].shape
    count = freq_devs * 2 * per_dev * ROWS
    own = 2 * per_dev * ROWS

    def body(place_ref, u_ref, c_ref, s_ref, f_ref, g_ref, *rest):
        refs, out = rest[:freq_devs], rest[freq_devs]
        matrix_here = g_ref[place_ref[0] * 2 + 1, :own]

        def one(at):
            for base in range(0, rows, 2 * ROWS):
                pair = slice(base, base + 2 * ROWS)
                data = [ref[:, :, pair, at].astype(F32) for ref in refs]
                made = []
                for half in range(2):
                    plain = [value[:, :, half * ROWS : (half + 1) * ROWS] for value in data]
                    cut = slice(first_row + base + half * ROWS, first_row + base + (half + 1) * ROWS)
                    cos = [c_ref[step, :, cut, at] for step in range(freq_devs)]
                    sin = [s_ref[step, :, cut, at] for step in range(freq_devs)]
                    up, low = mixed_fields(plain, cos, sin, matrix_here)
                    change = unturned(up[0], low[0], plain[0], cos[0], sin[0], f_ref[cut, at])
                    made.append(u_ref[:, :, cut, at] - change)
                out[:, :, pair, at] = jnp.concatenate(made, 2).astype(BF16)

        tiles(rcv, one)

    inputs = (sums, cosines, sines, fraction, matrix, *messages)
    shape = jax.ShapeDtypeStruct(messages[0].shape, BF16)
    (out,) = call(
        body,
        (freq_place,),
        [(v, whole(v)) for v in inputs],
        [(shape, whole(shape))],
        (1,),
        flops=2 * own * count * 2 * rcv * rows // ROWS,
    )
    return out


def updated(initial, onset, messages, table, places, first, rows, target):
    freq_devs = len(messages)
    half_rows, own, rcv = initial.shape
    per_dev = messages[0].shape[1]
    tile = 2 * ROWS
    count = table.shape[2]

    def body(place_ref, _, sblk, x_ref, o_ref, t_ref, *rest):
        refs = rest[:freq_devs]
        out, spread_ref = rest[-2:]
        step = pl.program_id(0)

        @pl.when(step == 0)
        def _():
            base = t_ref[place_ref[0]].astype(F32)
            lane = lax.broadcasted_iota(jnp.int32, (own, count), 1) % ROWS
            for row in range(ROWS):
                spread_ref[row * own : (row + 1) * own] = jnp.where(lane == row, base, 0.0).astype(BF16)

        here = pl.ds(pl.multiple_of(step * tile, tile), tile)
        data = [ref[:, :, here, :].astype(F32) for ref in refs]
        onsets = o_ref[pl.ds(pl.multiple_of(sblk[0] * half_rows + first + step * tile, tile), tile), :]
        time = lax.broadcasted_iota(jnp.int32, (own, rcv), 0) + place_ref[0] * own
        for half in range(2):
            cut = slice(half * ROWS, (half + 1) * ROWS)
            flat = jnp.stack([v[:, :, cut] for v in data]).reshape(count, rcv).astype(BF16)
            change = jnp.dot(spread_ref[...], flat, preferred_element_type=F32)
            for row in range(ROWS):
                spot = half * ROWS + row
                on = time < onsets[spot : spot + 1, :]
                moved = jnp.where(on, change[row * own : (row + 1) * own], 0.0)
                out[spot] = (x_ref[first + step * tile + spot].astype(F32) - moved).astype(BF16)

    inputs = [(v, whole(v)) for v in (initial, onset, table, *messages)]
    aliases = {}
    if target is not None:
        inputs.append((target, pl.BlockSpec(memory_space=pl.ANY)))
        aliases = {len(places) + len(inputs) - 1: 0}
    (out,) = call(
        body,
        places,
        inputs,
        [(jax.ShapeDtypeStruct(initial.shape, BF16), pl.BlockSpec((tile, own, rcv), lambda i, *_: (first // tile + i, 0, 0)))],
        (rows // tile,),
        scratch=[pltpu.VMEM((ROWS * own, count), BF16)],
        aliases=aliases,
        flops=2 * 2 * freq_devs * per_dev * own * rows * rcv,
    )
    return out


def exchanged(value, axis, step):
    return lax.ppermute(value, axis, [(i, i ^ step) for i in range(lax.axis_size(axis))])


def dealt_out(parts):
    return [exchanged(part, "freq", step) if step else part for part, step in zip(parts, ways(len(parts)))]


def dealt_by_core(parts):
    count = len(parts)
    out = [parts[0]]
    for slot in range(1, count):
        steps = [order[slot] for order in slot_ways(count)]
        pairs = [(f * 2 + core, (f ^ steps[core]) * 2 + core) for f in range(count) for core in range(2)]
        out.append(lax.ppermute(parts[slot], ("freq", "sblk"), pairs))
    return out


def spread(value, count):
    held = {0: value}
    bit = count // 2
    while bit:
        held.update({way | bit: exchanged(held[way], "freq", bit) for way in sorted(held)})
        bit //= 2
    return [held[way] for way in ways(count)]


def on_device(initial, response, aperture, onset_rcv, onset_src):
    freq_devs = lax.axis_size("freq")
    per_dev = response.shape[0]
    samples = initial.shape[1] * freq_devs
    half_rows = initial.shape[0]
    src_width = response.shape[2] // 2
    rows = half_rows // CHUNKS
    share = half_rows // freq_devs
    places = tuple(lax.axis_index(axis).reshape(1) for axis in ("freq", "rblk", "sblk"))
    freq_place = places[0]
    inverse = jnp.asarray(inverse_tables(samples, freq_devs, per_dev))
    matrix = jnp.asarray(window_tables(samples, freq_devs, per_dev))

    kept, sent = masked_halves(response, aperture, places)
    moved = [exchanged(v, "rblk", 1) for v in sent]
    kept_pair = [exchanged(v, "sblk", 1) for v in kept]
    sums, spectra = summed(dealt_out(first_spectra(initial, places, freq_devs, per_dev)))
    far = exchanged(spectra, "rblk", 1)
    moved_pair = []
    for index in range(PARTS):
        if index:
            moved[index], far = lax.optimization_barrier((moved[index], far))
        else:
            moved[index], spectra = lax.optimization_barrier((moved[index], spectra))
        moved_pair.append(exchanged(moved[index], "sblk", 1))
    parts = [((kept[i], moved[i]), (kept_pair[i], moved_pair[i])) for i in range(PARTS)]

    own, other = src_onsets(onset_src, places, half_rows, share, src_width)
    onsets = (own, exchanged(other, "sblk", 1))
    src_tables, rcv_tables = phase_tables(onsets, onset_rcv, places, freq_devs, per_dev, samples, PARTS, half_rows)

    near, far, result = [spectra], [far], None
    for step in range(ITERS):
        held = down_products(None, near, parts, 0, 0, places)
        at = 0 if step else PARTS - 1
        if at:
            held = down_products(held, far, parts[:at], 1, 0, places)
        first = at * 2 * kept[0].shape[1]
        by_core = step == 0
        deal = dealt_by_core if by_core else dealt_out
        messages = deal(down_products(held, far, parts[at:], 1, first, places, freq_devs, by_core))
        messages = deal(windowed(messages, src_tables, matrix, places, per_dev, share, by_core))
        received = [exchanged(v, "rblk", 1) for v in up_products(messages, parts, places, half_rows, 1, by_core)]
        keep = up_products(messages, parts, places, half_rows, 0, by_core)
        near, far = [], []
        for chunk in range(CHUNKS):
            back = spread(added(keep[chunk], received[chunk]), freq_devs)
            if step < ITERS - 1:
                near.append(next_spectra(sums, back, rcv_tables, matrix, freq_place, chunk * rows))
                far.append(exchanged(near[chunk], "rblk", 1))
            else:
                result = updated(initial, onset_rcv, back, inverse, places, chunk * rows, rows, result)
    return result


def transform_tables(length, count):
    table = fields(length, count).reshape(2 * count, length)
    forward_table = jnp.asarray(table.astype(np.float32).astype(BF16))
    inverse_table = jnp.asarray((table.T * (2.0 / length)).astype(np.float32).astype(BF16))
    return forward_table, inverse_table


def settle(values):
    return lax.optimization_barrier(values.astype(BF16)).astype(F32)


def samples_into_spectra(values, forward_table, freq_total):
    out = jnp.einsum("kt,ptn->pkn", forward_table, values, preferred_element_type=F32)
    return out.reshape(values.shape[0], 2, freq_total, values.shape[2]).astype(BF16)


def spectra_into_samples(trace_spectra, inverse_table):
    flat = trace_spectra.reshape(trace_spectra.shape[0], -1, trace_spectra.shape[3])
    return jnp.einsum("tk,pkn->ptn", inverse_table, flat, preferred_element_type=F32)


def dense(spec, gated, real, imag, sign):
    dot = functools.partial(jnp.einsum, spec, preferred_element_type=F32)
    return jnp.stack(
        [dot(gated[:, 0], real) - sign * dot(gated[:, 1], imag), dot(gated[:, 0], imag) + sign * dot(gated[:, 1], real)], 1
    )


def general_device(initial, response, aperture, onset_rcv, onset_src):
    freq_devs, rblk_devs, sblk_devs = (lax.axis_size(a) for a in ("freq", "rblk", "sblk"))
    freq_index, rblk_index, sblk_index = (lax.axis_index(a) for a in ("freq", "rblk", "sblk"))
    freq_total = response.shape[0] * freq_devs
    samples = initial.shape[1] * freq_devs
    focal_all = onset_rcv.shape[0]
    forward_table, inverse_table = transform_tables(samples, freq_total)
    steps_axis = lax.iota(jnp.int32, samples)
    own_axis = freq_index * initial.shape[1] + lax.iota(jnp.int32, initial.shape[1])
    half_rows = focal_all // sblk_devs
    own_onsets = lax.dynamic_slice_in_dim(onset_rcv, sblk_index * half_rows, half_rows, 0)
    rcv_gate = (own_axis[None, :, None] < own_onsets[:, None, :]).astype(F32)
    src_rows = focal_all // (rblk_devs * freq_devs)
    src_first = rblk_index * (focal_all // rblk_devs) + freq_index * src_rows
    src_onsets = lax.dynamic_slice_in_dim(onset_src, src_first, src_rows, 0)
    src_gate = (steps_axis[None, :, None] < src_onsets[:, None, :]).astype(F32)
    mask_full = jnp.repeat(jnp.repeat(aperture, BLOCK, 1), BLOCK, 2).astype(BF16)
    gated = response * mask_full[:, None]
    own_forward = lax.dynamic_slice_in_dim(forward_table, freq_index * initial.shape[1], initial.shape[1], 1)
    own_inverse = lax.dynamic_slice_in_dim(inverse_table, freq_index * initial.shape[1], initial.shape[1], 0)
    current = initial
    for _ in range(ITERS):
        partial = samples_into_spectra(current, own_forward, freq_total)
        spec_back = lax.psum_scatter(partial.astype(F32), "freq", scatter_dimension=2, tiled=True).astype(BF16)
        spec_all = lax.all_gather(spec_back, "sblk", axis=0, tiled=True)
        down = lax.psum_scatter(
            settle(dense("euk,bek->beu", gated, spec_all[:, 0], spec_all[:, 1], 1.0)).astype(BF16),
            "rblk",
            scatter_dimension=0,
            tiled=True,
        )
        src_traces = lax.all_to_all(down, "freq", split_axis=0, concat_axis=2, tiled=True)
        upgoing = (src_gate * spectra_into_samples(src_traces, inverse_table)).astype(BF16)
        upspec = samples_into_spectra(upgoing, forward_table, freq_total)
        up_back = lax.all_to_all(upspec, "freq", split_axis=2, concat_axis=0, tiled=True)
        up_all = lax.all_gather(up_back, "rblk", axis=0, tiled=True)
        sums = dense("qao,bqa->bqo", gated, up_all[:, 0], up_all[:, 1], -1.0).astype(BF16)
        back = lax.psum_scatter(sums, "sblk", scatter_dimension=0, tiled=True)
        traces = lax.all_gather(back, "freq", axis=2, tiled=True)
        update = rcv_gate * spectra_into_samples(traces, own_inverse)
        current = (initial.astype(F32) - update).astype(BF16)
    return current


def fits(initial, response, aperture, onset_rcv, onset_src):
    freq_devs = lax.axis_size("freq")
    if lax.axis_size("rblk") != 2 or lax.axis_size("sblk") != 2 or freq_devs & (freq_devs - 1):
        return False
    whole_rows = initial.shape[0] % (max(2, CHUNKS) * ROWS * freq_devs) == 0
    whole_width = response.shape[2] % (2 * PARTS * BLOCK) == 0 and response.shape[3] % BLOCK == 0
    return whole_rows and whole_width and onset_rcv.shape[0] == 2 * initial.shape[0]


def chosen(*arrays):
    return on_device(*arrays) if fits(*arrays) else general_device(*arrays)


def solution(mesh):
    in_specs = (
        P(("group", "sblk"), "freq", "rblk"),
        P(("group", "freq"), None, "sblk", "rblk"),
        P(("group", "freq"), "sblk", "rblk"),
        P("group", "rblk"),
        P("group", "sblk"),
    )
    out_specs = P(("group", "sblk"), "freq", "rblk")
    return jax.shard_map(chosen, mesh=mesh, in_specs=in_specs, out_specs=out_specs, check_vma=False)
```

```python
import functools
import itertools
import math

import jax
import jax.numpy as jnp
import numpy as np
from jax import lax
from jax.experimental import pallas as pl
from jax.experimental.pallas import tpu as pltpu
from jax.sharding import PartitionSpec as P

BLOCK = 128
ITERS = 2
ROWS = 8
CHUNKS = 2
PARTS = 2
VMEM_BYTES = 6 * 1024 * 1024

BF16 = jnp.bfloat16
F32 = jnp.float32


def ways(count):
    far = sorted(range(1, count), key=lambda step: (step.bit_length() < count.bit_length() - 1, step))
    return [0] + far


def slot_ways(count):
    lead = ways(count)
    return [lead, [0] + lead[:0:-1]]


def way_of(slot, core, count):
    first, second = (order[slot] for order in slot_ways(count))
    return first + core * (second - first) if first != second else first


def field_rows(place, freq_devs, per_dev, order=None):
    rows = []
    for step in order or ways(freq_devs):
        first = (place ^ step) * per_dev
        for part in range(2):
            rows.extend((part, first + local) for local in range(per_dev))
    return rows


def fields(samples, freq_total):
    phase = (np.arange(1, freq_total + 1)[:, None] * np.arange(samples)[None, :]) % samples
    angle = phase * (2.0 * math.pi / samples)
    return np.stack([np.cos(angle), -np.sin(angle)])


def inverse_tables(samples, freq_devs, per_dev):
    exact = fields(samples, freq_devs * per_dev) * (2.0 / samples)
    own = samples // freq_devs
    out = []
    for place in range(freq_devs):
        part = [exact[c, j, place * own : (place + 1) * own] for c, j in field_rows(place, freq_devs, per_dev)]
        out.append(np.repeat(np.stack(part), ROWS, 0).T)
    return np.stack(out).astype(np.float32).astype(BF16)


def window_tables(samples, freq_devs, per_dev):
    freq_total = freq_devs * per_dev
    order = np.arange(1, freq_total + 1)
    unit = 2j * math.pi / samples
    diff = order[None, :] - order[:, None]
    total = order[None, :] + order[:, None]
    same = np.where(diff == 0, 0.0, 1.0 / (samples * (np.exp(unit * np.where(diff == 0, 1, diff)) - 1.0)))
    mixed = 1.0 / (samples * (np.exp(-unit * total) - 1.0))
    full = np.zeros((2, freq_total, 2, freq_total))
    full[0, :, 0, :] = same.real + mixed.real
    full[0, :, 1, :] = mixed.imag - same.imag
    full[1, :, 0, :] = same.imag + mixed.imag
    full[1, :, 1, :] = same.real - mixed.real
    out = []
    for place, order in itertools.product(range(freq_devs), slot_ways(freq_devs)):
        rows = [c * freq_total + j for c, j in field_rows(place, freq_devs, per_dev, order)]
        flat = full.reshape(2 * freq_total, 2 * freq_total)[np.ix_(rows, rows)]
        out.append(np.kron(flat, np.eye(ROWS)))
    return np.stack(out).astype(np.float32).astype(BF16)


def call(body, scalars, inputs, outputs, grid, scratch=(), aliases=None, flops=0):
    in_arrays = [value for value, _ in inputs]
    bytes_all = sum(v.size * v.dtype.itemsize for v in in_arrays)
    bytes_all += sum(math.prod(s.shape) * s.dtype.itemsize for s, _ in outputs)
    return pl.pallas_call(
        body,
        grid_spec=pltpu.PrefetchScalarGridSpec(
            num_scalar_prefetch=len(scalars),
            grid=grid,
            in_specs=[spec for _, spec in inputs],
            out_specs=[spec for _, spec in outputs],
            scratch_shapes=list(scratch),
        ),
        out_shape=[shape for shape, _ in outputs],
        input_output_aliases=aliases or {},
        compiler_params=pltpu.CompilerParams(vmem_limit_bytes=VMEM_BYTES),
        cost_estimate=pl.CostEstimate(flops=flops, bytes_accessed=bytes_all, transcendentals=0),
    )(*scalars, *in_arrays)


def whole(array):
    zeros = (0,) * array.ndim
    return pl.BlockSpec(array.shape, lambda *_: zeros)


def sine_terms():
    square = (np.cos(np.linspace(0.0, math.pi, 200)) + 1.0) / 32.0
    y = np.sqrt(np.maximum(square, 1e-12))
    return [float(v) for v in np.polynomial.polynomial.polyfit(square, np.sin(2.0 * math.pi * y) / y, 6)]


def turned(turn):
    terms = sine_terms()

    def sine(y):
        square = y * y
        total = jnp.full_like(y, terms[-1])
        for term in terms[-2::-1]:
            total = total * square + term
        return total * y

    turn = turn - jnp.floor(turn + 0.5)
    size = jnp.abs(turn)
    folded = jnp.where(size > 0.25, jnp.where(turn > 0.0, 0.5, -0.5) - turn, turn)
    return sine(0.25 - size), sine(folded)


def first_spectra(initial, places, freq_devs, per_dev):
    rows, own, rcv = initial.shape
    samples = own * freq_devs
    tile = 2 * ROWS
    count = freq_devs * 2 * per_dev * ROWS

    def body(freq, rblk, sblk, x_ref, *rest):
        outs, spread_ref = rest[:freq_devs], rest[freq_devs]
        time = lax.broadcasted_iota(jnp.int32, (ROWS, own), 1) + freq[0] * own
        time = time.astype(F32) * (1.0 / samples)
        table = []
        for way in ways(freq_devs):
            waves = [turned(time * ((freq[0] ^ way) * per_dev + j + 1).astype(F32)) for j in range(per_dev)]
            table += [cosine for cosine, _ in waves] + [-sine for _, sine in waves]
        table = jnp.concatenate(table, 0)
        lane = lax.broadcasted_iota(jnp.int32, (count, own), 0) % ROWS
        for row in range(ROWS):
            spread_ref[:, row * own : (row + 1) * own] = jnp.where(lane == row, table, 0.0).astype(BF16)
        for at in range(rows // tile):
            parts = []
            for half in range(2):
                start = at * tile + half * ROWS
                flat = x_ref[start : start + ROWS].reshape(ROWS * own, rcv)
                value = jnp.dot(spread_ref[...], flat, preferred_element_type=F32)
                parts.append(value.reshape(freq_devs, 2, per_dev, ROWS, rcv))
            both = jnp.concatenate(parts, 3).astype(BF16)
            for step, out in enumerate(outs):
                out[:, :, at * tile : (at + 1) * tile, :] = both[step]

    shape = jax.ShapeDtypeStruct((2, per_dev, rows, rcv), BF16)
    return call(
        body,
        places,
        [(initial, whole(initial))],
        [(shape, whole(shape))] * freq_devs,
        (1,),
        scratch=[pltpu.VMEM((count, ROWS * own), BF16)],
        flops=2 * 2 * freq_devs * per_dev * own * rows * rcv,
    )


def masked_halves(response, aperture, places):
    per_dev, _, src, rcv = response.shape
    half = src // 2
    width = half // PARTS

    def body(_, rblk, __, flags, x_ref, *outs):
        lane = lax.broadcasted_iota(jnp.int32, (1, rcv), 1) // BLOCK
        for flip in (1, 0):
            for j in range(per_dev):
                for step in range(half // BLOCK):
                    block = (rblk[0] ^ flip) * (half // BLOCK) + step
                    on = flags[j, pl.ds(block, 1), :].astype(F32)
                    row = sum(jnp.where(lane == r, on[:, r : r + 1], 0.0) for r in range(rcv // BLOCK))
                    gate = jnp.broadcast_to(row, (BLOCK, rcv)).astype(BF16)
                    rows = pl.ds(pl.multiple_of(block * BLOCK, BLOCK), BLOCK)
                    part, at = divmod(step * BLOCK, width)
                    out = outs[flip * PARTS + part]
                    for c in range(2):
                        out[j, at : at + BLOCK, c * rcv : (c + 1) * rcv] = x_ref[j, c, rows, :] * gate

    shape = jax.ShapeDtypeStruct((per_dev, width, 2 * rcv), BF16)
    inputs = [(v, whole(v)) for v in (aperture, response)]
    outs = call(body, places, inputs, [(shape, whole(shape))] * (2 * PARTS), (1,))
    return list(outs[:PARTS]), list(outs[PARTS:])


def summed(parts):
    def body(*refs):
        total = sum(ref[...].astype(F32) for ref in refs[:-2])
        refs[-2][...] = total
        refs[-1][...] = total.astype(BF16)

    shapes = [jax.ShapeDtypeStruct(parts[0].shape, kind) for kind in (F32, BF16)]
    return call(body, (), [(v, whole(v)) for v in parts], [(v, whole(v)) for v in shapes], (1,))


def added(keep, received):
    def body(k_ref, r_ref, out):
        out[...] = (k_ref[...] + r_ref[...].astype(F32)).astype(BF16)

    shape = jax.ShapeDtypeStruct(keep.shape, BF16)
    (out,) = call(body, (), [(v, whole(v)) for v in (keep, received)], [(shape, whole(shape))], (1,))
    return out


def src_onsets(onset, places, half_rows, share, width):

    def body(freq, rblk, sblk, o_ref, own, other):
        lanes = pl.ds(pl.multiple_of(rblk[0] * width, BLOCK), width)
        for core, out in ((sblk[0], own), (1 - sblk[0], other)):
            spot = pl.multiple_of(core * half_rows + freq[0] * share, ROWS)
            out[...] = o_ref[pl.ds(spot, share), lanes]

    shape = jax.ShapeDtypeStruct((share, width), onset.dtype)
    return call(body, places, [(onset, whole(onset))], [(shape, whole(shape))] * 2, (1,))


def phase_tables(src, rcv, places, freq_devs, per_dev, samples, parts, rows):
    width = src[0].shape[1] // parts

    def fill(outs, value, to, freq, order_of):
        cosines, sines, fraction = outs
        value = value.astype(F32) * (1.0 / samples)
        fraction[:, to] = value
        for step, way in enumerate(order_of):
            for j in range(per_dev):
                order = ((freq[0] ^ way) * per_dev + j + 1).astype(F32)
                cosines[step, j, :, to], sines[step, j, :, to] = turned(value * order)

    def body(freq, _, sblk, own, other, r_ref, *outs):
        slots = [way_of(slot, sblk[0], freq_devs) for slot in range(freq_devs)]
        for part in range(parts):
            for spot, ref in enumerate((own, other)):
                at = (part * 2 + spot) * width
                fill(outs[:3], ref[:, part * width : (part + 1) * width], slice(at, at + width), freq, slots)
        value = r_ref[pl.ds(pl.multiple_of(sblk[0] * rows, ROWS), rows), :]
        fill(outs[3:], value, slice(0, value.shape[1]), freq, ways(freq_devs))

    shapes = []
    for count, total in ((src[0].shape[0], 2 * src[0].shape[1]), (rows, rcv.shape[1])):
        table = jax.ShapeDtypeStruct((freq_devs, per_dev, count, total), F32)
        shapes += [table, table, jax.ShapeDtypeStruct(table.shape[2:], F32)]
    outs = call(body, places, [(v, whole(v)) for v in (*src, rcv)], [(v, whole(v)) for v in shapes], (1,))
    return tuple(outs[:3]), tuple(outs[3:])


def down_products(before, spectra, parts, side, first, places, freq_devs=0, by_core=False):
    _, per_dev, _, rcv = spectra[0].shape
    rows = sum(v.shape[2] for v in spectra)
    flat = [pair[side] for part in parts for pair in part]
    width = flat[0].shape[1]
    total_width = before.shape[-1] if before is not None else first + width * len(flat)
    share = rows // freq_devs if freq_devs else 0
    old = [] if before is None else [before]

    def body(freq, _, sblk, *rest):
        held_ref, rest = (rest[0], rest[1:]) if old else (None, rest)
        refs, resp, outs = rest[: len(spectra)], rest[len(spectra) : len(spectra) + len(flat)], rest[len(spectra) + len(flat) :]
        held = outs[-1]
        for j in range(per_dev):
            real = jnp.concatenate([ref[0, j] for ref in refs], 0)
            imag = jnp.concatenate([ref[1, j] for ref in refs], 0)
            lhs = jnp.concatenate([jnp.concatenate([real, -imag], 1), jnp.concatenate([imag, real], 1)], 0)
            for at, ref in enumerate(resp):
                total = lax.dot_general(lhs, ref[j], (((1,), (1,)), ((), ())), preferred_element_type=F32)
                to = slice(first + at * width, first + (at + 1) * width)
                for part in range(2):
                    value = total[part * rows : (part + 1) * rows]
                    held[part, j, :, to] = value + held_ref[part, j, :, to] if old else value
        if old:
            for to in (slice(0, first), slice(first + len(flat) * width, total_width)):
                if to.start < to.stop:
                    held[:, :, :, to] = held_ref[:, :, :, to]
        if freq_devs:
            for slot, out in enumerate(outs[:freq_devs]):
                way = way_of(slot, sblk[0] if by_core else 0, freq_devs)
                start = pl.multiple_of((freq[0] ^ way) * share, share)
                out[...] = held[:, :, pl.ds(start, share), :].reshape(out.shape).astype(BF16)

    sums = (2, per_dev, rows, total_width)
    if freq_devs:
        shapes = [jax.ShapeDtypeStruct((2 * per_dev * share, total_width), BF16)] * freq_devs
    else:
        shapes = [jax.ShapeDtypeStruct(sums, F32)]
    outs = call(
        body,
        places,
        [(v, whole(v)) for v in (*old, *spectra, *flat)],
        [(v, whole(v)) for v in shapes],
        (1,),
        scratch=[pltpu.VMEM(sums, F32)] if freq_devs else [],
        flops=2 * 4 * per_dev * rows * len(flat) * width * rcv,
    )
    return outs if freq_devs else outs[0]


def mixed_fields(plain, cos, sin, matrix):
    tile = plain[0].shape[-1]
    turned = [
        jnp.stack([v[0] * c - v[1] * s, v[0] * s + v[1] * c]) for v, c, s in zip(plain, cos, sin)
    ]
    flat = [jnp.stack(v).reshape(matrix.shape[1], tile).astype(BF16) for v in (turned, plain)]
    mixed = jnp.dot(matrix, jnp.concatenate(flat, 1), preferred_element_type=F32)
    shape = (-1, 2) + plain[0].shape[1:]
    return mixed[:, :tile].reshape(shape), mixed[:, tile:].reshape(shape)


def unturned(up, low, value, cos, sin, part):
    real = cos * up[0] + sin * up[1] - low[0] + part * value[0]
    imag = cos * up[1] - sin * up[0] - low[1] + part * value[1]
    return jnp.stack([real, imag])


def tiles(width, body):
    def at(step, carry):
        body(pl.ds(pl.multiple_of(step * BLOCK, BLOCK), BLOCK))
        return carry

    lax.fori_loop(0, width // BLOCK, at, 0, unroll=2)


def windowed(messages, tables, matrix, places, per_dev, share, by_core):
    cosines, sines, fraction = tables
    freq_devs = len(messages)
    width = messages[0].shape[-1]
    count = freq_devs * 2 * per_dev * ROWS

    def body(freq, _, sblk, c_ref, s_ref, f_ref, g_ref, *rest):
        refs, outs = rest[:freq_devs], rest[freq_devs:]
        matrix_here = g_ref[freq[0] * 2 + (sblk[0] if by_core else 0)]
        spots = list(range(freq_devs))
        if not by_core:
            first, second = slot_ways(freq_devs)
            spots = [slot + sblk[0] * (second.index(way) - slot) for slot, way in enumerate(first)]

        def one(at):
            data = [ref[:, at].astype(F32).reshape(2, per_dev, share, BLOCK) for ref in refs]
            made = [[] for _ in outs]
            for first in range(0, share, ROWS):
                cut = slice(first, first + ROWS)
                plain = [value[:, :, cut] for value in data]
                cos = [c_ref[spot, :, cut, at] for spot in spots]
                sin = [s_ref[spot, :, cut, at] for spot in spots]
                up, low = mixed_fields(plain, cos, sin, matrix_here)
                part = f_ref[cut, at]
                for step in range(freq_devs):
                    made[step].append(unturned(up[step], low[step], plain[step], cos[step], sin[step], part))
            for out, value in zip(outs, made):
                out[:, at] = jnp.concatenate(value, 2).reshape(out.shape[0], BLOCK).astype(BF16)

        tiles(width, one)

    inputs = (cosines, sines, fraction, matrix, *messages)
    return call(
        body,
        places,
        [(v, whole(v)) for v in inputs],
        [(jax.ShapeDtypeStruct(v.shape, BF16), whole(v)) for v in messages],
        (1,),
        flops=2 * count * count * 2 * width * share // ROWS,
    )


def up_products(messages, parts, places, rows, side, by_core):
    freq_devs = len(messages)
    flat = [pair[side] for part in parts for pair in part]
    per_dev, src, rcv = flat[0].shape[0], flat[0].shape[1], flat[0].shape[2] // 2
    group = rows // CHUNKS
    share = rows // freq_devs
    total_width = src * len(flat)
    kind = BF16 if side else F32

    def body(freq, _, sblk, *rest):
        resp, refs = rest[: len(flat)], rest[len(flat) : len(flat) + freq_devs]
        outs, held = rest[len(flat) + freq_devs : -1], rest[-1]
        for slot, ref in enumerate(refs):
            way = way_of(slot, sblk[0] if by_core else 0, freq_devs)
            start = pl.multiple_of((freq[0] ^ way) * share, share)
            value = ref[...].reshape(2, per_dev, share, total_width)
            for part in range(2):
                for j in range(per_dev):
                    held[part, j, pl.ds(start, share), :] = value[part, j]
        for j in range(per_dev):
            both = jnp.concatenate([held[0, j], held[1, j]], 0)
            total = sum(
                jnp.dot(both[:, at * src : (at + 1) * src], ref[j], preferred_element_type=F32)
                for at, ref in enumerate(resp)
            )
            real = total[:rows, :rcv] + total[rows:, rcv:]
            imag = total[rows:, :rcv] - total[:rows, rcv:]
            for index, out in enumerate(outs):
                cut = slice(index * group, (index + 1) * group)
                out[0, j] = real[cut].astype(kind)
                out[1, j] = imag[cut].astype(kind)

    shape = jax.ShapeDtypeStruct((2, per_dev, group, rcv), kind)
    return call(
        body,
        places,
        [(v, whole(v)) for v in (*flat, *messages)],
        [(shape, whole(shape))] * CHUNKS,
        (1,),
        scratch=[pltpu.VMEM((2, per_dev, rows, total_width), BF16)],
        flops=2 * 4 * per_dev * rows * total_width * rcv,
    )


def next_spectra(sums, messages, tables, matrix, freq_place, first_row):
    cosines, sines, fraction = tables
    freq_devs = len(messages)
    _, per_dev, rows, rcv = messages[0].shape
    count = freq_devs * 2 * per_dev * ROWS
    own = 2 * per_dev * ROWS

    def body(place_ref, u_ref, c_ref, s_ref, f_ref, g_ref, *rest):
        refs, out = rest[:freq_devs], rest[freq_devs]
        matrix_here = g_ref[place_ref[0] * 2, :own]

        def one(at):
            for base in range(0, rows, 2 * ROWS):
                pair = slice(base, base + 2 * ROWS)
                data = [ref[:, :, pair, at].astype(F32) for ref in refs]
                made = []
                for half in range(2):
                    plain = [value[:, :, half * ROWS : (half + 1) * ROWS] for value in data]
                    cut = slice(first_row + base + half * ROWS, first_row + base + (half + 1) * ROWS)
                    cos = [c_ref[step, :, cut, at] for step in range(freq_devs)]
                    sin = [s_ref[step, :, cut, at] for step in range(freq_devs)]
                    up, low = mixed_fields(plain, cos, sin, matrix_here)
                    change = unturned(up[0], low[0], plain[0], cos[0], sin[0], f_ref[cut, at])
                    made.append(u_ref[:, :, cut, at] - change)
                out[:, :, pair, at] = jnp.concatenate(made, 2).astype(BF16)

        tiles(rcv, one)

    inputs = (sums, cosines, sines, fraction, matrix, *messages)
    shape = jax.ShapeDtypeStruct(messages[0].shape, BF16)
    (out,) = call(
        body,
        (freq_place,),
        [(v, whole(v)) for v in inputs],
        [(shape, whole(shape))],
        (1,),
        flops=2 * own * count * 2 * rcv * rows // ROWS,
    )
    return out


def updated(initial, onset, messages, table, places, first, rows, target):
    freq_devs = len(messages)
    half_rows, own, rcv = initial.shape
    per_dev = messages[0].shape[1]
    tile = 2 * ROWS
    count = table.shape[2]

    def body(place_ref, _, sblk, x_ref, o_ref, t_ref, *rest):
        refs = rest[:freq_devs]
        out, spread_ref = rest[-2:]
        step = pl.program_id(0)

        @pl.when(step == 0)
        def _():
            base = t_ref[place_ref[0]].astype(F32)
            lane = lax.broadcasted_iota(jnp.int32, (own, count), 1) % ROWS
            for row in range(ROWS):
                spread_ref[row * own : (row + 1) * own] = jnp.where(lane == row, base, 0.0).astype(BF16)

        here = pl.ds(pl.multiple_of(step * tile, tile), tile)
        data = [ref[:, :, here, :].astype(F32) for ref in refs]
        onsets = o_ref[pl.ds(pl.multiple_of(sblk[0] * half_rows + first + step * tile, tile), tile), :]
        time = lax.broadcasted_iota(jnp.int32, (own, rcv), 0) + place_ref[0] * own
        for half in range(2):
            cut = slice(half * ROWS, (half + 1) * ROWS)
            flat = jnp.stack([v[:, :, cut] for v in data]).reshape(count, rcv).astype(BF16)
            change = jnp.dot(spread_ref[...], flat, preferred_element_type=F32)
            for row in range(ROWS):
                spot = half * ROWS + row
                on = time < onsets[spot : spot + 1, :]
                moved = jnp.where(on, change[row * own : (row + 1) * own], 0.0)
                out[spot] = (x_ref[first + step * tile + spot].astype(F32) - moved).astype(BF16)

    inputs = [(v, whole(v)) for v in (initial, onset, table, *messages)]
    aliases = {}
    if target is not None:
        inputs.append((target, pl.BlockSpec(memory_space=pl.ANY)))
        aliases = {len(places) + len(inputs) - 1: 0}
    (out,) = call(
        body,
        places,
        inputs,
        [(jax.ShapeDtypeStruct(initial.shape, BF16), pl.BlockSpec((tile, own, rcv), lambda i, *_: (first // tile + i, 0, 0)))],
        (rows // tile,),
        scratch=[pltpu.VMEM((ROWS * own, count), BF16)],
        aliases=aliases,
        flops=2 * 2 * freq_devs * per_dev * own * rows * rcv,
    )
    return out


def exchanged(value, axis, step):
    return lax.ppermute(value, axis, [(i, i ^ step) for i in range(lax.axis_size(axis))])


def dealt_out(parts):
    return [exchanged(part, "freq", step) if step else part for part, step in zip(parts, ways(len(parts)))]


def dealt_by_core(parts):
    count = len(parts)
    out = [parts[0]]
    for slot in range(1, count):
        steps = [order[slot] for order in slot_ways(count)]
        pairs = [(f * 2 + core, (f ^ steps[core]) * 2 + core) for f in range(count) for core in range(2)]
        out.append(lax.ppermute(parts[slot], ("freq", "sblk"), pairs))
    return out


def spread(value, count):
    held = {0: value}
    bit = count // 2
    while bit:
        held.update({way | bit: exchanged(held[way], "freq", bit) for way in sorted(held)})
        bit //= 2
    return [held[way] for way in ways(count)]


def on_device(initial, response, aperture, onset_rcv, onset_src):
    freq_devs = lax.axis_size("freq")
    per_dev = response.shape[0]
    samples = initial.shape[1] * freq_devs
    half_rows = initial.shape[0]
    src_width = response.shape[2] // 2
    rows = half_rows // CHUNKS
    share = half_rows // freq_devs
    places = tuple(lax.axis_index(axis).reshape(1) for axis in ("freq", "rblk", "sblk"))
    freq_place = places[0]
    inverse = jnp.asarray(inverse_tables(samples, freq_devs, per_dev))
    matrix = jnp.asarray(window_tables(samples, freq_devs, per_dev))

    kept, sent = masked_halves(response, aperture, places)
    moved = [exchanged(v, "rblk", 1) for v in sent]
    kept_pair = [exchanged(v, "sblk", 1) for v in kept]
    sums, spectra = summed(dealt_out(first_spectra(initial, places, freq_devs, per_dev)))
    far = exchanged(spectra, "rblk", 1)
    moved_pair = []
    for index in range(PARTS):
        if index:
            moved[index], far = lax.optimization_barrier((moved[index], far))
        else:
            moved[index], spectra = lax.optimization_barrier((moved[index], spectra))
        moved_pair.append(exchanged(moved[index], "sblk", 1))
    parts = [((kept[i], moved[i]), (kept_pair[i], moved_pair[i])) for i in range(PARTS)]

    own, other = src_onsets(onset_src, places, half_rows, share, src_width)
    onsets = (own, exchanged(other, "sblk", 1))
    src_tables, rcv_tables = phase_tables(onsets, onset_rcv, places, freq_devs, per_dev, samples, PARTS, half_rows)

    near, far, result = [spectra], [far], None
    for step in range(ITERS):
        held = down_products(None, near, parts, 0, 0, places)
        at = 0 if step else PARTS - 1
        if at:
            held = down_products(held, far, parts[:at], 1, 0, places)
        first = at * 2 * kept[0].shape[1]
        by_core = step > 0
        deal = dealt_by_core if by_core else dealt_out
        messages = deal(down_products(held, far, parts[at:], 1, first, places, freq_devs, by_core))
        messages = deal(windowed(messages, src_tables, matrix, places, per_dev, share, by_core))
        received = [exchanged(v, "rblk", 1) for v in up_products(messages, parts, places, half_rows, 1, by_core)]
        keep = up_products(messages, parts, places, half_rows, 0, by_core)
        near, far = [], []
        for chunk in range(CHUNKS):
            back = spread(added(keep[chunk], received[chunk]), freq_devs)
            if step < ITERS - 1:
                near.append(next_spectra(sums, back, rcv_tables, matrix, freq_place, chunk * rows))
                far.append(exchanged(near[chunk], "rblk", 1))
            else:
                result = updated(initial, onset_rcv, back, inverse, places, chunk * rows, rows, result)
    return result


def transform_tables(length, count):
    table = fields(length, count).reshape(2 * count, length)
    forward_table = jnp.asarray(table.astype(np.float32).astype(BF16))
    inverse_table = jnp.asarray((table.T * (2.0 / length)).astype(np.float32).astype(BF16))
    return forward_table, inverse_table


def settle(values):
    return lax.optimization_barrier(values.astype(BF16)).astype(F32)


def samples_into_spectra(values, forward_table, freq_total):
    out = jnp.einsum("kt,ptn->pkn", forward_table, values, preferred_element_type=F32)
    return out.reshape(values.shape[0], 2, freq_total, values.shape[2]).astype(BF16)


def spectra_into_samples(trace_spectra, inverse_table):
    flat = trace_spectra.reshape(trace_spectra.shape[0], -1, trace_spectra.shape[3])
    return jnp.einsum("tk,pkn->ptn", inverse_table, flat, preferred_element_type=F32)


def dense(spec, gated, real, imag, sign):
    dot = functools.partial(jnp.einsum, spec, preferred_element_type=F32)
    return jnp.stack(
        [dot(gated[:, 0], real) - sign * dot(gated[:, 1], imag), dot(gated[:, 0], imag) + sign * dot(gated[:, 1], real)], 1
    )


def general_device(initial, response, aperture, onset_rcv, onset_src):
    freq_devs, rblk_devs, sblk_devs = (lax.axis_size(a) for a in ("freq", "rblk", "sblk"))
    freq_index, rblk_index, sblk_index = (lax.axis_index(a) for a in ("freq", "rblk", "sblk"))
    freq_total = response.shape[0] * freq_devs
    samples = initial.shape[1] * freq_devs
    focal_all = onset_rcv.shape[0]
    forward_table, inverse_table = transform_tables(samples, freq_total)
    steps_axis = lax.iota(jnp.int32, samples)
    own_axis = freq_index * initial.shape[1] + lax.iota(jnp.int32, initial.shape[1])
    half_rows = focal_all // sblk_devs
    own_onsets = lax.dynamic_slice_in_dim(onset_rcv, sblk_index * half_rows, half_rows, 0)
    rcv_gate = (own_axis[None, :, None] < own_onsets[:, None, :]).astype(F32)
    src_rows = focal_all // (rblk_devs * freq_devs)
    src_first = rblk_index * (focal_all // rblk_devs) + freq_index * src_rows
    src_onsets = lax.dynamic_slice_in_dim(onset_src, src_first, src_rows, 0)
    src_gate = (steps_axis[None, :, None] < src_onsets[:, None, :]).astype(F32)
    mask_full = jnp.repeat(jnp.repeat(aperture, BLOCK, 1), BLOCK, 2).astype(BF16)
    gated = response * mask_full[:, None]
    own_forward = lax.dynamic_slice_in_dim(forward_table, freq_index * initial.shape[1], initial.shape[1], 1)
    own_inverse = lax.dynamic_slice_in_dim(inverse_table, freq_index * initial.shape[1], initial.shape[1], 0)
    current = initial
    for _ in range(ITERS):
        partial = samples_into_spectra(current, own_forward, freq_total)
        spec_back = lax.psum_scatter(partial.astype(F32), "freq", scatter_dimension=2, tiled=True).astype(BF16)
        spec_all = lax.all_gather(spec_back, "sblk", axis=0, tiled=True)
        down = lax.psum_scatter(
            settle(dense("euk,bek->beu", gated, spec_all[:, 0], spec_all[:, 1], 1.0)).astype(BF16),
            "rblk",
            scatter_dimension=0,
            tiled=True,
        )
        src_traces = lax.all_to_all(down, "freq", split_axis=0, concat_axis=2, tiled=True)
        upgoing = (src_gate * spectra_into_samples(src_traces, inverse_table)).astype(BF16)
        upspec = samples_into_spectra(upgoing, forward_table, freq_total)
        up_back = lax.all_to_all(upspec, "freq", split_axis=2, concat_axis=0, tiled=True)
        up_all = lax.all_gather(up_back, "rblk", axis=0, tiled=True)
        sums = dense("qao,bqa->bqo", gated, up_all[:, 0], up_all[:, 1], -1.0).astype(BF16)
        back = lax.psum_scatter(sums, "sblk", scatter_dimension=0, tiled=True)
        traces = lax.all_gather(back, "freq", axis=2, tiled=True)
        update = rcv_gate * spectra_into_samples(traces, own_inverse)
        current = (initial.astype(F32) - update).astype(BF16)
    return current


def fits(initial, response, aperture, onset_rcv, onset_src):
    freq_devs = lax.axis_size("freq")
    if lax.axis_size("rblk") != 2 or lax.axis_size("sblk") != 2 or freq_devs & (freq_devs - 1):
        return False
    whole_rows = initial.shape[0] % (max(2, CHUNKS) * ROWS * freq_devs) == 0
    whole_width = response.shape[2] % (2 * PARTS * BLOCK) == 0 and response.shape[3] % BLOCK == 0
    return whole_rows and whole_width and onset_rcv.shape[0] == 2 * initial.shape[0]


def chosen(*arrays):
    return on_device(*arrays) if fits(*arrays) else general_device(*arrays)


def solution(mesh):
    in_specs = (
        P(("group", "sblk"), "freq", "rblk"),
        P(("group", "freq"), None, "sblk", "rblk"),
        P(("group", "freq"), "sblk", "rblk"),
        P("group", "rblk"),
        P("group", "sblk"),
    )
    out_specs = P(("group", "sblk"), "freq", "rblk")
    return jax.shard_map(chosen, mesh=mesh, in_specs=in_specs, out_specs=out_specs, check_vma=False)
```

```python
import functools
import math

import jax
import jax.numpy as jnp
import numpy as np
from jax import lax
from jax.experimental import pallas as pl
from jax.experimental.pallas import tpu as pltpu
from jax.sharding import PartitionSpec as P

BLOCK = 128
ITERS = 2
ROWS = 8
CHUNKS = 2
PARTS = 2
VMEM_BYTES = 6 * 1024 * 1024

BF16 = jnp.bfloat16
F32 = jnp.float32


def ways(count):
    far = sorted(range(1, count), key=lambda step: (step.bit_length() < count.bit_length() - 1, step))
    return [0] + far


def field_rows(place, freq_devs, per_dev):
    rows = []
    for step in ways(freq_devs):
        first = (place ^ step) * per_dev
        for part in range(2):
            rows.extend((part, first + local) for local in range(per_dev))
    return rows


def fields(samples, freq_total):
    phase = (np.arange(1, freq_total + 1)[:, None] * np.arange(samples)[None, :]) % samples
    angle = phase * (2.0 * math.pi / samples)
    return np.stack([np.cos(angle), -np.sin(angle)])


def inverse_tables(samples, freq_devs, per_dev):
    exact = fields(samples, freq_devs * per_dev) * (2.0 / samples)
    own = samples // freq_devs
    out = []
    for place in range(freq_devs):
        part = [exact[c, j, place * own : (place + 1) * own] for c, j in field_rows(place, freq_devs, per_dev)]
        out.append(np.repeat(np.stack(part), ROWS, 0).T)
    return np.stack(out).astype(np.float32).astype(BF16)


def window_tables(samples, freq_devs, per_dev):
    freq_total = freq_devs * per_dev
    order = np.arange(1, freq_total + 1)
    unit = 2j * math.pi / samples
    diff = order[None, :] - order[:, None]
    total = order[None, :] + order[:, None]
    same = np.where(diff == 0, 0.0, 1.0 / (samples * (np.exp(unit * np.where(diff == 0, 1, diff)) - 1.0)))
    mixed = 1.0 / (samples * (np.exp(-unit * total) - 1.0))
    full = np.zeros((2, freq_total, 2, freq_total))
    full[0, :, 0, :] = same.real + mixed.real
    full[0, :, 1, :] = mixed.imag - same.imag
    full[1, :, 0, :] = same.imag + mixed.imag
    full[1, :, 1, :] = same.real - mixed.real
    out = []
    for place in range(freq_devs):
        rows = [c * freq_total + j for c, j in field_rows(place, freq_devs, per_dev)]
        flat = full.reshape(2 * freq_total, 2 * freq_total)[np.ix_(rows, rows)]
        out.append(np.kron(flat, np.eye(ROWS)))
    return np.stack(out).astype(np.float32).astype(BF16)


def call(body, scalars, inputs, outputs, grid, scratch=(), aliases=None, flops=0):
    in_arrays = [value for value, _ in inputs]
    bytes_all = sum(v.size * v.dtype.itemsize for v in in_arrays)
    bytes_all += sum(math.prod(s.shape) * s.dtype.itemsize for s, _ in outputs)
    return pl.pallas_call(
        body,
        grid_spec=pltpu.PrefetchScalarGridSpec(
            num_scalar_prefetch=len(scalars),
            grid=grid,
            in_specs=[spec for _, spec in inputs],
            out_specs=[spec for _, spec in outputs],
            scratch_shapes=list(scratch),
        ),
        out_shape=[shape for shape, _ in outputs],
        input_output_aliases=aliases or {},
        compiler_params=pltpu.CompilerParams(vmem_limit_bytes=VMEM_BYTES),
        cost_estimate=pl.CostEstimate(flops=flops, bytes_accessed=bytes_all, transcendentals=0),
    )(*scalars, *in_arrays)


def whole(array):
    zeros = (0,) * array.ndim
    return pl.BlockSpec(array.shape, lambda *_: zeros)


def sine_terms():
    square = (np.cos(np.linspace(0.0, math.pi, 200)) + 1.0) / 32.0
    y = np.sqrt(np.maximum(square, 1e-12))
    return [float(v) for v in np.polynomial.polynomial.polyfit(square, np.sin(2.0 * math.pi * y) / y, 6)]


def turned(turn):
    terms = sine_terms()

    def sine(y):
        square = y * y
        total = jnp.full_like(y, terms[-1])
        for term in terms[-2::-1]:
            total = total * square + term
        return total * y

    turn = turn - jnp.floor(turn + 0.5)
    size = jnp.abs(turn)
    folded = jnp.where(size > 0.25, jnp.where(turn > 0.0, 0.5, -0.5) - turn, turn)
    return sine(0.25 - size), sine(folded)


def first_spectra(initial, places, freq_devs, per_dev):
    rows, own, rcv = initial.shape
    samples = own * freq_devs
    tile = 2 * ROWS
    count = freq_devs * 2 * per_dev * ROWS

    def body(freq, rblk, sblk, x_ref, *rest):
        outs, spread_ref = rest[:freq_devs], rest[freq_devs]
        time = lax.broadcasted_iota(jnp.int32, (ROWS, own), 1) + freq[0] * own
        time = time.astype(F32) * (1.0 / samples)
        table = []
        for way in ways(freq_devs):
            waves = [turned(time * ((freq[0] ^ way) * per_dev + j + 1).astype(F32)) for j in range(per_dev)]
            table += [cosine for cosine, _ in waves] + [-sine for _, sine in waves]
        table = jnp.concatenate(table, 0)
        lane = lax.broadcasted_iota(jnp.int32, (count, own), 0) % ROWS
        for row in range(ROWS):
            spread_ref[:, row * own : (row + 1) * own] = jnp.where(lane == row, table, 0.0).astype(BF16)
        for at in range(rows // tile):
            parts = []
            for half in range(2):
                start = at * tile + half * ROWS
                flat = x_ref[start : start + ROWS].reshape(ROWS * own, rcv)
                value = jnp.dot(spread_ref[...], flat, preferred_element_type=F32)
                parts.append(value.reshape(freq_devs, 2, per_dev, ROWS, rcv))
            both = jnp.concatenate(parts, 3).astype(BF16)
            for step, out in enumerate(outs):
                out[:, :, at * tile : (at + 1) * tile, :] = both[step]

    shape = jax.ShapeDtypeStruct((2, per_dev, rows, rcv), BF16)
    return call(
        body,
        places,
        [(initial, whole(initial))],
        [(shape, whole(shape))] * freq_devs,
        (1,),
        scratch=[pltpu.VMEM((count, ROWS * own), BF16)],
        flops=2 * 2 * freq_devs * per_dev * own * rows * rcv,
    )


def masked_halves(response, aperture, places):
    per_dev, _, src, rcv = response.shape
    half = src // 2
    width = half // PARTS

    def body(_, rblk, __, flags, x_ref, *outs):
        lane = lax.broadcasted_iota(jnp.int32, (1, rcv), 1) // BLOCK
        for flip in (1, 0):
            for j in range(per_dev):
                for step in range(half // BLOCK):
                    block = (rblk[0] ^ flip) * (half // BLOCK) + step
                    on = flags[j, pl.ds(block, 1), :].astype(F32)
                    row = sum(jnp.where(lane == r, on[:, r : r + 1], 0.0) for r in range(rcv // BLOCK))
                    gate = jnp.broadcast_to(row, (BLOCK, rcv)).astype(BF16)
                    rows = pl.ds(pl.multiple_of(block * BLOCK, BLOCK), BLOCK)
                    part, at = divmod(step * BLOCK, width)
                    out = outs[flip * PARTS + part]
                    for c in range(2):
                        out[j, at : at + BLOCK, c * rcv : (c + 1) * rcv] = x_ref[j, c, rows, :] * gate

    shape = jax.ShapeDtypeStruct((per_dev, width, 2 * rcv), BF16)
    inputs = [(v, whole(v)) for v in (aperture, response)]
    outs = call(body, places, inputs, [(shape, whole(shape))] * (2 * PARTS), (1,))
    return list(outs[:PARTS]), list(outs[PARTS:])


def summed(parts):
    def body(*refs):
        total = sum(ref[...].astype(F32) for ref in refs[:-2])
        refs[-2][...] = total
        refs[-1][...] = total.astype(BF16)

    shapes = [jax.ShapeDtypeStruct(parts[0].shape, kind) for kind in (F32, BF16)]
    return call(body, (), [(v, whole(v)) for v in parts], [(v, whole(v)) for v in shapes], (1,))


def added(keep, received):
    def body(k_ref, r_ref, out):
        out[...] = (k_ref[...] + r_ref[...].astype(F32)).astype(BF16)

    shape = jax.ShapeDtypeStruct(keep.shape, BF16)
    (out,) = call(body, (), [(v, whole(v)) for v in (keep, received)], [(shape, whole(shape))], (1,))
    return out


def src_onsets(onset, places, half_rows, share, width):

    def body(freq, rblk, sblk, o_ref, own, other):
        lanes = pl.ds(pl.multiple_of(rblk[0] * width, BLOCK), width)
        for core, out in ((sblk[0], own), (1 - sblk[0], other)):
            spot = pl.multiple_of(core * half_rows + freq[0] * share, ROWS)
            out[...] = o_ref[pl.ds(spot, share), lanes]

    shape = jax.ShapeDtypeStruct((share, width), onset.dtype)
    return call(body, places, [(onset, whole(onset))], [(shape, whole(shape))] * 2, (1,))


def phase_tables(src, rcv, places, freq_devs, per_dev, samples, parts, rows):
    width = src[0].shape[1] // parts

    def fill(outs, value, to, freq):
        cosines, sines, fraction = outs
        value = value.astype(F32) * (1.0 / samples)
        fraction[:, to] = value
        for step, way in enumerate(ways(freq_devs)):
            for j in range(per_dev):
                order = ((freq[0] ^ way) * per_dev + j + 1).astype(F32)
                cosines[step, j, :, to], sines[step, j, :, to] = turned(value * order)

    def body(freq, _, sblk, own, other, r_ref, *outs):
        for part in range(parts):
            for spot, ref in enumerate((own, other)):
                at = (part * 2 + spot) * width
                fill(outs[:3], ref[:, part * width : (part + 1) * width], slice(at, at + width), freq)
        value = r_ref[pl.ds(pl.multiple_of(sblk[0] * rows, ROWS), rows), :]
        fill(outs[3:], value, slice(0, value.shape[1]), freq)

    shapes = []
    for count, total in ((src[0].shape[0], 2 * src[0].shape[1]), (rows, rcv.shape[1])):
        table = jax.ShapeDtypeStruct((freq_devs, per_dev, count, total), F32)
        shapes += [table, table, jax.ShapeDtypeStruct(table.shape[2:], F32)]
    outs = call(body, places, [(v, whole(v)) for v in (*src, rcv)], [(v, whole(v)) for v in shapes], (1,))
    return tuple(outs[:3]), tuple(outs[3:])


def down_products(before, spectra, parts, side, first, freq_place, freq_devs=0):
    _, per_dev, _, rcv = spectra[0].shape
    rows = sum(v.shape[2] for v in spectra)
    flat = [pair[side] for part in parts for pair in part]
    width = flat[0].shape[1]
    total_width = before.shape[-1] if before is not None else first + width * len(flat)
    share = rows // freq_devs if freq_devs else 0
    old = [] if before is None else [before]

    def body(place_ref, *rest):
        held_ref, rest = (rest[0], rest[1:]) if old else (None, rest)
        refs, resp, outs = rest[: len(spectra)], rest[len(spectra) : len(spectra) + len(flat)], rest[len(spectra) + len(flat) :]
        held = outs[-1]
        for j in range(per_dev):
            real = jnp.concatenate([ref[0, j] for ref in refs], 0)
            imag = jnp.concatenate([ref[1, j] for ref in refs], 0)
            lhs = jnp.concatenate([jnp.concatenate([real, -imag], 1), jnp.concatenate([imag, real], 1)], 0)
            for at, ref in enumerate(resp):
                total = lax.dot_general(lhs, ref[j], (((1,), (1,)), ((), ())), preferred_element_type=F32)
                to = slice(first + at * width, first + (at + 1) * width)
                for part in range(2):
                    value = total[part * rows : (part + 1) * rows]
                    held[part, j, :, to] = value + held_ref[part, j, :, to] if old else value
        if old:
            for to in (slice(0, first), slice(first + len(flat) * width, total_width)):
                if to.start < to.stop:
                    held[:, :, :, to] = held_ref[:, :, :, to]
        if freq_devs:
            for way, out in zip(ways(freq_devs), outs):
                start = pl.multiple_of((place_ref[0] ^ way) * share, share)
                out[...] = held[:, :, pl.ds(start, share), :].reshape(out.shape).astype(BF16)

    sums = (2, per_dev, rows, total_width)
    if freq_devs:
        shapes = [jax.ShapeDtypeStruct((2 * per_dev * share, total_width), BF16)] * freq_devs
    else:
        shapes = [jax.ShapeDtypeStruct(sums, F32)]
    outs = call(
        body,
        (freq_place,),
        [(v, whole(v)) for v in (*old, *spectra, *flat)],
        [(v, whole(v)) for v in shapes],
        (1,),
        scratch=[pltpu.VMEM(sums, F32)] if freq_devs else [],
        flops=2 * 4 * per_dev * rows * len(flat) * width * rcv,
    )
    return outs if freq_devs else outs[0]


def mixed_fields(plain, cos, sin, matrix):
    tile = plain[0].shape[-1]
    turned = [
        jnp.stack([v[0] * c - v[1] * s, v[0] * s + v[1] * c]) for v, c, s in zip(plain, cos, sin)
    ]
    flat = [jnp.stack(v).reshape(matrix.shape[1], tile).astype(BF16) for v in (turned, plain)]
    mixed = jnp.dot(matrix, jnp.concatenate(flat, 1), preferred_element_type=F32)
    shape = (-1, 2) + plain[0].shape[1:]
    return mixed[:, :tile].reshape(shape), mixed[:, tile:].reshape(shape)


def unturned(up, low, value, cos, sin, part):
    real = cos * up[0] + sin * up[1] - low[0] + part * value[0]
    imag = cos * up[1] - sin * up[0] - low[1] + part * value[1]
    return jnp.stack([real, imag])


def tiles(width, body):
    def at(step, carry):
        body(pl.ds(pl.multiple_of(step * BLOCK, BLOCK), BLOCK))
        return carry

    lax.fori_loop(0, width // BLOCK, at, 0, unroll=2)


def windowed(messages, tables, matrix, freq_place, per_dev, share):
    cosines, sines, fraction = tables
    freq_devs = len(messages)
    width = messages[0].shape[-1]
    count = freq_devs * 2 * per_dev * ROWS

    def body(place_ref, c_ref, s_ref, f_ref, g_ref, *rest):
        refs, outs = rest[:freq_devs], rest[freq_devs:]
        matrix_here = g_ref[place_ref[0]]

        def one(at):
            data = [ref[:, at].astype(F32).reshape(2, per_dev, share, BLOCK) for ref in refs]
            made = [[] for _ in outs]
            for first in range(0, share, ROWS):
                cut = slice(first, first + ROWS)
                plain = [value[:, :, cut] for value in data]
                cos = [c_ref[step, :, cut, at] for step in range(freq_devs)]
                sin = [s_ref[step, :, cut, at] for step in range(freq_devs)]
                up, low = mixed_fields(plain, cos, sin, matrix_here)
                part = f_ref[cut, at]
                for step in range(freq_devs):
                    made[step].append(unturned(up[step], low[step], plain[step], cos[step], sin[step], part))
            for out, value in zip(outs, made):
                out[:, at] = jnp.concatenate(value, 2).reshape(out.shape[0], BLOCK).astype(BF16)

        tiles(width, one)

    inputs = (cosines, sines, fraction, matrix, *messages)
    return call(
        body,
        (freq_place,),
        [(v, whole(v)) for v in inputs],
        [(jax.ShapeDtypeStruct(v.shape, BF16), whole(v)) for v in messages],
        (1,),
        flops=2 * count * count * 2 * width * share // ROWS,
    )


def up_products(messages, parts, freq_place, rows, side):
    freq_devs = len(messages)
    flat = [pair[side] for part in parts for pair in part]
    per_dev, src, rcv = flat[0].shape[0], flat[0].shape[1], flat[0].shape[2] // 2
    group = rows // CHUNKS
    share = rows // freq_devs
    total_width = src * len(flat)
    kind = BF16 if side else F32

    def body(place_ref, *rest):
        resp, refs = rest[: len(flat)], rest[len(flat) : len(flat) + freq_devs]
        outs, held = rest[len(flat) + freq_devs : -1], rest[-1]
        for way, ref in zip(ways(freq_devs), refs):
            start = pl.multiple_of((place_ref[0] ^ way) * share, share)
            value = ref[...].reshape(2, per_dev, share, total_width)
            for part in range(2):
                for j in range(per_dev):
                    held[part, j, pl.ds(start, share), :] = value[part, j]
        for j in range(per_dev):
            both = jnp.concatenate([held[0, j], held[1, j]], 0)
            total = sum(
                jnp.dot(both[:, at * src : (at + 1) * src], ref[j], preferred_element_type=F32)
                for at, ref in enumerate(resp)
            )
            real = total[:rows, :rcv] + total[rows:, rcv:]
            imag = total[rows:, :rcv] - total[:rows, rcv:]
            for index, out in enumerate(outs):
                cut = slice(index * group, (index + 1) * group)
                out[0, j] = real[cut].astype(kind)
                out[1, j] = imag[cut].astype(kind)

    shape = jax.ShapeDtypeStruct((2, per_dev, group, rcv), kind)
    return call(
        body,
        (freq_place,),
        [(v, whole(v)) for v in (*flat, *messages)],
        [(shape, whole(shape))] * CHUNKS,
        (1,),
        scratch=[pltpu.VMEM((2, per_dev, rows, total_width), BF16)],
        flops=2 * 4 * per_dev * rows * total_width * rcv,
    )


def next_spectra(sums, messages, tables, matrix, freq_place, first_row):
    cosines, sines, fraction = tables
    freq_devs = len(messages)
    _, per_dev, rows, rcv = messages[0].shape
    count = freq_devs * 2 * per_dev * ROWS
    own = 2 * per_dev * ROWS

    def body(place_ref, u_ref, c_ref, s_ref, f_ref, g_ref, *rest):
        refs, out = rest[:freq_devs], rest[freq_devs]
        matrix_here = g_ref[place_ref[0], :own]

        def one(at):
            for base in range(0, rows, 2 * ROWS):
                pair = slice(base, base + 2 * ROWS)
                data = [ref[:, :, pair, at].astype(F32) for ref in refs]
                made = []
                for half in range(2):
                    plain = [value[:, :, half * ROWS : (half + 1) * ROWS] for value in data]
                    cut = slice(first_row + base + half * ROWS, first_row + base + (half + 1) * ROWS)
                    cos = [c_ref[step, :, cut, at] for step in range(freq_devs)]
                    sin = [s_ref[step, :, cut, at] for step in range(freq_devs)]
                    up, low = mixed_fields(plain, cos, sin, matrix_here)
                    change = unturned(up[0], low[0], plain[0], cos[0], sin[0], f_ref[cut, at])
                    made.append(u_ref[:, :, cut, at] - change)
                out[:, :, pair, at] = jnp.concatenate(made, 2).astype(BF16)

        tiles(rcv, one)

    inputs = (sums, cosines, sines, fraction, matrix, *messages)
    shape = jax.ShapeDtypeStruct(messages[0].shape, BF16)
    (out,) = call(
        body,
        (freq_place,),
        [(v, whole(v)) for v in inputs],
        [(shape, whole(shape))],
        (1,),
        flops=2 * own * count * 2 * rcv * rows // ROWS,
    )
    return out


def updated(initial, onset, messages, table, places, first, rows, target):
    freq_devs = len(messages)
    half_rows, own, rcv = initial.shape
    per_dev = messages[0].shape[1]
    tile = 2 * ROWS
    count = table.shape[2]

    def body(place_ref, _, sblk, x_ref, o_ref, t_ref, *rest):
        refs = rest[:freq_devs][::-1]
        out, spread_ref = rest[-2:]
        step = pl.program_id(0)

        @pl.when(step == 0)
        def _():
            base = t_ref[place_ref[0]].astype(F32)
            lane = lax.broadcasted_iota(jnp.int32, (own, count), 1) % ROWS
            for row in range(ROWS):
                spread_ref[row * own : (row + 1) * own] = jnp.where(lane == row, base, 0.0).astype(BF16)

        here = pl.ds(pl.multiple_of(step * tile, tile), tile)
        data = [ref[:, :, here, :].astype(F32) for ref in refs]
        onsets = o_ref[pl.ds(pl.multiple_of(sblk[0] * half_rows + first + step * tile, tile), tile), :]
        time = lax.broadcasted_iota(jnp.int32, (own, rcv), 0) + place_ref[0] * own
        for half in range(2):
            cut = slice(half * ROWS, (half + 1) * ROWS)
            flat = jnp.stack([v[:, :, cut] for v in data]).reshape(count, rcv).astype(BF16)
            change = jnp.dot(spread_ref[...], flat, preferred_element_type=F32)
            for row in range(ROWS):
                spot = half * ROWS + row
                on = time < onsets[spot : spot + 1, :]
                moved = jnp.where(on, change[row * own : (row + 1) * own], 0.0)
                out[spot] = (x_ref[first + step * tile + spot].astype(F32) - moved).astype(BF16)

    inputs = [(v, whole(v)) for v in (initial, onset, table, *messages[::-1])]
    aliases = {}
    if target is not None:
        inputs.append((target, pl.BlockSpec(memory_space=pl.ANY)))
        aliases = {len(places) + len(inputs) - 1: 0}
    (out,) = call(
        body,
        places,
        inputs,
        [(jax.ShapeDtypeStruct(initial.shape, BF16), pl.BlockSpec((tile, own, rcv), lambda i, *_: (first // tile + i, 0, 0)))],
        (rows // tile,),
        scratch=[pltpu.VMEM((ROWS * own, count), BF16)],
        aliases=aliases,
        flops=2 * 2 * freq_devs * per_dev * own * rows * rcv,
    )
    return out


def exchanged(value, axis, step):
    return lax.ppermute(value, axis, [(i, i ^ step) for i in range(lax.axis_size(axis))])


def dealt_out(parts):
    return [exchanged(part, "freq", step) if step else part for part, step in zip(parts, ways(len(parts)))]


def spread(value, count):
    held = {0: value}
    bit = count // 2
    while bit:
        held.update({way | bit: exchanged(held[way], "freq", bit) for way in sorted(held)})
        bit //= 2
    return [held[way] for way in ways(count)]


def on_device(initial, response, aperture, onset_rcv, onset_src):
    freq_devs = lax.axis_size("freq")
    per_dev = response.shape[0]
    samples = initial.shape[1] * freq_devs
    half_rows = initial.shape[0]
    src_width = response.shape[2] // 2
    rows = half_rows // CHUNKS
    share = half_rows // freq_devs
    places = tuple(lax.axis_index(axis).reshape(1) for axis in ("freq", "rblk", "sblk"))
    freq_place = places[0]
    inverse = jnp.asarray(inverse_tables(samples, freq_devs, per_dev))
    matrix = jnp.asarray(window_tables(samples, freq_devs, per_dev))

    kept, sent = masked_halves(response, aperture, places)
    moved = [exchanged(v, "rblk", 1) for v in sent]
    kept_pair = [exchanged(v, "sblk", 1) for v in kept]
    sums, spectra = summed(dealt_out(first_spectra(initial, places, freq_devs, per_dev)))
    far = exchanged(spectra, "rblk", 1)
    moved_pair = []
    for index in range(PARTS):
        if index:
            moved[index], far = lax.optimization_barrier((moved[index], far))
        else:
            moved[index], spectra = lax.optimization_barrier((moved[index], spectra))
        moved_pair.append(exchanged(moved[index], "sblk", 1))
    parts = [((kept[i], moved[i]), (kept_pair[i], moved_pair[i])) for i in range(PARTS)]

    own, other = src_onsets(onset_src, places, half_rows, share, src_width)
    onsets = (own, exchanged(other, "sblk", 1))
    src_tables, rcv_tables = phase_tables(onsets, onset_rcv, places, freq_devs, per_dev, samples, PARTS, half_rows)

    near, far, result = [spectra], [far], None
    for step in range(ITERS):
        held = down_products(None, near, parts, 0, 0, freq_place)
        at = 0 if step else PARTS - 1
        if at:
            held = down_products(held, far, parts[:at], 1, 0, freq_place)
        first = at * 2 * kept[0].shape[1]
        messages = dealt_out(down_products(held, far, parts[at:], 1, first, freq_place, freq_devs))
        messages = dealt_out(windowed(messages, src_tables, matrix, freq_place, per_dev, share))
        received = [exchanged(v, "rblk", 1) for v in up_products(messages, parts, freq_place, half_rows, 1)]
        keep = up_products(messages, parts, freq_place, half_rows, 0)
        near, far = [], []
        for chunk in range(CHUNKS):
            back = added(keep[chunk], received[chunk])
            back = spread(back, freq_devs) if step < ITERS - 1 else dealt_out([back] * freq_devs)
            if step < ITERS - 1:
                near.append(next_spectra(sums, back, rcv_tables, matrix, freq_place, chunk * rows))
                far.append(exchanged(near[chunk], "rblk", 1))
            else:
                result = updated(initial, onset_rcv, back, inverse, places, chunk * rows, rows, result)
    return result


def transform_tables(length, count):
    table = fields(length, count).reshape(2 * count, length)
    forward_table = jnp.asarray(table.astype(np.float32).astype(BF16))
    inverse_table = jnp.asarray((table.T * (2.0 / length)).astype(np.float32).astype(BF16))
    return forward_table, inverse_table


def settle(values):
    return lax.optimization_barrier(values.astype(BF16)).astype(F32)


def samples_into_spectra(values, forward_table, freq_total):
    out = jnp.einsum("kt,ptn->pkn", forward_table, values, preferred_element_type=F32)
    return out.reshape(values.shape[0], 2, freq_total, values.shape[2]).astype(BF16)


def spectra_into_samples(trace_spectra, inverse_table):
    flat = trace_spectra.reshape(trace_spectra.shape[0], -1, trace_spectra.shape[3])
    return jnp.einsum("tk,pkn->ptn", inverse_table, flat, preferred_element_type=F32)


def dense(spec, gated, real, imag, sign):
    dot = functools.partial(jnp.einsum, spec, preferred_element_type=F32)
    return jnp.stack(
        [dot(gated[:, 0], real) - sign * dot(gated[:, 1], imag), dot(gated[:, 0], imag) + sign * dot(gated[:, 1], real)], 1
    )


def general_device(initial, response, aperture, onset_rcv, onset_src):
    freq_devs, rblk_devs, sblk_devs = (lax.axis_size(a) for a in ("freq", "rblk", "sblk"))
    freq_index, rblk_index, sblk_index = (lax.axis_index(a) for a in ("freq", "rblk", "sblk"))
    freq_total = response.shape[0] * freq_devs
    samples = initial.shape[1] * freq_devs
    focal_all = onset_rcv.shape[0]
    forward_table, inverse_table = transform_tables(samples, freq_total)
    steps_axis = lax.iota(jnp.int32, samples)
    own_axis = freq_index * initial.shape[1] + lax.iota(jnp.int32, initial.shape[1])
    half_rows = focal_all // sblk_devs
    own_onsets = lax.dynamic_slice_in_dim(onset_rcv, sblk_index * half_rows, half_rows, 0)
    rcv_gate = (own_axis[None, :, None] < own_onsets[:, None, :]).astype(F32)
    src_rows = focal_all // (rblk_devs * freq_devs)
    src_first = rblk_index * (focal_all // rblk_devs) + freq_index * src_rows
    src_onsets = lax.dynamic_slice_in_dim(onset_src, src_first, src_rows, 0)
    src_gate = (steps_axis[None, :, None] < src_onsets[:, None, :]).astype(F32)
    mask_full = jnp.repeat(jnp.repeat(aperture, BLOCK, 1), BLOCK, 2).astype(BF16)
    gated = response * mask_full[:, None]
    own_forward = lax.dynamic_slice_in_dim(forward_table, freq_index * initial.shape[1], initial.shape[1], 1)
    own_inverse = lax.dynamic_slice_in_dim(inverse_table, freq_index * initial.shape[1], initial.shape[1], 0)
    current = initial
    for _ in range(ITERS):
        partial = samples_into_spectra(current, own_forward, freq_total)
        spec_back = lax.psum_scatter(partial.astype(F32), "freq", scatter_dimension=2, tiled=True).astype(BF16)
        spec_all = lax.all_gather(spec_back, "sblk", axis=0, tiled=True)
        down = lax.psum_scatter(
            settle(dense("euk,bek->beu", gated, spec_all[:, 0], spec_all[:, 1], 1.0)).astype(BF16),
            "rblk",
            scatter_dimension=0,
            tiled=True,
        )
        src_traces = lax.all_to_all(down, "freq", split_axis=0, concat_axis=2, tiled=True)
        upgoing = (src_gate * spectra_into_samples(src_traces, inverse_table)).astype(BF16)
        upspec = samples_into_spectra(upgoing, forward_table, freq_total)
        up_back = lax.all_to_all(upspec, "freq", split_axis=2, concat_axis=0, tiled=True)
        up_all = lax.all_gather(up_back, "rblk", axis=0, tiled=True)
        sums = dense("qao,bqa->bqo", gated, up_all[:, 0], up_all[:, 1], -1.0).astype(BF16)
        back = lax.psum_scatter(sums, "sblk", scatter_dimension=0, tiled=True)
        traces = lax.all_gather(back, "freq", axis=2, tiled=True)
        update = rcv_gate * spectra_into_samples(traces, own_inverse)
        current = (initial.astype(F32) - update).astype(BF16)
    return current


def fits(initial, response, aperture, onset_rcv, onset_src):
    freq_devs = lax.axis_size("freq")
    if lax.axis_size("rblk") != 2 or lax.axis_size("sblk") != 2 or freq_devs & (freq_devs - 1):
        return False
    whole_rows = initial.shape[0] % (max(2, CHUNKS) * ROWS * freq_devs) == 0
    whole_width = response.shape[2] % (2 * PARTS * BLOCK) == 0 and response.shape[3] % BLOCK == 0
    return whole_rows and whole_width and onset_rcv.shape[0] == 2 * initial.shape[0]


def chosen(*arrays):
    return on_device(*arrays) if fits(*arrays) else general_device(*arrays)


def solution(mesh):
    in_specs = (
        P(("group", "sblk"), "freq", "rblk"),
        P(("group", "freq"), None, "sblk", "rblk"),
        P(("group", "freq"), "sblk", "rblk"),
        P("group", "rblk"),
        P("group", "sblk"),
    )
    out_specs = P(("group", "sblk"), "freq", "rblk")
    return jax.shard_map(chosen, mesh=mesh, in_specs=in_specs, out_specs=out_specs, check_vma=False)
```

```python
import functools
import math

import jax
import jax.numpy as jnp
import numpy as np
from jax import lax
from jax.experimental import pallas as pl
from jax.experimental.pallas import tpu as pltpu
from jax.sharding import PartitionSpec as P

BLOCK = 128
ITERS = 2
ROWS = 8
CHUNKS = 2
PARTS = 2
VMEM_BYTES = 6 * 1024 * 1024

BF16 = jnp.bfloat16
F32 = jnp.float32


def ways(count):
    far = sorted(range(1, count), key=lambda step: (step.bit_length() < count.bit_length() - 1, step))
    return [0] + far


def field_rows(place, freq_devs, per_dev):
    rows = []
    for step in ways(freq_devs):
        first = (place ^ step) * per_dev
        for part in range(2):
            rows.extend((part, first + local) for local in range(per_dev))
    return rows


def fields(samples, freq_total):
    phase = (np.arange(1, freq_total + 1)[:, None] * np.arange(samples)[None, :]) % samples
    angle = phase * (2.0 * math.pi / samples)
    return np.stack([np.cos(angle), -np.sin(angle)])


def inverse_tables(samples, freq_devs, per_dev):
    exact = fields(samples, freq_devs * per_dev) * (2.0 / samples)
    own = samples // freq_devs
    out = []
    for place in range(freq_devs):
        part = [exact[c, j, place * own : (place + 1) * own] for c, j in field_rows(place, freq_devs, per_dev)]
        out.append(np.repeat(np.stack(part), ROWS, 0).T)
    return np.stack(out).astype(np.float32).astype(BF16)


def window_tables(samples, freq_devs, per_dev):
    freq_total = freq_devs * per_dev
    order = np.arange(1, freq_total + 1)
    unit = 2j * math.pi / samples
    diff = order[None, :] - order[:, None]
    total = order[None, :] + order[:, None]
    same = np.where(diff == 0, 0.0, 1.0 / (samples * (np.exp(unit * np.where(diff == 0, 1, diff)) - 1.0)))
    mixed = 1.0 / (samples * (np.exp(-unit * total) - 1.0))
    full = np.zeros((2, freq_total, 2, freq_total))
    full[0, :, 0, :] = same.real + mixed.real
    full[0, :, 1, :] = mixed.imag - same.imag
    full[1, :, 0, :] = same.imag + mixed.imag
    full[1, :, 1, :] = same.real - mixed.real
    out = []
    for place in range(freq_devs):
        rows = [c * freq_total + j for c, j in field_rows(place, freq_devs, per_dev)]
        flat = full.reshape(2 * freq_total, 2 * freq_total)[np.ix_(rows, rows)]
        out.append(np.kron(flat, np.eye(ROWS)))
    return np.stack(out).astype(np.float32).astype(BF16)


def call(body, scalars, inputs, outputs, grid, scratch=(), aliases=None, flops=0):
    in_arrays = [value for value, _ in inputs]
    bytes_all = sum(v.size * v.dtype.itemsize for v in in_arrays)
    bytes_all += sum(math.prod(s.shape) * s.dtype.itemsize for s, _ in outputs)
    return pl.pallas_call(
        body,
        grid_spec=pltpu.PrefetchScalarGridSpec(
            num_scalar_prefetch=len(scalars),
            grid=grid,
            in_specs=[spec for _, spec in inputs],
            out_specs=[spec for _, spec in outputs],
            scratch_shapes=list(scratch),
        ),
        out_shape=[shape for shape, _ in outputs],
        input_output_aliases=aliases or {},
        compiler_params=pltpu.CompilerParams(vmem_limit_bytes=VMEM_BYTES),
        cost_estimate=pl.CostEstimate(flops=flops, bytes_accessed=bytes_all, transcendentals=0),
    )(*scalars, *in_arrays)


def whole(array):
    zeros = (0,) * array.ndim
    return pl.BlockSpec(array.shape, lambda *_: zeros)


def sine_terms():
    square = (np.cos(np.linspace(0.0, math.pi, 200)) + 1.0) / 32.0
    y = np.sqrt(np.maximum(square, 1e-12))
    return [float(v) for v in np.polynomial.polynomial.polyfit(square, np.sin(2.0 * math.pi * y) / y, 6)]


def turned(turn):
    terms = sine_terms()

    def sine(y):
        square = y * y
        total = jnp.full_like(y, terms[-1])
        for term in terms[-2::-1]:
            total = total * square + term
        return total * y

    turn = turn - jnp.floor(turn + 0.5)
    size = jnp.abs(turn)
    folded = jnp.where(size > 0.25, jnp.where(turn > 0.0, 0.5, -0.5) - turn, turn)
    return sine(0.25 - size), sine(folded)


def first_spectra(initial, places, freq_devs, per_dev):
    rows, own, rcv = initial.shape
    samples = own * freq_devs
    tile = 2 * ROWS
    count = freq_devs * 2 * per_dev * ROWS

    def body(freq, rblk, sblk, x_ref, *rest):
        outs, spread_ref = rest[:freq_devs], rest[freq_devs]
        time = lax.broadcasted_iota(jnp.int32, (ROWS, own), 1) + freq[0] * own
        time = time.astype(F32) * (1.0 / samples)
        table = []
        for way in ways(freq_devs):
            waves = [turned(time * ((freq[0] ^ way) * per_dev + j + 1).astype(F32)) for j in range(per_dev)]
            table += [cosine for cosine, _ in waves] + [-sine for _, sine in waves]
        table = jnp.concatenate(table, 0)
        lane = lax.broadcasted_iota(jnp.int32, (count, own), 0) % ROWS
        for row in range(ROWS):
            spread_ref[:, row * own : (row + 1) * own] = jnp.where(lane == row, table, 0.0).astype(BF16)
        for at in range(rows // tile):
            parts = []
            for half in range(2):
                start = at * tile + half * ROWS
                flat = x_ref[start : start + ROWS].reshape(ROWS * own, rcv)
                value = jnp.dot(spread_ref[...], flat, preferred_element_type=F32)
                parts.append(value.reshape(freq_devs, 2, per_dev, ROWS, rcv))
            both = jnp.concatenate(parts, 3).astype(BF16)
            for step, out in enumerate(outs):
                out[:, :, at * tile : (at + 1) * tile, :] = both[step]

    shape = jax.ShapeDtypeStruct((2, per_dev, rows, rcv), BF16)
    return call(
        body,
        places,
        [(initial, whole(initial))],
        [(shape, whole(shape))] * freq_devs,
        (1,),
        scratch=[pltpu.VMEM((count, ROWS * own), BF16)],
        flops=2 * 2 * freq_devs * per_dev * own * rows * rcv,
    )


def masked_halves(response, aperture, places):
    per_dev, _, src, rcv = response.shape
    half = src // 2
    width = half // PARTS
    aperture = jnp.swapaxes(aperture, 1, 2)

    def body(_, rblk, __, flags, x_ref, *outs):
        lane = lax.broadcasted_iota(jnp.int32, (1, rcv), 1) // BLOCK
        spot = lax.broadcasted_iota(jnp.int32, aperture.shape[1:], 1)
        for flip in (1, 0):
            for j in range(per_dev):
                for step in range(half // BLOCK):
                    block = (rblk[0] ^ flip) * (half // BLOCK) + step
                    on = jnp.sum(jnp.where(spot == block, flags[j].astype(F32), 0.0), 1, keepdims=True)
                    row = sum(jnp.where(lane == r, on[r : r + 1, :], 0.0) for r in range(rcv // BLOCK))
                    gate = jnp.broadcast_to(row, (BLOCK, rcv)).astype(BF16)
                    rows = pl.ds(pl.multiple_of(block * BLOCK, BLOCK), BLOCK)
                    part, at = divmod(step * BLOCK, width)
                    out = outs[flip * PARTS + part]
                    for c in range(2):
                        out[j, at : at + BLOCK, c * rcv : (c + 1) * rcv] = x_ref[j, c, rows, :] * gate

    shape = jax.ShapeDtypeStruct((per_dev, width, 2 * rcv), BF16)
    inputs = [(v, whole(v)) for v in (aperture, response)]
    outs = call(body, places, inputs, [(shape, whole(shape))] * (2 * PARTS), (1,))
    return list(outs[:PARTS]), list(outs[PARTS:])


def summed(parts):
    def body(*refs):
        total = sum(ref[...].astype(F32) for ref in refs[:-2])
        refs[-2][...] = total
        refs[-1][...] = total.astype(BF16)

    shapes = [jax.ShapeDtypeStruct(parts[0].shape, kind) for kind in (F32, BF16)]
    return call(body, (), [(v, whole(v)) for v in parts], [(v, whole(v)) for v in shapes], (1,))


def added(keep, received):
    def body(k_ref, r_ref, out):
        out[...] = (k_ref[...] + r_ref[...].astype(F32)).astype(BF16)

    shape = jax.ShapeDtypeStruct(keep.shape, BF16)
    (out,) = call(body, (), [(v, whole(v)) for v in (keep, received)], [(shape, whole(shape))], (1,))
    return out


def src_onsets(onset, places, half_rows, share, width):

    def body(freq, rblk, sblk, o_ref, own, other):
        lanes = pl.ds(pl.multiple_of(rblk[0] * width, BLOCK), width)
        for core, out in ((sblk[0], own), (1 - sblk[0], other)):
            spot = pl.multiple_of(core * half_rows + freq[0] * share, ROWS)
            out[...] = o_ref[pl.ds(spot, share), lanes]

    shape = jax.ShapeDtypeStruct((share, width), onset.dtype)
    return call(body, places, [(onset, whole(onset))], [(shape, whole(shape))] * 2, (1,))


def phase_tables(src, rcv, places, freq_devs, per_dev, samples, parts, rows):
    width = src[0].shape[1] // parts

    def fill(outs, value, to, freq):
        cosines, sines, fraction = outs
        value = value.astype(F32) * (1.0 / samples)
        fraction[:, to] = value
        for step, way in enumerate(ways(freq_devs)):
            for j in range(per_dev):
                order = ((freq[0] ^ way) * per_dev + j + 1).astype(F32)
                cosines[step, j, :, to], sines[step, j, :, to] = turned(value * order)

    def body(freq, _, sblk, own, other, r_ref, *outs):
        for part in range(parts):
            for spot, ref in enumerate((own, other)):
                at = (part * 2 + spot) * width
                fill(outs[:3], ref[:, part * width : (part + 1) * width], slice(at, at + width), freq)
        value = r_ref[pl.ds(pl.multiple_of(sblk[0] * rows, ROWS), rows), :]
        fill(outs[3:], value, slice(0, value.shape[1]), freq)

    shapes = []
    for count, total in ((src[0].shape[0], 2 * src[0].shape[1]), (rows, rcv.shape[1])):
        table = jax.ShapeDtypeStruct((freq_devs, per_dev, count, total), F32)
        shapes += [table, table, jax.ShapeDtypeStruct(table.shape[2:], F32)]
    outs = call(body, places, [(v, whole(v)) for v in (*src, rcv)], [(v, whole(v)) for v in shapes], (1,))
    return tuple(outs[:3]), tuple(outs[3:])


def down_products(before, spectra, parts, side, first, freq_place, freq_devs=0):
    _, per_dev, _, rcv = spectra[0].shape
    rows = sum(v.shape[2] for v in spectra)
    flat = [pair[side] for part in parts for pair in part]
    width = flat[0].shape[1]
    total_width = before.shape[-1] if before is not None else first + width * len(flat)
    share = rows // freq_devs if freq_devs else 0
    old = [] if before is None else [before]

    def body(place_ref, *rest):
        held_ref, rest = (rest[0], rest[1:]) if old else (None, rest)
        refs, resp, outs = rest[: len(spectra)], rest[len(spectra) : len(spectra) + len(flat)], rest[len(spectra) + len(flat) :]
        held = outs[-1]
        for j in range(per_dev):
            real = jnp.concatenate([ref[0, j] for ref in refs], 0)
            imag = jnp.concatenate([ref[1, j] for ref in refs], 0)
            lhs = jnp.concatenate([jnp.concatenate([real, -imag], 1), jnp.concatenate([imag, real], 1)], 0)
            for at, ref in enumerate(resp):
                total = lax.dot_general(lhs, ref[j], (((1,), (1,)), ((), ())), preferred_element_type=F32)
                to = slice(first + at * width, first + (at + 1) * width)
                for part in range(2):
                    value = total[part * rows : (part + 1) * rows]
                    held[part, j, :, to] = value + held_ref[part, j, :, to] if old else value
        if old:
            for to in (slice(0, first), slice(first + len(flat) * width, total_width)):
                if to.start < to.stop:
                    held[:, :, :, to] = held_ref[:, :, :, to]
        if freq_devs:
            for way, out in zip(ways(freq_devs), outs):
                start = pl.multiple_of((place_ref[0] ^ way) * share, share)
                out[...] = held[:, :, pl.ds(start, share), :].reshape(out.shape).astype(BF16)

    sums = (2, per_dev, rows, total_width)
    if freq_devs:
        shapes = [jax.ShapeDtypeStruct((2 * per_dev * share, total_width), BF16)] * freq_devs
    else:
        shapes = [jax.ShapeDtypeStruct(sums, F32)]
    outs = call(
        body,
        (freq_place,),
        [(v, whole(v)) for v in (*old, *spectra, *flat)],
        [(v, whole(v)) for v in shapes],
        (1,),
        scratch=[pltpu.VMEM(sums, F32)] if freq_devs else [],
        flops=2 * 4 * per_dev * rows * len(flat) * width * rcv,
    )
    return outs if freq_devs else outs[0]


def mixed_fields(plain, cos, sin, matrix):
    tile = plain[0].shape[-1]
    turned = [
        jnp.stack([v[0] * c - v[1] * s, v[0] * s + v[1] * c]) for v, c, s in zip(plain, cos, sin)
    ]
    flat = [jnp.stack(v).reshape(matrix.shape[1], tile).astype(BF16) for v in (turned, plain)]
    mixed = jnp.dot(matrix, jnp.concatenate(flat, 1), preferred_element_type=F32)
    shape = (-1, 2) + plain[0].shape[1:]
    return mixed[:, :tile].reshape(shape), mixed[:, tile:].reshape(shape)


def unturned(up, low, value, cos, sin, part):
    real = cos * up[0] + sin * up[1] - low[0] + part * value[0]
    imag = cos * up[1] - sin * up[0] - low[1] + part * value[1]
    return jnp.stack([real, imag])


def tiles(width, body, unroll):
    def at(step, carry):
        body(pl.ds(pl.multiple_of(step * BLOCK, BLOCK), BLOCK))
        return carry

    lax.fori_loop(0, width // BLOCK, at, 0, unroll=unroll)


def windowed(messages, tables, matrix, freq_place, per_dev, share):
    cosines, sines, fraction = tables
    freq_devs = len(messages)
    width = messages[0].shape[-1]
    count = freq_devs * 2 * per_dev * ROWS

    def body(place_ref, c_ref, s_ref, f_ref, g_ref, *rest):
        refs, outs = rest[:freq_devs], rest[freq_devs:]
        matrix_here = g_ref[place_ref[0]]

        def one(at):
            data = [ref[:, at].astype(F32).reshape(2, per_dev, share, BLOCK) for ref in refs]
            made = [[] for _ in outs]
            for first in range(0, share, ROWS):
                cut = slice(first, first + ROWS)
                plain = [value[:, :, cut] for value in data]
                cos = [c_ref[step, :, cut, at] for step in range(freq_devs)]
                sin = [s_ref[step, :, cut, at] for step in range(freq_devs)]
                up, low = mixed_fields(plain, cos, sin, matrix_here)
                part = f_ref[cut, at]
                for step in range(freq_devs):
                    made[step].append(unturned(up[step], low[step], plain[step], cos[step], sin[step], part))
            for out, value in zip(outs, made):
                out[:, at] = jnp.concatenate(value, 2).reshape(out.shape[0], BLOCK).astype(BF16)

        tiles(width, one, 4)

    inputs = (cosines, sines, fraction, matrix, *messages)
    return call(
        body,
        (freq_place,),
        [(v, whole(v)) for v in inputs],
        [(jax.ShapeDtypeStruct(v.shape, BF16), whole(v)) for v in messages],
        (1,),
        flops=2 * count * count * 2 * width * share // ROWS,
    )


def up_products(messages, parts, freq_place, rows, side):
    freq_devs = len(messages)
    flat = [pair[side] for part in parts for pair in part]
    per_dev, src, rcv = flat[0].shape[0], flat[0].shape[1], flat[0].shape[2] // 2
    group = rows // CHUNKS
    share = rows // freq_devs
    total_width = src * len(flat)
    kind = BF16 if side else F32

    def body(place_ref, *rest):
        resp, refs = rest[: len(flat)], rest[len(flat) : len(flat) + freq_devs]
        outs, held = rest[len(flat) + freq_devs : -1], rest[-1]
        for way, ref in zip(ways(freq_devs), refs):
            start = pl.multiple_of((place_ref[0] ^ way) * share, share)
            value = ref[...].reshape(2, per_dev, share, total_width)
            for part in range(2):
                for j in range(per_dev):
                    held[part, j, pl.ds(start, share), :] = value[part, j]
        for j in range(per_dev):
            both = jnp.concatenate([held[0, j], held[1, j]], 0)
            total = sum(
                jnp.dot(both[:, at * src : (at + 1) * src], ref[j], preferred_element_type=F32)
                for at, ref in enumerate(resp)
            )
            real = total[:rows, :rcv] + total[rows:, rcv:]
            imag = total[rows:, :rcv] - total[:rows, rcv:]
            for index, out in enumerate(outs):
                cut = slice(index * group, (index + 1) * group)
                out[0, j] = real[cut].astype(kind)
                out[1, j] = imag[cut].astype(kind)

    shape = jax.ShapeDtypeStruct((2, per_dev, group, rcv), kind)
    return call(
        body,
        (freq_place,),
        [(v, whole(v)) for v in (*flat, *messages)],
        [(shape, whole(shape))] * CHUNKS,
        (1,),
        scratch=[pltpu.VMEM((2, per_dev, rows, total_width), BF16)],
        flops=2 * 4 * per_dev * rows * total_width * rcv,
    )


def next_spectra(sums, messages, tables, matrix, freq_place, first_row):
    cosines, sines, fraction = tables
    freq_devs = len(messages)
    _, per_dev, rows, rcv = messages[0].shape
    count = freq_devs * 2 * per_dev * ROWS
    own = 2 * per_dev * ROWS

    def body(place_ref, u_ref, c_ref, s_ref, f_ref, g_ref, *rest):
        refs, out = rest[:freq_devs], rest[freq_devs]
        matrix_here = g_ref[place_ref[0], :own]

        def one(at):
            for base in range(0, rows, 2 * ROWS):
                pair = slice(base, base + 2 * ROWS)
                data = [ref[:, :, pair, at].astype(F32) for ref in refs]
                made = []
                for half in range(2):
                    plain = [value[:, :, half * ROWS : (half + 1) * ROWS] for value in data]
                    cut = slice(first_row + base + half * ROWS, first_row + base + (half + 1) * ROWS)
                    cos = [c_ref[step, :, cut, at] for step in range(freq_devs)]
                    sin = [s_ref[step, :, cut, at] for step in range(freq_devs)]
                    up, low = mixed_fields(plain, cos, sin, matrix_here)
                    change = unturned(up[0], low[0], plain[0], cos[0], sin[0], f_ref[cut, at])
                    made.append(u_ref[:, :, cut, at] - change)
                out[:, :, pair, at] = jnp.concatenate(made, 2).astype(BF16)

        tiles(rcv, one, 2)

    inputs = (sums, cosines, sines, fraction, matrix, *messages)
    shape = jax.ShapeDtypeStruct(messages[0].shape, BF16)
    (out,) = call(
        body,
        (freq_place,),
        [(v, whole(v)) for v in inputs],
        [(shape, whole(shape))],
        (1,),
        flops=2 * own * count * 2 * rcv * rows // ROWS,
    )
    return out


def updated(initial, onset, messages, table, places, first, rows, target):
    freq_devs = len(messages)
    half_rows, own, rcv = initial.shape
    per_dev = messages[0].shape[1]
    tile = 2 * ROWS
    count = table.shape[2]

    def body(place_ref, _, sblk, x_ref, o_ref, t_ref, *rest):
        refs = rest[:freq_devs]
        out, spread_ref = rest[-2:]
        step = pl.program_id(0)

        @pl.when(step == 0)
        def _():
            base = t_ref[place_ref[0]].astype(F32)
            lane = lax.broadcasted_iota(jnp.int32, (own, count), 1) % ROWS
            for row in range(ROWS):
                spread_ref[row * own : (row + 1) * own] = jnp.where(lane == row, base, 0.0).astype(BF16)

        here = pl.ds(pl.multiple_of(step * tile, tile), tile)
        data = [ref[:, :, here, :].astype(F32) for ref in refs]
        onsets = o_ref[pl.ds(pl.multiple_of(sblk[0] * half_rows + first + step * tile, tile), tile), :]
        time = lax.broadcasted_iota(jnp.int32, (own, rcv), 0) + place_ref[0] * own
        for half in range(2):
            cut = slice(half * ROWS, (half + 1) * ROWS)
            flat = jnp.stack([v[:, :, cut] for v in data]).reshape(count, rcv).astype(BF16)
            change = jnp.dot(spread_ref[...], flat, preferred_element_type=F32)
            for row in range(ROWS):
                spot = half * ROWS + row
                on = time < onsets[spot : spot + 1, :]
                moved = jnp.where(on, change[row * own : (row + 1) * own], 0.0)
                out[spot] = (x_ref[first + step * tile + spot].astype(F32) - moved).astype(BF16)

    inputs = [(v, whole(v)) for v in (initial, onset, table, *messages)]
    aliases = {}
    if target is not None:
        inputs.append((target, pl.BlockSpec(memory_space=pl.ANY)))
        aliases = {len(places) + len(inputs) - 1: 0}
    (out,) = call(
        body,
        places,
        inputs,
        [(jax.ShapeDtypeStruct(initial.shape, BF16), pl.BlockSpec((tile, own, rcv), lambda i, *_: (first // tile + i, 0, 0)))],
        (rows // tile,),
        scratch=[pltpu.VMEM((ROWS * own, count), BF16)],
        aliases=aliases,
        flops=2 * 2 * freq_devs * per_dev * own * rows * rcv,
    )
    return out


def exchanged(value, axis, step):
    return lax.ppermute(value, axis, [(i, i ^ step) for i in range(lax.axis_size(axis))])


def dealt_out(parts):
    return [exchanged(part, "freq", step) if step else part for part, step in zip(parts, ways(len(parts)))]


def spread(value, count):
    held = {0: value}
    bit = count // 2
    while bit:
        held.update({way | bit: exchanged(held[way], "freq", bit) for way in sorted(held)})
        bit //= 2
    return [held[way] for way in ways(count)]


def on_device(initial, response, aperture, onset_rcv, onset_src):
    freq_devs = lax.axis_size("freq")
    per_dev = response.shape[0]
    samples = initial.shape[1] * freq_devs
    half_rows = initial.shape[0]
    src_width = response.shape[2] // 2
    rows = half_rows // CHUNKS
    share = half_rows // freq_devs
    places = tuple(lax.axis_index(axis).reshape(1) for axis in ("freq", "rblk", "sblk"))
    freq_place = places[0]
    inverse = jnp.asarray(inverse_tables(samples, freq_devs, per_dev))
    matrix = jnp.asarray(window_tables(samples, freq_devs, per_dev))

    kept, sent = masked_halves(response, aperture, places)
    moved = [exchanged(v, "rblk", 1) for v in sent]
    kept_pair = [exchanged(v, "sblk", 1) for v in kept]
    sums, spectra = summed(dealt_out(first_spectra(initial, places, freq_devs, per_dev)))
    far = exchanged(spectra, "rblk", 1)
    moved_pair = []
    for index in range(PARTS):
        if index:
            moved[index], far = lax.optimization_barrier((moved[index], far))
        else:
            moved[index], spectra = lax.optimization_barrier((moved[index], spectra))
        moved_pair.append(exchanged(moved[index], "sblk", 1))
    parts = [((kept[i], moved[i]), (kept_pair[i], moved_pair[i])) for i in range(PARTS)]

    own, other = src_onsets(onset_src, places, half_rows, share, src_width)
    onsets = (own, exchanged(other, "sblk", 1))
    src_tables, rcv_tables = phase_tables(onsets, onset_rcv, places, freq_devs, per_dev, samples, PARTS, half_rows)

    near, far, result = [spectra], [far], None
    for step in range(ITERS):
        held = down_products(None, near, parts, 0, 0, freq_place)
        at = 0 if step else PARTS - 1
        if at:
            held = down_products(held, far, parts[:at], 1, 0, freq_place)
        first = at * 2 * kept[0].shape[1]
        messages = dealt_out(down_products(held, far, parts[at:], 1, first, freq_place, freq_devs))
        messages = dealt_out(windowed(messages, src_tables, matrix, freq_place, per_dev, share))
        received = [exchanged(v, "rblk", 1) for v in up_products(messages, parts, freq_place, half_rows, 1)]
        keep = up_products(messages, parts, freq_place, half_rows, 0)
        near, far = [], []
        for chunk in range(CHUNKS):
            back = spread(added(keep[chunk], received[chunk]), freq_devs)
            if step < ITERS - 1:
                near.append(next_spectra(sums, back, rcv_tables, matrix, freq_place, chunk * rows))
                far.append(exchanged(near[chunk], "rblk", 1))
            else:
                result = updated(initial, onset_rcv, back, inverse, places, chunk * rows, rows, result)
    return result


def transform_tables(length, count):
    table = fields(length, count).reshape(2 * count, length)
    forward_table = jnp.asarray(table.astype(np.float32).astype(BF16))
    inverse_table = jnp.asarray((table.T * (2.0 / length)).astype(np.float32).astype(BF16))
    return forward_table, inverse_table


def settle(values):
    return lax.optimization_barrier(values.astype(BF16)).astype(F32)


def samples_into_spectra(values, forward_table, freq_total):
    out = jnp.einsum("kt,ptn->pkn", forward_table, values, preferred_element_type=F32)
    return out.reshape(values.shape[0], 2, freq_total, values.shape[2]).astype(BF16)


def spectra_into_samples(trace_spectra, inverse_table):
    flat = trace_spectra.reshape(trace_spectra.shape[0], -1, trace_spectra.shape[3])
    return jnp.einsum("tk,pkn->ptn", inverse_table, flat, preferred_element_type=F32)


def dense(spec, gated, real, imag, sign):
    dot = functools.partial(jnp.einsum, spec, preferred_element_type=F32)
    return jnp.stack(
        [dot(gated[:, 0], real) - sign * dot(gated[:, 1], imag), dot(gated[:, 0], imag) + sign * dot(gated[:, 1], real)], 1
    )


def general_device(initial, response, aperture, onset_rcv, onset_src):
    freq_devs, rblk_devs, sblk_devs = (lax.axis_size(a) for a in ("freq", "rblk", "sblk"))
    freq_index, rblk_index, sblk_index = (lax.axis_index(a) for a in ("freq", "rblk", "sblk"))
    freq_total = response.shape[0] * freq_devs
    samples = initial.shape[1] * freq_devs
    focal_all = onset_rcv.shape[0]
    forward_table, inverse_table = transform_tables(samples, freq_total)
    steps_axis = lax.iota(jnp.int32, samples)
    own_axis = freq_index * initial.shape[1] + lax.iota(jnp.int32, initial.shape[1])
    half_rows = focal_all // sblk_devs
    own_onsets = lax.dynamic_slice_in_dim(onset_rcv, sblk_index * half_rows, half_rows, 0)
    rcv_gate = (own_axis[None, :, None] < own_onsets[:, None, :]).astype(F32)
    src_rows = focal_all // (rblk_devs * freq_devs)
    src_first = rblk_index * (focal_all // rblk_devs) + freq_index * src_rows
    src_onsets = lax.dynamic_slice_in_dim(onset_src, src_first, src_rows, 0)
    src_gate = (steps_axis[None, :, None] < src_onsets[:, None, :]).astype(F32)
    mask_full = jnp.repeat(jnp.repeat(aperture, BLOCK, 1), BLOCK, 2).astype(BF16)
    gated = response * mask_full[:, None]
    own_forward = lax.dynamic_slice_in_dim(forward_table, freq_index * initial.shape[1], initial.shape[1], 1)
    own_inverse = lax.dynamic_slice_in_dim(inverse_table, freq_index * initial.shape[1], initial.shape[1], 0)
    current = initial
    for _ in range(ITERS):
        partial = samples_into_spectra(current, own_forward, freq_total)
        spec_back = lax.psum_scatter(partial.astype(F32), "freq", scatter_dimension=2, tiled=True).astype(BF16)
        spec_all = lax.all_gather(spec_back, "sblk", axis=0, tiled=True)
        down = lax.psum_scatter(
            settle(dense("euk,bek->beu", gated, spec_all[:, 0], spec_all[:, 1], 1.0)).astype(BF16),
            "rblk",
            scatter_dimension=0,
            tiled=True,
        )
        src_traces = lax.all_to_all(down, "freq", split_axis=0, concat_axis=2, tiled=True)
        upgoing = (src_gate * spectra_into_samples(src_traces, inverse_table)).astype(BF16)
        upspec = samples_into_spectra(upgoing, forward_table, freq_total)
        up_back = lax.all_to_all(upspec, "freq", split_axis=2, concat_axis=0, tiled=True)
        up_all = lax.all_gather(up_back, "rblk", axis=0, tiled=True)
        sums = dense("qao,bqa->bqo", gated, up_all[:, 0], up_all[:, 1], -1.0).astype(BF16)
        back = lax.psum_scatter(sums, "sblk", scatter_dimension=0, tiled=True)
        traces = lax.all_gather(back, "freq", axis=2, tiled=True)
        update = rcv_gate * spectra_into_samples(traces, own_inverse)
        current = (initial.astype(F32) - update).astype(BF16)
    return current


def fits(initial, response, aperture, onset_rcv, onset_src):
    freq_devs = lax.axis_size("freq")
    if lax.axis_size("rblk") != 2 or lax.axis_size("sblk") != 2 or freq_devs & (freq_devs - 1):
        return False
    whole_rows = initial.shape[0] % (max(2, CHUNKS) * ROWS * freq_devs) == 0
    whole_width = response.shape[2] % (2 * PARTS * BLOCK) == 0 and response.shape[3] % BLOCK == 0
    return whole_rows and whole_width and onset_rcv.shape[0] == 2 * initial.shape[0]


def chosen(*arrays):
    return on_device(*arrays) if fits(*arrays) else general_device(*arrays)


def solution(mesh):
    in_specs = (
        P(("group", "sblk"), "freq", "rblk"),
        P(("group", "freq"), None, "sblk", "rblk"),
        P(("group", "freq"), "sblk", "rblk"),
        P("group", "rblk"),
        P("group", "sblk"),
    )
    out_specs = P(("group", "sblk"), "freq", "rblk")
    return jax.shard_map(chosen, mesh=mesh, in_specs=in_specs, out_specs=out_specs, check_vma=False)
```

```python
import functools
import math

import jax
import jax.numpy as jnp
import numpy as np
from jax import lax
from jax.experimental import pallas as pl
from jax.experimental.pallas import tpu as pltpu
from jax.sharding import PartitionSpec as P

BLOCK = 128
ITERS = 2
ROWS = 8
CHUNKS = 2
PARTS = 2
VMEM_BYTES = 6 * 1024 * 1024

BF16 = jnp.bfloat16
F32 = jnp.float32


def ways(count):
    far = sorted(range(1, count), key=lambda step: (step.bit_length() < count.bit_length() - 1, step))
    return [0] + far


def field_rows(place, freq_devs, per_dev):
    rows = []
    for step in ways(freq_devs):
        first = (place ^ step) * per_dev
        for part in range(2):
            rows.extend((part, first + local) for local in range(per_dev))
    return rows


def fields(samples, freq_total):
    phase = (np.arange(1, freq_total + 1)[:, None] * np.arange(samples)[None, :]) % samples
    angle = phase * (2.0 * math.pi / samples)
    return np.stack([np.cos(angle), -np.sin(angle)])


def inverse_tables(samples, freq_devs, per_dev):
    exact = fields(samples, freq_devs * per_dev) * (2.0 / samples)
    own = samples // freq_devs
    out = []
    for place in range(freq_devs):
        part = [exact[c, j, place * own : (place + 1) * own] for c, j in field_rows(place, freq_devs, per_dev)]
        out.append(np.repeat(np.stack(part), ROWS, 0).T)
    return np.stack(out).astype(np.float32).astype(BF16)


def window_tables(samples, freq_devs, per_dev):
    freq_total = freq_devs * per_dev
    order = np.arange(1, freq_total + 1)
    unit = 2j * math.pi / samples
    diff = order[None, :] - order[:, None]
    total = order[None, :] + order[:, None]
    same = np.where(diff == 0, 0.0, 1.0 / (samples * (np.exp(unit * np.where(diff == 0, 1, diff)) - 1.0)))
    mixed = 1.0 / (samples * (np.exp(-unit * total) - 1.0))
    full = np.zeros((2, freq_total, 2, freq_total))
    full[0, :, 0, :] = same.real + mixed.real
    full[0, :, 1, :] = mixed.imag - same.imag
    full[1, :, 0, :] = same.imag + mixed.imag
    full[1, :, 1, :] = same.real - mixed.real
    out = []
    for place in range(freq_devs):
        rows = [c * freq_total + j for c, j in field_rows(place, freq_devs, per_dev)]
        flat = full.reshape(2 * freq_total, 2 * freq_total)[np.ix_(rows, rows)]
        out.append(np.kron(flat, np.eye(ROWS)))
    return np.stack(out).astype(np.float32).astype(BF16)


def call(body, scalars, inputs, outputs, grid, scratch=(), aliases=None, flops=0):
    in_arrays = [value for value, _ in inputs]
    bytes_all = sum(v.size * v.dtype.itemsize for v in in_arrays)
    bytes_all += sum(math.prod(s.shape) * s.dtype.itemsize for s, _ in outputs)
    return pl.pallas_call(
        body,
        grid_spec=pltpu.PrefetchScalarGridSpec(
            num_scalar_prefetch=len(scalars),
            grid=grid,
            in_specs=[spec for _, spec in inputs],
            out_specs=[spec for _, spec in outputs],
            scratch_shapes=list(scratch),
        ),
        out_shape=[shape for shape, _ in outputs],
        input_output_aliases=aliases or {},
        compiler_params=pltpu.CompilerParams(vmem_limit_bytes=VMEM_BYTES),
        cost_estimate=pl.CostEstimate(flops=flops, bytes_accessed=bytes_all, transcendentals=0),
    )(*scalars, *in_arrays)


def whole(array):
    zeros = (0,) * array.ndim
    return pl.BlockSpec(array.shape, lambda *_: zeros)


def sine_terms():
    square = (np.cos(np.linspace(0.0, math.pi, 200)) + 1.0) / 32.0
    y = np.sqrt(np.maximum(square, 1e-12))
    return [float(v) for v in np.polynomial.polynomial.polyfit(square, np.sin(2.0 * math.pi * y) / y, 6)]


def turned(turn):
    terms = sine_terms()

    def sine(y):
        square = y * y
        total = jnp.full_like(y, terms[-1])
        for term in terms[-2::-1]:
            total = total * square + term
        return total * y

    turn = turn - jnp.floor(turn + 0.5)
    size = jnp.abs(turn)
    folded = jnp.where(size > 0.25, jnp.where(turn > 0.0, 0.5, -0.5) - turn, turn)
    return sine(0.25 - size), sine(folded)


def first_spectra(initial, places, freq_devs, per_dev):
    rows, own, rcv = initial.shape
    samples = own * freq_devs
    tile = 2 * ROWS
    count = freq_devs * 2 * per_dev * ROWS

    def body(freq, rblk, sblk, x_ref, *rest):
        outs, spread_ref = rest[:freq_devs], rest[freq_devs]
        time = lax.broadcasted_iota(jnp.int32, (ROWS, own), 1) + freq[0] * own
        time = time.astype(F32) * (1.0 / samples)
        table = []
        for way in ways(freq_devs):
            waves = [turned(time * ((freq[0] ^ way) * per_dev + j + 1).astype(F32)) for j in range(per_dev)]
            table += [cosine for cosine, _ in waves] + [-sine for _, sine in waves]
        table = jnp.concatenate(table, 0)
        lane = lax.broadcasted_iota(jnp.int32, (count, own), 0) % ROWS
        for row in range(ROWS):
            spread_ref[:, row * own : (row + 1) * own] = jnp.where(lane == row, table, 0.0).astype(BF16)
        for at in range(rows // tile):
            parts = []
            for half in range(2):
                start = at * tile + half * ROWS
                flat = x_ref[start : start + ROWS].reshape(ROWS * own, rcv)
                value = jnp.dot(spread_ref[...], flat, preferred_element_type=F32)
                parts.append(value.reshape(freq_devs, 2, per_dev, ROWS, rcv))
            both = jnp.concatenate(parts, 3).astype(BF16)
            for step, out in enumerate(outs):
                out[:, :, at * tile : (at + 1) * tile, :] = both[step]

    shape = jax.ShapeDtypeStruct((2, per_dev, rows, rcv), BF16)
    return call(
        body,
        places,
        [(initial, whole(initial))],
        [(shape, whole(shape))] * freq_devs,
        (1,),
        scratch=[pltpu.VMEM((count, ROWS * own), BF16)],
        flops=2 * 2 * freq_devs * per_dev * own * rows * rcv,
    )


def masked_halves(response, aperture, places):
    per_dev, _, src, rcv = response.shape
    half = src // 2
    width = half // PARTS

    def body(_, rblk, __, flags, x_ref, *outs):
        lane = lax.broadcasted_iota(jnp.int32, (1, rcv), 1) // BLOCK
        for flip in (1, 0):
            for j in range(per_dev):
                for step in range(half // BLOCK):
                    block = (rblk[0] ^ flip) * (half // BLOCK) + step
                    on = flags[j, pl.ds(block, 1), :].astype(F32)
                    row = sum(jnp.where(lane == r, on[:, r : r + 1], 0.0) for r in range(rcv // BLOCK))
                    gate = jnp.broadcast_to(row, (BLOCK, rcv)).astype(BF16)
                    rows = pl.ds(pl.multiple_of(block * BLOCK, BLOCK), BLOCK)
                    part, at = divmod(step * BLOCK, width)
                    out = outs[flip * PARTS + part]
                    for c in range(2):
                        out[j, at : at + BLOCK, c * rcv : (c + 1) * rcv] = x_ref[j, c, rows, :] * gate

    shape = jax.ShapeDtypeStruct((per_dev, width, 2 * rcv), BF16)
    inputs = [(v, whole(v)) for v in (aperture, response)]
    outs = call(body, places, inputs, [(shape, whole(shape))] * (2 * PARTS), (1,))
    return list(outs[:PARTS]), list(outs[PARTS:])


def summed(parts):
    def body(*refs):
        total = sum(ref[...].astype(F32) for ref in refs[:-2])
        refs[-2][...] = total
        refs[-1][...] = total.astype(BF16)

    shapes = [jax.ShapeDtypeStruct(parts[0].shape, kind) for kind in (F32, BF16)]
    return call(body, (), [(v, whole(v)) for v in parts], [(v, whole(v)) for v in shapes], (1,))


def added(keep, received):
    def body(k_ref, r_ref, out):
        out[...] = (k_ref[...] + r_ref[...].astype(F32)).astype(BF16)

    shape = jax.ShapeDtypeStruct(keep.shape, BF16)
    (out,) = call(body, (), [(v, whole(v)) for v in (keep, received)], [(shape, whole(shape))], (1,))
    return out


def src_onsets(onset, places, half_rows, share, width):

    def body(freq, rblk, sblk, o_ref, own, other):
        lanes = pl.ds(pl.multiple_of(rblk[0] * width, BLOCK), width)
        for core, out in ((sblk[0], own), (1 - sblk[0], other)):
            spot = pl.multiple_of(core * half_rows + freq[0] * share, ROWS)
            out[...] = o_ref[pl.ds(spot, share), lanes]

    shape = jax.ShapeDtypeStruct((share, width), onset.dtype)
    return call(body, places, [(onset, whole(onset))], [(shape, whole(shape))] * 2, (1,))


def phase_tables(src, rcv, places, freq_devs, per_dev, samples, parts, rows):
    width = src[0].shape[1] // parts

    def fill(outs, value, to, freq):
        cosines, sines, fraction = outs
        value = value.astype(F32) * (1.0 / samples)
        fraction[:, to] = value
        for step, way in enumerate(ways(freq_devs)):
            for j in range(per_dev):
                order = ((freq[0] ^ way) * per_dev + j + 1).astype(F32)
                cosines[step, j, :, to], sines[step, j, :, to] = turned(value * order)

    def body(freq, _, sblk, own, other, r_ref, *outs):
        for part in range(parts):
            for spot, ref in enumerate((own, other)):
                at = (part * 2 + spot) * width
                fill(outs[:3], ref[:, part * width : (part + 1) * width], slice(at, at + width), freq)
        value = r_ref[pl.ds(pl.multiple_of(sblk[0] * rows, ROWS), rows), :]
        fill(outs[3:], value, slice(0, value.shape[1]), freq)

    shapes = []
    for count, total in ((src[0].shape[0], 2 * src[0].shape[1]), (rows, rcv.shape[1])):
        table = jax.ShapeDtypeStruct((freq_devs, per_dev, count, total), F32)
        shapes += [table, table, jax.ShapeDtypeStruct(table.shape[2:], F32)]
    outs = call(body, places, [(v, whole(v)) for v in (*src, rcv)], [(v, whole(v)) for v in shapes], (1,))
    return tuple(outs[:3]), tuple(outs[3:])


def down_products(before, spectra, parts, side, first, freq_place, freq_devs=0):
    _, per_dev, _, rcv = spectra[0].shape
    rows = sum(v.shape[2] for v in spectra)
    flat = [pair[side] for part in parts for pair in part]
    width = flat[0].shape[1]
    total_width = before.shape[-1] if before is not None else first + width * len(flat)
    share = rows // freq_devs if freq_devs else 0
    old = [] if before is None else [before]

    def body(place_ref, *rest):
        held_ref, rest = (rest[0], rest[1:]) if old else (None, rest)
        refs, resp, outs = rest[: len(spectra)], rest[len(spectra) : len(spectra) + len(flat)], rest[len(spectra) + len(flat) :]
        held = outs[-1]
        for j in range(per_dev):
            real = jnp.concatenate([ref[0, j] for ref in refs], 0)
            imag = jnp.concatenate([ref[1, j] for ref in refs], 0)
            lhs = jnp.concatenate([jnp.concatenate([real, -imag], 1), jnp.concatenate([imag, real], 1)], 0)
            for at, ref in enumerate(resp):
                total = lax.dot_general(lhs, ref[j], (((1,), (1,)), ((), ())), preferred_element_type=F32)
                to = slice(first + at * width, first + (at + 1) * width)
                for part in range(2):
                    value = total[part * rows : (part + 1) * rows]
                    held[part, j, :, to] = value + held_ref[part, j, :, to] if old else value
        if old:
            for to in (slice(0, first), slice(first + len(flat) * width, total_width)):
                if to.start < to.stop:
                    held[:, :, :, to] = held_ref[:, :, :, to]
        if freq_devs:
            for way, out in zip(ways(freq_devs), outs):
                start = pl.multiple_of((place_ref[0] ^ way) * share, share)
                out[...] = held[:, :, pl.ds(start, share), :].reshape(out.shape).astype(BF16)

    sums = (2, per_dev, rows, total_width)
    if freq_devs:
        shapes = [jax.ShapeDtypeStruct((2 * per_dev * share, total_width), BF16)] * freq_devs
    else:
        shapes = [jax.ShapeDtypeStruct(sums, F32)]
    outs = call(
        body,
        (freq_place,),
        [(v, whole(v)) for v in (*old, *spectra, *flat)],
        [(v, whole(v)) for v in shapes],
        (1,),
        scratch=[pltpu.VMEM(sums, F32)] if freq_devs else [],
        flops=2 * 4 * per_dev * rows * len(flat) * width * rcv,
    )
    return outs if freq_devs else outs[0]


def mixed_fields(plain, cos, sin, matrix):
    tile = plain[0].shape[-1]
    turned = [
        jnp.stack([v[0] * c - v[1] * s, v[0] * s + v[1] * c]) for v, c, s in zip(plain, cos, sin)
    ]
    flat = [jnp.stack(v).reshape(matrix.shape[1], tile).astype(BF16) for v in (turned, plain)]
    mixed = jnp.dot(matrix, jnp.concatenate(flat, 1), preferred_element_type=F32)
    shape = (-1, 2) + plain[0].shape[1:]
    return mixed[:, :tile].reshape(shape), mixed[:, tile:].reshape(shape)


def unturned(up, low, value, cos, sin, part):
    real = cos * up[0] + sin * up[1] - low[0] + part * value[0]
    imag = cos * up[1] - sin * up[0] - low[1] + part * value[1]
    return jnp.stack([real, imag])


def tiles(width, body):
    def at(step, carry):
        body(pl.ds(pl.multiple_of(step * BLOCK, BLOCK), BLOCK))
        return carry

    lax.fori_loop(0, width // BLOCK, at, 0, unroll=2)


def windowed(messages, tables, matrix, freq_place, per_dev, share):
    cosines, sines, fraction = tables
    freq_devs = len(messages)
    width = messages[0].shape[-1]
    count = freq_devs * 2 * per_dev * ROWS

    def body(place_ref, c_ref, s_ref, f_ref, g_ref, *rest):
        refs, outs = rest[:freq_devs], rest[freq_devs:]
        matrix_here = g_ref[place_ref[0]]

        def one(at):
            data = [ref[:, at].astype(F32).reshape(2, per_dev, share, BLOCK) for ref in refs]
            made = [[] for _ in outs]
            for first in range(0, share, ROWS):
                cut = slice(first, first + ROWS)
                plain = [value[:, :, cut] for value in data]
                cos = [c_ref[step, :, cut, at] for step in range(freq_devs)]
                sin = [s_ref[step, :, cut, at] for step in range(freq_devs)]
                up, low = mixed_fields(plain, cos, sin, matrix_here)
                part = f_ref[cut, at]
                for step in range(freq_devs):
                    made[step].append(unturned(up[step], low[step], plain[step], cos[step], sin[step], part))
            for out, value in zip(outs, made):
                out[:, at] = jnp.concatenate(value, 2).reshape(out.shape[0], BLOCK).astype(BF16)

        tiles(width, one)

    inputs = (cosines, sines, fraction, matrix, *messages)
    return call(
        body,
        (freq_place,),
        [(v, whole(v)) for v in inputs],
        [(jax.ShapeDtypeStruct(v.shape, BF16), whole(v)) for v in messages],
        (1,),
        flops=2 * count * count * 2 * width * share // ROWS,
    )


def up_products(messages, parts, freq_place, rows, side):
    freq_devs = len(messages)
    flat = [pair[side] for part in parts for pair in part]
    per_dev, src, rcv = flat[0].shape[0], flat[0].shape[1], flat[0].shape[2] // 2
    group = rows // CHUNKS
    share = rows // freq_devs
    total_width = src * len(flat)
    kind = BF16 if side else F32

    def body(place_ref, *rest):
        resp, refs = rest[: len(flat)], rest[len(flat) : len(flat) + freq_devs]
        outs, held = rest[len(flat) + freq_devs : -1], rest[-1]
        for way, ref in zip(ways(freq_devs), refs):
            start = pl.multiple_of((place_ref[0] ^ way) * share, share)
            value = ref[...].reshape(2, per_dev, share, total_width)
            for part in range(2):
                for j in range(per_dev):
                    held[part, j, pl.ds(start, share), :] = value[part, j]
        for j in range(per_dev):
            both = jnp.concatenate([held[0, j], held[1, j]], 0)
            total = sum(
                jnp.dot(both[:, at * src : (at + 1) * src], ref[j], preferred_element_type=F32)
                for at, ref in enumerate(resp)
            )
            real = total[:rows, :rcv] + total[rows:, rcv:]
            imag = total[rows:, :rcv] - total[:rows, rcv:]
            for index, out in enumerate(outs):
                cut = slice(index * group, (index + 1) * group)
                out[0, j] = real[cut].astype(kind)
                out[1, j] = imag[cut].astype(kind)

    shape = jax.ShapeDtypeStruct((2, per_dev, group, rcv), kind)
    return call(
        body,
        (freq_place,),
        [(v, whole(v)) for v in (*flat, *messages)],
        [(shape, whole(shape))] * CHUNKS,
        (1,),
        scratch=[pltpu.VMEM((2, per_dev, rows, total_width), BF16)],
        flops=2 * 4 * per_dev * rows * total_width * rcv,
    )


def next_spectra(sums, messages, tables, matrix, freq_place, first_row):
    cosines, sines, fraction = tables
    freq_devs = len(messages)
    _, per_dev, rows, rcv = messages[0].shape
    count = freq_devs * 2 * per_dev * ROWS
    own = 2 * per_dev * ROWS

    def body(place_ref, u_ref, c_ref, s_ref, f_ref, g_ref, *rest):
        refs, out = rest[:freq_devs], rest[freq_devs]
        matrix_here = g_ref[place_ref[0], :own]

        def one(at):
            for base in range(0, rows, 2 * ROWS):
                pair = slice(base, base + 2 * ROWS)
                data = [ref[:, :, pair, at].astype(F32) for ref in refs]
                made = []
                for half in range(2):
                    plain = [value[:, :, half * ROWS : (half + 1) * ROWS] for value in data]
                    cut = slice(first_row + base + half * ROWS, first_row + base + (half + 1) * ROWS)
                    cos = [c_ref[step, :, cut, at] for step in range(freq_devs)]
                    sin = [s_ref[step, :, cut, at] for step in range(freq_devs)]
                    up, low = mixed_fields(plain, cos, sin, matrix_here)
                    change = unturned(up[0], low[0], plain[0], cos[0], sin[0], f_ref[cut, at])
                    made.append(u_ref[:, :, cut, at] - change)
                out[:, :, pair, at] = jnp.concatenate(made, 2).astype(BF16)

        tiles(rcv, one)

    inputs = (sums, cosines, sines, fraction, matrix, *messages)
    shape = jax.ShapeDtypeStruct(messages[0].shape, BF16)
    (out,) = call(
        body,
        (freq_place,),
        [(v, whole(v)) for v in inputs],
        [(shape, whole(shape))],
        (1,),
        flops=2 * own * count * 2 * rcv * rows // ROWS,
    )
    return out


def updated(initial, onset, messages, table, places, first, rows, target):
    freq_devs = len(messages)
    half_rows, own, rcv = initial.shape
    per_dev = messages[0].shape[1]
    tile = 2 * ROWS
    count = table.shape[2]

    def body(place_ref, _, sblk, x_ref, o_ref, t_ref, *rest):
        refs = rest[:freq_devs]
        out, spread_ref = rest[-2:]
        step = pl.program_id(0)

        @pl.when(step == 0)
        def _():
            base = t_ref[place_ref[0]].astype(F32)
            lane = lax.broadcasted_iota(jnp.int32, (own, count), 1) % ROWS
            for row in range(ROWS):
                spread_ref[row * own : (row + 1) * own] = jnp.where(lane == row, base, 0.0).astype(BF16)

        here = pl.ds(pl.multiple_of(step * tile, tile), tile)
        data = [ref[:, :, here, :].astype(F32) for ref in refs]
        onsets = o_ref[pl.ds(pl.multiple_of(sblk[0] * half_rows + first + step * tile, tile), tile), :]
        time = lax.broadcasted_iota(jnp.int32, (own, rcv), 0) + place_ref[0] * own
        for half in range(2):
            cut = slice(half * ROWS, (half + 1) * ROWS)
            flat = jnp.stack([v[:, :, cut] for v in data]).reshape(count, rcv).astype(BF16)
            change = jnp.dot(spread_ref[...], flat, preferred_element_type=F32)
            for row in range(ROWS):
                spot = half * ROWS + row
                on = time < onsets[spot : spot + 1, :]
                moved = jnp.where(on, change[row * own : (row + 1) * own], 0.0)
                out[spot] = (x_ref[first + step * tile + spot].astype(F32) - moved).astype(BF16)

    inputs = [(v, whole(v)) for v in (initial, onset, table, *messages)]
    aliases = {}
    if target is not None:
        inputs.append((target, pl.BlockSpec(memory_space=pl.ANY)))
        aliases = {len(places) + len(inputs) - 1: 0}
    (out,) = call(
        body,
        places,
        inputs,
        [(jax.ShapeDtypeStruct(initial.shape, BF16), pl.BlockSpec((tile, own, rcv), lambda i, *_: (first // tile + i, 0, 0)))],
        (rows // tile,),
        scratch=[pltpu.VMEM((ROWS * own, count), BF16)],
        aliases=aliases,
        flops=2 * 2 * freq_devs * per_dev * own * rows * rcv,
    )
    return out


def exchanged(value, axis, step):
    return lax.ppermute(value, axis, [(i, i ^ step) for i in range(lax.axis_size(axis))])


def dealt_out(parts):
    return [exchanged(part, "freq", step) if step else part for part, step in zip(parts, ways(len(parts)))]


def spread(value, count):
    held = {0: value}
    bit = count // 2
    while bit:
        held.update({way | bit: exchanged(held[way], "freq", bit) for way in sorted(held)})
        bit //= 2
    return [held[way] for way in ways(count)]


def on_device(initial, response, aperture, onset_rcv, onset_src):
    freq_devs = lax.axis_size("freq")
    per_dev = response.shape[0]
    samples = initial.shape[1] * freq_devs
    half_rows = initial.shape[0]
    src_width = response.shape[2] // 2
    rows = half_rows // CHUNKS
    share = half_rows // freq_devs
    places = tuple(lax.axis_index(axis).reshape(1) for axis in ("freq", "rblk", "sblk"))
    freq_place = places[0]
    inverse = jnp.asarray(inverse_tables(samples, freq_devs, per_dev))
    matrix = jnp.asarray(window_tables(samples, freq_devs, per_dev))

    kept, sent = masked_halves(response, aperture, places)
    moved = [exchanged(v, "rblk", 1) for v in sent]
    kept_pair = [exchanged(v, "sblk", 1) for v in kept]
    sums, spectra = summed(dealt_out(first_spectra(initial, places, freq_devs, per_dev)))
    far = exchanged(spectra, "rblk", 1)
    parts = [((kept[i], None), (kept_pair[i], None)) for i in range(PARTS)]
    moved[0], spectra = lax.optimization_barrier((moved[0], spectra))
    held = down_products(None, [spectra], parts, 0, 0, freq_place)
    moved_pair = [exchanged(moved[0], "sblk", 1)]
    for index in range(1, PARTS):
        moved[index], held = lax.optimization_barrier((moved[index], held))
        moved_pair.append(exchanged(moved[index], "sblk", 1))
    parts = [((kept[i], moved[i]), (kept_pair[i], moved_pair[i])) for i in range(PARTS)]

    own, other = src_onsets(onset_src, places, half_rows, share, src_width)
    onsets = (own, exchanged(other, "sblk", 1))
    src_tables, rcv_tables = phase_tables(onsets, onset_rcv, places, freq_devs, per_dev, samples, PARTS, half_rows)

    near, far, result = [spectra], [far], None
    for step in range(ITERS):
        held = down_products(None, near, parts, 0, 0, freq_place) if step else held
        messages = dealt_out(down_products(held, far, parts, 1, 0, freq_place, freq_devs))
        messages = dealt_out(windowed(messages, src_tables, matrix, freq_place, per_dev, share))
        received = [exchanged(v, "rblk", 1) for v in up_products(messages, parts, freq_place, half_rows, 1)]
        keep = up_products(messages, parts, freq_place, half_rows, 0)
        near, far = [], []
        for chunk in range(CHUNKS):
            back = spread(added(keep[chunk], received[chunk]), freq_devs)
            if step < ITERS - 1:
                near.append(next_spectra(sums, back, rcv_tables, matrix, freq_place, chunk * rows))
                far.append(exchanged(near[chunk], "rblk", 1))
            else:
                result = updated(initial, onset_rcv, back, inverse, places, chunk * rows, rows, result)
    return result


def transform_tables(length, count):
    table = fields(length, count).reshape(2 * count, length)
    forward_table = jnp.asarray(table.astype(np.float32).astype(BF16))
    inverse_table = jnp.asarray((table.T * (2.0 / length)).astype(np.float32).astype(BF16))
    return forward_table, inverse_table


def settle(values):
    return lax.optimization_barrier(values.astype(BF16)).astype(F32)


def samples_into_spectra(values, forward_table, freq_total):
    out = jnp.einsum("kt,ptn->pkn", forward_table, values, preferred_element_type=F32)
    return out.reshape(values.shape[0], 2, freq_total, values.shape[2]).astype(BF16)


def spectra_into_samples(trace_spectra, inverse_table):
    flat = trace_spectra.reshape(trace_spectra.shape[0], -1, trace_spectra.shape[3])
    return jnp.einsum("tk,pkn->ptn", inverse_table, flat, preferred_element_type=F32)


def dense(spec, gated, real, imag, sign):
    dot = functools.partial(jnp.einsum, spec, preferred_element_type=F32)
    return jnp.stack(
        [dot(gated[:, 0], real) - sign * dot(gated[:, 1], imag), dot(gated[:, 0], imag) + sign * dot(gated[:, 1], real)], 1
    )


def general_device(initial, response, aperture, onset_rcv, onset_src):
    freq_devs, rblk_devs, sblk_devs = (lax.axis_size(a) for a in ("freq", "rblk", "sblk"))
    freq_index, rblk_index, sblk_index = (lax.axis_index(a) for a in ("freq", "rblk", "sblk"))
    freq_total = response.shape[0] * freq_devs
    samples = initial.shape[1] * freq_devs
    focal_all = onset_rcv.shape[0]
    forward_table, inverse_table = transform_tables(samples, freq_total)
    steps_axis = lax.iota(jnp.int32, samples)
    own_axis = freq_index * initial.shape[1] + lax.iota(jnp.int32, initial.shape[1])
    half_rows = focal_all // sblk_devs
    own_onsets = lax.dynamic_slice_in_dim(onset_rcv, sblk_index * half_rows, half_rows, 0)
    rcv_gate = (own_axis[None, :, None] < own_onsets[:, None, :]).astype(F32)
    src_rows = focal_all // (rblk_devs * freq_devs)
    src_first = rblk_index * (focal_all // rblk_devs) + freq_index * src_rows
    src_onsets = lax.dynamic_slice_in_dim(onset_src, src_first, src_rows, 0)
    src_gate = (steps_axis[None, :, None] < src_onsets[:, None, :]).astype(F32)
    mask_full = jnp.repeat(jnp.repeat(aperture, BLOCK, 1), BLOCK, 2).astype(BF16)
    gated = response * mask_full[:, None]
    own_forward = lax.dynamic_slice_in_dim(forward_table, freq_index * initial.shape[1], initial.shape[1], 1)
    own_inverse = lax.dynamic_slice_in_dim(inverse_table, freq_index * initial.shape[1], initial.shape[1], 0)
    current = initial
    for _ in range(ITERS):
        partial = samples_into_spectra(current, own_forward, freq_total)
        spec_back = lax.psum_scatter(partial.astype(F32), "freq", scatter_dimension=2, tiled=True).astype(BF16)
        spec_all = lax.all_gather(spec_back, "sblk", axis=0, tiled=True)
        down = lax.psum_scatter(
            settle(dense("euk,bek->beu", gated, spec_all[:, 0], spec_all[:, 1], 1.0)).astype(BF16),
            "rblk",
            scatter_dimension=0,
            tiled=True,
        )
        src_traces = lax.all_to_all(down, "freq", split_axis=0, concat_axis=2, tiled=True)
        upgoing = (src_gate * spectra_into_samples(src_traces, inverse_table)).astype(BF16)
        upspec = samples_into_spectra(upgoing, forward_table, freq_total)
        up_back = lax.all_to_all(upspec, "freq", split_axis=2, concat_axis=0, tiled=True)
        up_all = lax.all_gather(up_back, "rblk", axis=0, tiled=True)
        sums = dense("qao,bqa->bqo", gated, up_all[:, 0], up_all[:, 1], -1.0).astype(BF16)
        back = lax.psum_scatter(sums, "sblk", scatter_dimension=0, tiled=True)
        traces = lax.all_gather(back, "freq", axis=2, tiled=True)
        update = rcv_gate * spectra_into_samples(traces, own_inverse)
        current = (initial.astype(F32) - update).astype(BF16)
    return current


def fits(initial, response, aperture, onset_rcv, onset_src):
    freq_devs = lax.axis_size("freq")
    if lax.axis_size("rblk") != 2 or lax.axis_size("sblk") != 2 or freq_devs & (freq_devs - 1):
        return False
    whole_rows = initial.shape[0] % (max(2, CHUNKS) * ROWS * freq_devs) == 0
    whole_width = response.shape[2] % (2 * PARTS * BLOCK) == 0 and response.shape[3] % BLOCK == 0
    return whole_rows and whole_width and onset_rcv.shape[0] == 2 * initial.shape[0]


def chosen(*arrays):
    return on_device(*arrays) if fits(*arrays) else general_device(*arrays)


def solution(mesh):
    in_specs = (
        P(("group", "sblk"), "freq", "rblk"),
        P(("group", "freq"), None, "sblk", "rblk"),
        P(("group", "freq"), "sblk", "rblk"),
        P("group", "rblk"),
        P("group", "sblk"),
    )
    out_specs = P(("group", "sblk"), "freq", "rblk")
    return jax.shard_map(chosen, mesh=mesh, in_specs=in_specs, out_specs=out_specs, check_vma=False)
```

```python
import functools
import math

import jax
import jax.numpy as jnp
import numpy as np
from jax import lax
from jax.experimental import pallas as pl
from jax.experimental.pallas import tpu as pltpu
from jax.sharding import PartitionSpec as P

BLOCK = 128
ITERS = 2
ROWS = 8
CHUNKS = 2
PARTS = 1
VMEM_BYTES = 6 * 1024 * 1024

BF16 = jnp.bfloat16
F32 = jnp.float32


def ways(count):
    far = sorted(range(1, count), key=lambda step: (step.bit_length() < count.bit_length() - 1, step))
    return [0] + far


def field_rows(place, freq_devs, per_dev):
    rows = []
    for step in ways(freq_devs):
        first = (place ^ step) * per_dev
        for part in range(2):
            rows.extend((part, first + local) for local in range(per_dev))
    return rows


def fields(samples, freq_total):
    phase = (np.arange(1, freq_total + 1)[:, None] * np.arange(samples)[None, :]) % samples
    angle = phase * (2.0 * math.pi / samples)
    return np.stack([np.cos(angle), -np.sin(angle)])


def inverse_tables(samples, freq_devs, per_dev):
    exact = fields(samples, freq_devs * per_dev) * (2.0 / samples)
    own = samples // freq_devs
    out = []
    for place in range(freq_devs):
        part = [exact[c, j, place * own : (place + 1) * own] for c, j in field_rows(place, freq_devs, per_dev)]
        out.append(np.repeat(np.stack(part), ROWS, 0).T)
    return np.stack(out).astype(np.float32).astype(BF16)


def window_tables(samples, freq_devs, per_dev):
    freq_total = freq_devs * per_dev
    order = np.arange(1, freq_total + 1)
    unit = 2j * math.pi / samples
    diff = order[None, :] - order[:, None]
    total = order[None, :] + order[:, None]
    same = np.where(diff == 0, 0.0, 1.0 / (samples * (np.exp(unit * np.where(diff == 0, 1, diff)) - 1.0)))
    mixed = 1.0 / (samples * (np.exp(-unit * total) - 1.0))
    full = np.zeros((2, freq_total, 2, freq_total))
    full[0, :, 0, :] = same.real + mixed.real
    full[0, :, 1, :] = mixed.imag - same.imag
    full[1, :, 0, :] = same.imag + mixed.imag
    full[1, :, 1, :] = same.real - mixed.real
    out = []
    for place in range(freq_devs):
        rows = [c * freq_total + j for c, j in field_rows(place, freq_devs, per_dev)]
        flat = full.reshape(2 * freq_total, 2 * freq_total)[np.ix_(rows, rows)]
        out.append(np.kron(flat, np.eye(ROWS)))
    return np.stack(out).astype(np.float32).astype(BF16)


def call(body, scalars, inputs, outputs, grid, scratch=(), aliases=None, flops=0):
    in_arrays = [value for value, _ in inputs]
    bytes_all = sum(v.size * v.dtype.itemsize for v in in_arrays)
    bytes_all += sum(math.prod(s.shape) * s.dtype.itemsize for s, _ in outputs)
    return pl.pallas_call(
        body,
        grid_spec=pltpu.PrefetchScalarGridSpec(
            num_scalar_prefetch=len(scalars),
            grid=grid,
            in_specs=[spec for _, spec in inputs],
            out_specs=[spec for _, spec in outputs],
            scratch_shapes=list(scratch),
        ),
        out_shape=[shape for shape, _ in outputs],
        input_output_aliases=aliases or {},
        compiler_params=pltpu.CompilerParams(vmem_limit_bytes=VMEM_BYTES),
        cost_estimate=pl.CostEstimate(flops=flops, bytes_accessed=bytes_all, transcendentals=0),
    )(*scalars, *in_arrays)


def whole(array):
    zeros = (0,) * array.ndim
    return pl.BlockSpec(array.shape, lambda *_: zeros)


def sine_terms():
    square = (np.cos(np.linspace(0.0, math.pi, 200)) + 1.0) / 32.0
    y = np.sqrt(np.maximum(square, 1e-12))
    return [float(v) for v in np.polynomial.polynomial.polyfit(square, np.sin(2.0 * math.pi * y) / y, 6)]


def turned(turn):
    terms = sine_terms()

    def sine(y):
        square = y * y
        total = jnp.full_like(y, terms[-1])
        for term in terms[-2::-1]:
            total = total * square + term
        return total * y

    turn = turn - jnp.floor(turn + 0.5)
    size = jnp.abs(turn)
    folded = jnp.where(size > 0.25, jnp.where(turn > 0.0, 0.5, -0.5) - turn, turn)
    return sine(0.25 - size), sine(folded)


def first_spectra(initial, places, freq_devs, per_dev):
    rows, own, rcv = initial.shape
    samples = own * freq_devs
    tile = 2 * ROWS
    count = freq_devs * 2 * per_dev * ROWS

    def body(freq, rblk, sblk, x_ref, *rest):
        outs, spread_ref = rest[:freq_devs], rest[freq_devs]
        time = lax.broadcasted_iota(jnp.int32, (ROWS, own), 1) + freq[0] * own
        time = time.astype(F32) * (1.0 / samples)
        table = []
        for way in ways(freq_devs):
            waves = [turned(time * ((freq[0] ^ way) * per_dev + j + 1).astype(F32)) for j in range(per_dev)]
            table += [cosine for cosine, _ in waves] + [-sine for _, sine in waves]
        table = jnp.concatenate(table, 0)
        lane = lax.broadcasted_iota(jnp.int32, (count, own), 0) % ROWS
        for row in range(ROWS):
            spread_ref[:, row * own : (row + 1) * own] = jnp.where(lane == row, table, 0.0).astype(BF16)
        for at in range(rows // tile):
            parts = []
            for half in range(2):
                start = at * tile + half * ROWS
                flat = x_ref[start : start + ROWS].reshape(ROWS * own, rcv)
                value = jnp.dot(spread_ref[...], flat, preferred_element_type=F32)
                parts.append(value.reshape(freq_devs, 2, per_dev, ROWS, rcv))
            both = jnp.concatenate(parts, 3).astype(BF16)
            for step, out in enumerate(outs):
                out[:, :, at * tile : (at + 1) * tile, :] = both[step]

    shape = jax.ShapeDtypeStruct((2, per_dev, rows, rcv), BF16)
    return call(
        body,
        places,
        [(initial, whole(initial))],
        [(shape, whole(shape))] * freq_devs,
        (1,),
        scratch=[pltpu.VMEM((count, ROWS * own), BF16)],
        flops=2 * 2 * freq_devs * per_dev * own * rows * rcv,
    )


def masked_halves(response, aperture, places):
    per_dev, _, src, rcv = response.shape
    half = src // 2
    width = half // PARTS

    def body(_, rblk, __, flags, x_ref, *outs):
        lane = lax.broadcasted_iota(jnp.int32, (1, rcv), 1) // BLOCK
        for flip in (1, 0):
            for j in range(per_dev):
                for step in range(half // BLOCK):
                    block = (rblk[0] ^ flip) * (half // BLOCK) + step
                    on = flags[j, pl.ds(block, 1), :].astype(F32)
                    row = sum(jnp.where(lane == r, on[:, r : r + 1], 0.0) for r in range(rcv // BLOCK))
                    gate = jnp.broadcast_to(row, (BLOCK, rcv)).astype(BF16)
                    rows = pl.ds(pl.multiple_of(block * BLOCK, BLOCK), BLOCK)
                    part, at = divmod(step * BLOCK, width)
                    out = outs[flip * PARTS + part]
                    for c in range(2):
                        out[j, at : at + BLOCK, c * rcv : (c + 1) * rcv] = x_ref[j, c, rows, :] * gate

    shape = jax.ShapeDtypeStruct((per_dev, width, 2 * rcv), BF16)
    inputs = [(v, whole(v)) for v in (aperture, response)]
    outs = call(body, places, inputs, [(shape, whole(shape))] * (2 * PARTS), (1,))
    return list(outs[:PARTS]), list(outs[PARTS:])


def summed(parts):
    def body(*refs):
        total = sum(ref[...].astype(F32) for ref in refs[:-2])
        refs[-2][...] = total
        refs[-1][...] = total.astype(BF16)

    shapes = [jax.ShapeDtypeStruct(parts[0].shape, kind) for kind in (F32, BF16)]
    return call(body, (), [(v, whole(v)) for v in parts], [(v, whole(v)) for v in shapes], (1,))


def added(keep, received):
    def body(k_ref, r_ref, out):
        out[...] = (k_ref[...] + r_ref[...].astype(F32)).astype(BF16)

    shape = jax.ShapeDtypeStruct(keep.shape, BF16)
    (out,) = call(body, (), [(v, whole(v)) for v in (keep, received)], [(shape, whole(shape))], (1,))
    return out


def src_onsets(onset, places, half_rows, share, width):

    def body(freq, rblk, sblk, o_ref, own, other):
        lanes = pl.ds(pl.multiple_of(rblk[0] * width, BLOCK), width)
        for core, out in ((sblk[0], own), (1 - sblk[0], other)):
            spot = pl.multiple_of(core * half_rows + freq[0] * share, ROWS)
            out[...] = o_ref[pl.ds(spot, share), lanes]

    shape = jax.ShapeDtypeStruct((share, width), onset.dtype)
    return call(body, places, [(onset, whole(onset))], [(shape, whole(shape))] * 2, (1,))


def phase_tables(src, rcv, places, freq_devs, per_dev, samples, parts, rows):
    width = src[0].shape[1] // parts

    def fill(outs, value, to, freq):
        cosines, sines, fraction = outs
        value = value.astype(F32) * (1.0 / samples)
        fraction[:, to] = value
        for step, way in enumerate(ways(freq_devs)):
            for j in range(per_dev):
                order = ((freq[0] ^ way) * per_dev + j + 1).astype(F32)
                cosines[step, j, :, to], sines[step, j, :, to] = turned(value * order)

    def body(freq, _, sblk, own, other, r_ref, *outs):
        for part in range(parts):
            for spot, ref in enumerate((own, other)):
                at = (part * 2 + spot) * width
                fill(outs[:3], ref[:, part * width : (part + 1) * width], slice(at, at + width), freq)
        value = r_ref[pl.ds(pl.multiple_of(sblk[0] * rows, ROWS), rows), :]
        fill(outs[3:], value, slice(0, value.shape[1]), freq)

    shapes = []
    for count, total in ((src[0].shape[0], 2 * src[0].shape[1]), (rows, rcv.shape[1])):
        table = jax.ShapeDtypeStruct((freq_devs, per_dev, count, total), F32)
        shapes += [table, table, jax.ShapeDtypeStruct(table.shape[2:], F32)]
    outs = call(body, places, [(v, whole(v)) for v in (*src, rcv)], [(v, whole(v)) for v in shapes], (1,))
    return tuple(outs[:3]), tuple(outs[3:])


def down_products(before, spectra, parts, side, first, freq_place, freq_devs=0):
    _, per_dev, _, rcv = spectra[0].shape
    rows = sum(v.shape[2] for v in spectra)
    flat = [pair[side] for part in parts for pair in part]
    width = flat[0].shape[1]
    total_width = before.shape[-1] if before is not None else first + width * len(flat)
    share = rows // freq_devs if freq_devs else 0
    old = [] if before is None else [before]

    def body(place_ref, *rest):
        held_ref, rest = (rest[0], rest[1:]) if old else (None, rest)
        refs, resp, outs = rest[: len(spectra)], rest[len(spectra) : len(spectra) + len(flat)], rest[len(spectra) + len(flat) :]
        held = outs[-1]
        for j in range(per_dev):
            real = jnp.concatenate([ref[0, j] for ref in refs], 0)
            imag = jnp.concatenate([ref[1, j] for ref in refs], 0)
            lhs = jnp.concatenate([jnp.concatenate([real, -imag], 1), jnp.concatenate([imag, real], 1)], 0)
            for at, ref in enumerate(resp):
                total = lax.dot_general(lhs, ref[j], (((1,), (1,)), ((), ())), preferred_element_type=F32)
                to = slice(first + at * width, first + (at + 1) * width)
                for part in range(2):
                    value = total[part * rows : (part + 1) * rows]
                    held[part, j, :, to] = value + held_ref[part, j, :, to] if old else value
        if old:
            for to in (slice(0, first), slice(first + len(flat) * width, total_width)):
                if to.start < to.stop:
                    held[:, :, :, to] = held_ref[:, :, :, to]
        if freq_devs:
            for way, out in zip(ways(freq_devs), outs):
                start = pl.multiple_of((place_ref[0] ^ way) * share, share)
                out[...] = held[:, :, pl.ds(start, share), :].reshape(out.shape).astype(BF16)

    sums = (2, per_dev, rows, total_width)
    if freq_devs:
        shapes = [jax.ShapeDtypeStruct((2 * per_dev * share, total_width), BF16)] * freq_devs
    else:
        shapes = [jax.ShapeDtypeStruct(sums, F32)]
    outs = call(
        body,
        (freq_place,),
        [(v, whole(v)) for v in (*old, *spectra, *flat)],
        [(v, whole(v)) for v in shapes],
        (1,),
        scratch=[pltpu.VMEM(sums, F32)] if freq_devs else [],
        flops=2 * 4 * per_dev * rows * len(flat) * width * rcv,
    )
    return outs if freq_devs else outs[0]


def mixed_fields(plain, cos, sin, matrix):
    tile = plain[0].shape[-1]
    turned = [
        jnp.stack([v[0] * c - v[1] * s, v[0] * s + v[1] * c]) for v, c, s in zip(plain, cos, sin)
    ]
    flat = [jnp.stack(v).reshape(matrix.shape[1], tile).astype(BF16) for v in (turned, plain)]
    mixed = jnp.dot(matrix, jnp.concatenate(flat, 1), preferred_element_type=F32)
    shape = (-1, 2) + plain[0].shape[1:]
    return mixed[:, :tile].reshape(shape), mixed[:, tile:].reshape(shape)


def unturned(up, low, value, cos, sin, part):
    real = cos * up[0] + sin * up[1] - low[0] + part * value[0]
    imag = cos * up[1] - sin * up[0] - low[1] + part * value[1]
    return jnp.stack([real, imag])


def tiles(width, body):
    def at(step, carry):
        body(pl.ds(pl.multiple_of(step * BLOCK, BLOCK), BLOCK))
        return carry

    lax.fori_loop(0, width // BLOCK, at, 0, unroll=2)


def windowed(messages, tables, matrix, freq_place, per_dev, share):
    cosines, sines, fraction = tables
    freq_devs = len(messages)
    width = messages[0].shape[-1]
    count = freq_devs * 2 * per_dev * ROWS

    def body(place_ref, c_ref, s_ref, f_ref, g_ref, *rest):
        refs, outs = rest[:freq_devs], rest[freq_devs:]
        matrix_here = g_ref[place_ref[0]]

        def one(at):
            data = [ref[:, at].astype(F32).reshape(2, per_dev, share, BLOCK) for ref in refs]
            made = [[] for _ in outs]
            for first in range(0, share, ROWS):
                cut = slice(first, first + ROWS)
                plain = [value[:, :, cut] for value in data]
                cos = [c_ref[step, :, cut, at] for step in range(freq_devs)]
                sin = [s_ref[step, :, cut, at] for step in range(freq_devs)]
                up, low = mixed_fields(plain, cos, sin, matrix_here)
                part = f_ref[cut, at]
                for step in range(freq_devs):
                    made[step].append(unturned(up[step], low[step], plain[step], cos[step], sin[step], part))
            for out, value in zip(outs, made):
                out[:, at] = jnp.concatenate(value, 2).reshape(out.shape[0], BLOCK).astype(BF16)

        tiles(width, one)

    inputs = (cosines, sines, fraction, matrix, *messages)
    return call(
        body,
        (freq_place,),
        [(v, whole(v)) for v in inputs],
        [(jax.ShapeDtypeStruct(v.shape, BF16), whole(v)) for v in messages],
        (1,),
        flops=2 * count * count * 2 * width * share // ROWS,
    )


def up_products(messages, parts, freq_place, rows, side):
    freq_devs = len(messages)
    flat = [pair[side] for part in parts for pair in part]
    per_dev, src, rcv = flat[0].shape[0], flat[0].shape[1], flat[0].shape[2] // 2
    group = rows // CHUNKS
    share = rows // freq_devs
    total_width = src * len(flat)
    kind = BF16 if side else F32

    def body(place_ref, *rest):
        resp, refs = rest[: len(flat)], rest[len(flat) : len(flat) + freq_devs]
        outs, held = rest[len(flat) + freq_devs : -1], rest[-1]
        for way, ref in zip(ways(freq_devs), refs):
            start = pl.multiple_of((place_ref[0] ^ way) * share, share)
            value = ref[...].reshape(2, per_dev, share, total_width)
            for part in range(2):
                for j in range(per_dev):
                    held[part, j, pl.ds(start, share), :] = value[part, j]
        for j in range(per_dev):
            both = jnp.concatenate([held[0, j], held[1, j]], 0)
            total = sum(
                jnp.dot(both[:, at * src : (at + 1) * src], ref[j], preferred_element_type=F32)
                for at, ref in enumerate(resp)
            )
            real = total[:rows, :rcv] + total[rows:, rcv:]
            imag = total[rows:, :rcv] - total[:rows, rcv:]
            for index, out in enumerate(outs):
                cut = slice(index * group, (index + 1) * group)
                out[0, j] = real[cut].astype(kind)
                out[1, j] = imag[cut].astype(kind)

    shape = jax.ShapeDtypeStruct((2, per_dev, group, rcv), kind)
    return call(
        body,
        (freq_place,),
        [(v, whole(v)) for v in (*flat, *messages)],
        [(shape, whole(shape))] * CHUNKS,
        (1,),
        scratch=[pltpu.VMEM((2, per_dev, rows, total_width), BF16)],
        flops=2 * 4 * per_dev * rows * total_width * rcv,
    )


def next_spectra(sums, messages, tables, matrix, freq_place, first_row):
    cosines, sines, fraction = tables
    freq_devs = len(messages)
    _, per_dev, rows, rcv = messages[0].shape
    count = freq_devs * 2 * per_dev * ROWS
    own = 2 * per_dev * ROWS

    def body(place_ref, u_ref, c_ref, s_ref, f_ref, g_ref, *rest):
        refs, out = rest[:freq_devs], rest[freq_devs]
        matrix_here = g_ref[place_ref[0], :own]

        def one(at):
            for base in range(0, rows, 2 * ROWS):
                pair = slice(base, base + 2 * ROWS)
                data = [ref[:, :, pair, at].astype(F32) for ref in refs]
                made = []
                for half in range(2):
                    plain = [value[:, :, half * ROWS : (half + 1) * ROWS] for value in data]
                    cut = slice(first_row + base + half * ROWS, first_row + base + (half + 1) * ROWS)
                    cos = [c_ref[step, :, cut, at] for step in range(freq_devs)]
                    sin = [s_ref[step, :, cut, at] for step in range(freq_devs)]
                    up, low = mixed_fields(plain, cos, sin, matrix_here)
                    change = unturned(up[0], low[0], plain[0], cos[0], sin[0], f_ref[cut, at])
                    made.append(u_ref[:, :, cut, at] - change)
                out[:, :, pair, at] = jnp.concatenate(made, 2).astype(BF16)

        tiles(rcv, one)

    inputs = (sums, cosines, sines, fraction, matrix, *messages)
    shape = jax.ShapeDtypeStruct(messages[0].shape, BF16)
    (out,) = call(
        body,
        (freq_place,),
        [(v, whole(v)) for v in inputs],
        [(shape, whole(shape))],
        (1,),
        flops=2 * own * count * 2 * rcv * rows // ROWS,
    )
    return out


def updated(initial, onset, messages, table, places, first, rows, target):
    freq_devs = len(messages)
    half_rows, own, rcv = initial.shape
    per_dev = messages[0].shape[1]
    tile = 2 * ROWS
    count = table.shape[2]

    def body(place_ref, _, sblk, x_ref, o_ref, t_ref, *rest):
        refs = rest[:freq_devs]
        out, spread_ref = rest[-2:]
        step = pl.program_id(0)

        @pl.when(step == 0)
        def _():
            base = t_ref[place_ref[0]].astype(F32)
            lane = lax.broadcasted_iota(jnp.int32, (own, count), 1) % ROWS
            for row in range(ROWS):
                spread_ref[row * own : (row + 1) * own] = jnp.where(lane == row, base, 0.0).astype(BF16)

        here = pl.ds(pl.multiple_of(step * tile, tile), tile)
        data = [ref[:, :, here, :].astype(F32) for ref in refs]
        onsets = o_ref[pl.ds(pl.multiple_of(sblk[0] * half_rows + first + step * tile, tile), tile), :]
        time = lax.broadcasted_iota(jnp.int32, (own, rcv), 0) + place_ref[0] * own
        for half in range(2):
            cut = slice(half * ROWS, (half + 1) * ROWS)
            flat = jnp.stack([v[:, :, cut] for v in data]).reshape(count, rcv).astype(BF16)
            change = jnp.dot(spread_ref[...], flat, preferred_element_type=F32)
            for row in range(ROWS):
                spot = half * ROWS + row
                on = time < onsets[spot : spot + 1, :]
                moved = jnp.where(on, change[row * own : (row + 1) * own], 0.0)
                out[spot] = (x_ref[first + step * tile + spot].astype(F32) - moved).astype(BF16)

    inputs = [(v, whole(v)) for v in (initial, onset, table, *messages)]
    aliases = {}
    if target is not None:
        inputs.append((target, pl.BlockSpec(memory_space=pl.ANY)))
        aliases = {len(places) + len(inputs) - 1: 0}
    (out,) = call(
        body,
        places,
        inputs,
        [(jax.ShapeDtypeStruct(initial.shape, BF16), pl.BlockSpec((tile, own, rcv), lambda i, *_: (first // tile + i, 0, 0)))],
        (rows // tile,),
        scratch=[pltpu.VMEM((ROWS * own, count), BF16)],
        aliases=aliases,
        flops=2 * 2 * freq_devs * per_dev * own * rows * rcv,
    )
    return out


def exchanged(value, axis, step):
    return lax.ppermute(value, axis, [(i, i ^ step) for i in range(lax.axis_size(axis))])


def dealt_out(parts):
    return [exchanged(part, "freq", step) if step else part for part, step in zip(parts, ways(len(parts)))]


def spread(value, count):
    held = {0: value}
    bit = count // 2
    while bit:
        held.update({way | bit: exchanged(held[way], "freq", bit) for way in sorted(held)})
        bit //= 2
    return [held[way] for way in ways(count)]


def on_device(initial, response, aperture, onset_rcv, onset_src):
    freq_devs = lax.axis_size("freq")
    per_dev = response.shape[0]
    samples = initial.shape[1] * freq_devs
    half_rows = initial.shape[0]
    src_width = response.shape[2] // 2
    rows = half_rows // CHUNKS
    share = half_rows // freq_devs
    places = tuple(lax.axis_index(axis).reshape(1) for axis in ("freq", "rblk", "sblk"))
    freq_place = places[0]
    inverse = jnp.asarray(inverse_tables(samples, freq_devs, per_dev))
    matrix = jnp.asarray(window_tables(samples, freq_devs, per_dev))

    kept, sent = masked_halves(response, aperture, places)
    moved = [exchanged(v, "rblk", 1) for v in sent]
    kept_pair = [exchanged(v, "sblk", 1) for v in kept]
    sums, spectra = summed(dealt_out(first_spectra(initial, places, freq_devs, per_dev)))
    far = exchanged(spectra, "rblk", 1)
    parts = [((kept[i], None), (kept_pair[i], None)) for i in range(PARTS)]
    held = down_products(None, [spectra], parts, 0, 0, freq_place)
    moved, held = lax.optimization_barrier((moved, held))
    moved_pair = [exchanged(v, "sblk", 1) for v in moved]
    parts = [((kept[i], moved[i]), (kept_pair[i], moved_pair[i])) for i in range(PARTS)]

    own, other = src_onsets(onset_src, places, half_rows, share, src_width)
    onsets = (own, exchanged(other, "sblk", 1))
    src_tables, rcv_tables = phase_tables(onsets, onset_rcv, places, freq_devs, per_dev, samples, PARTS, half_rows)

    near, far, result = [spectra], [far], None
    for step in range(ITERS):
        held = down_products(None, near, parts, 0, 0, freq_place) if step else held
        messages = dealt_out(down_products(held, far, parts, 1, 0, freq_place, freq_devs))
        messages = dealt_out(windowed(messages, src_tables, matrix, freq_place, per_dev, share))
        received = [exchanged(v, "rblk", 1) for v in up_products(messages, parts, freq_place, half_rows, 1)]
        keep = up_products(messages, parts, freq_place, half_rows, 0)
        near, far = [], []
        for chunk in range(CHUNKS):
            back = spread(added(keep[chunk], received[chunk]), freq_devs)
            if step < ITERS - 1:
                near.append(next_spectra(sums, back, rcv_tables, matrix, freq_place, chunk * rows))
                far.append(exchanged(near[chunk], "rblk", 1))
            else:
                result = updated(initial, onset_rcv, back, inverse, places, chunk * rows, rows, result)
    return result


def transform_tables(length, count):
    table = fields(length, count).reshape(2 * count, length)
    forward_table = jnp.asarray(table.astype(np.float32).astype(BF16))
    inverse_table = jnp.asarray((table.T * (2.0 / length)).astype(np.float32).astype(BF16))
    return forward_table, inverse_table


def settle(values):
    return lax.optimization_barrier(values.astype(BF16)).astype(F32)


def samples_into_spectra(values, forward_table, freq_total):
    out = jnp.einsum("kt,ptn->pkn", forward_table, values, preferred_element_type=F32)
    return out.reshape(values.shape[0], 2, freq_total, values.shape[2]).astype(BF16)


def spectra_into_samples(trace_spectra, inverse_table):
    flat = trace_spectra.reshape(trace_spectra.shape[0], -1, trace_spectra.shape[3])
    return jnp.einsum("tk,pkn->ptn", inverse_table, flat, preferred_element_type=F32)


def dense(spec, gated, real, imag, sign):
    dot = functools.partial(jnp.einsum, spec, preferred_element_type=F32)
    return jnp.stack(
        [dot(gated[:, 0], real) - sign * dot(gated[:, 1], imag), dot(gated[:, 0], imag) + sign * dot(gated[:, 1], real)], 1
    )


def general_device(initial, response, aperture, onset_rcv, onset_src):
    freq_devs, rblk_devs, sblk_devs = (lax.axis_size(a) for a in ("freq", "rblk", "sblk"))
    freq_index, rblk_index, sblk_index = (lax.axis_index(a) for a in ("freq", "rblk", "sblk"))
    freq_total = response.shape[0] * freq_devs
    samples = initial.shape[1] * freq_devs
    focal_all = onset_rcv.shape[0]
    forward_table, inverse_table = transform_tables(samples, freq_total)
    steps_axis = lax.iota(jnp.int32, samples)
    own_axis = freq_index * initial.shape[1] + lax.iota(jnp.int32, initial.shape[1])
    half_rows = focal_all // sblk_devs
    own_onsets = lax.dynamic_slice_in_dim(onset_rcv, sblk_index * half_rows, half_rows, 0)
    rcv_gate = (own_axis[None, :, None] < own_onsets[:, None, :]).astype(F32)
    src_rows = focal_all // (rblk_devs * freq_devs)
    src_first = rblk_index * (focal_all // rblk_devs) + freq_index * src_rows
    src_onsets = lax.dynamic_slice_in_dim(onset_src, src_first, src_rows, 0)
    src_gate = (steps_axis[None, :, None] < src_onsets[:, None, :]).astype(F32)
    mask_full = jnp.repeat(jnp.repeat(aperture, BLOCK, 1), BLOCK, 2).astype(BF16)
    gated = response * mask_full[:, None]
    own_forward = lax.dynamic_slice_in_dim(forward_table, freq_index * initial.shape[1], initial.shape[1], 1)
    own_inverse = lax.dynamic_slice_in_dim(inverse_table, freq_index * initial.shape[1], initial.shape[1], 0)
    current = initial
    for _ in range(ITERS):
        partial = samples_into_spectra(current, own_forward, freq_total)
        spec_back = lax.psum_scatter(partial.astype(F32), "freq", scatter_dimension=2, tiled=True).astype(BF16)
        spec_all = lax.all_gather(spec_back, "sblk", axis=0, tiled=True)
        down = lax.psum_scatter(
            settle(dense("euk,bek->beu", gated, spec_all[:, 0], spec_all[:, 1], 1.0)).astype(BF16),
            "rblk",
            scatter_dimension=0,
            tiled=True,
        )
        src_traces = lax.all_to_all(down, "freq", split_axis=0, concat_axis=2, tiled=True)
        upgoing = (src_gate * spectra_into_samples(src_traces, inverse_table)).astype(BF16)
        upspec = samples_into_spectra(upgoing, forward_table, freq_total)
        up_back = lax.all_to_all(upspec, "freq", split_axis=2, concat_axis=0, tiled=True)
        up_all = lax.all_gather(up_back, "rblk", axis=0, tiled=True)
        sums = dense("qao,bqa->bqo", gated, up_all[:, 0], up_all[:, 1], -1.0).astype(BF16)
        back = lax.psum_scatter(sums, "sblk", scatter_dimension=0, tiled=True)
        traces = lax.all_gather(back, "freq", axis=2, tiled=True)
        update = rcv_gate * spectra_into_samples(traces, own_inverse)
        current = (initial.astype(F32) - update).astype(BF16)
    return current


def fits(initial, response, aperture, onset_rcv, onset_src):
    freq_devs = lax.axis_size("freq")
    if lax.axis_size("rblk") != 2 or lax.axis_size("sblk") != 2 or freq_devs & (freq_devs - 1):
        return False
    whole_rows = initial.shape[0] % (max(2, CHUNKS) * ROWS * freq_devs) == 0
    whole_width = response.shape[2] % (2 * PARTS * BLOCK) == 0 and response.shape[3] % BLOCK == 0
    return whole_rows and whole_width and onset_rcv.shape[0] == 2 * initial.shape[0]


def chosen(*arrays):
    return on_device(*arrays) if fits(*arrays) else general_device(*arrays)


def solution(mesh):
    in_specs = (
        P(("group", "sblk"), "freq", "rblk"),
        P(("group", "freq"), None, "sblk", "rblk"),
        P(("group", "freq"), "sblk", "rblk"),
        P("group", "rblk"),
        P("group", "sblk"),
    )
    out_specs = P(("group", "sblk"), "freq", "rblk")
    return jax.shard_map(chosen, mesh=mesh, in_specs=in_specs, out_specs=out_specs, check_vma=False)
```

```python
import functools
import math

import jax
import jax.numpy as jnp
import numpy as np
from jax import lax
from jax.experimental import pallas as pl
from jax.experimental.pallas import tpu as pltpu
from jax.sharding import PartitionSpec as P

BLOCK = 128
ITERS = 2
ROWS = 8
CHUNKS = 2
PARTS = 2
VMEM_BYTES = 6 * 1024 * 1024

BF16 = jnp.bfloat16
F32 = jnp.float32


def ways(count):
    return [0] + list(range(count - 1, 0, -1))


def field_rows(place, freq_devs, per_dev):
    rows = []
    for step in ways(freq_devs):
        first = (place ^ step) * per_dev
        for part in range(2):
            rows.extend((part, first + local) for local in range(per_dev))
    return rows


def fields(samples, freq_total):
    phase = (np.arange(1, freq_total + 1)[:, None] * np.arange(samples)[None, :]) % samples
    angle = phase * (2.0 * math.pi / samples)
    return np.stack([np.cos(angle), -np.sin(angle)])


def inverse_tables(samples, freq_devs, per_dev):
    exact = fields(samples, freq_devs * per_dev) * (2.0 / samples)
    own = samples // freq_devs
    out = []
    for place in range(freq_devs):
        part = [exact[c, j, place * own : (place + 1) * own] for c, j in field_rows(place, freq_devs, per_dev)]
        out.append(np.repeat(np.stack(part), ROWS, 0).T)
    return np.stack(out).astype(np.float32).astype(BF16)


def window_tables(samples, freq_devs, per_dev):
    freq_total = freq_devs * per_dev
    order = np.arange(1, freq_total + 1)
    unit = 2j * math.pi / samples
    diff = order[None, :] - order[:, None]
    total = order[None, :] + order[:, None]
    same = np.where(diff == 0, 0.0, 1.0 / (samples * (np.exp(unit * np.where(diff == 0, 1, diff)) - 1.0)))
    mixed = 1.0 / (samples * (np.exp(-unit * total) - 1.0))
    full = np.zeros((2, freq_total, 2, freq_total))
    full[0, :, 0, :] = same.real + mixed.real
    full[0, :, 1, :] = mixed.imag - same.imag
    full[1, :, 0, :] = same.imag + mixed.imag
    full[1, :, 1, :] = same.real - mixed.real
    out = []
    for place in range(freq_devs):
        rows = [c * freq_total + j for c, j in field_rows(place, freq_devs, per_dev)]
        flat = full.reshape(2 * freq_total, 2 * freq_total)[np.ix_(rows, rows)]
        out.append(np.kron(flat, np.eye(ROWS)))
    return np.stack(out).astype(np.float32).astype(BF16)


def call(body, scalars, inputs, outputs, grid, scratch=(), aliases=None, flops=0):
    in_arrays = [value for value, _ in inputs]
    bytes_all = sum(v.size * v.dtype.itemsize for v in in_arrays)
    bytes_all += sum(math.prod(s.shape) * s.dtype.itemsize for s, _ in outputs)
    return pl.pallas_call(
        body,
        grid_spec=pltpu.PrefetchScalarGridSpec(
            num_scalar_prefetch=len(scalars),
            grid=grid,
            in_specs=[spec for _, spec in inputs],
            out_specs=[spec for _, spec in outputs],
            scratch_shapes=list(scratch),
        ),
        out_shape=[shape for shape, _ in outputs],
        input_output_aliases=aliases or {},
        compiler_params=pltpu.CompilerParams(vmem_limit_bytes=VMEM_BYTES),
        cost_estimate=pl.CostEstimate(flops=flops, bytes_accessed=bytes_all, transcendentals=0),
    )(*scalars, *in_arrays)


def whole(array):
    zeros = (0,) * array.ndim
    return pl.BlockSpec(array.shape, lambda *_: zeros)


def sine_terms():
    square = (np.cos(np.linspace(0.0, math.pi, 200)) + 1.0) / 32.0
    y = np.sqrt(np.maximum(square, 1e-12))
    return [float(v) for v in np.polynomial.polynomial.polyfit(square, np.sin(2.0 * math.pi * y) / y, 6)]


def turned(turn):
    terms = sine_terms()

    def sine(y):
        square = y * y
        total = jnp.full_like(y, terms[-1])
        for term in terms[-2::-1]:
            total = total * square + term
        return total * y

    turn = turn - jnp.floor(turn + 0.5)
    size = jnp.abs(turn)
    folded = jnp.where(size > 0.25, jnp.where(turn > 0.0, 0.5, -0.5) - turn, turn)
    return sine(0.25 - size), sine(folded)


def first_spectra(initial, places, freq_devs, per_dev):
    rows, own, rcv = initial.shape
    samples = own * freq_devs
    tile = 2 * ROWS
    count = freq_devs * 2 * per_dev * ROWS

    def body(freq, rblk, sblk, x_ref, *rest):
        outs, spread_ref = rest[:freq_devs], rest[freq_devs]
        time = lax.broadcasted_iota(jnp.int32, (ROWS, own), 1) + freq[0] * own
        time = time.astype(F32) * (1.0 / samples)
        table = []
        for way in ways(freq_devs):
            waves = [turned(time * ((freq[0] ^ way) * per_dev + j + 1).astype(F32)) for j in range(per_dev)]
            table += [cosine for cosine, _ in waves] + [-sine for _, sine in waves]
        table = jnp.concatenate(table, 0)
        lane = lax.broadcasted_iota(jnp.int32, (count, own), 0) % ROWS
        for row in range(ROWS):
            spread_ref[:, row * own : (row + 1) * own] = jnp.where(lane == row, table, 0.0).astype(BF16)
        for at in range(rows // tile):
            parts = []
            for half in range(2):
                start = at * tile + half * ROWS
                flat = x_ref[start : start + ROWS].reshape(ROWS * own, rcv)
                value = jnp.dot(spread_ref[...], flat, preferred_element_type=F32)
                parts.append(value.reshape(freq_devs, 2, per_dev, ROWS, rcv))
            both = jnp.concatenate(parts, 3).astype(BF16)
            for step, out in enumerate(outs):
                out[:, :, at * tile : (at + 1) * tile, :] = both[step]

    shape = jax.ShapeDtypeStruct((2, per_dev, rows, rcv), BF16)
    return call(
        body,
        places,
        [(initial, whole(initial))],
        [(shape, whole(shape))] * freq_devs,
        (1,),
        scratch=[pltpu.VMEM((count, ROWS * own), BF16)],
        flops=2 * 2 * freq_devs * per_dev * own * rows * rcv,
    )


def masked_halves(response, aperture, places):
    per_dev, _, src, rcv = response.shape
    half = src // 2
    width = half // PARTS

    def body(_, rblk, __, flags, x_ref, *outs):
        lane = lax.broadcasted_iota(jnp.int32, (1, rcv), 1) // BLOCK
        for flip in (1, 0):
            for j in range(per_dev):
                for step in range(half // BLOCK):
                    block = (rblk[0] ^ flip) * (half // BLOCK) + step
                    on = flags[j, pl.ds(block, 1), :].astype(F32)
                    row = sum(jnp.where(lane == r, on[:, r : r + 1], 0.0) for r in range(rcv // BLOCK))
                    gate = jnp.broadcast_to(row, (BLOCK, rcv)).astype(BF16)
                    rows = pl.ds(pl.multiple_of(block * BLOCK, BLOCK), BLOCK)
                    part, at = divmod(step * BLOCK, width)
                    out = outs[flip * PARTS + part]
                    for c in range(2):
                        out[j, at : at + BLOCK, c * rcv : (c + 1) * rcv] = x_ref[j, c, rows, :] * gate

    shape = jax.ShapeDtypeStruct((per_dev, width, 2 * rcv), BF16)
    inputs = [(v, whole(v)) for v in (aperture, response)]
    outs = call(body, places, inputs, [(shape, whole(shape))] * (2 * PARTS), (1,))
    return list(outs[:PARTS]), list(outs[PARTS:])


def summed(parts):
    def body(*refs):
        total = sum(ref[...].astype(F32) for ref in refs[:-2])
        refs[-2][...] = total
        refs[-1][...] = total.astype(BF16)

    shapes = [jax.ShapeDtypeStruct(parts[0].shape, kind) for kind in (F32, BF16)]
    return call(body, (), [(v, whole(v)) for v in parts], [(v, whole(v)) for v in shapes], (1,))


def added(keep, received):
    def body(k_ref, r_ref, out):
        out[...] = (k_ref[...] + r_ref[...].astype(F32)).astype(BF16)

    shape = jax.ShapeDtypeStruct(keep.shape, BF16)
    (out,) = call(body, (), [(v, whole(v)) for v in (keep, received)], [(shape, whole(shape))], (1,))
    return out


def src_onsets(onset, places, half_rows, share, width):

    def body(freq, rblk, sblk, o_ref, own, other):
        lanes = pl.ds(pl.multiple_of(rblk[0] * width, BLOCK), width)
        for core, out in ((sblk[0], own), (1 - sblk[0], other)):
            spot = pl.multiple_of(core * half_rows + freq[0] * share, ROWS)
            out[...] = o_ref[pl.ds(spot, share), lanes]

    shape = jax.ShapeDtypeStruct((share, width), onset.dtype)
    return call(body, places, [(onset, whole(onset))], [(shape, whole(shape))] * 2, (1,))


def phase_tables(src, rcv, places, freq_devs, per_dev, samples, parts, rows):
    width = src[0].shape[1] // parts

    def fill(outs, value, to, freq):
        cosines, sines, fraction = outs
        value = value.astype(F32) * (1.0 / samples)
        fraction[:, to] = value
        for step, way in enumerate(ways(freq_devs)):
            for j in range(per_dev):
                order = ((freq[0] ^ way) * per_dev + j + 1).astype(F32)
                cosines[step, j, :, to], sines[step, j, :, to] = turned(value * order)

    def body(freq, _, sblk, own, other, r_ref, *outs):
        for part in range(parts):
            for spot, ref in enumerate((own, other)):
                at = (part * 2 + spot) * width
                fill(outs[:3], ref[:, part * width : (part + 1) * width], slice(at, at + width), freq)
        value = r_ref[pl.ds(pl.multiple_of(sblk[0] * rows, ROWS), rows), :]
        fill(outs[3:], value, slice(0, value.shape[1]), freq)

    shapes = []
    for count, total in ((src[0].shape[0], 2 * src[0].shape[1]), (rows, rcv.shape[1])):
        table = jax.ShapeDtypeStruct((freq_devs, per_dev, count, total), F32)
        shapes += [table, table, jax.ShapeDtypeStruct(table.shape[2:], F32)]
    outs = call(body, places, [(v, whole(v)) for v in (*src, rcv)], [(v, whole(v)) for v in shapes], (1,))
    return tuple(outs[:3]), tuple(outs[3:])


def down_products(before, spectra, parts, side, first, freq_place, freq_devs=0):
    _, per_dev, _, rcv = spectra[0].shape
    rows = sum(v.shape[2] for v in spectra)
    flat = [pair[side] for part in parts for pair in part]
    width = flat[0].shape[1]
    total_width = before.shape[-1] if before is not None else first + width * len(flat)
    share = rows // freq_devs if freq_devs else 0
    old = [] if before is None else [before]

    def body(place_ref, *rest):
        held_ref, rest = (rest[0], rest[1:]) if old else (None, rest)
        refs, resp, outs = rest[: len(spectra)], rest[len(spectra) : len(spectra) + len(flat)], rest[len(spectra) + len(flat) :]
        held = outs[-1]
        for j in range(per_dev):
            real = jnp.concatenate([ref[0, j] for ref in refs], 0)
            imag = jnp.concatenate([ref[1, j] for ref in refs], 0)
            lhs = jnp.concatenate([jnp.concatenate([real, -imag], 1), jnp.concatenate([imag, real], 1)], 0)
            for at, ref in enumerate(resp):
                total = lax.dot_general(lhs, ref[j], (((1,), (1,)), ((), ())), preferred_element_type=F32)
                to = slice(first + at * width, first + (at + 1) * width)
                for part in range(2):
                    value = total[part * rows : (part + 1) * rows]
                    held[part, j, :, to] = value + held_ref[part, j, :, to] if old else value
        if old:
            for to in (slice(0, first), slice(first + len(flat) * width, total_width)):
                if to.start < to.stop:
                    held[:, :, :, to] = held_ref[:, :, :, to]
        if freq_devs:
            for way, out in zip(ways(freq_devs), outs):
                start = pl.multiple_of((place_ref[0] ^ way) * share, share)
                out[...] = held[:, :, pl.ds(start, share), :].reshape(out.shape).astype(BF16)

    sums = (2, per_dev, rows, total_width)
    if freq_devs:
        shapes = [jax.ShapeDtypeStruct((2 * per_dev * share, total_width), BF16)] * freq_devs
    else:
        shapes = [jax.ShapeDtypeStruct(sums, F32)]
    outs = call(
        body,
        (freq_place,),
        [(v, whole(v)) for v in (*old, *spectra, *flat)],
        [(v, whole(v)) for v in shapes],
        (1,),
        scratch=[pltpu.VMEM(sums, F32)] if freq_devs else [],
        flops=2 * 4 * per_dev * rows * len(flat) * width * rcv,
    )
    return outs if freq_devs else outs[0]


def mixed_fields(plain, cos, sin, matrix):
    tile = plain[0].shape[-1]
    turned = [
        jnp.stack([v[0] * c - v[1] * s, v[0] * s + v[1] * c]) for v, c, s in zip(plain, cos, sin)
    ]
    flat = [jnp.stack(v).reshape(matrix.shape[1], tile).astype(BF16) for v in (turned, plain)]
    mixed = jnp.dot(matrix, jnp.concatenate(flat, 1), preferred_element_type=F32)
    shape = (-1, 2) + plain[0].shape[1:]
    return mixed[:, :tile].reshape(shape), mixed[:, tile:].reshape(shape)


def unturned(up, low, value, cos, sin, part):
    real = cos * up[0] + sin * up[1] - low[0] + part * value[0]
    imag = cos * up[1] - sin * up[0] - low[1] + part * value[1]
    return jnp.stack([real, imag])


def tiles(width, body):
    def at(step, carry):
        body(pl.ds(pl.multiple_of(step * BLOCK, BLOCK), BLOCK))
        return carry

    lax.fori_loop(0, width // BLOCK, at, 0, unroll=2)


def windowed(messages, tables, matrix, freq_place, per_dev, share):
    cosines, sines, fraction = tables
    freq_devs = len(messages)
    width = messages[0].shape[-1]
    count = freq_devs * 2 * per_dev * ROWS

    def body(place_ref, c_ref, s_ref, f_ref, g_ref, *rest):
        refs, outs = rest[:freq_devs], rest[freq_devs:]
        matrix_here = g_ref[place_ref[0]]

        def one(at):
            data = [ref[:, at].astype(F32).reshape(2, per_dev, share, BLOCK) for ref in refs]
            made = [[] for _ in outs]
            for first in range(0, share, ROWS):
                cut = slice(first, first + ROWS)
                plain = [value[:, :, cut] for value in data]
                cos = [c_ref[step, :, cut, at] for step in range(freq_devs)]
                sin = [s_ref[step, :, cut, at] for step in range(freq_devs)]
                up, low = mixed_fields(plain, cos, sin, matrix_here)
                part = f_ref[cut, at]
                for step in range(freq_devs):
                    made[step].append(unturned(up[step], low[step], plain[step], cos[step], sin[step], part))
            for out, value in zip(outs, made):
                out[:, at] = jnp.concatenate(value, 2).reshape(out.shape[0], BLOCK).astype(BF16)

        tiles(width, one)

    inputs = (cosines, sines, fraction, matrix, *messages)
    return call(
        body,
        (freq_place,),
        [(v, whole(v)) for v in inputs],
        [(jax.ShapeDtypeStruct(v.shape, BF16), whole(v)) for v in messages],
        (1,),
        flops=2 * count * count * 2 * width * share // ROWS,
    )


def up_products(messages, parts, freq_place, rows, side):
    freq_devs = len(messages)
    flat = [pair[side] for part in parts for pair in part]
    per_dev, src, rcv = flat[0].shape[0], flat[0].shape[1], flat[0].shape[2] // 2
    group = rows // CHUNKS
    share = rows // freq_devs
    total_width = src * len(flat)
    kind = BF16 if side else F32

    def body(place_ref, *rest):
        resp, refs = rest[: len(flat)], rest[len(flat) : len(flat) + freq_devs]
        outs, held = rest[len(flat) + freq_devs : -1], rest[-1]
        for way, ref in zip(ways(freq_devs), refs):
            start = pl.multiple_of((place_ref[0] ^ way) * share, share)
            value = ref[...].reshape(2, per_dev, share, total_width)
            for part in range(2):
                for j in range(per_dev):
                    held[part, j, pl.ds(start, share), :] = value[part, j]
        for j in range(per_dev):
            both = jnp.concatenate([held[0, j], held[1, j]], 0)
            total = sum(
                jnp.dot(both[:, at * src : (at + 1) * src], ref[j], preferred_element_type=F32)
                for at, ref in enumerate(resp)
            )
            real = total[:rows, :rcv] + total[rows:, rcv:]
            imag = total[rows:, :rcv] - total[:rows, rcv:]
            for index, out in enumerate(outs):
                cut = slice(index * group, (index + 1) * group)
                out[0, j] = real[cut].astype(kind)
                out[1, j] = imag[cut].astype(kind)

    shape = jax.ShapeDtypeStruct((2, per_dev, group, rcv), kind)
    return call(
        body,
        (freq_place,),
        [(v, whole(v)) for v in (*flat, *messages)],
        [(shape, whole(shape))] * CHUNKS,
        (1,),
        scratch=[pltpu.VMEM((2, per_dev, rows, total_width), BF16)],
        flops=2 * 4 * per_dev * rows * total_width * rcv,
    )


def next_spectra(sums, messages, tables, matrix, freq_place, first_row):
    cosines, sines, fraction = tables
    freq_devs = len(messages)
    _, per_dev, rows, rcv = messages[0].shape
    count = freq_devs * 2 * per_dev * ROWS
    own = 2 * per_dev * ROWS

    def body(place_ref, u_ref, c_ref, s_ref, f_ref, g_ref, *rest):
        refs, out = rest[:freq_devs], rest[freq_devs]
        matrix_here = g_ref[place_ref[0], :own]

        def one(at):
            for base in range(0, rows, 2 * ROWS):
                pair = slice(base, base + 2 * ROWS)
                data = [ref[:, :, pair, at].astype(F32) for ref in refs]
                made = []
                for half in range(2):
                    plain = [value[:, :, half * ROWS : (half + 1) * ROWS] for value in data]
                    cut = slice(first_row + base + half * ROWS, first_row + base + (half + 1) * ROWS)
                    cos = [c_ref[step, :, cut, at] for step in range(freq_devs)]
                    sin = [s_ref[step, :, cut, at] for step in range(freq_devs)]
                    up, low = mixed_fields(plain, cos, sin, matrix_here)
                    change = unturned(up[0], low[0], plain[0], cos[0], sin[0], f_ref[cut, at])
                    made.append(u_ref[:, :, cut, at] - change)
                out[:, :, pair, at] = jnp.concatenate(made, 2).astype(BF16)

        tiles(rcv, one)

    inputs = (sums, cosines, sines, fraction, matrix, *messages)
    shape = jax.ShapeDtypeStruct(messages[0].shape, BF16)
    (out,) = call(
        body,
        (freq_place,),
        [(v, whole(v)) for v in inputs],
        [(shape, whole(shape))],
        (1,),
        flops=2 * own * count * 2 * rcv * rows // ROWS,
    )
    return out


def updated(initial, onset, messages, table, places, first, rows, target):
    freq_devs = len(messages)
    half_rows, own, rcv = initial.shape
    per_dev = messages[0].shape[1]
    tile = 2 * ROWS
    count = table.shape[2]

    def body(place_ref, _, sblk, x_ref, o_ref, t_ref, *rest):
        refs = rest[:freq_devs]
        out, spread_ref = rest[-2:]
        step = pl.program_id(0)

        @pl.when(step == 0)
        def _():
            base = t_ref[place_ref[0]].astype(F32)
            lane = lax.broadcasted_iota(jnp.int32, (own, count), 1) % ROWS
            for row in range(ROWS):
                spread_ref[row * own : (row + 1) * own] = jnp.where(lane == row, base, 0.0).astype(BF16)

        here = pl.ds(pl.multiple_of(step * tile, tile), tile)
        data = [ref[:, :, here, :].astype(F32) for ref in refs]
        onsets = o_ref[pl.ds(pl.multiple_of(sblk[0] * half_rows + first + step * tile, tile), tile), :]
        time = lax.broadcasted_iota(jnp.int32, (own, rcv), 0) + place_ref[0] * own
        for half in range(2):
            cut = slice(half * ROWS, (half + 1) * ROWS)
            flat = jnp.stack([v[:, :, cut] for v in data]).reshape(count, rcv).astype(BF16)
            change = jnp.dot(spread_ref[...], flat, preferred_element_type=F32)
            for row in range(ROWS):
                spot = half * ROWS + row
                on = time < onsets[spot : spot + 1, :]
                moved = jnp.where(on, change[row * own : (row + 1) * own], 0.0)
                out[spot] = (x_ref[first + step * tile + spot].astype(F32) - moved).astype(BF16)

    inputs = [(v, whole(v)) for v in (initial, onset, table, *messages)]
    aliases = {}
    if target is not None:
        inputs.append((target, pl.BlockSpec(memory_space=pl.ANY)))
        aliases = {len(places) + len(inputs) - 1: 0}
    (out,) = call(
        body,
        places,
        inputs,
        [(jax.ShapeDtypeStruct(initial.shape, BF16), pl.BlockSpec((tile, own, rcv), lambda i, *_: (first // tile + i, 0, 0)))],
        (rows // tile,),
        scratch=[pltpu.VMEM((ROWS * own, count), BF16)],
        aliases=aliases,
        flops=2 * 2 * freq_devs * per_dev * own * rows * rcv,
    )
    return out


def exchanged(value, axis, step):
    return lax.ppermute(value, axis, [(i, i ^ step) for i in range(lax.axis_size(axis))])


def dealt_out(parts):
    return [exchanged(part, "freq", step) if step else part for part, step in zip(parts, ways(len(parts)))]


def spread(value, count):
    held = {0: value}
    bit = count // 2
    while bit:
        held.update({way | bit: exchanged(held[way], "freq", bit) for way in sorted(held)})
        bit //= 2
    return [held[way] for way in ways(count)]


def on_device(initial, response, aperture, onset_rcv, onset_src):
    freq_devs = lax.axis_size("freq")
    per_dev = response.shape[0]
    samples = initial.shape[1] * freq_devs
    half_rows = initial.shape[0]
    src_width = response.shape[2] // 2
    rows = half_rows // CHUNKS
    share = half_rows // freq_devs
    places = tuple(lax.axis_index(axis).reshape(1) for axis in ("freq", "rblk", "sblk"))
    freq_place = places[0]
    inverse = jnp.asarray(inverse_tables(samples, freq_devs, per_dev))
    matrix = jnp.asarray(window_tables(samples, freq_devs, per_dev))

    kept, sent = masked_halves(response, aperture, places)
    moved = [exchanged(v, "rblk", 1) for v in sent]
    kept_pair = [exchanged(v, "sblk", 1) for v in kept]
    sums, spectra = summed(dealt_out(first_spectra(initial, places, freq_devs, per_dev)))
    far = exchanged(spectra, "rblk", 1)
    moved_pair = []
    for index in range(PARTS):
        if index:
            moved[index], far = lax.optimization_barrier((moved[index], far))
        else:
            moved[index], spectra = lax.optimization_barrier((moved[index], spectra))
        moved_pair.append(exchanged(moved[index], "sblk", 1))
    parts = [((kept[i], moved[i]), (kept_pair[i], moved_pair[i])) for i in range(PARTS)]

    own, other = src_onsets(onset_src, places, half_rows, share, src_width)
    onsets = (own, exchanged(other, "sblk", 1))
    src_tables, rcv_tables = phase_tables(onsets, onset_rcv, places, freq_devs, per_dev, samples, PARTS, half_rows)

    near, far, result = [spectra], [far], None
    for step in range(ITERS):
        held = down_products(None, near, parts, 0, 0, freq_place)
        at = 0 if step else PARTS - 1
        if at:
            held = down_products(held, far, parts[:at], 1, 0, freq_place)
        first = at * 2 * kept[0].shape[1]
        messages = dealt_out(down_products(held, far, parts[at:], 1, first, freq_place, freq_devs))
        messages = dealt_out(windowed(messages, src_tables, matrix, freq_place, per_dev, share))
        received = [exchanged(v, "rblk", 1) for v in up_products(messages, parts, freq_place, half_rows, 1)]
        keep = up_products(messages, parts, freq_place, half_rows, 0)
        near, far = [], []
        for chunk in range(CHUNKS):
            back = spread(added(keep[chunk], received[chunk]), freq_devs)
            if step < ITERS - 1:
                near.append(next_spectra(sums, back, rcv_tables, matrix, freq_place, chunk * rows))
                far.append(exchanged(near[chunk], "rblk", 1))
            else:
                result = updated(initial, onset_rcv, back, inverse, places, chunk * rows, rows, result)
    return result


def transform_tables(length, count):
    table = fields(length, count).reshape(2 * count, length)
    forward_table = jnp.asarray(table.astype(np.float32).astype(BF16))
    inverse_table = jnp.asarray((table.T * (2.0 / length)).astype(np.float32).astype(BF16))
    return forward_table, inverse_table


def settle(values):
    return lax.optimization_barrier(values.astype(BF16)).astype(F32)


def samples_into_spectra(values, forward_table, freq_total):
    out = jnp.einsum("kt,ptn->pkn", forward_table, values, preferred_element_type=F32)
    return out.reshape(values.shape[0], 2, freq_total, values.shape[2]).astype(BF16)


def spectra_into_samples(trace_spectra, inverse_table):
    flat = trace_spectra.reshape(trace_spectra.shape[0], -1, trace_spectra.shape[3])
    return jnp.einsum("tk,pkn->ptn", inverse_table, flat, preferred_element_type=F32)


def dense(spec, gated, real, imag, sign):
    dot = functools.partial(jnp.einsum, spec, preferred_element_type=F32)
    return jnp.stack(
        [dot(gated[:, 0], real) - sign * dot(gated[:, 1], imag), dot(gated[:, 0], imag) + sign * dot(gated[:, 1], real)], 1
    )


def general_device(initial, response, aperture, onset_rcv, onset_src):
    freq_devs, rblk_devs, sblk_devs = (lax.axis_size(a) for a in ("freq", "rblk", "sblk"))
    freq_index, rblk_index, sblk_index = (lax.axis_index(a) for a in ("freq", "rblk", "sblk"))
    freq_total = response.shape[0] * freq_devs
    samples = initial.shape[1] * freq_devs
    focal_all = onset_rcv.shape[0]
    forward_table, inverse_table = transform_tables(samples, freq_total)
    steps_axis = lax.iota(jnp.int32, samples)
    own_axis = freq_index * initial.shape[1] + lax.iota(jnp.int32, initial.shape[1])
    half_rows = focal_all // sblk_devs
    own_onsets = lax.dynamic_slice_in_dim(onset_rcv, sblk_index * half_rows, half_rows, 0)
    rcv_gate = (own_axis[None, :, None] < own_onsets[:, None, :]).astype(F32)
    src_rows = focal_all // (rblk_devs * freq_devs)
    src_first = rblk_index * (focal_all // rblk_devs) + freq_index * src_rows
    src_onsets = lax.dynamic_slice_in_dim(onset_src, src_first, src_rows, 0)
    src_gate = (steps_axis[None, :, None] < src_onsets[:, None, :]).astype(F32)
    mask_full = jnp.repeat(jnp.repeat(aperture, BLOCK, 1), BLOCK, 2).astype(BF16)
    gated = response * mask_full[:, None]
    own_forward = lax.dynamic_slice_in_dim(forward_table, freq_index * initial.shape[1], initial.shape[1], 1)
    own_inverse = lax.dynamic_slice_in_dim(inverse_table, freq_index * initial.shape[1], initial.shape[1], 0)
    current = initial
    for _ in range(ITERS):
        partial = samples_into_spectra(current, own_forward, freq_total)
        spec_back = lax.psum_scatter(partial.astype(F32), "freq", scatter_dimension=2, tiled=True).astype(BF16)
        spec_all = lax.all_gather(spec_back, "sblk", axis=0, tiled=True)
        down = lax.psum_scatter(
            settle(dense("euk,bek->beu", gated, spec_all[:, 0], spec_all[:, 1], 1.0)).astype(BF16),
            "rblk",
            scatter_dimension=0,
            tiled=True,
        )
        src_traces = lax.all_to_all(down, "freq", split_axis=0, concat_axis=2, tiled=True)
        upgoing = (src_gate * spectra_into_samples(src_traces, inverse_table)).astype(BF16)
        upspec = samples_into_spectra(upgoing, forward_table, freq_total)
        up_back = lax.all_to_all(upspec, "freq", split_axis=2, concat_axis=0, tiled=True)
        up_all = lax.all_gather(up_back, "rblk", axis=0, tiled=True)
        sums = dense("qao,bqa->bqo", gated, up_all[:, 0], up_all[:, 1], -1.0).astype(BF16)
        back = lax.psum_scatter(sums, "sblk", scatter_dimension=0, tiled=True)
        traces = lax.all_gather(back, "freq", axis=2, tiled=True)
        update = rcv_gate * spectra_into_samples(traces, own_inverse)
        current = (initial.astype(F32) - update).astype(BF16)
    return current


def fits(initial, response, aperture, onset_rcv, onset_src):
    freq_devs = lax.axis_size("freq")
    if lax.axis_size("rblk") != 2 or lax.axis_size("sblk") != 2 or freq_devs & (freq_devs - 1):
        return False
    whole_rows = initial.shape[0] % (max(2, CHUNKS) * ROWS * freq_devs) == 0
    whole_width = response.shape[2] % (2 * PARTS * BLOCK) == 0 and response.shape[3] % BLOCK == 0
    return whole_rows and whole_width and onset_rcv.shape[0] == 2 * initial.shape[0]


def chosen(*arrays):
    return on_device(*arrays) if fits(*arrays) else general_device(*arrays)


def solution(mesh):
    in_specs = (
        P(("group", "sblk"), "freq", "rblk"),
        P(("group", "freq"), None, "sblk", "rblk"),
        P(("group", "freq"), "sblk", "rblk"),
        P("group", "rblk"),
        P("group", "sblk"),
    )
    out_specs = P(("group", "sblk"), "freq", "rblk")
    return jax.shard_map(chosen, mesh=mesh, in_specs=in_specs, out_specs=out_specs, check_vma=False)
```

```python
import functools
import math

import jax
import jax.numpy as jnp
import numpy as np
from jax import lax
from jax.experimental import pallas as pl
from jax.experimental.pallas import tpu as pltpu
from jax.sharding import PartitionSpec as P

BLOCK = 128
ITERS = 2
ROWS = 8
CHUNKS = 2
PARTS = 2
VMEM_BYTES = 6 * 1024 * 1024

BF16 = jnp.bfloat16
F32 = jnp.float32


def ways(count):
    far = sorted(range(1, count), key=lambda step: (step.bit_length() < count.bit_length() - 1, step))
    return [0] + far


def field_rows(place, freq_devs, per_dev):
    rows = []
    for step in ways(freq_devs):
        first = (place ^ step) * per_dev
        for part in range(2):
            rows.extend((part, first + local) for local in range(per_dev))
    return rows


def fields(samples, freq_total):
    phase = (np.arange(1, freq_total + 1)[:, None] * np.arange(samples)[None, :]) % samples
    angle = phase * (2.0 * math.pi / samples)
    return np.stack([np.cos(angle), -np.sin(angle)])


def inverse_tables(samples, freq_devs, per_dev):
    exact = fields(samples, freq_devs * per_dev) * (2.0 / samples)
    own = samples // freq_devs
    out = []
    for place in range(freq_devs):
        part = [exact[c, j, place * own : (place + 1) * own] for c, j in field_rows(place, freq_devs, per_dev)]
        out.append(np.repeat(np.stack(part), ROWS, 0).T)
    return np.stack(out).astype(np.float32).astype(BF16)


def window_tables(samples, freq_devs, per_dev):
    freq_total = freq_devs * per_dev
    order = np.arange(1, freq_total + 1)
    unit = 2j * math.pi / samples
    diff = order[None, :] - order[:, None]
    total = order[None, :] + order[:, None]
    same = np.where(diff == 0, 0.0, 1.0 / (samples * (np.exp(unit * np.where(diff == 0, 1, diff)) - 1.0)))
    mixed = 1.0 / (samples * (np.exp(-unit * total) - 1.0))
    full = np.zeros((2, freq_total, 2, freq_total))
    full[0, :, 0, :] = same.real + mixed.real
    full[0, :, 1, :] = mixed.imag - same.imag
    full[1, :, 0, :] = same.imag + mixed.imag
    full[1, :, 1, :] = same.real - mixed.real
    out = []
    for place in range(freq_devs):
        rows = [c * freq_total + j for c, j in field_rows(place, freq_devs, per_dev)]
        flat = full.reshape(2 * freq_total, 2 * freq_total)[np.ix_(rows, rows)]
        out.append(np.kron(flat, np.eye(ROWS)))
    return np.stack(out).astype(np.float32).astype(BF16)


def call(body, scalars, inputs, outputs, grid, scratch=(), aliases=None, flops=0):
    in_arrays = [value for value, _ in inputs]
    bytes_all = sum(v.size * v.dtype.itemsize for v in in_arrays)
    bytes_all += sum(math.prod(s.shape) * s.dtype.itemsize for s, _ in outputs)
    return pl.pallas_call(
        body,
        grid_spec=pltpu.PrefetchScalarGridSpec(
            num_scalar_prefetch=len(scalars),
            grid=grid,
            in_specs=[spec for _, spec in inputs],
            out_specs=[spec for _, spec in outputs],
            scratch_shapes=list(scratch),
        ),
        out_shape=[shape for shape, _ in outputs],
        input_output_aliases=aliases or {},
        compiler_params=pltpu.CompilerParams(vmem_limit_bytes=VMEM_BYTES),
        cost_estimate=pl.CostEstimate(flops=flops, bytes_accessed=bytes_all, transcendentals=0),
    )(*scalars, *in_arrays)


def whole(array):
    zeros = (0,) * array.ndim
    return pl.BlockSpec(array.shape, lambda *_: zeros)


def sine_terms():
    square = (np.cos(np.linspace(0.0, math.pi, 200)) + 1.0) / 32.0
    y = np.sqrt(np.maximum(square, 1e-12))
    return [float(v) for v in np.polynomial.polynomial.polyfit(square, np.sin(2.0 * math.pi * y) / y, 6)]


def turned(turn):
    terms = sine_terms()

    def sine(y):
        square = y * y
        total = jnp.full_like(y, terms[-1])
        for term in terms[-2::-1]:
            total = total * square + term
        return total * y

    turn = turn - jnp.floor(turn + 0.5)
    size = jnp.abs(turn)
    folded = jnp.where(size > 0.25, jnp.where(turn > 0.0, 0.5, -0.5) - turn, turn)
    return sine(0.25 - size), sine(folded)


def first_spectra(initial, places, freq_devs, per_dev):
    rows, own, rcv = initial.shape
    samples = own * freq_devs
    tile = 2 * ROWS
    count = freq_devs * 2 * per_dev * ROWS

    def body(freq, rblk, sblk, x_ref, *rest):
        outs, spread_ref = rest[:freq_devs], rest[freq_devs]
        time = lax.broadcasted_iota(jnp.int32, (ROWS, own), 1) + freq[0] * own
        time = time.astype(F32) * (1.0 / samples)
        table = []
        for way in ways(freq_devs):
            waves = [turned(time * ((freq[0] ^ way) * per_dev + j + 1).astype(F32)) for j in range(per_dev)]
            table += [cosine for cosine, _ in waves] + [-sine for _, sine in waves]
        table = jnp.concatenate(table, 0)
        lane = lax.broadcasted_iota(jnp.int32, (count, own), 0) % ROWS
        for row in range(ROWS):
            spread_ref[:, row * own : (row + 1) * own] = jnp.where(lane == row, table, 0.0).astype(BF16)
        for at in range(rows // tile):
            parts = []
            for half in range(2):
                start = at * tile + half * ROWS
                flat = x_ref[start : start + ROWS].reshape(ROWS * own, rcv)
                value = jnp.dot(spread_ref[...], flat, preferred_element_type=F32)
                parts.append(value.reshape(freq_devs, 2, per_dev, ROWS, rcv))
            both = jnp.concatenate(parts, 3).astype(BF16)
            for step, out in enumerate(outs):
                out[:, :, at * tile : (at + 1) * tile, :] = both[step]

    shape = jax.ShapeDtypeStruct((2, per_dev, rows, rcv), BF16)
    return call(
        body,
        places,
        [(initial, whole(initial))],
        [(shape, whole(shape))] * freq_devs,
        (1,),
        scratch=[pltpu.VMEM((count, ROWS * own), BF16)],
        flops=2 * 2 * freq_devs * per_dev * own * rows * rcv,
    )


def masked_halves(response, aperture, places):
    per_dev, _, src, rcv = response.shape
    half = src // 2
    width = half // PARTS

    def body(_, rblk, __, flags, x_ref, *outs):
        lane = lax.broadcasted_iota(jnp.int32, (1, rcv), 1) // BLOCK
        for flip in (1, 0):
            for j in range(per_dev):
                for step in range(half // BLOCK):
                    block = (rblk[0] ^ flip) * (half // BLOCK) + step
                    on = flags[j, pl.ds(block, 1), :].astype(F32)
                    row = sum(jnp.where(lane == r, on[:, r : r + 1], 0.0) for r in range(rcv // BLOCK))
                    gate = jnp.broadcast_to(row, (BLOCK, rcv)).astype(BF16)
                    rows = pl.ds(pl.multiple_of(block * BLOCK, BLOCK), BLOCK)
                    part, at = divmod(step * BLOCK, width)
                    out = outs[flip * PARTS + part]
                    for c in range(2):
                        out[j, at : at + BLOCK, c * rcv : (c + 1) * rcv] = x_ref[j, c, rows, :] * gate

    shape = jax.ShapeDtypeStruct((per_dev, width, 2 * rcv), BF16)
    inputs = [(v, whole(v)) for v in (aperture, response)]
    outs = call(body, places, inputs, [(shape, whole(shape))] * (2 * PARTS), (1,))
    return list(outs[:PARTS]), list(outs[PARTS:])


def summed(parts):
    def body(*refs):
        total = sum(ref[...].astype(F32) for ref in refs[:-2])
        refs[-2][...] = total
        refs[-1][...] = total.astype(BF16)

    shapes = [jax.ShapeDtypeStruct(parts[0].shape, kind) for kind in (F32, BF16)]
    return call(body, (), [(v, whole(v)) for v in parts], [(v, whole(v)) for v in shapes], (1,))


def added(keep, received):
    def body(k_ref, r_ref, out):
        out[...] = (k_ref[...] + r_ref[...].astype(F32)).astype(BF16)

    shape = jax.ShapeDtypeStruct(keep.shape, BF16)
    (out,) = call(body, (), [(v, whole(v)) for v in (keep, received)], [(shape, whole(shape))], (1,))
    return out


def src_onsets(onset, places, half_rows, share, width):

    def body(freq, rblk, sblk, o_ref, own, other):
        lanes = pl.ds(pl.multiple_of(rblk[0] * width, BLOCK), width)
        for core, out in ((sblk[0], own), (1 - sblk[0], other)):
            spot = pl.multiple_of(core * half_rows + freq[0] * share, ROWS)
            out[...] = o_ref[pl.ds(spot, share), lanes]

    shape = jax.ShapeDtypeStruct((share, width), onset.dtype)
    return call(body, places, [(onset, whole(onset))], [(shape, whole(shape))] * 2, (1,))


def phase_tables(src, rcv, places, freq_devs, per_dev, samples, parts, rows):
    width = src[0].shape[1] // parts

    def fill(outs, value, to, freq):
        cosines, sines, fraction = outs
        value = value.astype(F32) * (1.0 / samples)
        fraction[:, to] = value
        for step, way in enumerate(ways(freq_devs)):
            for j in range(per_dev):
                order = ((freq[0] ^ way) * per_dev + j + 1).astype(F32)
                cosines[step, j, :, to], sines[step, j, :, to] = turned(value * order)

    def body(freq, _, sblk, own, other, r_ref, *outs):
        for part in range(parts):
            for spot, ref in enumerate((own, other)):
                at = (part * 2 + spot) * width
                fill(outs[:3], ref[:, part * width : (part + 1) * width], slice(at, at + width), freq)
        value = r_ref[pl.ds(pl.multiple_of(sblk[0] * rows, ROWS), rows), :]
        fill(outs[3:], value, slice(0, value.shape[1]), freq)

    shapes = []
    for count, total in ((src[0].shape[0], 2 * src[0].shape[1]), (rows, rcv.shape[1])):
        table = jax.ShapeDtypeStruct((freq_devs, per_dev, count, total), F32)
        shapes += [table, table, jax.ShapeDtypeStruct(table.shape[2:], F32)]
    outs = call(body, places, [(v, whole(v)) for v in (*src, rcv)], [(v, whole(v)) for v in shapes], (1,))
    return tuple(outs[:3]), tuple(outs[3:])


def down_products(before, spectra, parts, side, first, freq_place, freq_devs=0):
    _, per_dev, _, rcv = spectra[0].shape
    rows = sum(v.shape[2] for v in spectra)
    flat = [pair[side] for part in parts for pair in part]
    width = flat[0].shape[1]
    total_width = before.shape[-1] if before is not None else first + width * len(flat)
    share = rows // freq_devs if freq_devs else 0
    old = [] if before is None else [before]

    def body(place_ref, *rest):
        held_ref, rest = (rest[0], rest[1:]) if old else (None, rest)
        refs, resp, outs = rest[: len(spectra)], rest[len(spectra) : len(spectra) + len(flat)], rest[len(spectra) + len(flat) :]
        held = outs[-1]
        for j in range(per_dev):
            real = jnp.concatenate([ref[0, j] for ref in refs], 0)
            imag = jnp.concatenate([ref[1, j] for ref in refs], 0)
            lhs = jnp.concatenate([jnp.concatenate([real, -imag], 1), jnp.concatenate([imag, real], 1)], 0)
            for at, ref in enumerate(resp):
                total = lax.dot_general(lhs, ref[j], (((1,), (1,)), ((), ())), preferred_element_type=F32)
                to = slice(first + at * width, first + (at + 1) * width)
                for part in range(2):
                    value = total[part * rows : (part + 1) * rows]
                    held[part, j, :, to] = value + held_ref[part, j, :, to] if old else value
        if old:
            for to in (slice(0, first), slice(first + len(flat) * width, total_width)):
                if to.start < to.stop:
                    held[:, :, :, to] = held_ref[:, :, :, to]
        if freq_devs:
            for way, out in zip(ways(freq_devs), outs):
                start = pl.multiple_of((place_ref[0] ^ way) * share, share)
                out[...] = held[:, :, pl.ds(start, share), :].reshape(out.shape).astype(BF16)

    sums = (2, per_dev, rows, total_width)
    if freq_devs:
        shapes = [jax.ShapeDtypeStruct((2 * per_dev * share, total_width), BF16)] * freq_devs
    else:
        shapes = [jax.ShapeDtypeStruct(sums, F32)]
    outs = call(
        body,
        (freq_place,),
        [(v, whole(v)) for v in (*old, *spectra, *flat)],
        [(v, whole(v)) for v in shapes],
        (1,),
        scratch=[pltpu.VMEM(sums, F32)] if freq_devs else [],
        flops=2 * 4 * per_dev * rows * len(flat) * width * rcv,
    )
    return outs if freq_devs else outs[0]


def mixed_fields(plain, cos, sin, matrix):
    tile = plain[0].shape[-1]
    turned = [
        jnp.stack([v[0] * c - v[1] * s, v[0] * s + v[1] * c]) for v, c, s in zip(plain, cos, sin)
    ]
    flat = [jnp.stack(v).reshape(matrix.shape[1], tile).astype(BF16) for v in (turned, plain)]
    mixed = jnp.dot(matrix, jnp.concatenate(flat, 1), preferred_element_type=F32)
    shape = (-1, 2) + plain[0].shape[1:]
    return mixed[:, :tile].reshape(shape), mixed[:, tile:].reshape(shape)


def unturned(up, low, value, cos, sin, part):
    real = cos * up[0] + sin * up[1] - low[0] + part * value[0]
    imag = cos * up[1] - sin * up[0] - low[1] + part * value[1]
    return jnp.stack([real, imag])


def tiles(width, body):
    def at(step, carry):
        body(pl.ds(pl.multiple_of(step * BLOCK, BLOCK), BLOCK))
        return carry

    lax.fori_loop(0, width // BLOCK, at, 0, unroll=2)


def windowed(messages, tables, matrix, freq_place, per_dev, share):
    cosines, sines, fraction = tables
    freq_devs = len(messages)
    width = messages[0].shape[-1]
    count = freq_devs * 2 * per_dev * ROWS

    def body(place_ref, c_ref, s_ref, f_ref, g_ref, *rest):
        refs, outs = rest[:freq_devs], rest[freq_devs:]
        matrix_here = g_ref[place_ref[0]]

        def one(at):
            data = [ref[:, at].astype(F32).reshape(2, per_dev, share, BLOCK) for ref in refs]
            made = [[] for _ in outs]
            for first in range(0, share, ROWS):
                cut = slice(first, first + ROWS)
                plain = [value[:, :, cut] for value in data]
                cos = [c_ref[step, :, cut, at] for step in range(freq_devs)]
                sin = [s_ref[step, :, cut, at] for step in range(freq_devs)]
                up, low = mixed_fields(plain, cos, sin, matrix_here)
                part = f_ref[cut, at]
                for step in range(freq_devs):
                    made[step].append(unturned(up[step], low[step], plain[step], cos[step], sin[step], part))
            for out, value in zip(outs, made):
                out[:, at] = jnp.concatenate(value, 2).reshape(out.shape[0], BLOCK).astype(BF16)

        tiles(width, one)

    inputs = (cosines, sines, fraction, matrix, *messages)
    return call(
        body,
        (freq_place,),
        [(v, whole(v)) for v in inputs],
        [(jax.ShapeDtypeStruct(v.shape, BF16), whole(v)) for v in messages],
        (1,),
        flops=2 * count * count * 2 * width * share // ROWS,
    )


def up_products(messages, parts, freq_place, rows, side):
    freq_devs = len(messages)
    flat = [pair[side] for part in parts for pair in part]
    per_dev, src, rcv = flat[0].shape[0], flat[0].shape[1], flat[0].shape[2] // 2
    group = rows // CHUNKS
    share = rows // freq_devs
    total_width = src * len(flat)
    kind = BF16 if side else F32

    def body(place_ref, *rest):
        resp, refs = rest[: len(flat)], rest[len(flat) : len(flat) + freq_devs]
        outs, held = rest[len(flat) + freq_devs : -1], rest[-1]
        for way, ref in zip(ways(freq_devs), refs):
            start = pl.multiple_of((place_ref[0] ^ way) * share, share)
            value = ref[...].reshape(2, per_dev, share, total_width)
            for part in range(2):
                for j in range(per_dev):
                    held[part, j, pl.ds(start, share), :] = value[part, j]
        for j in range(per_dev):
            both = jnp.concatenate([held[0, j], held[1, j]], 0)
            total = sum(
                jnp.dot(both[:, at * src : (at + 1) * src], ref[j], preferred_element_type=F32)
                for at, ref in enumerate(resp)
            )
            real = total[:rows, :rcv] + total[rows:, rcv:]
            imag = total[rows:, :rcv] - total[:rows, rcv:]
            for index, out in enumerate(outs):
                cut = slice(index * group, (index + 1) * group)
                out[0, j] = real[cut].astype(kind)
                out[1, j] = imag[cut].astype(kind)

    shape = jax.ShapeDtypeStruct((2, per_dev, group, rcv), kind)
    return call(
        body,
        (freq_place,),
        [(v, whole(v)) for v in (*flat, *messages)],
        [(shape, whole(shape))] * CHUNKS,
        (1,),
        scratch=[pltpu.VMEM((2, per_dev, rows, total_width), BF16)],
        flops=2 * 4 * per_dev * rows * total_width * rcv,
    )


def next_spectra(sums, messages, tables, matrix, freq_place, first_row):
    cosines, sines, fraction = tables
    freq_devs = len(messages)
    _, per_dev, rows, rcv = messages[0].shape
    count = freq_devs * 2 * per_dev * ROWS
    own = 2 * per_dev * ROWS

    def body(place_ref, u_ref, c_ref, s_ref, f_ref, g_ref, *rest):
        refs, out = rest[:freq_devs], rest[freq_devs]
        matrix_here = g_ref[place_ref[0], :own]

        def one(at):
            for base in range(0, rows, 2 * ROWS):
                pair = slice(base, base + 2 * ROWS)
                data = [ref[:, :, pair, at].astype(F32) for ref in refs]
                made = []
                for half in range(2):
                    plain = [value[:, :, half * ROWS : (half + 1) * ROWS] for value in data]
                    cut = slice(first_row + base + half * ROWS, first_row + base + (half + 1) * ROWS)
                    cos = [c_ref[step, :, cut, at] for step in range(freq_devs)]
                    sin = [s_ref[step, :, cut, at] for step in range(freq_devs)]
                    up, low = mixed_fields(plain, cos, sin, matrix_here)
                    change = unturned(up[0], low[0], plain[0], cos[0], sin[0], f_ref[cut, at])
                    made.append(u_ref[:, :, cut, at] - change)
                out[:, :, pair, at] = jnp.concatenate(made, 2).astype(BF16)

        tiles(rcv, one)

    inputs = (sums, cosines, sines, fraction, matrix, *messages)
    shape = jax.ShapeDtypeStruct(messages[0].shape, BF16)
    (out,) = call(
        body,
        (freq_place,),
        [(v, whole(v)) for v in inputs],
        [(shape, whole(shape))],
        (1,),
        flops=2 * own * count * 2 * rcv * rows // ROWS,
    )
    return out


def updated(initial, onset, messages, table, places, first, rows, target):
    freq_devs = len(messages)
    half_rows, own, rcv = initial.shape
    per_dev = messages[0].shape[1]
    tile = ROWS
    count = table.shape[2]

    def body(place_ref, _, sblk, x_ref, o_ref, t_ref, *rest):
        refs = rest[:freq_devs]
        out, spread_ref = rest[-2:]
        step = pl.program_id(0)

        @pl.when(step == 0)
        def _():
            base = t_ref[place_ref[0]].astype(F32)
            lane = lax.broadcasted_iota(jnp.int32, (own, count), 1) % ROWS
            for row in range(ROWS):
                spread_ref[row * own : (row + 1) * own] = jnp.where(lane == row, base, 0.0).astype(BF16)

        pair = pl.ds(pl.multiple_of(step // 2 * (2 * ROWS), 2 * ROWS), 2 * ROWS)
        data = [ref[:, :, pair, :].astype(F32) for ref in refs]
        data = [jnp.where(step % 2 == 0, v[:, :, :ROWS], v[:, :, ROWS:]) for v in data]
        onsets = o_ref[pl.ds(pl.multiple_of(sblk[0] * half_rows + first + step * tile, tile), tile), :]
        time = lax.broadcasted_iota(jnp.int32, (own, rcv), 0) + place_ref[0] * own
        flat = jnp.stack(data).reshape(count, rcv).astype(BF16)
        change = jnp.dot(spread_ref[...], flat, preferred_element_type=F32)
        for row in range(ROWS):
            on = time < onsets[row : row + 1, :]
            moved = jnp.where(on, change[row * own : (row + 1) * own], 0.0)
            out[row] = (x_ref[first + step * tile + row].astype(F32) - moved).astype(BF16)

    inputs = [(v, whole(v)) for v in (initial, onset, table, *messages)]
    aliases = {}
    if target is not None:
        inputs.append((target, pl.BlockSpec(memory_space=pl.ANY)))
        aliases = {len(places) + len(inputs) - 1: 0}
    (out,) = call(
        body,
        places,
        inputs,
        [(jax.ShapeDtypeStruct(initial.shape, BF16), pl.BlockSpec((tile, own, rcv), lambda i, *_: (first // tile + i, 0, 0)))],
        (rows // tile,),
        scratch=[pltpu.VMEM((ROWS * own, count), BF16)],
        aliases=aliases,
        flops=2 * 2 * freq_devs * per_dev * own * rows * rcv,
    )
    return out


def exchanged(value, axis, step):
    return lax.ppermute(value, axis, [(i, i ^ step) for i in range(lax.axis_size(axis))])


def dealt_out(parts):
    return [exchanged(part, "freq", step) if step else part for part, step in zip(parts, ways(len(parts)))]


def spread(value, count):
    held = {0: value}
    bit = count // 2
    while bit:
        held.update({way | bit: exchanged(held[way], "freq", bit) for way in sorted(held)})
        bit //= 2
    return [held[way] for way in ways(count)]


def on_device(initial, response, aperture, onset_rcv, onset_src):
    freq_devs = lax.axis_size("freq")
    per_dev = response.shape[0]
    samples = initial.shape[1] * freq_devs
    half_rows = initial.shape[0]
    src_width = response.shape[2] // 2
    rows = half_rows // CHUNKS
    share = half_rows // freq_devs
    places = tuple(lax.axis_index(axis).reshape(1) for axis in ("freq", "rblk", "sblk"))
    freq_place = places[0]
    inverse = jnp.asarray(inverse_tables(samples, freq_devs, per_dev))
    matrix = jnp.asarray(window_tables(samples, freq_devs, per_dev))

    kept, sent = masked_halves(response, aperture, places)
    moved = [exchanged(v, "rblk", 1) for v in sent]
    kept_pair = [exchanged(v, "sblk", 1) for v in kept]
    sums, spectra = summed(dealt_out(first_spectra(initial, places, freq_devs, per_dev)))
    far = exchanged(spectra, "rblk", 1)
    moved_pair = []
    for index in range(PARTS):
        if index:
            moved[index], far = lax.optimization_barrier((moved[index], far))
        else:
            moved[index], spectra = lax.optimization_barrier((moved[index], spectra))
        moved_pair.append(exchanged(moved[index], "sblk", 1))
    parts = [((kept[i], moved[i]), (kept_pair[i], moved_pair[i])) for i in range(PARTS)]

    own, other = src_onsets(onset_src, places, half_rows, share, src_width)
    onsets = (own, exchanged(other, "sblk", 1))
    src_tables, rcv_tables = phase_tables(onsets, onset_rcv, places, freq_devs, per_dev, samples, PARTS, half_rows)

    near, far, result = [spectra], [far], None
    for step in range(ITERS):
        held = down_products(None, near, parts, 0, 0, freq_place)
        at = 0 if step else PARTS - 1
        if at:
            held = down_products(held, far, parts[:at], 1, 0, freq_place)
        first = at * 2 * kept[0].shape[1]
        messages = dealt_out(down_products(held, far, parts[at:], 1, first, freq_place, freq_devs))
        messages = dealt_out(windowed(messages, src_tables, matrix, freq_place, per_dev, share))
        received = [exchanged(v, "rblk", 1) for v in up_products(messages, parts, freq_place, half_rows, 1)]
        keep = up_products(messages, parts, freq_place, half_rows, 0)
        near, far = [], []
        for chunk in range(CHUNKS):
            back = spread(added(keep[chunk], received[chunk]), freq_devs)
            if step < ITERS - 1:
                near.append(next_spectra(sums, back, rcv_tables, matrix, freq_place, chunk * rows))
                far.append(exchanged(near[chunk], "rblk", 1))
            else:
                result = updated(initial, onset_rcv, back, inverse, places, chunk * rows, rows, result)
    return result


def transform_tables(length, count):
    table = fields(length, count).reshape(2 * count, length)
    forward_table = jnp.asarray(table.astype(np.float32).astype(BF16))
    inverse_table = jnp.asarray((table.T * (2.0 / length)).astype(np.float32).astype(BF16))
    return forward_table, inverse_table


def settle(values):
    return lax.optimization_barrier(values.astype(BF16)).astype(F32)


def samples_into_spectra(values, forward_table, freq_total):
    out = jnp.einsum("kt,ptn->pkn", forward_table, values, preferred_element_type=F32)
    return out.reshape(values.shape[0], 2, freq_total, values.shape[2]).astype(BF16)


def spectra_into_samples(trace_spectra, inverse_table):
    flat = trace_spectra.reshape(trace_spectra.shape[0], -1, trace_spectra.shape[3])
    return jnp.einsum("tk,pkn->ptn", inverse_table, flat, preferred_element_type=F32)


def dense(spec, gated, real, imag, sign):
    dot = functools.partial(jnp.einsum, spec, preferred_element_type=F32)
    return jnp.stack(
        [dot(gated[:, 0], real) - sign * dot(gated[:, 1], imag), dot(gated[:, 0], imag) + sign * dot(gated[:, 1], real)], 1
    )


def general_device(initial, response, aperture, onset_rcv, onset_src):
    freq_devs, rblk_devs, sblk_devs = (lax.axis_size(a) for a in ("freq", "rblk", "sblk"))
    freq_index, rblk_index, sblk_index = (lax.axis_index(a) for a in ("freq", "rblk", "sblk"))
    freq_total = response.shape[0] * freq_devs
    samples = initial.shape[1] * freq_devs
    focal_all = onset_rcv.shape[0]
    forward_table, inverse_table = transform_tables(samples, freq_total)
    steps_axis = lax.iota(jnp.int32, samples)
    own_axis = freq_index * initial.shape[1] + lax.iota(jnp.int32, initial.shape[1])
    half_rows = focal_all // sblk_devs
    own_onsets = lax.dynamic_slice_in_dim(onset_rcv, sblk_index * half_rows, half_rows, 0)
    rcv_gate = (own_axis[None, :, None] < own_onsets[:, None, :]).astype(F32)
    src_rows = focal_all // (rblk_devs * freq_devs)
    src_first = rblk_index * (focal_all // rblk_devs) + freq_index * src_rows
    src_onsets = lax.dynamic_slice_in_dim(onset_src, src_first, src_rows, 0)
    src_gate = (steps_axis[None, :, None] < src_onsets[:, None, :]).astype(F32)
    mask_full = jnp.repeat(jnp.repeat(aperture, BLOCK, 1), BLOCK, 2).astype(BF16)
    gated = response * mask_full[:, None]
    own_forward = lax.dynamic_slice_in_dim(forward_table, freq_index * initial.shape[1], initial.shape[1], 1)
    own_inverse = lax.dynamic_slice_in_dim(inverse_table, freq_index * initial.shape[1], initial.shape[1], 0)
    current = initial
    for _ in range(ITERS):
        partial = samples_into_spectra(current, own_forward, freq_total)
        spec_back = lax.psum_scatter(partial.astype(F32), "freq", scatter_dimension=2, tiled=True).astype(BF16)
        spec_all = lax.all_gather(spec_back, "sblk", axis=0, tiled=True)
        down = lax.psum_scatter(
            settle(dense("euk,bek->beu", gated, spec_all[:, 0], spec_all[:, 1], 1.0)).astype(BF16),
            "rblk",
            scatter_dimension=0,
            tiled=True,
        )
        src_traces = lax.all_to_all(down, "freq", split_axis=0, concat_axis=2, tiled=True)
        upgoing = (src_gate * spectra_into_samples(src_traces, inverse_table)).astype(BF16)
        upspec = samples_into_spectra(upgoing, forward_table, freq_total)
        up_back = lax.all_to_all(upspec, "freq", split_axis=2, concat_axis=0, tiled=True)
        up_all = lax.all_gather(up_back, "rblk", axis=0, tiled=True)
        sums = dense("qao,bqa->bqo", gated, up_all[:, 0], up_all[:, 1], -1.0).astype(BF16)
        back = lax.psum_scatter(sums, "sblk", scatter_dimension=0, tiled=True)
        traces = lax.all_gather(back, "freq", axis=2, tiled=True)
        update = rcv_gate * spectra_into_samples(traces, own_inverse)
        current = (initial.astype(F32) - update).astype(BF16)
    return current


def fits(initial, response, aperture, onset_rcv, onset_src):
    freq_devs = lax.axis_size("freq")
    if lax.axis_size("rblk") != 2 or lax.axis_size("sblk") != 2 or freq_devs & (freq_devs - 1):
        return False
    whole_rows = initial.shape[0] % (max(2, CHUNKS) * ROWS * freq_devs) == 0
    whole_width = response.shape[2] % (2 * PARTS * BLOCK) == 0 and response.shape[3] % BLOCK == 0
    return whole_rows and whole_width and onset_rcv.shape[0] == 2 * initial.shape[0]


def chosen(*arrays):
    return on_device(*arrays) if fits(*arrays) else general_device(*arrays)


def solution(mesh):
    in_specs = (
        P(("group", "sblk"), "freq", "rblk"),
        P(("group", "freq"), None, "sblk", "rblk"),
        P(("group", "freq"), "sblk", "rblk"),
        P("group", "rblk"),
        P("group", "sblk"),
    )
    out_specs = P(("group", "sblk"), "freq", "rblk")
    return jax.shard_map(chosen, mesh=mesh, in_specs=in_specs, out_specs=out_specs, check_vma=False)
```
